32 devices in a mesh: grp: 16 (over z, y, x), exp: 2 (over core).
Axes of the slice: x: 2, y: 2, z: 4, core: 2. Of those that a mesh axis runs over, the one named last changes fastest.
Arguments:
- tokens: bfloat16 [64, 512, 768], P(('grp', 'exp')), may hold values from -6 to 6
- lengths: int32 [64], P(('grp', 'exp')), may hold values from 1 to 512, 22937 in all
- expert_ids: int32 [64, 512], P(('grp', 'exp')), may hold values from 0 to 31, as said below
- slots: int32 [64, 512], P(('grp', 'exp')), may hold values from -1 to 1279, as said below
- w_query: bfloat16 [768, 768], replicated, may hold values from -0.3125 to 0.3125
- w_key: bfloat16 [768, 768], replicated, may hold values from -0.3125 to 0.3125
- w_value: bfloat16 [768, 768], replicated, may hold values from -0.21875 to 0.21875
- w_output: bfloat16 [768, 768], replicated, may hold values from -0.875 to 0.875
- gain_attn: float32 [768], replicated, may hold values from 0.5 to 1.5
- gain_ffn: float32 [768], replicated, may hold values from 0.5 to 1.5
- bias_table: float32 [32, 12], replicated, may hold values from -4 to 4
- w_router: bfloat16 [768, 32], replicated, may hold values from -0.109375 to 0.109375
- w_in: bfloat16 [32, 768, 3072], P(('grp', 'exp')), may hold values from -0.4375 to 0.4375
- w_out: bfloat16 [32, 3072, 768], P(('grp', 'exp')), may hold values from -3 to 3
- cotangent: bfloat16 [64, 512, 768], P(('grp', 'exp')), may hold values from -6 to 6
Outputs:
- mixed: bfloat16 [64, 512, 768], P(('grp', 'exp'))
- grad_tokens: float32 [64, 512, 768], P(('grp', 'exp'))
- grad_query: float32 [768, 768], replicated
- grad_key: float32 [768, 768], replicated
- grad_value: float32 [768, 768], replicated
- grad_output: float32 [768, 768], replicated
- grad_gain_attn: float32 [768], replicated
- grad_gain_ffn: float32 [768], replicated
- grad_bias_table: float32 [32, 12], replicated
- grad_router: float32 [768, 32], replicated
- grad_in: float32 [32, 768, 3072], P(('grp', 'exp'))
- grad_out: float32 [32, 3072, 768], P(('grp', 'exp'))
The draws below stay inside these ranges and needn't reach their ends.
Inputs may be any that keep to these rules, and one draw needn't show every extreme that they name: `expert_ids`: at most 64 of one device's 1024 tokens name one expert; in every draw one expert is named by exactly 64 tokens of every device. `slots`: a token's slot is the number of earlier tokens (rows in order, then positions) with the same expert, or -1 where that number is 1280 or more; every draw drops some tokens.
All inputs are finite; a program needn't handle non-finite values. No bound on the sum of `lengths` on one device may be relied on, other than what follows from the above.
Results may differ from the reference program's by a relative error of at most 0.02.
Values may be sent and summed in bfloat16 or wider, within the bound.
A program may use at most 320 MiB of HBM per device.

```python
import math
import jax
import jax.numpy as jnp
import numpy as np
from jax import lax

D = 768
HEADS = 12
HEAD_DIM = 64
FF = 3072
BUCKETS = 32
SEQ = 512
SEQ_DEV = 2
SEQS = 64
TOKENS = 32768
EXPERTS = 32
C_SRC = 64
CAP = 1280


def route_table(key):
    devices = SEQS // SEQ_DEV
    per_device = SEQ_DEV * SEQ
    pool_size = EXPERTS * C_SRC
    hot_expert = jax.random.randint(jax.random.fold_in(key, 11), (), 0, EXPERTS)
    pool_ids = jnp.arange(pool_size, dtype=jnp.int32) // C_SRC
    ranks_all = jnp.arange(pool_size, dtype=jnp.int32)
    noise_ints = jax.random.randint(jax.random.fold_in(key, 12), (devices, pool_size), 0, 65536)
    priority = jnp.where(pool_ids[None, :] == hot_expert, ranks_all[None, :], (noise_ints + 1) * pool_size + ranks_all[None, :])
    order_idx = jnp.argsort(priority, axis=1)[:, :per_device]
    chosen = pool_ids[order_idx]
    shuffle_ints = jax.random.randint(jax.random.fold_in(key, 13), (devices, per_device), 0, 65536)
    shuffle_ints = shuffle_ints * per_device + jnp.arange(per_device, dtype=jnp.int32)[None, :]
    shuffle_idx = jnp.argsort(shuffle_ints, axis=1)
    chosen = jnp.take_along_axis(chosen, shuffle_idx, axis=1)
    return chosen.reshape(SEQS, SEQ).astype(jnp.int32)


def draw_expert_ids(key, part):
    route_ids = route_table(key)
    return route_ids


def draw_slots(key, part):
    route_ids = route_table(key).reshape(-1)
    hit_table = (route_ids[:, None] == jnp.arange(EXPERTS, dtype=jnp.int32)[None, :]).astype(jnp.int32)
    earlier = jnp.cumsum(hit_table, axis=0) - hit_table
    rank_all = jnp.sum(earlier * hit_table, axis=1)
    return jnp.where(rank_all < CAP, rank_all, -1).reshape(SEQS, SEQ).astype(jnp.int32)


def shard_levels(own_key, extent, shards, smallest, largest):
    def one(dim, parts):
        steps = jax.random.uniform(jax.random.fold_in(jax.random.fold_in(own_key, 6), dim), (parts,), jnp.float32, smallest / len(shards), largest / len(shards))
        return jnp.repeat(jnp.exp(steps), extent[dim] // parts).reshape((-1,) + (1,) * (len(extent) - dim - 1))

    level = one(*shards[0])
    for cut in shards[1:]:
        level = level * one(*cut)
    return level


def split_up(count, total, most, lean):
    portions = [(1 << 20) // math.isqrt(grade ** lean) + 1 for grade in range(2, count + 1)]
    surplus, counts = total - most - (count - 1), [1] * (count - 1)
    while surplus > 0:
        movable = [i for i in range(count - 1) if counts[i] < most]
        pool, left = sum([portions[i] for i in movable]), surplus
        for i in movable:
            more = min(most - counts[i], max(1, left * portions[i] // pool), surplus)
            counts[i] = counts[i] + more
            surplus = surplus - more
    return np.array([most] + counts)


def ragged(stream_key, count, total, reach, slope):
    if count == 2:
        one = jax.random.randint(stream_key, (), max(1, total - reach), min(reach, total - 1) + 1)
        return jnp.stack([one, total - one])
    sizes = jnp.asarray(split_up(count, total, reach, slope), jnp.int32)
    twos = (count - 1) // 2
    source_of, receiver = sizes[1:1 + 2 * twos:2], sizes[2:2 + 2 * twos:2]
    slack = jnp.minimum(source_of - 1, reach - receiver)
    passed = jax.random.randint(jax.random.fold_in(stream_key, 1), (twos,), 0, 1 << 20) % (slack + 1)
    sizes = sizes.at[1:1 + 2 * twos:2].set(source_of - passed).at[2:2 + 2 * twos:2].set(receiver + passed)
    return sizes[jax.random.permutation(jax.random.fold_in(stream_key, 2), count)]


def scatter_about(rng, extent, deviation, reach, split=(), held_as=jnp.bfloat16):
    values = deviation * jax.random.normal(rng, extent, jnp.float32)
    if split:
        values = values * shard_levels(rng, extent, split, -0.22, 0.18)
    return jnp.clip(values, -reach, reach).astype(held_as)


def setup_inputs(seed: int = 0) -> dict:
    seeds = jax.random.split(jax.random.key(seed), 16)
    tokens = scatter_about(seeds[0], (SEQS, SEQ, D), 1.0, 6.0, ((0, 32),))
    lengths = ragged(seeds[1], SEQS, SEQS * SEQ * 7 // 10, SEQ, 2).astype(jnp.int32)
    expert_ids = draw_expert_ids(jax.random.fold_in(seeds[15], 71), 0)
    slots = draw_slots(jax.random.fold_in(seeds[15], 71), 0)
    w_query = scatter_about(seeds[4], (D, D), (D // 2) ** -0.5, 0.3125)
    w_key = scatter_about(seeds[5], (D, D), (D // 2) ** -0.5, 0.3125)
    w_value = scatter_about(seeds[6], (D, D), D ** -0.5, 0.21875)
    w_output = scatter_about(seeds[7], (D, D), (D // 16) ** -0.5, 0.875)
    gain_attn = jnp.clip(1.0 + 0.1 * jax.random.normal(seeds[8], (D,), jnp.float32), 0.5, 1.5)
    gain_ffn = jnp.clip(1.0 + 0.1 * jax.random.normal(seeds[9], (D,), jnp.float32), 0.5, 1.5)
    bias_table = scatter_about(seeds[10], (BUCKETS, HEADS), 1.0, 4.0, (), jnp.float32)
    w_router = scatter_about(seeds[11], (D, EXPERTS), (4 * D) ** -0.5, 0.109375)
    w_in = scatter_about(seeds[12], (EXPERTS, D, FF), (D // 4) ** -0.5, 0.4375, ((0, 32),))
    w_out = scatter_about(seeds[13], (EXPERTS, FF, D), (max(1, 4096 // (EXPERTS * EXPERTS))) ** -0.5, 3.0, ((0, 32),))
    cotangent = scatter_about(seeds[14], (SEQS, SEQ, D), 1.0, 6.0, ((0, 32),))
    return dict(tokens=tokens, lengths=lengths, expert_ids=expert_ids, slots=slots, w_query=w_query, w_key=w_key, w_value=w_value, w_output=w_output, gain_attn=gain_attn, gain_ffn=gain_ffn, bias_table=bias_table, w_router=w_router, w_in=w_in, w_out=w_out, cotangent=cotangent)


@jax.custom_vjp
def low(v):
    return lax.optimization_barrier(v.astype(jnp.bfloat16)).astype(jnp.float32)

@jax.custom_vjp
def low_back(v):
    return v

def low_keep(v):
    return (low(v), None)

def low_pass(kept, grad):
    return (grad,)

def back_keep(v):
    return (v, None)

def back_low(kept, grad):
    return (low(grad),)
low.defvjp(low_keep, low_pass)
low_back.defvjp(back_keep, back_low)
EPSILON = 1e-06
NEGATIVE = -1e+30
THRESHOLDS = (12, 16, 23, 32, 46, 64, 91)

def bucket_table(length):
    positions = jnp.arange(length, dtype=jnp.int32)
    offset = positions[None, :] - positions[:, None]
    distance = jnp.abs(offset)
    far_bucket = jnp.full_like(distance, 8)
    for border in THRESHOLDS:
        far_bucket = far_bucket + (distance >= border).astype(jnp.int32)
    return jnp.where(distance < 8, distance, far_bucket) + jnp.where(offset > 0, 16, 0).astype(jnp.int32)

def reference(tokens, lengths, expert_ids, slots, w_query, w_key, w_value, w_output, gain_attn, gain_ffn, bias_table, w_router, w_in, w_out, cotangent):
    highest = lax.Precision.HIGHEST
    buckets = bucket_table(SEQ)
    one_hot = (buckets[:, :, None] == jnp.arange(BUCKETS, dtype=jnp.int32)[None, None, :]).astype(jnp.float32)
    group = math.gcd(SEQS, max(1, 4096 // SEQ))
    blocks = SEQS // group
    key_mask = (jnp.arange(SEQ, dtype=jnp.int32)[None, :] < lengths[:, None]).reshape(blocks, group, SEQ)
    flat_expert = expert_ids.reshape(-1).astype(jnp.int32)
    flat_slot = slots.reshape(-1).astype(jnp.int32)
    dest_index = jnp.where(flat_slot >= 0, flat_expert * CAP + flat_slot, EXPERTS * CAP).astype(jnp.int32)

    def forward(inputs, query_w, key_w, value_w, out_w, gain_one, gain_two, table_w, router_w, inner_w, outer_w):
        rms_one = lax.rsqrt(lax.optimization_barrier(jnp.mean(inputs * inputs, axis=-1, keepdims=True)) + EPSILON)
        normed = low(inputs * rms_one * gain_one)
        bias_all = jnp.einsum('qkn,nh->hqk', one_hot, table_w, precision=highest)

        def block(carry, pieces):
            rows_in, mask_rows = pieces

            def project(weight):
                made = jnp.einsum('gsd,de->gse', rows_in, weight, precision=highest)
                return low(low_back(made)).reshape(group, SEQ, HEADS, HEAD_DIM)
            queries = project(query_w)
            key_rows = project(key_w)
            value_rows = project(value_w)
            scores = jnp.einsum('gqhd,gkhd->ghqk', queries, key_rows, precision=highest) * 0.125 + bias_all[None]
            scores = low_back(jnp.where(mask_rows[:, None, None, :], scores, NEGATIVE))
            weights = jax.nn.softmax(scores, axis=-1)
            mixed_heads = jnp.einsum('ghqk,gkhd->gqhd', low(weights), value_rows, precision=highest)
            joined = low(low_back(mixed_heads.reshape(group, SEQ, D)))
            return (carry, low_back(jnp.einsum('gsd,de->gse', joined, out_w, precision=highest)))
        start = jnp.zeros((), jnp.float32)
        _, attended = lax.scan(jax.checkpoint(block), start, (normed.reshape(blocks, group, SEQ, D), key_mask))
        resid = inputs + attended.reshape(SEQS, SEQ, D)
        rms_two = lax.rsqrt(lax.optimization_barrier(jnp.mean(resid * resid, axis=-1, keepdims=True)) + EPSILON)
        normed_two = low(resid * rms_two * gain_two).reshape(TOKENS, D)
        logits = low_back(jnp.dot(normed_two, router_w, precision=highest))
        router = jax.nn.softmax(logits, axis=-1)
        gate = jnp.take_along_axis(router, flat_expert[:, None], axis=1)[:, 0]
        expert_in = low_back(normed_two)
        buffer = jnp.zeros((EXPERTS * CAP, D), jnp.float32).at[dest_index].set(expert_in, mode='drop')
        buffer = buffer.reshape(EXPERTS, CAP, D)

        def one_expert(pieces):
            rows_e, first_w, second_w = pieces
            inner = low_back(jnp.dot(rows_e, first_w, precision=highest))
            hidden = low(jax.nn.gelu(inner))
            return low(low_back(jnp.dot(hidden, second_w, precision=highest)))
        finished = lax.map(jax.checkpoint(one_expert), (buffer, inner_w, outer_w)).reshape(EXPERTS * CAP, D)
        ff_tok = jnp.take(finished, dest_index, axis=0, mode='fill', fill_value=0.0)
        result = resid.reshape(TOKENS, D) + gate[:, None] * ff_tok
        return result.reshape(SEQS, SEQ, D)
    primal = (tokens.astype(jnp.float32), w_query.astype(jnp.float32), w_key.astype(jnp.float32), w_value.astype(jnp.float32), w_output.astype(jnp.float32), gain_attn, gain_ffn, bias_table, w_router.astype(jnp.float32), w_in.astype(jnp.float32), w_out.astype(jnp.float32))
    output, pullback = jax.vjp(forward, *primal)
    grads = pullback(cotangent.astype(jnp.float32))
    return (output.astype(jnp.bfloat16), grads[0], grads[1], grads[2], grads[3], grads[4], grads[5], grads[6], grads[7], grads[8], grads[9], grads[10])
```

```python
import functools

import jax
import jax.numpy as jnp
from jax import lax
from jax.experimental import pallas as pl
from jax.experimental.pallas import tpu as pltpu
from jax.sharding import PartitionSpec as P

EPSILON = 1e-06
NEGATIVE = -1e30
THRESHOLDS = (12, 16, 23, 32, 46, 64, 91)
LOG2E = 1.4426950408889634
TILE = 128
GELU_A = 0.7978845608028654
GELU_B = GELU_A * 0.044715
AXES = ("grp", "exp")
LOW = jnp.bfloat16


def dot(a, b):
    return jnp.dot(a, b, preferred_element_type=jnp.float32)


def dot_t(a, b):
    return lax.dot_general(a, b, (((1,), (1,)), ((), ())), preferred_element_type=jnp.float32)


def params(mib, **more):
    return pltpu.CompilerParams(vmem_limit_bytes=mib << 20, **more)


def whole(shape):
    return pl.BlockSpec(shape, lambda *_: (0,) * len(shape), pipeline_mode=pl.Buffered(1))


def cost(flops, bytes_accessed, transcendentals=0):
    return pl.CostEstimate(
        flops=flops, bytes_accessed=bytes_accessed, transcendentals=transcendentals
    )


def bucket_of(offset):
    distance = jnp.abs(offset)
    far = jnp.full_like(distance, 8)
    for border in THRESHOLDS:
        far = far + (distance >= border).astype(jnp.int32)
    return jnp.where(distance < 8, distance, far) + jnp.where(offset > 0, 16, 0).astype(jnp.int32)


def route_kernel(experts, room, eid_c, eid_r, slot_c, slot_r, g_ref, dest_c, dest_r, g_out):
    tokens = g_ref.shape[0]
    wide = max(128, experts)
    at = lax.broadcasted_iota(jnp.int32, (tokens, tokens), 0)
    to = lax.broadcasted_iota(jnp.int32, (tokens, tokens), 1)
    ids = eid_c[...]
    picked = ids == lax.broadcasted_iota(jnp.int32, (tokens, wide), 1)
    earlier = dot((to < at).astype(LOW), picked.astype(LOW))
    place = jnp.sum(jnp.where(picked, earlier, 0.0), axis=1, keepdims=True).astype(jnp.int32)
    dest_c[...] = jnp.where(slot_c[...] >= 0, ids * room + place, -1)
    ids = eid_r[...]
    picked = ids == lax.broadcasted_iota(jnp.int32, (wide, tokens), 0)
    earlier = dot(picked.astype(LOW), (at < to).astype(LOW))
    place = jnp.sum(jnp.where(picked, earlier, 0.0), axis=0, keepdims=True).astype(jnp.int32)
    dest = jnp.where(slot_r[...] >= 0, ids * room + place, -1)
    dest_r[...] = dest
    spread(dest, g_ref[...], g_out)


def spread(dest, values, out):
    rows = out.shape[0]
    step = 256
    for start in range(0, rows, step):
        here = lax.broadcasted_iota(jnp.int32, (step, dest.shape[1]), 0) + start
        out[start : start + step] = dot((dest == here).astype(LOW), values).astype(LOW)


def collect(dest, values):
    rows = values.shape[0]
    here = lax.broadcasted_iota(jnp.int32, (dest.shape[0], rows), 1)
    return dot((dest == here).astype(LOW), values)


def route(expert_ids, slots, upstream, experts, room):
    tokens, width = upstream.shape
    flat = lambda a, shape: a.reshape(shape)
    return pl.pallas_call(
        functools.partial(route_kernel, experts, room),
        out_shape=[
            jax.ShapeDtypeStruct((tokens, 1), jnp.int32),
            jax.ShapeDtypeStruct((1, tokens), jnp.int32),
            jax.ShapeDtypeStruct((experts * room, width), LOW),
        ],
        compiler_params=params(48),
        cost_estimate=cost(2 * experts * room * tokens * width, 8 << 20),
        name="route",
    )(
        flat(expert_ids, (tokens, 1)),
        flat(expert_ids, (1, tokens)),
        flat(slots, (tokens, 1)),
        flat(slots, (1, tokens)),
        upstream,
    )


def exchange(buffer, devices):
    shaped = buffer.reshape(devices, buffer.shape[0] // devices, buffer.shape[1])
    moved = lax.all_to_all(shaped, AXES, split_axis=0, concat_axis=0, tiled=True)
    return moved.reshape(buffer.shape)


def project_kernel(x_ref, gain_ref, w_ref, normed_ref, out_ref):
    x = x_ref[...].astype(jnp.float32)
    rms = lax.rsqrt(jnp.mean(x * x, axis=-1, keepdims=True) + EPSILON)
    normed = (x * rms * gain_ref[...]).astype(LOW)
    normed_ref[...] = normed
    out_ref[...] = dot(normed, w_ref[...]).astype(LOW)


def project(x, gain, w_qkv):
    tokens, width = x.shape
    out = w_qkv.shape[1]
    step = 256
    rows = lambda w: pl.BlockSpec((step, w), lambda i: (i, 0))
    return pl.pallas_call(
        project_kernel,
        grid=(tokens // step,),
        in_specs=[rows(width), whole((1, width)), whole((width, out))],
        out_specs=[rows(width), rows(out)],
        out_shape=[
            jax.ShapeDtypeStruct((tokens, width), LOW),
            jax.ShapeDtypeStruct((tokens, out), LOW),
        ],
        compiler_params=params(40),
        cost_estimate=cost(2 * tokens * width * out, 12 << 20),
        name="project",
    )(x, gain, w_qkv)


def after_attention_kernel(o_ref, x_ref, w_ref, gain_ref, dest_ref, y_ref, out_ref, held):
    step = o_ref.shape[0]
    i = pl.program_id(0)
    y = x_ref[...].astype(jnp.float32) + dot(o_ref[...], w_ref[...])
    y_ref[...] = y
    rms = lax.rsqrt(jnp.mean(y * y, axis=-1, keepdims=True) + EPSILON)
    held[pl.ds(pl.multiple_of(i * step, step), step), :] = (y * rms * gain_ref[...]).astype(LOW)

    @pl.when(i == pl.num_programs(0) - 1)
    def _():
        spread(dest_ref[...], held[...], out_ref)


def after_attention(joined, x, w_output, gain, dest_r, rows_out):
    tokens, width = x.shape
    step = 256
    rows = pl.BlockSpec((step, width), lambda i: (i, 0))
    return pl.pallas_call(
        after_attention_kernel,
        grid=(tokens // step,),
        in_specs=[rows, rows, whole((width, width)), whole((1, width)), whole((1, tokens))],
        out_specs=[rows, pl.BlockSpec((rows_out, width), lambda i: (0, 0))],
        out_shape=[
            jax.ShapeDtypeStruct((tokens, width), jnp.float32),
            jax.ShapeDtypeStruct((rows_out, width), LOW),
        ],
        scratch_shapes=[pltpu.VMEM((tokens, width), LOW)],
        compiler_params=params(48),
        cost_estimate=cost(2 * tokens * width * (width + rows_out), 12 << 20),
        name="after_attention",
    )(joined, x, w_output, gain, dest_r)


def mix_kernel(experts, ff_ref, dest_ref, eid_ref, y_ref, gain_ref, wr_ref, out_ref):
    y = y_ref[...]
    rms = lax.rsqrt(jnp.mean(y * y, axis=-1, keepdims=True) + EPSILON)
    normed = (y * rms * gain_ref[...]).astype(LOW)
    router = route_softmax(dot(normed, wr_ref[...]), experts)
    lane = lax.broadcasted_iota(jnp.int32, router.shape, 1)
    gate = jnp.sum(jnp.where(lane == eid_ref[...], router, 0.0), axis=-1, keepdims=True)
    out_ref[...] = (y + gate * collect(dest_ref[...], ff_ref[...])).astype(LOW)


def route_softmax(logits, experts):
    lane = lax.broadcasted_iota(jnp.int32, logits.shape, 1)
    logits = jnp.where(lane < experts, logits, NEGATIVE)
    e = jnp.exp(logits - jnp.max(logits, axis=-1, keepdims=True))
    return e / jnp.sum(e, axis=-1, keepdims=True)


def mix(ff, dest_c, expert_ids, y, gain, w_router, experts):
    tokens, width = y.shape
    step = 256
    rows = lambda w: pl.BlockSpec((step, w), lambda i: (i, 0))
    return pl.pallas_call(
        functools.partial(mix_kernel, experts),
        grid=(tokens // step,),
        in_specs=[whole(ff.shape), rows(1), rows(1), rows(width), whole((1, width)), whole(w_router.shape)],
        out_specs=rows(width),
        out_shape=jax.ShapeDtypeStruct((tokens, width), LOW),
        compiler_params=params(40),
        cost_estimate=cost(2 * tokens * width * ff.shape[0], 8 << 20),
        name="mix",
    )(ff, dest_c, expert_ids.reshape(tokens, 1), y, gain, w_router)


def before_attention_kernel(
    dh_ref, dest_ref, y_ref, g_ref, gain_ref, wt_ref, o_ref, dy_ref, do_ref, gw_ref, gg_ref
):
    i = pl.program_id(0)

    @pl.when(i == 0)
    def _():
        gw_ref[...] = jnp.zeros_like(gw_ref)
        gg_ref[...] = jnp.zeros_like(gg_ref)

    dh = collect(dest_ref[...], dh_ref[...])
    y = y_ref[...]
    rms = lax.rsqrt(jnp.mean(y * y, axis=-1, keepdims=True) + EPSILON)
    gg_ref[...] += jnp.sum(dh * y * rms, axis=0, keepdims=True)
    u = dh * gain_ref[...]
    dy = (
        g_ref[...].astype(jnp.float32)
        + rms * u
        - y * (rms * rms * rms) * jnp.mean(u * y, axis=-1, keepdims=True)
    )
    dy_ref[...] = dy
    low = dy.astype(LOW)
    do_ref[...] = dot(low, wt_ref[...]).astype(LOW)
    gw_ref[...] += dot(o_ref[...].T, low)


def before_attention(dh, dest_c, y, g, gain, w_output_t, joined):
    tokens, width = y.shape
    step = 256
    rows = lambda w: pl.BlockSpec((step, w), lambda i: (i, 0))
    return pl.pallas_call(
        before_attention_kernel,
        grid=(tokens // step,),
        in_specs=[
            whole(dh.shape), rows(1), rows(width), rows(width), whole((1, width)),
            whole((width, width)), rows(width),
        ],
        out_specs=[
            rows(width), rows(width),
            pl.BlockSpec((width, width), lambda i: (0, 0)),
            pl.BlockSpec((1, width), lambda i: (0, 0)),
        ],
        out_shape=[
            jax.ShapeDtypeStruct((tokens, width), jnp.float32),
            jax.ShapeDtypeStruct((tokens, width), LOW),
            jax.ShapeDtypeStruct((width, width), jnp.float32),
            jax.ShapeDtypeStruct((1, width), jnp.float32),
        ],
        compiler_params=params(40),
        cost_estimate=cost(2 * tokens * width * (dh.shape[0] + 2 * width), 16 << 20),
        name="before_attention",
    )(dh, dest_c, y, g, gain, w_output_t, joined)


def finish_kernel(
    dq_ref, dk_ref, dv_ref, wt_ref, normed_ref, x_ref, dy_ref, gain_ref, out_ref, gw_ref, gg_ref
):
    i = pl.program_id(0)

    @pl.when(i == 0)
    def _():
        gw_ref[...] = jnp.zeros_like(gw_ref)
        gg_ref[...] = jnp.zeros_like(gg_ref)

    width = x_ref.shape[1]
    grads = (dq_ref[...], dk_ref[...], dv_ref[...])
    normed_t = normed_ref[...].T
    dh = None
    for n, d in enumerate(grads):
        gw_ref[n * width : (n + 1) * width] += dot(normed_t, d)
        part = dot(d, wt_ref[n * width : (n + 1) * width])
        dh = part if dh is None else dh + part
    x = x_ref[...].astype(jnp.float32)
    rms = lax.rsqrt(jnp.mean(x * x, axis=-1, keepdims=True) + EPSILON)
    gg_ref[...] += jnp.sum(dh * x * rms, axis=0, keepdims=True)
    u = dh * gain_ref[...]
    out_ref[...] = (
        dy_ref[...]
        + rms * u
        - x * (rms * rms * rms) * jnp.mean(u * x, axis=-1, keepdims=True)
    )


def finish(dq, dk, dv, w_qkv_t, normed, x, dy, gain):
    tokens, width = x.shape
    step = 256
    rows = pl.BlockSpec((step, width), lambda i: (i, 0))
    return pl.pallas_call(
        finish_kernel,
        grid=(tokens // step,),
        in_specs=[rows, rows, rows, whole((3 * width, width)), rows, rows, rows, whole((1, width))],
        out_specs=[
            rows,
            pl.BlockSpec((3 * width, width), lambda i: (0, 0)),
            pl.BlockSpec((1, width), lambda i: (0, 0)),
        ],
        out_shape=[
            jax.ShapeDtypeStruct((tokens, width), jnp.float32),
            jax.ShapeDtypeStruct((3 * width, width), jnp.float32),
            jax.ShapeDtypeStruct((1, width), jnp.float32),
        ],
        compiler_params=params(48),
        cost_estimate=cost(12 * tokens * width * width, 24 << 20),
        name="finish",
    )(dq, dk, dv, w_qkv_t, normed, x, dy, gain)


def attention_forward_kernel(len_ref, q_ref, k_ref, v_ref, near_ref, far_ref, o_ref, p_ref, s_ref):
    seq = q_ref.shape[0]
    tiles = seq // TILE
    half = q_ref.shape[1] // 2
    row = pl.program_id(0)
    pair = pl.program_id(1)
    live = len_ref[row]
    lane = lax.broadcasted_iota(jnp.int32, (seq, 2 * half), 1)
    dead = lax.broadcasted_iota(jnp.int32, (seq, 2 * half), 0) >= live
    q = q_ref[...]
    k = k_ref[...]
    v_t = v_ref[...].T
    outs = []
    for h in range(2):
        mine = (lane >= h * half) & (lane < (h + 1) * half)
        flag = lane == (1 - h) * half
        k_h = jnp.where(mine, k, jnp.where(flag & dead, -1e30, 0.0).astype(k.dtype))
        q_h = jnp.where(flag, jnp.ones_like(q), q)
        after = far_ref[2 * pair + h, 0]
        before = far_ref[2 * pair + h, 1]
        tops = []
        for i in range(tiles):
            q_i = q_h[i * TILE:(i + 1) * TILE]
            raw = lax.dot_general(k_h, q_i, (((1,), (1,)), ((), ())), preferred_element_type=jnp.float32)
            top = None
            for j in range(tiles):
                x = raw[j * TILE:(j + 1) * TILE] * (0.125 * LOG2E)
                d = j - i
                if -1 <= d <= 1:
                    x = x + near_ref[h, d + 1]
                else:
                    x = x + (after if d > 0 else before)
                s_ref[j * TILE:(j + 1) * TILE, i * TILE:(i + 1) * TILE] = x
                m = jnp.max(x, axis=0, keepdims=True)
                top = m if top is None else jnp.maximum(top, m)
            tops.append(top)
        for i in range(tiles):
            e = jnp.exp2(s_ref[:, i * TILE:(i + 1) * TILE] - tops[i])
            total = jnp.sum(e, axis=0, keepdims=True)
            p_ref[0, h, :, i * TILE:(i + 1) * TILE] = (e * (1.0 / total)).astype(LOW)
        outs.append(lax.dot_general(v_t[h * half:(h + 1) * half], p_ref[0, h], (((1,), (0,)), ((), ())), preferred_element_type=jnp.float32))
    o_ref[...] = jnp.concatenate(outs, axis=0).T.astype(o_ref.dtype)

def attention_forward(lengths, projected, near, far, rows, seq, heads, head):
    width = heads * head
    pairs = heads // 2
    spec = lambda off: pl.BlockSpec((seq, 2 * head), lambda b, p: (b, off + p))
    return pl.pallas_call(
        attention_forward_kernel,
        grid=(rows, pairs),
        in_specs=[
            pl.BlockSpec(memory_space=pltpu.SMEM),
            spec(0), spec(pairs), spec(2 * pairs),
            pl.BlockSpec((2, 3, TILE, TILE), lambda b, p: (p, 0, 0, 0)),
            pl.BlockSpec(memory_space=pltpu.SMEM),
        ],
        out_specs=[
            pl.BlockSpec((seq, 2 * head), lambda b, p: (b, p)),
            pl.BlockSpec((1, 2, seq, seq), lambda b, p: (b, p, 0, 0)),
        ],
        out_shape=[
            jax.ShapeDtypeStruct((rows * seq, width), LOW),
            jax.ShapeDtypeStruct((rows, heads, seq, seq), LOW),
        ],
        scratch_shapes=[pltpu.VMEM((seq, seq), jnp.float32)],
        compiler_params=params(40),
        cost_estimate=cost(flops=4 * rows * heads * seq * seq * head * 4, bytes_accessed=rows * heads * seq * seq * 2, transcendentals=rows * heads * seq * seq),
        name="attention_forward",
    )(lengths, projected, projected, projected, near, far)

def attention_backward_kernel(q_ref, k_ref, v_ref, do_ref, o_ref, p_ref, dq_ref, dk_ref, dv_ref, near_ref, far_ref, d_ref):
    seq = q_ref.shape[0]
    tiles = seq // TILE
    half = q_ref.shape[1] // 2
    row = pl.program_id(1)
    lane = lax.broadcasted_iota(jnp.int32, (seq, 2 * half), 1)
    q = q_ref[...]
    k = k_ref[...]
    k_t = k.T
    v = v_ref[...]
    do = do_ref[...]
    weighed = (do.astype(jnp.float32) * o_ref[...].astype(jnp.float32)).T
    dq_parts = []
    dk_all = None
    dv_all = None

    @pl.when(row == 0)
    def _():
        near_ref[...] = jnp.zeros_like(near_ref)
        far_ref[...] = jnp.zeros_like(far_ref)

    for h in range(2):
        mine = (lane >= h * half) & (lane < (h + 1) * half)
        v_h = jnp.where(mine, v, jnp.zeros_like(v))
        delta = jnp.sum(weighed[h * half:(h + 1) * half], axis=0, keepdims=True)
        far_sum = [jnp.zeros((8, TILE), jnp.float32), jnp.zeros((8, TILE), jnp.float32)]
        for i in range(tiles):
            cols = slice(i * TILE, (i + 1) * TILE)
            dp = lax.dot_general(v_h, do[cols], (((1,), (1,)), ((), ())), preferred_element_type=jnp.float32)
            for j in range(tiles):
                rws = slice(j * TILE, (j + 1) * TILE)
                ds = p_ref[0, h, rws, cols].astype(jnp.float32) * (dp[rws] - delta[:, cols])
                d = j - i
                if -1 <= d <= 1:
                    near_ref[h, d + 1] += ds
                else:
                    which = 0 if d > 0 else 1
                    far_sum[which] = far_sum[which] + jnp.sum(ds.reshape(TILE // 8, 8, TILE), axis=0)
                d_ref[rws, cols] = ds.astype(LOW)
        far_ref[h, 0] += far_sum[0]
        far_ref[h, 1] += far_sum[1]
        ds_all = d_ref[...]
        dq_parts.append(lax.dot_general(k_t[h * half:(h + 1) * half], ds_all, (((1,), (0,)), ((), ())), preferred_element_type=jnp.float32))
        dk_h = lax.dot_general(ds_all, q, (((1,), (0,)), ((), ())), preferred_element_type=jnp.float32)
        dv_h = lax.dot_general(p_ref[0, h], do, (((1,), (0,)), ((), ())), preferred_element_type=jnp.float32)
        dk_all = dk_h if h == 0 else jnp.where(mine, dk_h, dk_all)
        dv_all = dv_h if h == 0 else jnp.where(mine, dv_h, dv_all)
    dq_ref[...] = (jnp.concatenate(dq_parts, axis=0).T * 0.125).astype(LOW)
    dk_ref[...] = (dk_all * 0.125).astype(LOW)
    dv_ref[...] = dv_all.astype(LOW)

def attention_backward(projected, do, joined, weights, rows, seq, heads, head):
    width = heads * head
    pairs = heads // 2
    spec = lambda off: pl.BlockSpec((seq, 2 * head), lambda p, b: (b, off + p))
    return pl.pallas_call(
        attention_backward_kernel,
        grid=(pairs, rows),
        in_specs=[
            spec(0), spec(pairs), spec(2 * pairs), spec(0), spec(0),
            pl.BlockSpec((1, 2, seq, seq), lambda p, b: (b, p, 0, 0)),
        ],
        out_specs=[
            spec(0), spec(0), spec(0),
            pl.BlockSpec((2, 3, TILE, TILE), lambda p, b: (p, 0, 0, 0)),
            pl.BlockSpec((2, 2, 8, TILE), lambda p, b: (p, 0, 0, 0)),
        ],
        out_shape=[jax.ShapeDtypeStruct((rows * seq, width), LOW)] * 3 + [
            jax.ShapeDtypeStruct((heads, 3, TILE, TILE), jnp.float32),
            jax.ShapeDtypeStruct((heads, 2, 8, TILE), jnp.float32),
        ],
        scratch_shapes=[pltpu.VMEM((seq, seq), LOW)],
        compiler_params=params(40),
        cost_estimate=cost(flops=8 * rows * heads * seq * seq * head * 4, bytes_accessed=rows * heads * seq * seq * 2, transcendentals=0),
        name="attention_backward",
    )(projected, projected, projected, do, joined, weights)

def bias_tiles(table):
    j = lax.broadcasted_iota(jnp.int32, (3, TILE, TILE), 1)
    i = lax.broadcasted_iota(jnp.int32, (3, TILE, TILE), 2)
    d = lax.broadcasted_iota(jnp.int32, (3, TILE, TILE), 0) - 1
    b = bucket_of(d * TILE + j - i)
    scaled = table.T * LOG2E
    hot = (b.reshape(1, -1) == jnp.arange(table.shape[0], dtype=jnp.int32)[:, None]).astype(jnp.float32)
    near = jnp.dot(scaled, hot, precision=lax.Precision.HIGHEST).reshape(-1, 3, TILE, TILE)
    far = jnp.stack([scaled[:, -1], scaled[:, table.shape[0] // 2 - 1]], axis=1)
    return near, far, hot


def expert_kernel(experts, chunk, x_ref, g_ref, mine_ref, wr_ref, wrt_ref, wi_ref, wit_ref, wo_ref, wot_ref,
                  ff_ref, dx_ref, hid_ref, da_ref, xt_ref, dfft_ref, gr_ref):
    x = x_ref[...]
    g = g_ref[...].astype(jnp.float32)
    mine = mine_ref[...]
    lane = lax.broadcasted_iota(jnp.int32, (1, wr_ref.shape[1]), 1)
    logits = jnp.dot(x, wr_ref[...], preferred_element_type=jnp.float32)
    logits = jnp.where(lane < experts, logits, -1e30)
    e = jnp.exp(logits - jnp.max(logits, axis=-1, keepdims=True))
    router = e / jnp.sum(e, axis=-1, keepdims=True)
    gate = jnp.sum(router * mine, axis=-1, keepdims=True)
    dff = (g * gate).astype(LOW)
    inner = wi_ref.shape[1]
    ff = None
    dx = None
    def first(f):
        cols = slice(f, f + chunk)
        return (jnp.dot(x, wi_ref[:, cols], preferred_element_type=jnp.float32),
                jnp.dot(dff, wot_ref[:, cols], preferred_element_type=jnp.float32))
    ahead = first(0)
    for f in range(0, inner, chunk):
        cols = slice(f, f + chunk)
        a, dhid = ahead
        if f + chunk < inner:
            ahead = first(f + chunk)
        u = a * a
        t = jnp.tanh(a * (GELU_A + GELU_B * u))
        h = 0.5 + 0.5 * t
        hid = a * h
        slope = h + hid * ((1.0 - t) * (GELU_A + (3.0 * GELU_B) * u))
        da = (dhid * slope).astype(LOW)
        hid = hid.astype(LOW)
        hid_ref[:, cols] = hid
        da_ref[:, cols] = da
        ff_part = jnp.dot(hid, wo_ref[cols, :], preferred_element_type=jnp.float32)
        dx_part = jnp.dot(da, wit_ref[cols, :], preferred_element_type=jnp.float32)
        ff = ff_part if ff is None else ff + ff_part
        dx = dx_part if dx is None else dx + dx_part
    ff = ff.astype(LOW)
    ff_ref[...] = ff
    dgate = jnp.sum(g * ff.astype(jnp.float32), axis=-1, keepdims=True)
    dlogits = ((gate * dgate) * (mine - router)).astype(LOW)
    dx = dx + jnp.dot(dlogits, wrt_ref[...], preferred_element_type=jnp.float32)
    dx_ref[...] = dx.astype(LOW)
    x_t = x.T
    xt_ref[...] = x_t
    dfft_ref[...] = dff.T

    @pl.when(pl.program_id(0) == 0)
    def _():
        gr_ref[...] = jnp.zeros_like(gr_ref)
    gr_ref[...] += jnp.dot(x_t, dlogits, preferred_element_type=jnp.float32)

def expert_rows(x, g, mine, wr, wrt, wi, wit, wo, wot, experts, tile=256, chunk=768):
    n, width = x.shape
    inner = wi.shape[1]
    while n % tile: tile //= 2
    once = lambda s: pl.BlockSpec(s, lambda i: (0,) * len(s), pipeline_mode=pl.Buffered(1))
    rowspec = lambda w: pl.BlockSpec((tile, w), lambda i: (i, 0))
    return pl.pallas_call(
        functools.partial(expert_kernel, experts, chunk),
        grid=(n // tile,),
        in_specs=[rowspec(width), rowspec(width), once(mine.shape), once(wr.shape), once(wrt.shape), once(wi.shape), once(wit.shape), once(wo.shape), once(wot.shape)],
        out_specs=[rowspec(width), rowspec(width), rowspec(inner), rowspec(inner),
                   pl.BlockSpec((width, tile), lambda i: (0, i)), pl.BlockSpec((width, tile), lambda i: (0, i)),
                   pl.BlockSpec((width, wr.shape[1]), lambda i: (0, 0))],
        out_shape=[jax.ShapeDtypeStruct((n, width), LOW)] * 2 + [jax.ShapeDtypeStruct((n, inner), LOW)] * 2
            + [jax.ShapeDtypeStruct((width, n), LOW)] * 2 + [jax.ShapeDtypeStruct((width, wr.shape[1]), jnp.float32)],
        compiler_params=params(56),
        cost_estimate=cost(flops=8 * n * width * inner, bytes_accessed=4 * n * inner + 8 * width * inner, transcendentals=n * inner),
        name="expert_rows",
    )(x, g, mine, wr, wrt, wi, wit, wo, wot)

def expert_weights_kernel(parts, *refs):
    ins, (gi_ref, go_ref) = refs[:4 * parts], refs[4 * parts:]
    gi = None
    go = None
    for c in range(parts):
        xt, dfft, hid, da = ins[4 * c:4 * c + 4]
        gi_c = jnp.dot(xt[...], da[...], preferred_element_type=jnp.float32)
        go_c = jnp.dot(dfft[...], hid[...], preferred_element_type=jnp.float32)
        gi = gi_c if gi is None else gi + gi_c
        go = go_c if go is None else go + go_c
    gi_ref[0] = gi
    go_ref[0] = go.T

def expert_weights(parts, tile=256):
    inner = parts[0][2].shape[1]
    width = parts[0][0].shape[0]
    specs, args, rows = [], [], 0
    for xt, dfft, hid, da in parts:
        n = hid.shape[0]
        rows += n
        specs += [pl.BlockSpec((width, n), lambda f: (0, 0), pipeline_mode=pl.Buffered(1))] * 2
        specs += [pl.BlockSpec((n, tile), lambda f: (0, f))] * 2
        args += [xt, dfft, hid, da]
    return pl.pallas_call(
        functools.partial(expert_weights_kernel, len(parts)),
        grid=(inner // tile,),
        in_specs=specs,
        out_specs=[pl.BlockSpec((1, width, tile), lambda f: (0, 0, f)), pl.BlockSpec((1, tile, width), lambda f: (0, f, 0))],
        out_shape=[jax.ShapeDtypeStruct((1, width, inner), jnp.float32), jax.ShapeDtypeStruct((1, inner, width), jnp.float32)],
        compiler_params=params(56),
        cost_estimate=cost(flops=4 * rows * width * inner, bytes_accessed=4 * rows * inner + 8 * width * inner, transcendentals=0),
        name="expert_weights",
    )(*args)


def local(
    tokens, lengths, expert_ids, slots, w_query, w_key, w_value, w_output,
    gain_attn, gain_ffn, bias_table, w_router, w_in, w_out, cotangent,
):
    rows, seq, width = tokens.shape
    count = rows * seq
    buckets, heads = bias_table.shape
    head = width // heads
    experts = w_router.shape[1]
    devices = lax.axis_size(AXES)
    room = max(4, 2 * count // experts)
    me = lax.axis_index(AXES)
    x = tokens.reshape(count, width)
    g = cotangent.reshape(count, width)
    gain_one = gain_attn.reshape(1, width)
    gain_two = gain_ffn.reshape(1, width)
    wide = max(128, experts)
    router_w = jnp.pad(w_router, ((0, 0), (0, wide - experts)))
    mine = (jnp.arange(wide, dtype=jnp.int32) == me).astype(jnp.float32).reshape(1, wide)

    dest_c, dest_r, g_out = route(expert_ids, slots, g, experts, room)
    g_in = exchange(g_out, devices)

    w_qkv = jnp.concatenate([w_query, w_key, w_value], axis=1)
    normed, projected = project(x, gain_one, w_qkv)
    near, far, hot = bias_tiles(bias_table)
    joined, weights = attention_forward(lengths, projected, near, far, rows, seq, heads, head)
    y, h_out = after_attention(joined, x, w_output, gain_two, dest_r, experts * room)
    h_in = exchange(h_out, devices)

    ff, dx, hid, da, x_t, dff_t, grad_router = expert_rows(
        h_in, g_in, mine, router_w, router_w.T, w_in[0], w_in[0].T, w_out[0], w_out[0].T, experts
    )
    dh_back = exchange(dx, devices)
    ff_back = exchange(ff, devices)
    grad_in, grad_out = expert_weights([(x_t, dff_t, hid, da)])

    dy, do, grad_output, grad_gain_two = before_attention(
        dh_back, dest_c, y, g, gain_two, w_output.T, joined
    )
    dq, dk, dv, near_sum, far_sum = attention_backward(
        projected, do, joined, weights, rows, seq, heads, head
    )
    grad_tokens, grad_qkv, grad_gain_one = finish(
        dq, dk, dv, w_qkv.T, normed, x, dy, gain_one
    )
    table = jnp.dot(hot, near_sum.reshape(heads, -1).T, precision=lax.Precision.HIGHEST)
    far_total = jnp.sum(far_sum, axis=(2, 3))
    table = table.at[buckets - 1].add(far_total[:, 0]).at[buckets // 2 - 1].add(far_total[:, 1])
    mixed = mix(ff_back, dest_c, expert_ids, y, gain_two, router_w, experts)
    summed = lax.psum(
        (
            grad_qkv[:width], grad_qkv[width : 2 * width], grad_qkv[2 * width :], grad_output,
            grad_gain_one.reshape(width), grad_gain_two.reshape(width), table,
            grad_router[:, :experts],
        ),
        AXES,
    )
    return (
        mixed.reshape(rows, seq, width),
        grad_tokens.reshape(rows, seq, width),
        *summed,
        grad_in,
        grad_out,
    )


def solution(mesh):
    split = P(AXES)
    in_specs = (split,) * 4 + (P(),) * 8 + (split,) * 3
    out_specs = (split,) * 2 + (P(),) * 8 + (split,) * 2
    return jax.shard_map(local, mesh=mesh, in_specs=in_specs, out_specs=out_specs, check_vma=False)
```

```python
import functools

import jax
import jax.numpy as jnp
from jax import lax
from jax.experimental import pallas as pl
from jax.experimental.pallas import tpu as pltpu
from jax.sharding import PartitionSpec as P

EPSILON = 1e-06
NEGATIVE = -1e30
THRESHOLDS = (12, 16, 23, 32, 46, 64, 91)
LOG2E = 1.4426950408889634
TILE = 128
GELU_A = 0.7978845608028654
GELU_B = GELU_A * 0.044715
AXES = ("grp", "exp")
LOW = jnp.bfloat16


def dot(a, b):
    return jnp.dot(a, b, preferred_element_type=jnp.float32)


def dot_t(a, b):
    return lax.dot_general(a, b, (((1,), (1,)), ((), ())), preferred_element_type=jnp.float32)


def params(mib, **more):
    return pltpu.CompilerParams(vmem_limit_bytes=mib << 20, **more)


def whole(shape):
    return pl.BlockSpec(shape, lambda *_: (0,) * len(shape), pipeline_mode=pl.Buffered(1))


def cost(flops, bytes_accessed, transcendentals=0):
    return pl.CostEstimate(
        flops=flops, bytes_accessed=bytes_accessed, transcendentals=transcendentals
    )


def bucket_of(offset):
    distance = jnp.abs(offset)
    far = jnp.full_like(distance, 8)
    for border in THRESHOLDS:
        far = far + (distance >= border).astype(jnp.int32)
    return jnp.where(distance < 8, distance, far) + jnp.where(offset > 0, 16, 0).astype(jnp.int32)


def route_kernel(experts, room, eid_c, eid_r, slot_c, slot_r, g_ref, dest_c, dest_r, g_out):
    tokens = g_ref.shape[0]
    wide = max(128, experts)
    at = lax.broadcasted_iota(jnp.int32, (tokens, tokens), 0)
    to = lax.broadcasted_iota(jnp.int32, (tokens, tokens), 1)
    ids = eid_c[...]
    picked = ids == lax.broadcasted_iota(jnp.int32, (tokens, wide), 1)
    earlier = dot((to < at).astype(LOW), picked.astype(LOW))
    place = jnp.sum(jnp.where(picked, earlier, 0.0), axis=1, keepdims=True).astype(jnp.int32)
    dest_c[...] = jnp.where(slot_c[...] >= 0, ids * room + place, -1)
    ids = eid_r[...]
    picked = ids == lax.broadcasted_iota(jnp.int32, (wide, tokens), 0)
    earlier = dot(picked.astype(LOW), (at < to).astype(LOW))
    place = jnp.sum(jnp.where(picked, earlier, 0.0), axis=0, keepdims=True).astype(jnp.int32)
    dest = jnp.where(slot_r[...] >= 0, ids * room + place, -1)
    dest_r[...] = dest
    spread(dest, g_ref[...], g_out)


def spread(dest, values, out):
    rows = out.shape[0]
    step = 256
    for start in range(0, rows, step):
        here = lax.broadcasted_iota(jnp.int32, (step, dest.shape[1]), 0) + start
        out[start : start + step] = dot((dest == here).astype(LOW), values).astype(LOW)


def collect(dest, values):
    rows = values.shape[0]
    here = lax.broadcasted_iota(jnp.int32, (dest.shape[0], rows), 1)
    return dot((dest == here).astype(LOW), values)


def route(expert_ids, slots, upstream, experts, room):
    tokens, width = upstream.shape
    flat = lambda a, shape: a.reshape(shape)
    return pl.pallas_call(
        functools.partial(route_kernel, experts, room),
        out_shape=[
            jax.ShapeDtypeStruct((tokens, 1), jnp.int32),
            jax.ShapeDtypeStruct((1, tokens), jnp.int32),
            jax.ShapeDtypeStruct((experts * room, width), LOW),
        ],
        compiler_params=params(48),
        cost_estimate=cost(2 * experts * room * tokens * width, 8 << 20),
        name="route",
    )(
        flat(expert_ids, (tokens, 1)),
        flat(expert_ids, (1, tokens)),
        flat(slots, (tokens, 1)),
        flat(slots, (1, tokens)),
        upstream,
    )


def exchange(buffer, devices):
    shaped = buffer.reshape(devices, buffer.shape[0] // devices, buffer.shape[1])
    moved = lax.all_to_all(shaped, AXES, split_axis=0, concat_axis=0, tiled=True)
    return moved.reshape(buffer.shape)


def project_kernel(x_ref, gain_ref, w_ref, normed_ref, out_ref):
    x = x_ref[...].astype(jnp.float32)
    rms = lax.rsqrt(jnp.mean(x * x, axis=-1, keepdims=True) + EPSILON)
    normed = (x * rms * gain_ref[...]).astype(LOW)
    normed_ref[...] = normed
    out_ref[...] = dot(normed, w_ref[...]).astype(LOW)


def project(x, gain, w_qkv):
    tokens, width = x.shape
    out = w_qkv.shape[1]
    step = 256
    rows = lambda w: pl.BlockSpec((step, w), lambda i: (i, 0))
    return pl.pallas_call(
        project_kernel,
        grid=(tokens // step,),
        in_specs=[rows(width), whole((1, width)), whole((width, out))],
        out_specs=[rows(width), rows(out)],
        out_shape=[
            jax.ShapeDtypeStruct((tokens, width), LOW),
            jax.ShapeDtypeStruct((tokens, out), LOW),
        ],
        compiler_params=params(40),
        cost_estimate=cost(2 * tokens * width * out, 12 << 20),
        name="project",
    )(x, gain, w_qkv)


def after_attention_kernel(o_ref, x_ref, w_ref, gain_ref, dest_ref, y_ref, out_ref, held):
    step = o_ref.shape[0]
    i = pl.program_id(0)
    y = x_ref[...].astype(jnp.float32) + dot(o_ref[...], w_ref[...])
    y_ref[...] = y
    rms = lax.rsqrt(jnp.mean(y * y, axis=-1, keepdims=True) + EPSILON)
    held[pl.ds(pl.multiple_of(i * step, step), step), :] = (y * rms * gain_ref[...]).astype(LOW)

    @pl.when(i == pl.num_programs(0) - 1)
    def _():
        spread(dest_ref[...], held[...], out_ref)


def after_attention(joined, x, w_output, gain, dest_r, rows_out):
    tokens, width = x.shape
    step = 256
    rows = pl.BlockSpec((step, width), lambda i: (i, 0))
    return pl.pallas_call(
        after_attention_kernel,
        grid=(tokens // step,),
        in_specs=[rows, rows, whole((width, width)), whole((1, width)), whole((1, tokens))],
        out_specs=[rows, pl.BlockSpec((rows_out, width), lambda i: (0, 0))],
        out_shape=[
            jax.ShapeDtypeStruct((tokens, width), jnp.float32),
            jax.ShapeDtypeStruct((rows_out, width), LOW),
        ],
        scratch_shapes=[pltpu.VMEM((tokens, width), LOW)],
        compiler_params=params(48),
        cost_estimate=cost(2 * tokens * width * (width + rows_out), 12 << 20),
        name="after_attention",
    )(joined, x, w_output, gain, dest_r)


def mix_kernel(experts, ff_ref, dest_ref, eid_ref, y_ref, gain_ref, wr_ref, out_ref):
    y = y_ref[...]
    rms = lax.rsqrt(jnp.mean(y * y, axis=-1, keepdims=True) + EPSILON)
    normed = (y * rms * gain_ref[...]).astype(LOW)
    router = route_softmax(dot(normed, wr_ref[...]), experts)
    lane = lax.broadcasted_iota(jnp.int32, router.shape, 1)
    gate = jnp.sum(jnp.where(lane == eid_ref[...], router, 0.0), axis=-1, keepdims=True)
    out_ref[...] = (y + gate * collect(dest_ref[...], ff_ref[...])).astype(LOW)


def route_softmax(logits, experts):
    lane = lax.broadcasted_iota(jnp.int32, logits.shape, 1)
    logits = jnp.where(lane < experts, logits, NEGATIVE)
    e = jnp.exp(logits - jnp.max(logits, axis=-1, keepdims=True))
    return e / jnp.sum(e, axis=-1, keepdims=True)


def mix(ff, dest_c, expert_ids, y, gain, w_router, experts):
    tokens, width = y.shape
    step = 256
    rows = lambda w: pl.BlockSpec((step, w), lambda i: (i, 0))
    return pl.pallas_call(
        functools.partial(mix_kernel, experts),
        grid=(tokens // step,),
        in_specs=[whole(ff.shape), rows(1), rows(1), rows(width), whole((1, width)), whole(w_router.shape)],
        out_specs=rows(width),
        out_shape=jax.ShapeDtypeStruct((tokens, width), LOW),
        compiler_params=params(40),
        cost_estimate=cost(2 * tokens * width * ff.shape[0], 8 << 20),
        name="mix",
    )(ff, dest_c, expert_ids.reshape(tokens, 1), y, gain, w_router)


def pack(values, first, height, out, at):
    for c in range(values.shape[1] // TILE):
        out[at + c * height : at + (c + 1) * height] = values[
            first : first + height, c * TILE : (c + 1) * TILE
        ].astype(LOW)


def before_attention_kernel(
    dh_ref, dest_ref, y_ref, g_ref, gain_ref, wt_ref, o_ref, dy_ref, do_ref, pack_ref, gg_ref, gw_ref
):
    i = pl.program_id(0)

    @pl.when(i == 0)
    def _():
        gw_ref[...] = jnp.zeros_like(gw_ref)
        gg_ref[...] = jnp.zeros_like(gg_ref)

    dh = collect(dest_ref[...], dh_ref[...])
    y = y_ref[...]
    rms = lax.rsqrt(jnp.mean(y * y, axis=-1, keepdims=True) + EPSILON)
    gg_ref[...] += jnp.sum(dh * y * rms, axis=0, keepdims=True)
    u = dh * gain_ref[...]
    dy = (
        g_ref[...].astype(jnp.float32)
        + rms * u
        - y * (rms * rms * rms) * jnp.mean(u * y, axis=-1, keepdims=True)
    )
    dy_ref[...] = dy
    low = dy.astype(LOW)
    do_ref[...] = dot(low, wt_ref[...]).astype(LOW)
    gw_ref[...] += dot(o_ref[...].T, low)

    @pl.when(i == pl.num_programs(0) - 1)
    def _():
        pack(gw_ref, 0, gw_ref.shape[0], pack_ref, 0)


def before_attention(dh, dest_c, y, g, gain, w_output_t, joined):
    tokens, width = y.shape
    step = 256
    rows = lambda w: pl.BlockSpec((step, w), lambda i: (i, 0))
    return pl.pallas_call(
        before_attention_kernel,
        grid=(tokens // step,),
        in_specs=[
            whole(dh.shape), rows(1), rows(width), rows(width), whole((1, width)),
            whole((width, width)), rows(width),
        ],
        out_specs=[
            rows(width), rows(width),
            pl.BlockSpec((width * width // TILE, TILE), lambda i: (0, 0)),
            pl.BlockSpec((1, width), lambda i: (0, 0)),
        ],
        out_shape=[
            jax.ShapeDtypeStruct((tokens, width), jnp.float32),
            jax.ShapeDtypeStruct((tokens, width), LOW),
            jax.ShapeDtypeStruct((width * width // TILE, TILE), LOW),
            jax.ShapeDtypeStruct((1, width), jnp.float32),
        ],
        scratch_shapes=[pltpu.VMEM((width, width), jnp.float32)],
        compiler_params=params(40),
        cost_estimate=cost(2 * tokens * width * (dh.shape[0] + 2 * width), 16 << 20),
        name="before_attention",
    )(dh, dest_c, y, g, gain, w_output_t, joined)


def finish_kernel(
    dq_ref, dk_ref, dv_ref, wt_ref, normed_ref, x_ref, dy_ref, gain_ref, go_ref, gr_ref, gg2_ref, table_ref,
    out_ref, pack_ref, gw_ref, gg_ref,
):
    i = pl.program_id(0)

    @pl.when(i == 0)
    def _():
        gw_ref[...] = jnp.zeros_like(gw_ref)
        gg_ref[...] = jnp.zeros_like(gg_ref)

    width = x_ref.shape[1]
    grads = (dq_ref[...], dk_ref[...], dv_ref[...])
    normed_t = normed_ref[...].T
    dh = None
    for n, d in enumerate(grads):
        gw_ref[n * width : (n + 1) * width] += dot(normed_t, d)
        part = dot(d, wt_ref[n * width : (n + 1) * width])
        dh = part if dh is None else dh + part
    x = x_ref[...].astype(jnp.float32)
    rms = lax.rsqrt(jnp.mean(x * x, axis=-1, keepdims=True) + EPSILON)
    gg_ref[...] += jnp.sum(dh * x * rms, axis=0, keepdims=True)
    u = dh * gain_ref[...]
    out_ref[...] = (
        dy_ref[...]
        + rms * u
        - x * (rms * rms * rms) * jnp.mean(u * x, axis=-1, keepdims=True)
    )

    @pl.when(i == pl.num_programs(0) - 1)
    def _():
        block = width * width // TILE
        for n in range(3):
            pack(gw_ref, n * width, width, pack_ref, n * block)
        pack_ref[3 * block : 4 * block] = go_ref[...]
        at = 4 * block
        routed = gr_ref.shape[0]
        pack_ref[at : at + routed] = gr_ref[...].astype(LOW)
        at = at + routed
        rows = width // TILE
        gains = [gg_ref[:, c * TILE : (c + 1) * TILE] for c in range(rows)]
        gains += [gg2_ref[:, c * TILE : (c + 1) * TILE] for c in range(rows)]
        gains += [jnp.zeros((16 - 2 * rows % 16, TILE), jnp.float32)] if 2 * rows % 16 else []
        gains = jnp.concatenate(gains, axis=0)
        pack_ref[at : at + gains.shape[0]] = gains.astype(LOW)
        at = at + gains.shape[0]
        heads, buckets, _ = table_ref.shape
        lane = lax.broadcasted_iota(jnp.int32, (buckets, TILE), 1)
        table = jnp.zeros((buckets, TILE), jnp.float32)
        for h in range(heads):
            table = jnp.where(lane == h, jnp.sum(table_ref[h], axis=1, keepdims=True), table)
        pack_ref[at : at + buckets] = table.astype(LOW)
        at = at + buckets
        pack_ref[at:] = jnp.zeros((pack_ref.shape[0] - at, TILE), LOW)


def finish(dq, dk, dv, w_qkv_t, normed, x, dy, gain, go, gr, gg2, table, rows_packed):
    tokens, width = x.shape
    step = 256
    rows = pl.BlockSpec((step, width), lambda i: (i, 0))
    return pl.pallas_call(
        finish_kernel,
        grid=(tokens // step,),
        in_specs=[
            rows, rows, rows, whole((3 * width, width)), rows, rows, rows, whole((1, width)),
            whole(go.shape), whole(gr.shape), whole(gg2.shape), whole(table.shape),
        ],
        out_specs=[rows, pl.BlockSpec((rows_packed, TILE), lambda i: (0, 0))],
        out_shape=[
            jax.ShapeDtypeStruct((tokens, width), jnp.float32),
            jax.ShapeDtypeStruct((rows_packed, TILE), LOW),
        ],
        scratch_shapes=[
            pltpu.VMEM((3 * width, width), jnp.float32),
            pltpu.VMEM((1, width), jnp.float32),
        ],
        compiler_params=params(56),
        cost_estimate=cost(12 * tokens * width * width, 24 << 20),
        name="finish",
    )(dq, dk, dv, w_qkv_t, normed, x, dy, gain, go, gr, gg2, table)


def unpack_kernel(packed_ref, out_ref):
    height = out_ref.shape[1]
    for c in range(out_ref.shape[2] // TILE):
        out_ref[0, :, c * TILE : (c + 1) * TILE] = packed_ref[c * height : (c + 1) * height].astype(
            jnp.float32
        )


def unpack(packed, width):
    block = width * width // TILE
    return pl.pallas_call(
        unpack_kernel,
        grid=(4,),
        in_specs=[pl.BlockSpec((block, TILE), lambda i: (i, 0))],
        out_specs=pl.BlockSpec((1, width, width), lambda i: (i, 0, 0)),
        out_shape=jax.ShapeDtypeStruct((4, width, width), jnp.float32),
        compiler_params=params(32),
        name="unpack",
    )(packed)


def attention_forward_kernel(len_ref, q_ref, k_ref, v_ref, near_ref, far_ref, o_ref, p_ref, s_ref):
    seq = q_ref.shape[0]
    tiles = seq // TILE
    half = q_ref.shape[1] // 2
    row = pl.program_id(0)
    pair = pl.program_id(1)
    live = len_ref[row]
    lane = lax.broadcasted_iota(jnp.int32, (seq, 2 * half), 1)
    dead = lax.broadcasted_iota(jnp.int32, (seq, 2 * half), 0) >= live
    q = q_ref[...]
    k = k_ref[...]
    v_t = v_ref[...].T
    outs = []
    for h in range(2):
        mine = (lane >= h * half) & (lane < (h + 1) * half)
        flag = lane == (1 - h) * half
        k_h = jnp.where(mine, k, jnp.where(flag & dead, -1e30, 0.0).astype(k.dtype))
        q_h = jnp.where(flag, jnp.ones_like(q), q)
        after = far_ref[2 * pair + h, 0]
        before = far_ref[2 * pair + h, 1]
        tops = []
        for i in range(tiles):
            q_i = q_h[i * TILE:(i + 1) * TILE]
            raw = lax.dot_general(k_h, q_i, (((1,), (1,)), ((), ())), preferred_element_type=jnp.float32)
            top = None
            for j in range(tiles):
                x = raw[j * TILE:(j + 1) * TILE] * (0.125 * LOG2E)
                d = j - i
                if -1 <= d <= 1:
                    x = x + near_ref[h, d + 1]
                else:
                    x = x + (after if d > 0 else before)
                s_ref[j * TILE:(j + 1) * TILE, i * TILE:(i + 1) * TILE] = x
                m = jnp.max(x, axis=0, keepdims=True)
                top = m if top is None else jnp.maximum(top, m)
            tops.append(top)
        for i in range(tiles):
            e = jnp.exp2(s_ref[:, i * TILE:(i + 1) * TILE] - tops[i])
            total = jnp.sum(e, axis=0, keepdims=True)
            p_ref[0, h, :, i * TILE:(i + 1) * TILE] = (e * (1.0 / total)).astype(LOW)
        outs.append(lax.dot_general(v_t[h * half:(h + 1) * half], p_ref[0, h], (((1,), (0,)), ((), ())), preferred_element_type=jnp.float32))
    o_ref[...] = jnp.concatenate(outs, axis=0).T.astype(o_ref.dtype)

def attention_forward(lengths, projected, near, far, rows, seq, heads, head):
    width = heads * head
    pairs = heads // 2
    spec = lambda off: pl.BlockSpec((seq, 2 * head), lambda b, p: (b, off + p))
    return pl.pallas_call(
        attention_forward_kernel,
        grid=(rows, pairs),
        in_specs=[
            pl.BlockSpec(memory_space=pltpu.SMEM),
            spec(0), spec(pairs), spec(2 * pairs),
            pl.BlockSpec((2, 3, TILE, TILE), lambda b, p: (p, 0, 0, 0)),
            pl.BlockSpec(memory_space=pltpu.SMEM),
        ],
        out_specs=[
            pl.BlockSpec((seq, 2 * head), lambda b, p: (b, p)),
            pl.BlockSpec((1, 2, seq, seq), lambda b, p: (b, p, 0, 0)),
        ],
        out_shape=[
            jax.ShapeDtypeStruct((rows * seq, width), LOW),
            jax.ShapeDtypeStruct((rows, heads, seq, seq), LOW),
        ],
        scratch_shapes=[pltpu.VMEM((seq, seq), jnp.float32)],
        compiler_params=params(40),
        cost_estimate=cost(flops=4 * rows * heads * seq * seq * head * 4, bytes_accessed=rows * heads * seq * seq * 2, transcendentals=rows * heads * seq * seq),
        name="attention_forward",
    )(lengths, projected, projected, projected, near, far)

def attention_backward_kernel(q_ref, k_ref, v_ref, do_ref, o_ref, p_ref, dq_ref, dk_ref, dv_ref, table_ref, near_ref, far_ref, d_ref):
    seq = q_ref.shape[0]
    tiles = seq // TILE
    half = q_ref.shape[1] // 2
    row = pl.program_id(1)
    lane = lax.broadcasted_iota(jnp.int32, (seq, 2 * half), 1)
    q = q_ref[...]
    k = k_ref[...]
    k_t = k.T
    v = v_ref[...]
    do = do_ref[...]
    weighed = (do.astype(jnp.float32) * o_ref[...].astype(jnp.float32)).T
    dq_parts = []
    dk_all = None
    dv_all = None

    @pl.when(row == 0)
    def _():
        near_ref[...] = jnp.zeros_like(near_ref)
        far_ref[...] = jnp.zeros_like(far_ref)

    for h in range(2):
        mine = (lane >= h * half) & (lane < (h + 1) * half)
        v_h = jnp.where(mine, v, jnp.zeros_like(v))
        delta = jnp.sum(weighed[h * half:(h + 1) * half], axis=0, keepdims=True)
        far_sum = [jnp.zeros((8, TILE), jnp.float32), jnp.zeros((8, TILE), jnp.float32)]
        for i in range(tiles):
            cols = slice(i * TILE, (i + 1) * TILE)
            dp = lax.dot_general(v_h, do[cols], (((1,), (1,)), ((), ())), preferred_element_type=jnp.float32)
            for j in range(tiles):
                rws = slice(j * TILE, (j + 1) * TILE)
                ds = p_ref[0, h, rws, cols].astype(jnp.float32) * (dp[rws] - delta[:, cols])
                d = j - i
                if -1 <= d <= 1:
                    near_ref[h, d + 1] += ds
                else:
                    which = 0 if d > 0 else 1
                    far_sum[which] = far_sum[which] + jnp.sum(ds.reshape(TILE // 8, 8, TILE), axis=0)
                d_ref[rws, cols] = ds.astype(LOW)
        far_ref[h, 0] += far_sum[0]
        far_ref[h, 1] += far_sum[1]
        ds_all = d_ref[...]
        dq_parts.append(lax.dot_general(k_t[h * half:(h + 1) * half], ds_all, (((1,), (0,)), ((), ())), preferred_element_type=jnp.float32))
        dk_h = lax.dot_general(ds_all, q, (((1,), (0,)), ((), ())), preferred_element_type=jnp.float32)
        dv_h = lax.dot_general(p_ref[0, h], do, (((1,), (0,)), ((), ())), preferred_element_type=jnp.float32)
        dk_all = dk_h if h == 0 else jnp.where(mine, dk_h, dk_all)
        dv_all = dv_h if h == 0 else jnp.where(mine, dv_h, dv_all)
    @pl.when(row == pl.num_programs(1) - 1)
    def _():
        bucket_sums(near_ref, far_ref, table_ref)

    dq_ref[...] = (jnp.concatenate(dq_parts, axis=0).T * 0.125).astype(LOW)
    dk_ref[...] = (dk_all * 0.125).astype(LOW)
    dv_ref[...] = dv_all.astype(LOW)

def bucket_sums(near_ref, far_ref, table_ref):
    buckets = table_ref.shape[1]
    half = buckets // 2
    key = lax.broadcasted_iota(jnp.int32, (TILE, TILE), 0)
    query = lax.broadcasted_iota(jnp.int32, (TILE, TILE), 1)
    tiles = [bucket_of((d - 1) * TILE + key - query) for d in range(3)]
    for h in range(2):
        sums = []
        for n in range(buckets):
            total = far_ref[h, 0 if n >= half else 1] if n % half == half - 1 else None
            for d in range(3):
                if (d == 0 and n >= half) or (d == 2 and n < half):
                    continue
                part = jnp.where(tiles[d] == n, near_ref[h, d], 0.0)
                part = jnp.sum(part.reshape(TILE // 8, 8, TILE), axis=0)
                total = part if total is None else total + part
            sums.append(jnp.sum(total, axis=0, keepdims=True))
        table_ref[h] = jnp.concatenate(sums, axis=0)


def attention_backward(buckets, projected, do, joined, weights, rows, seq, heads, head):
    width = heads * head
    pairs = heads // 2
    spec = lambda off: pl.BlockSpec((seq, 2 * head), lambda p, b: (b, off + p))
    return pl.pallas_call(
        attention_backward_kernel,
        grid=(pairs, rows),
        in_specs=[
            spec(0), spec(pairs), spec(2 * pairs), spec(0), spec(0),
            pl.BlockSpec((1, 2, seq, seq), lambda p, b: (b, p, 0, 0)),
        ],
        out_specs=[
            spec(0), spec(0), spec(0),
            pl.BlockSpec((2, buckets, TILE), lambda p, b: (p, 0, 0)),
        ],
        out_shape=[jax.ShapeDtypeStruct((rows * seq, width), LOW)] * 3 + [
            jax.ShapeDtypeStruct((heads, buckets, TILE), jnp.float32),
        ],
        scratch_shapes=[
            pltpu.VMEM((2, 3, TILE, TILE), jnp.float32),
            pltpu.VMEM((2, 2, 8, TILE), jnp.float32),
            pltpu.VMEM((seq, seq), LOW),
        ],
        compiler_params=params(40),
        cost_estimate=cost(flops=8 * rows * heads * seq * seq * head * 4, bytes_accessed=rows * heads * seq * seq * 2, transcendentals=0),
        name="attention_backward",
    )(projected, projected, projected, do, joined, weights)

def bias_tiles(table):
    j = lax.broadcasted_iota(jnp.int32, (3, TILE, TILE), 1)
    i = lax.broadcasted_iota(jnp.int32, (3, TILE, TILE), 2)
    d = lax.broadcasted_iota(jnp.int32, (3, TILE, TILE), 0) - 1
    b = bucket_of(d * TILE + j - i)
    scaled = table.T * LOG2E
    hot = (b.reshape(1, -1) == jnp.arange(table.shape[0], dtype=jnp.int32)[:, None]).astype(jnp.float32)
    near = jnp.dot(scaled, hot, precision=lax.Precision.HIGHEST).reshape(-1, 3, TILE, TILE)
    far = jnp.stack([scaled[:, -1], scaled[:, table.shape[0] // 2 - 1]], axis=1)
    return near, far


def expert_kernel(experts, chunk, x_ref, g_ref, mine_ref, wr_ref, wrt_ref, wi_ref, wit_ref, wo_ref, wot_ref,
                  ff_ref, dx_ref, hid_ref, da_ref, xt_ref, dfft_ref, gr_ref):
    x = x_ref[...]
    g = g_ref[...].astype(jnp.float32)
    mine = mine_ref[...]
    lane = lax.broadcasted_iota(jnp.int32, (1, wr_ref.shape[1]), 1)
    logits = jnp.dot(x, wr_ref[...], preferred_element_type=jnp.float32)
    logits = jnp.where(lane < experts, logits, -1e30)
    e = jnp.exp(logits - jnp.max(logits, axis=-1, keepdims=True))
    router = e / jnp.sum(e, axis=-1, keepdims=True)
    gate = jnp.sum(router * mine, axis=-1, keepdims=True)
    dff = (g * gate).astype(LOW)
    inner = wi_ref.shape[1]
    ff = None
    dx = None
    def first(f):
        cols = slice(f, f + chunk)
        return (jnp.dot(x, wi_ref[:, cols], preferred_element_type=jnp.float32),
                jnp.dot(dff, wot_ref[:, cols], preferred_element_type=jnp.float32))
    ahead = first(0)
    for f in range(0, inner, chunk):
        cols = slice(f, f + chunk)
        a, dhid = ahead
        if f + chunk < inner:
            ahead = first(f + chunk)
        u = a * a
        t = jnp.tanh(a * (GELU_A + GELU_B * u))
        h = 0.5 + 0.5 * t
        hid = a * h
        slope = h + hid * ((1.0 - t) * (GELU_A + (3.0 * GELU_B) * u))
        da = (dhid * slope).astype(LOW)
        hid = hid.astype(LOW)
        hid_ref[:, cols] = hid
        da_ref[:, cols] = da
        ff_part = jnp.dot(hid, wo_ref[cols, :], preferred_element_type=jnp.float32)
        dx_part = jnp.dot(da, wit_ref[cols, :], preferred_element_type=jnp.float32)
        ff = ff_part if ff is None else ff + ff_part
        dx = dx_part if dx is None else dx + dx_part
    ff = ff.astype(LOW)
    ff_ref[...] = ff
    dgate = jnp.sum(g * ff.astype(jnp.float32), axis=-1, keepdims=True)
    dlogits = ((gate * dgate) * (mine - router)).astype(LOW)
    dx = dx + jnp.dot(dlogits, wrt_ref[...], preferred_element_type=jnp.float32)
    dx_ref[...] = dx.astype(LOW)
    x_t = x.T
    xt_ref[...] = x_t
    dfft_ref[...] = dff.T

    @pl.when(pl.program_id(0) == 0)
    def _():
        gr_ref[...] = jnp.zeros_like(gr_ref)
    gr_ref[...] += jnp.dot(x_t, dlogits, preferred_element_type=jnp.float32)

def expert_rows(x, g, mine, wr, wrt, wi, wit, wo, wot, experts, tile=256, chunk=768):
    n, width = x.shape
    inner = wi.shape[1]
    while n % tile: tile //= 2
    once = lambda s: pl.BlockSpec(s, lambda i: (0,) * len(s), pipeline_mode=pl.Buffered(1))
    rowspec = lambda w: pl.BlockSpec((tile, w), lambda i: (i, 0))
    return pl.pallas_call(
        functools.partial(expert_kernel, experts, chunk),
        grid=(n // tile,),
        in_specs=[rowspec(width), rowspec(width), once(mine.shape), once(wr.shape), once(wrt.shape), once(wi.shape), once(wit.shape), once(wo.shape), once(wot.shape)],
        out_specs=[rowspec(width), rowspec(width), rowspec(inner), rowspec(inner),
                   pl.BlockSpec((width, tile), lambda i: (0, i)), pl.BlockSpec((width, tile), lambda i: (0, i)),
                   pl.BlockSpec((width, wr.shape[1]), lambda i: (0, 0))],
        out_shape=[jax.ShapeDtypeStruct((n, width), LOW)] * 2 + [jax.ShapeDtypeStruct((n, inner), LOW)] * 2
            + [jax.ShapeDtypeStruct((width, n), LOW)] * 2 + [jax.ShapeDtypeStruct((width, wr.shape[1]), jnp.float32)],
        compiler_params=params(56),
        cost_estimate=cost(flops=8 * n * width * inner, bytes_accessed=4 * n * inner + 8 * width * inner, transcendentals=n * inner),
        name="expert_rows",
    )(x, g, mine, wr, wrt, wi, wit, wo, wot)

def expert_weights_kernel(parts, *refs):
    ins, (gi_ref, go_ref) = refs[:4 * parts], refs[4 * parts:]
    gi = None
    go = None
    for c in range(parts):
        xt, dfft, hid, da = ins[4 * c:4 * c + 4]
        gi_c = jnp.dot(xt[...], da[...], preferred_element_type=jnp.float32)
        go_c = jnp.dot(dfft[...], hid[...], preferred_element_type=jnp.float32)
        gi = gi_c if gi is None else gi + gi_c
        go = go_c if go is None else go + go_c
    gi_ref[0] = gi
    go_ref[0] = go.T

def expert_weights(parts, tile=256):
    inner = parts[0][2].shape[1]
    width = parts[0][0].shape[0]
    specs, args, rows = [], [], 0
    for xt, dfft, hid, da in parts:
        n = hid.shape[0]
        rows += n
        specs += [pl.BlockSpec((width, n), lambda f: (0, 0), pipeline_mode=pl.Buffered(1))] * 2
        specs += [pl.BlockSpec((n, tile), lambda f: (0, f))] * 2
        args += [xt, dfft, hid, da]
    return pl.pallas_call(
        functools.partial(expert_weights_kernel, len(parts)),
        grid=(inner // tile,),
        in_specs=specs,
        out_specs=[pl.BlockSpec((1, width, tile), lambda f: (0, 0, f)), pl.BlockSpec((1, tile, width), lambda f: (0, f, 0))],
        out_shape=[jax.ShapeDtypeStruct((1, width, inner), jnp.float32), jax.ShapeDtypeStruct((1, inner, width), jnp.float32)],
        compiler_params=params(56),
        cost_estimate=cost(flops=4 * rows * width * inner, bytes_accessed=4 * rows * inner + 8 * width * inner, transcendentals=0),
        name="expert_weights",
    )(*args)


def sum_parts(bits, units):
    upper = list(range(1, bits))
    turns = min(6, units, 2 * max(1, min(3, len(upper))))
    sizes = [(units + t) // turns for t in range(turns)]
    orders = [[0] + upper[t % 3 :] + upper[: t % 3] for t in range(turns)]
    return sizes, orders


def sum_kernel(cores, bits, sizes, orders, x_ref, out_ref, work_ref, got_ref, send, recv):
    n = 1 << bits
    me = lax.axis_index("grp") * cores + lax.axis_index("exp")
    barrier = pltpu.get_barrier_semaphore()
    def place(d):
        return dict(device_id=(d // cores, d % cores), device_id_type=pl.DeviceIdType.MESH)
    def other(b):
        bit = (me // (1 << b)) % 2
        return bit, me + (1 - 2 * bit) * (1 << b)
    for b in range(bits):
        pl.semaphore_signal(barrier, inc=1, **place(other(b)[1]))
    pl.semaphore_wait(barrier, bits)
    parts = len(sizes)
    starts = [sum(sizes[:p]) * 16 * n for p in range(parts)]
    base = list(starts)
    got_at = list(starts)
    def rows(start, length):
        return pl.ds(pl.multiple_of(start, 16), length)
    def halving(p, s):
        length = sizes[p] * 16 * (n >> (s + 1))
        bit, partner = other(orders[p][s])
        source = x_ref if s == 0 else work_ref
        return pltpu.make_async_remote_copy(
            src_ref=source.at[rows(base[p] + (1 - bit) * length, length)],
            dst_ref=got_ref.at[rows(got_at[p], length)],
            send_sem=send.at[p, s], recv_sem=recv.at[p, s], **place(partner))
    pending = {}
    for p in range(parts):
        pending[p] = halving(p, 0); pending[p].start()
    sends = []
    for s in range(bits):
        for p in range(parts):
            length = sizes[p] * 16 * (n >> (s + 1))
            bit, partner = other(orders[p][s])
            keep = base[p] + bit * length
            pending[p].wait_recv()
            sends.append(pending[p])
            step = sizes[p] * 16
            source = x_ref if s == 0 else work_ref
            target = work_ref if s + 1 < bits else out_ref
            def add(i, _, keep=keep, source=source, target=target, at=got_at[p], step=step):
                here = rows(keep + i * step, step)
                arrived = got_ref[rows(at + i * step, step), :].astype(jnp.float32)
                target[here, :] = (source[here, :].astype(jnp.float32) + arrived).astype(LOW)
                return 0
            lax.fori_loop(0, length // step, add, 0)
            base[p] = keep
            got_at[p] += length
            if s + 1 < bits:
                pending[p] = halving(p, s + 1); pending[p].start()
    for c in sends:
        c.wait_send()
    back = {}
    def doubling(p, s):
        length = sizes[p] * 16 * (n >> (s + 1))
        bit, partner = other(orders[p][s])
        return pltpu.make_async_remote_copy(
            src_ref=out_ref.at[rows(base[p], length)], dst_ref=out_ref.at[rows(base[p], length)],
            send_sem=send.at[p, bits + s], recv_sem=recv.at[p, bits + s], **place(partner))
    for p in range(parts):
        back[p] = doubling(p, bits - 1); back[p].start()
    sends = []
    for s in reversed(range(bits)):
        for p in range(parts):
            length = sizes[p] * 16 * (n >> (s + 1))
            bit, partner = other(orders[p][s])
            back[p].wait_recv()
            sends.append(back[p])
            base[p] = base[p] - bit * length
            if s > 0:
                back[p] = doubling(p, s - 1); back[p].start()
    for c in sends:
        c.wait_send()

def all_sum(x, cid=1):
    cores = lax.axis_size("exp")
    n = lax.axis_size(AXES)
    bits = n.bit_length() - 1
    units = x.shape[0] // (16 * n)
    sizes, orders = sum_parts(bits, units)
    parts = len(sizes)
    return pl.pallas_call(
        functools.partial(sum_kernel, cores, bits, sizes, orders),
        out_shape=jax.ShapeDtypeStruct(x.shape, x.dtype),
        in_specs=[pl.BlockSpec(memory_space=pltpu.VMEM)],
        out_specs=pl.BlockSpec(memory_space=pltpu.VMEM),
        scratch_shapes=[pltpu.VMEM(x.shape, x.dtype), pltpu.VMEM(x.shape, x.dtype), pltpu.SemaphoreType.DMA((parts, 2 * bits)), pltpu.SemaphoreType.DMA((parts, 2 * bits))],
        compiler_params=params(40, collective_id=cid, has_side_effects=True),
        name="all_sum",
    )(x)


def local(
    tokens, lengths, expert_ids, slots, w_query, w_key, w_value, w_output,
    gain_attn, gain_ffn, bias_table, w_router, w_in, w_out, cotangent,
):
    rows, seq, width = tokens.shape
    count = rows * seq
    buckets, heads = bias_table.shape
    head = width // heads
    experts = w_router.shape[1]
    devices = lax.axis_size(AXES)
    room = max(4, 2 * count // experts)
    me = lax.axis_index(AXES)
    x = tokens.reshape(count, width)
    g = cotangent.reshape(count, width)
    gain_one = gain_attn.reshape(1, width)
    gain_two = gain_ffn.reshape(1, width)
    wide = max(128, experts)
    mine = (jnp.arange(wide, dtype=jnp.int32) == me).astype(jnp.float32).reshape(1, wide)

    dest_c, dest_r, g_out = route(expert_ids, slots, g, experts, room)
    g_in = exchange(g_out, devices)
    dest_r, x, w_query, w_key, w_value, w_output, bias_table, w_router = lax.optimization_barrier(
        (dest_r, x, w_query, w_key, w_value, w_output, bias_table, w_router)
    )
    router_w = jnp.pad(w_router, ((0, 0), (0, wide - experts)))

    w_qkv = jnp.concatenate([w_query, w_key, w_value], axis=1)
    normed, projected = project(x, gain_one, w_qkv)
    near, far = bias_tiles(bias_table)
    joined, weights = attention_forward(lengths, projected, near, far, rows, seq, heads, head)
    y, h_out = after_attention(joined, x, w_output, gain_two, dest_r, experts * room)
    h_out, g_in = lax.optimization_barrier((h_out, g_in))
    h_in = exchange(h_out, devices)
    w_in, w_out, h_out = lax.optimization_barrier((w_in, w_out, h_out))

    ff, dx, hid, da, x_t, dff_t, grad_router = expert_rows(
        h_in, g_in, mine, router_w, router_w.T, w_in[0], w_in[0].T, w_out[0], w_out[0].T, experts
    )
    dh_back = exchange(dx, devices)
    grad_in, grad_out = expert_weights([(x_t, dff_t, hid, da)])
    dh_back, grad_in, grad_out, ff = lax.optimization_barrier((dh_back, grad_in, grad_out, ff))
    ff_back = exchange(ff, devices)
    grad_router = grad_router[:, :experts].reshape(width * experts // TILE, TILE)

    dy, do, grad_output, grad_gain_two = before_attention(
        dh_back, dest_c, y, g, gain_two, w_output.T, joined
    )
    dq, dk, dv, table = attention_backward(
        buckets, projected, do, joined, weights, rows, seq, heads, head
    )
    small = grad_router.shape[0] + -(-2 * width // TILE // 16) * 16 + buckets
    block = width * width // TILE
    rows_packed = -(-(4 * block + small) // (16 * devices)) * 16 * devices
    grad_tokens, packed = finish(
        dq, dk, dv, w_qkv.T, normed, x, dy, gain_one, grad_output, grad_router, grad_gain_two, table, rows_packed
    )
    summed = all_sum(packed)
    summed, ff_back = lax.optimization_barrier((summed, ff_back))
    mixed = mix(ff_back, dest_c, expert_ids, y, gain_two, router_w, experts)
    grads = unpack(summed, width)
    at = 4 * block
    rest = summed[at : at + small].astype(jnp.float32)
    routed = grad_router.shape[0]
    grad_router = rest[:routed].reshape(width, experts)
    lines = width // TILE
    grad_gain_one = rest[routed : routed + lines].reshape(width)
    grad_gain_two = rest[routed + lines : routed + 2 * lines].reshape(width)
    grad_table = rest[small - buckets :, :heads]
    return (
        mixed.reshape(rows, seq, width),
        grad_tokens.reshape(rows, seq, width),
        grads[0], grads[1], grads[2], grads[3],
        grad_gain_one, grad_gain_two, grad_table, grad_router,
        grad_in,
        grad_out,
    )


def solution(mesh):
    split = P(AXES)
    in_specs = (split,) * 4 + (P(),) * 8 + (split,) * 3
    out_specs = (split,) * 2 + (P(),) * 8 + (split,) * 2
    return jax.shard_map(local, mesh=mesh, in_specs=in_specs, out_specs=out_specs, check_vma=False)
```

```python
import functools

import jax
import jax.numpy as jnp
from jax import lax
from jax.experimental import pallas as pl
from jax.experimental.pallas import tpu as pltpu
from jax.sharding import PartitionSpec as P

EPSILON = 1e-06
NEGATIVE = -1e30
THRESHOLDS = (12, 16, 23, 32, 46, 64, 91)
LOG2E = 1.4426950408889634
TILE = 128
GELU_A = 0.7978845608028654
GELU_B = GELU_A * 0.044715
AXES = ("grp", "exp")
LOW = jnp.bfloat16


def dot(a, b):
    return jnp.dot(a, b, preferred_element_type=jnp.float32)


def dot_t(a, b):
    return lax.dot_general(a, b, (((1,), (1,)), ((), ())), preferred_element_type=jnp.float32)


def params(mib, **more):
    return pltpu.CompilerParams(vmem_limit_bytes=mib << 20, **more)


def whole(shape):
    return pl.BlockSpec(shape, lambda *_: (0,) * len(shape), pipeline_mode=pl.Buffered(1))


def cost(flops, bytes_accessed, transcendentals=0):
    return pl.CostEstimate(
        flops=flops, bytes_accessed=bytes_accessed, transcendentals=transcendentals
    )


def bucket_of(offset):
    distance = jnp.abs(offset)
    far = jnp.full_like(distance, 8)
    for border in THRESHOLDS:
        far = far + (distance >= border).astype(jnp.int32)
    return jnp.where(distance < 8, distance, far) + jnp.where(offset > 0, 16, 0).astype(jnp.int32)


def plan(room):
    if room % 64:
        return ((0, room),), 0
    return ((0, room // 2), (room // 2, room)), 0


def segment(code, room, low, high):
    expert = lax.div(code, room)
    place = code - expert * room
    inside = (code >= 0) & (place >= low) & (place < high)
    return jnp.where(inside, expert * (high - low) + place - low, -1)


def spread(dest, values, out):
    rows = out.shape[0]
    step = min(256, rows)
    for start in range(0, rows, step):
        here = lax.broadcasted_iota(jnp.int32, (step, dest.shape[1]), 0) + start
        out[start : start + step] = dot((dest == here).astype(LOW), values).astype(LOW)


def collect(dest, values):
    here = lax.broadcasted_iota(jnp.int32, (dest.shape[0], values.shape[0]), 1)
    return dot((dest == here).astype(LOW), values)


def spread_all(code, rank, room, values, outs):
    segments, extra = plan(room)
    for (low, high), out in zip(segments, outs):
        spread(segment(code, room, low, high), values, out)
    if extra:
        spread(rank, values, outs[-1])


def collect_all(code, rank, room, refs):
    segments, extra = plan(room)
    if len(refs) == 1:
        return collect(code, refs[0][...])
    total = None
    for (low, high), ref in zip(segments, refs):
        part = collect(segment(code, room, low, high), ref[...])
        total = part if total is None else total + part
    if extra:
        total = total + collect(rank, refs[len(segments)][...])
        total = total + refs[len(segments) + 1][...].astype(jnp.float32)
    return total


def buffers(experts, room, width):
    segments, extra = plan(room)
    shapes = [jax.ShapeDtypeStruct((experts * (high - low), width), LOW) for low, high in segments]
    return shapes + ([jax.ShapeDtypeStruct((extra, width), LOW)] if extra else [])


def route_kernel(
    experts, room, eid_c, eid_r, slot_c, slot_r, g_ref, code_c, code_r, rank_c, rank_r, tags, *outs
):
    tokens = g_ref.shape[0]
    wide = max(TILE, experts)
    segments, extra = plan(room)
    cut = segments[-1][1]
    at = lax.broadcasted_iota(jnp.int32, (tokens, tokens), 0)
    to = lax.broadcasted_iota(jnp.int32, (tokens, tokens), 1)
    before = (to < at).astype(LOW)
    after = (at < to).astype(LOW)

    ids = eid_c[...]
    picked = ids == lax.broadcasted_iota(jnp.int32, (tokens, wide), 1)
    place = jnp.sum(jnp.where(picked, dot(before, picked.astype(LOW)), 0.0), axis=1, keepdims=True)
    place = place.astype(jnp.int32)
    kept = slot_c[...] >= 0
    code_c[...] = jnp.where(kept, ids * room + place, -1)
    over = jnp.broadcast_to(jnp.where(kept & (place >= cut), 1.0, 0.0), (tokens, TILE))
    rank = jnp.where(over > 0, dot(before, over.astype(LOW)).astype(jnp.int32), -1)
    rank_c[...] = rank[:, :1]
    lane = lax.broadcasted_iota(jnp.int32, (tokens, TILE), 1)
    marks = jnp.where((rank == lane) & (lane < extra), ids + 1, 0)
    marks = marks + jnp.where((lane == TILE - 1) & (rank >= extra), 1, 0)
    tags[...] = jnp.sum(marks, axis=0, keepdims=True)

    ids = eid_r[...]
    picked = ids == lax.broadcasted_iota(jnp.int32, (wide, tokens), 0)
    place = jnp.sum(jnp.where(picked, dot(picked.astype(LOW), after), 0.0), axis=0, keepdims=True)
    place = place.astype(jnp.int32)
    kept = slot_r[...] >= 0
    code = jnp.where(kept, ids * room + place, -1)
    code_r[...] = code
    over = jnp.broadcast_to(jnp.where(kept & (place >= cut), 1.0, 0.0), (16, tokens))
    rank = jnp.where(over > 0, dot(over.astype(LOW), after).astype(jnp.int32), -1)[:1]
    rank_r[...] = rank
    spread(code, g_ref[...], outs[0])


def route(expert_ids, slots, upstream, experts, room):
    tokens, width = upstream.shape
    column = jax.ShapeDtypeStruct((tokens, 1), jnp.int32)
    line = jax.ShapeDtypeStruct((1, tokens), jnp.int32)
    return pl.pallas_call(
        functools.partial(route_kernel, experts, room),
        out_shape=[
            column, line, column, line, jax.ShapeDtypeStruct((1, TILE), jnp.int32),
            jax.ShapeDtypeStruct((experts * room, width), LOW),
        ],
        compiler_params=params(48),
        cost_estimate=cost(2 * experts * room * tokens * width, 8 << 20),
        name="route",
    )(
        expert_ids.reshape(tokens, 1), expert_ids.reshape(1, tokens),
        slots.reshape(tokens, 1), slots.reshape(1, tokens), upstream,
    )


def exchange(buffer, devices):
    shaped = buffer.reshape(devices, buffer.shape[0] // devices, buffer.shape[1])
    moved = lax.all_to_all(shaped, AXES, split_axis=0, concat_axis=0, tiled=True)
    return moved.reshape(buffer.shape)


def project_kernel(x_ref, gain_ref, wq_ref, wk_ref, wv_ref, normed_ref, out_ref):
    x = x_ref[...].astype(jnp.float32)
    rms = lax.rsqrt(jnp.mean(x * x, axis=-1, keepdims=True) + EPSILON)
    normed = (x * rms * gain_ref[...]).astype(LOW)
    normed_ref[...] = normed
    width = x.shape[1]
    for n, w_ref in enumerate((wq_ref, wk_ref, wv_ref)):
        out_ref[:, n * width : (n + 1) * width] = dot(normed, w_ref[...]).astype(LOW)


def project(x, gain, w_query, w_key, w_value):
    tokens, width = x.shape
    out = 3 * width
    step = 256
    rows = lambda w: pl.BlockSpec((step, w), lambda i: (i, 0))
    return pl.pallas_call(
        project_kernel,
        grid=(tokens // step,),
        in_specs=[rows(width), whole((1, width)), *[whole((width, width))] * 3],
        out_specs=[rows(width), rows(out)],
        out_shape=[
            jax.ShapeDtypeStruct((tokens, width), LOW),
            jax.ShapeDtypeStruct((tokens, out), LOW),
        ],
        compiler_params=params(40),
        cost_estimate=cost(2 * tokens * width * out, 12 << 20),
        name="project",
    )(x, gain, w_query, w_key, w_value)


def after_attention_kernel(room, o_ref, x_ref, w_ref, gain_ref, code_ref, rank_ref, y_ref, *rest):
    outs, held = rest[:-1], rest[-1]
    step = o_ref.shape[0]
    i = pl.program_id(0)
    y = x_ref[...].astype(jnp.float32) + dot(o_ref[...], w_ref[...])
    y_ref[...] = y
    rms = lax.rsqrt(jnp.mean(y * y, axis=-1, keepdims=True) + EPSILON)
    held[pl.ds(pl.multiple_of(i * step, step), step), :] = (y * rms * gain_ref[...]).astype(LOW)

    @pl.when(i == pl.num_programs(0) - 1)
    def _():
        spread_all(code_ref[...], rank_ref[...], room, held[...], outs)


def after_attention(joined, x, w_output, gain, code, rank, experts, room):
    tokens, width = x.shape
    step = 256
    rows = pl.BlockSpec((step, width), lambda i: (i, 0))
    outs = buffers(experts, room, width)
    return pl.pallas_call(
        functools.partial(after_attention_kernel, room),
        grid=(tokens // step,),
        in_specs=[
            rows, rows, whole((width, width)), whole((1, width)), whole((1, tokens)), whole((1, tokens)),
        ],
        out_specs=[rows] + [pl.BlockSpec(o.shape, lambda i: (0, 0)) for o in outs],
        out_shape=[jax.ShapeDtypeStruct((tokens, width), jnp.float32)] + outs,
        scratch_shapes=[pltpu.VMEM((tokens, width), LOW)],
        compiler_params=params(48),
        cost_estimate=cost(2 * tokens * width * (width + experts * room), 12 << 20),
        name="after_attention",
    )(joined, x, w_output, gain, code, rank)


def mix_kernel(experts, room, code_ref, rank_ref, eid_ref, y_ref, gain_ref, wr_ref, *rest):
    backs, out_ref = rest[:-1], rest[-1]
    y = y_ref[...]
    rms = lax.rsqrt(jnp.mean(y * y, axis=-1, keepdims=True) + EPSILON)
    normed = (y * rms * gain_ref[...]).astype(LOW)
    router = route_softmax(dot(normed, wr_ref[...]), experts)
    lane = lax.broadcasted_iota(jnp.int32, router.shape, 1)
    gate = jnp.sum(jnp.where(lane == eid_ref[...], router, 0.0), axis=-1, keepdims=True)
    out_ref[...] = (y + gate * collect_all(code_ref[...], rank_ref[...], room, backs)).astype(LOW)


def back_specs(backs, tokens, step):
    return [
        pl.BlockSpec((step, b.shape[1]), lambda i: (i, 0)) if b.shape[0] == tokens and n == 3
        else whole(b.shape)
        for n, b in enumerate(backs)
    ]


def route_softmax(logits, experts):
    lane = lax.broadcasted_iota(jnp.int32, logits.shape, 1)
    logits = jnp.where(lane < experts, logits, NEGATIVE)
    e = jnp.exp(logits - jnp.max(logits, axis=-1, keepdims=True))
    return e / jnp.sum(e, axis=-1, keepdims=True)


def mix(backs, code, rank, expert_ids, y, gain, w_router, experts, room):
    tokens, width = y.shape
    step = 256
    rows = lambda w: pl.BlockSpec((step, w), lambda i: (i, 0))
    return pl.pallas_call(
        functools.partial(mix_kernel, experts, room),
        grid=(tokens // step,),
        in_specs=[
            rows(1), rows(1), rows(1), rows(width), whole((1, width)), whole(w_router.shape),
            *back_specs(backs, tokens, step),
        ],
        out_specs=rows(width),
        out_shape=jax.ShapeDtypeStruct((tokens, width), LOW),
        compiler_params=params(40),
        cost_estimate=cost(2 * tokens * width * experts * room, 8 << 20),
        name="mix",
    )(code, rank, expert_ids.reshape(tokens, 1), y, gain, w_router, *backs)


def pack(values, first, height, out, at):
    for c in range(values.shape[1] // TILE):
        out[at + c * height : at + (c + 1) * height] = values[
            first : first + height, c * TILE : (c + 1) * TILE
        ].astype(LOW)


def before_attention_kernel(
    room, n_backs, code_ref, rank_ref, y_ref, g_ref, gain_ref, w_ref, o_ref, *rest
):
    backs = rest[:n_backs]
    dy_ref, do_ref, pack_ref, gg_ref, gw_ref = rest[n_backs:]
    i = pl.program_id(0)

    @pl.when(i == 0)
    def _():
        gw_ref[...] = jnp.zeros_like(gw_ref)
        gg_ref[...] = jnp.zeros_like(gg_ref)

    dh = collect_all(code_ref[...], rank_ref[...], room, backs)
    y = y_ref[...]
    rms = lax.rsqrt(jnp.mean(y * y, axis=-1, keepdims=True) + EPSILON)
    gg_ref[...] += jnp.sum(dh * y * rms, axis=0, keepdims=True)
    u = dh * gain_ref[...]
    dy = (
        g_ref[...].astype(jnp.float32)
        + rms * u
        - y * (rms * rms * rms) * jnp.mean(u * y, axis=-1, keepdims=True)
    )
    dy_ref[...] = dy
    low = dy.astype(LOW)
    do_ref[...] = dot_t(low, w_ref[...]).astype(LOW)
    gw_ref[...] += dot(o_ref[...].T, low)

    @pl.when(i == pl.num_programs(0) - 1)
    def _():
        pack(gw_ref, 0, gw_ref.shape[0], pack_ref, 0)


def before_attention(backs, code, rank, y, g, gain, w_output, joined, room):
    tokens, width = y.shape
    step = 256
    rows = lambda w: pl.BlockSpec((step, w), lambda i: (i, 0))
    return pl.pallas_call(
        functools.partial(before_attention_kernel, room, len(backs)),
        grid=(tokens // step,),
        in_specs=[
            rows(1), rows(1), rows(width), rows(width), whole((1, width)),
            whole((width, width)), rows(width), *back_specs(backs, tokens, step),
        ],
        out_specs=[
            rows(width), rows(width),
            pl.BlockSpec((width * width // TILE, TILE), lambda i: (0, 0)),
            pl.BlockSpec((1, width), lambda i: (0, 0)),
        ],
        out_shape=[
            jax.ShapeDtypeStruct((tokens, width), jnp.float32),
            jax.ShapeDtypeStruct((tokens, width), LOW),
            jax.ShapeDtypeStruct((width * width // TILE, TILE), LOW),
            jax.ShapeDtypeStruct((1, width), jnp.float32),
        ],
        scratch_shapes=[pltpu.VMEM((width, width), jnp.float32)],
        compiler_params=params(40),
        cost_estimate=cost(6 * tokens * width * width, 16 << 20),
        name="before_attention",
    )(code, rank, y, g, gain, w_output, joined, *backs)


def finish_kernel(
    buckets,
    dq_ref, dk_ref, dv_ref, wq_ref, wk_ref, wv_ref, normed_ref, x_ref, dy_ref, gain_ref, go_ref, gr_ref, gg2_ref, table_ref,
    out_ref, pack_ref, gw_ref, gg_ref,
):
    i = pl.program_id(0)

    @pl.when(i == 0)
    def _():
        gw_ref[...] = jnp.zeros_like(gw_ref)
        gg_ref[...] = jnp.zeros_like(gg_ref)

    width = x_ref.shape[1]
    grads = (dq_ref[...], dk_ref[...], dv_ref[...])
    normed_t = normed_ref[...].T
    dh = None
    for n, (d, w_ref) in enumerate(zip(grads, (wq_ref, wk_ref, wv_ref))):
        gw_ref[n * width : (n + 1) * width] += dot(normed_t, d)
        part = dot_t(d, w_ref[...])
        dh = part if dh is None else dh + part
    x = x_ref[...].astype(jnp.float32)
    rms = lax.rsqrt(jnp.mean(x * x, axis=-1, keepdims=True) + EPSILON)
    gg_ref[...] += jnp.sum(dh * x * rms, axis=0, keepdims=True)
    u = dh * gain_ref[...]
    out_ref[...] = (
        dy_ref[...]
        + rms * u
        - x * (rms * rms * rms) * jnp.mean(u * x, axis=-1, keepdims=True)
    )

    @pl.when(i == pl.num_programs(0) - 1)
    def _():
        block = width * width // TILE
        for n in range(3):
            pack(gw_ref, n * width, width, pack_ref, n * block)
        pack_ref[3 * block : 4 * block] = go_ref[...]
        at = 4 * block
        routed = gr_ref.shape[0]
        pack_ref[at : at + routed] = gr_ref[...].astype(LOW)
        at = at + routed
        rows = width // TILE
        gains = [gg_ref[:, c * TILE : (c + 1) * TILE] for c in range(rows)]
        gains += [gg2_ref[:, c * TILE : (c + 1) * TILE] for c in range(rows)]
        gains += [jnp.zeros((16 - 2 * rows % 16, TILE), jnp.float32)] if 2 * rows % 16 else []
        gains = jnp.concatenate(gains, axis=0)
        pack_ref[at : at + gains.shape[0]] = gains.astype(LOW)
        at = at + gains.shape[0]
        table = bucket_table(table_ref, buckets)
        table = jnp.concatenate([table, jnp.zeros((-table.shape[0] % 16, TILE), jnp.float32)], axis=0)
        pack_ref[at : at + table.shape[0]] = table.astype(LOW)
        at = at + table.shape[0]
        pack_ref[at:] = jnp.zeros((pack_ref.shape[0] - at, TILE), LOW)


def finish(dq, dk, dv, w_query, w_key, w_value, normed, x, dy, gain, go, gr, gg2, table, buckets, rows_packed):
    tokens, width = x.shape
    step = 512
    rows = pl.BlockSpec((step, width), lambda i: (i, 0))
    return pl.pallas_call(
        functools.partial(finish_kernel, buckets),
        grid=(tokens // step,),
        in_specs=[
            rows, rows, rows, *[whole((width, width))] * 3, rows, rows, rows, whole((1, width)),
            whole(go.shape), whole(gr.shape), whole(gg2.shape), whole(table.shape),
        ],
        out_specs=[rows, pl.BlockSpec((rows_packed, TILE), lambda i: (0, 0))],
        out_shape=[
            jax.ShapeDtypeStruct((tokens, width), jnp.float32),
            jax.ShapeDtypeStruct((rows_packed, TILE), LOW),
        ],
        scratch_shapes=[
            pltpu.VMEM((3 * width, width), jnp.float32),
            pltpu.VMEM((1, width), jnp.float32),
        ],
        compiler_params=params(56),
        cost_estimate=cost(12 * tokens * width * width, 24 << 20),
        name="finish",
    )(dq, dk, dv, w_query, w_key, w_value, normed, x, dy, gain, go, gr, gg2, table)


def unpack_kernel(*refs):
    for packed_ref, out_ref in zip(refs[:4], refs[4:]):
        out_ref[...] = packed_ref[...].astype(jnp.float32)


def unpack(packed, width):
    blocks = width // TILE
    source = lambda m: pl.BlockSpec((width, TILE), lambda i: (m * blocks + i, 0))
    return pl.pallas_call(
        unpack_kernel,
        grid=(blocks,),
        in_specs=[source(m) for m in range(4)],
        out_specs=[pl.BlockSpec((width, TILE), lambda i: (0, i))] * 4,
        out_shape=[jax.ShapeDtypeStruct((width, width), jnp.float32)] * 4,
        compiler_params=params(32),
        name="unpack",
    )(*[packed] * 4)


def attention_forward_kernel(len_ref, q_ref, k_ref, v_ref, near_ref, far_ref, o_ref, p_ref, s_ref):
    seq = q_ref.shape[0]
    tiles = seq // TILE
    half = q_ref.shape[1] // 2
    row = pl.program_id(0)
    pair = pl.program_id(1)
    live = len_ref[row]
    lane = lax.broadcasted_iota(jnp.int32, (seq, 2 * half), 1)
    dead = lax.broadcasted_iota(jnp.int32, (seq, 2 * half), 0) >= live
    q = q_ref[...]
    k = k_ref[...]
    v_t = v_ref[...].T
    outs = []
    for h in range(2):
        mine = (lane >= h * half) & (lane < (h + 1) * half)
        flag = lane == (1 - h) * half
        k_h = jnp.where(mine, k, jnp.where(flag & dead, -1e30, 0.0).astype(k.dtype))
        q_h = jnp.where(flag, jnp.ones_like(q), q)
        after = far_ref[2 * pair + h, 0]
        before = far_ref[2 * pair + h, 1]
        tops = []
        for i in range(tiles):
            q_i = q_h[i * TILE:(i + 1) * TILE]
            raw = lax.dot_general(k_h, q_i, (((1,), (1,)), ((), ())), preferred_element_type=jnp.float32)
            top = None
            for j in range(tiles):
                x = raw[j * TILE:(j + 1) * TILE] * (0.125 * LOG2E)
                d = j - i
                if -1 <= d <= 1:
                    x = x + near_ref[h, d + 1]
                else:
                    x = x + (after if d > 0 else before)
                s_ref[j * TILE:(j + 1) * TILE, i * TILE:(i + 1) * TILE] = x
                m = jnp.max(x, axis=0, keepdims=True)
                top = m if top is None else jnp.maximum(top, m)
            tops.append(top)
        for i in range(tiles):
            e = jnp.exp2(s_ref[:, i * TILE:(i + 1) * TILE] - tops[i])
            total = jnp.sum(e, axis=0, keepdims=True)
            p_ref[0, h, :, i * TILE:(i + 1) * TILE] = (e * (1.0 / total)).astype(LOW)
        outs.append(lax.dot_general(v_t[h * half:(h + 1) * half], p_ref[0, h], (((1,), (0,)), ((), ())), preferred_element_type=jnp.float32))
    o_ref[...] = jnp.concatenate(outs, axis=0).T.astype(o_ref.dtype)

def attention_forward(lengths, projected, near, far, rows, seq, heads, head):
    width = heads * head
    pairs = heads // 2
    spec = lambda off: pl.BlockSpec((seq, 2 * head), lambda b, p: (b, off + p))
    return pl.pallas_call(
        attention_forward_kernel,
        grid=(rows, pairs),
        in_specs=[
            pl.BlockSpec(memory_space=pltpu.SMEM),
            spec(0), spec(pairs), spec(2 * pairs),
            pl.BlockSpec((2, 3, TILE, TILE), lambda b, p: (p, 0, 0, 0)),
            pl.BlockSpec(memory_space=pltpu.SMEM),
        ],
        out_specs=[
            pl.BlockSpec((seq, 2 * head), lambda b, p: (b, p)),
            pl.BlockSpec((1, 2, seq, seq), lambda b, p: (b, p, 0, 0)),
        ],
        out_shape=[
            jax.ShapeDtypeStruct((rows * seq, width), LOW),
            jax.ShapeDtypeStruct((rows, heads, seq, seq), LOW),
        ],
        scratch_shapes=[pltpu.VMEM((seq, seq), jnp.float32)],
        compiler_params=params(40),
        cost_estimate=cost(flops=4 * rows * heads * seq * seq * head * 4, bytes_accessed=rows * heads * seq * seq * 2, transcendentals=rows * heads * seq * seq),
        name="attention_forward",
    )(lengths, projected, projected, projected, near, far)

def attention_backward_kernel(q_ref, k_ref, v_ref, do_ref, o_ref, p_ref, dq_ref, dk_ref, dv_ref, table_ref, near_ref, far_ref, d_ref):
    seq = q_ref.shape[0]
    tiles = seq // TILE
    half = q_ref.shape[1] // 2
    row = pl.program_id(1)
    lane = lax.broadcasted_iota(jnp.int32, (seq, 2 * half), 1)
    q = q_ref[...]
    k = k_ref[...]
    k_t = k.T
    v = v_ref[...]
    do = do_ref[...]
    weighed = (do.astype(jnp.float32) * o_ref[...].astype(jnp.float32)).T
    dq_parts = []
    dk_all = None
    dv_all = None

    @pl.when(row == 0)
    def _():
        near_ref[...] = jnp.zeros_like(near_ref)
        far_ref[...] = jnp.zeros_like(far_ref)

    for h in range(2):
        mine = (lane >= h * half) & (lane < (h + 1) * half)
        v_h = jnp.where(mine, v, jnp.zeros_like(v))
        delta = jnp.sum(weighed[h * half:(h + 1) * half], axis=0, keepdims=True)
        far_sum = [jnp.zeros((8, TILE), jnp.float32), jnp.zeros((8, TILE), jnp.float32)]
        for i in range(tiles):
            cols = slice(i * TILE, (i + 1) * TILE)
            dp = lax.dot_general(v_h, do[cols], (((1,), (1,)), ((), ())), preferred_element_type=jnp.float32)
            for j in range(tiles):
                rws = slice(j * TILE, (j + 1) * TILE)
                ds = p_ref[0, h, rws, cols].astype(jnp.float32) * (dp[rws] - delta[:, cols])
                d = j - i
                if -1 <= d <= 1:
                    near_ref[h, d + 1] += ds
                else:
                    which = 0 if d > 0 else 1
                    far_sum[which] = far_sum[which] + jnp.sum(ds.reshape(TILE // 8, 8, TILE), axis=0)
                d_ref[rws, cols] = ds.astype(LOW)
        far_ref[h, 0] += far_sum[0]
        far_ref[h, 1] += far_sum[1]
        ds_all = d_ref[...]
        dq_parts.append(lax.dot_general(k_t[h * half:(h + 1) * half], ds_all, (((1,), (0,)), ((), ())), preferred_element_type=jnp.float32))
        dk_h = lax.dot_general(ds_all, q, (((1,), (0,)), ((), ())), preferred_element_type=jnp.float32)
        dv_h = lax.dot_general(p_ref[0, h], do, (((1,), (0,)), ((), ())), preferred_element_type=jnp.float32)
        dk_all = dk_h if h == 0 else jnp.where(mine, dk_h, dk_all)
        dv_all = dv_h if h == 0 else jnp.where(mine, dv_h, dv_all)
    @pl.when(row == pl.num_programs(1) - 1)
    def _():
        bucket_sums(near_ref, far_ref, table_ref)

    dq_ref[...] = (jnp.concatenate(dq_parts, axis=0).T * 0.125).astype(LOW)
    dk_ref[...] = (dk_all * 0.125).astype(LOW)
    dv_ref[...] = dv_all.astype(LOW)

def bucket_sums(near_ref, far_ref, table_ref):
    empty = jnp.zeros((8, TILE), jnp.float32)
    sub = lax.broadcasted_iota(jnp.int32, (8, 2 * TILE), 0)
    for h in range(2):
        lines = []
        for d in range(3):
            turned = None
            for a in range(0, TILE, 8):
                part = jnp.concatenate([near_ref[h, d, a : a + 8], empty], axis=1)
                part = pltpu.roll(part, (2 * TILE - a) % (2 * TILE), 1) if a else part
                turned = part if turned is None else turned + part
            for b in (1, 2, 4):
                turned = jnp.where((sub & b) > 0, pltpu.roll(turned, 2 * TILE - b, 1), turned)
            lines.append(jnp.sum(turned, axis=0, keepdims=True))
        for side in range(2):
            total = jnp.sum(far_ref[h, side], axis=0, keepdims=True)
            lines.append(jnp.concatenate([total, jnp.zeros((1, TILE), jnp.float32)], axis=1))
        lines.append(jnp.zeros((3, 2 * TILE), jnp.float32))
        table_ref[h] = jnp.concatenate(lines, axis=0)


def bucket_table(lines_ref, buckets):
    heads = lines_ref.shape[0]
    lane = lax.broadcasted_iota(jnp.int32, (2 * TILE, TILE), 0)
    bucket = lax.broadcasted_iota(jnp.int32, (2 * TILE, TILE), 1)
    turn = jnp.where(lane >= TILE, lane - 2 * TILE, lane)
    total = None
    for r in range(5):
        if r < 3:
            hit = bucket_of((r - 1) * TILE - turn) == bucket
        else:
            hit = bucket == (buckets - 1 if r == 3 else buckets // 2 - 1)
        hit = hit.astype(LOW)
        line = jnp.concatenate([lines_ref[h, r : r + 1, :] for h in range(heads)], axis=0)
        high = line.astype(LOW)
        part = dot(high, hit) + dot((line - high.astype(jnp.float32)).astype(LOW), hit)
        total = part if total is None else total + part
    return total


def attention_backward(projected, do, joined, weights, rows, seq, heads, head):
    width = heads * head
    pairs = heads // 2
    spec = lambda off: pl.BlockSpec((seq, 2 * head), lambda p, b: (b, off + p))
    return pl.pallas_call(
        attention_backward_kernel,
        grid=(pairs, rows),
        in_specs=[
            spec(0), spec(pairs), spec(2 * pairs), spec(0), spec(0),
            pl.BlockSpec((1, 2, seq, seq), lambda p, b: (b, p, 0, 0)),
        ],
        out_specs=[
            spec(0), spec(0), spec(0),
            pl.BlockSpec((2, 8, 2 * TILE), lambda p, b: (p, 0, 0)),
        ],
        out_shape=[jax.ShapeDtypeStruct((rows * seq, width), LOW)] * 3 + [
            jax.ShapeDtypeStruct((heads, 8, 2 * TILE), jnp.float32),
        ],
        scratch_shapes=[
            pltpu.VMEM((2, 3, TILE, TILE), jnp.float32),
            pltpu.VMEM((2, 2, 8, TILE), jnp.float32),
            pltpu.VMEM((seq, seq), LOW),
        ],
        compiler_params=params(40),
        cost_estimate=cost(flops=8 * rows * heads * seq * seq * head * 4, bytes_accessed=rows * heads * seq * seq * 2, transcendentals=0),
        name="attention_backward",
    )(projected, projected, projected, do, joined, weights)

def bias_tiles(table):
    j = lax.broadcasted_iota(jnp.int32, (3, TILE, TILE), 1)
    i = lax.broadcasted_iota(jnp.int32, (3, TILE, TILE), 2)
    d = lax.broadcasted_iota(jnp.int32, (3, TILE, TILE), 0) - 1
    b = bucket_of(d * TILE + j - i)
    scaled = table.T * LOG2E
    hot = (b.reshape(1, -1) == jnp.arange(table.shape[0], dtype=jnp.int32)[:, None]).astype(jnp.float32)
    near = jnp.dot(scaled, hot, precision=lax.Precision.HIGHEST).reshape(-1, 3, TILE, TILE)
    far = jnp.stack([scaled[:, -1], scaled[:, table.shape[0] // 2 - 1]], axis=1)
    return near, far


def expert_kernel(experts, chunk, x_ref, g_ref, mine_ref, wr_ref, wi_any, wo_any,
                  ff_ref, dx_ref, hid_ref, da_ref, xt_ref, dfft_ref, gr_ref, wi_ref, wo_ref, sem):
    inner = wi_ref.shape[1]
    first_step = pl.program_id(0) == 0

    def loads(f):
        cols = pl.ds(f, chunk)
        return (pltpu.make_async_copy(wi_any.at[:, cols], wi_ref.at[:, cols], sem.at[0, f // chunk]),
                pltpu.make_async_copy(wo_any.at[cols, :], wo_ref.at[cols, :], sem.at[1, f // chunk]))

    @pl.when(first_step)
    def _():
        for f in range(0, inner, chunk):
            for c in loads(f):
                c.start()
        gr_ref[...] = jnp.zeros_like(gr_ref)

    x = x_ref[...]
    g = g_ref[...].reshape(x.shape).astype(jnp.float32)
    mine = mine_ref[...]
    lane = lax.broadcasted_iota(jnp.int32, (1, wr_ref.shape[1]), 1)
    logits = jnp.dot(x, wr_ref[...], preferred_element_type=jnp.float32)
    logits = jnp.where(lane < experts, logits, -1e30)
    e = jnp.exp(logits - jnp.max(logits, axis=-1, keepdims=True))
    router = e / jnp.sum(e, axis=-1, keepdims=True)
    gate = jnp.sum(router * mine, axis=-1, keepdims=True)
    dff = (g * gate).astype(LOW)
    ff = None
    dx = None
    def first(f):
        @pl.when(first_step)
        def _():
            for c in loads(f):
                c.wait()
        cols = slice(f, f + chunk)
        return (jnp.dot(x, wi_ref[:, cols], preferred_element_type=jnp.float32),
                lax.dot_general(dff, wo_ref[cols, :], (((1,), (1,)), ((), ())), preferred_element_type=jnp.float32))
    for f in range(0, inner, chunk):
        cols = slice(f, f + chunk)
        a, dhid = first(f)
        u = a * a
        t = jnp.tanh(a * (GELU_A + GELU_B * u))
        h = 0.5 + 0.5 * t
        hid = a * h
        slope = h + hid * ((1.0 - t) * (GELU_A + (3.0 * GELU_B) * u))
        da = (dhid * slope).astype(LOW)
        hid = hid.astype(LOW)
        hid_ref[:, cols] = hid
        da_ref[:, cols] = da
        ff_part = jnp.dot(hid, wo_ref[cols, :], preferred_element_type=jnp.float32)
        dx_part = lax.dot_general(da, wi_ref[:, cols], (((1,), (1,)), ((), ())), preferred_element_type=jnp.float32)
        ff = ff_part if ff is None else ff + ff_part
        dx = dx_part if dx is None else dx + dx_part
    ff = ff.astype(LOW)
    ff_ref[...] = ff
    dgate = jnp.sum(g * ff.astype(jnp.float32), axis=-1, keepdims=True)
    dlogits = ((gate * dgate) * (mine - router)).astype(LOW)
    dx = dx + lax.dot_general(dlogits, wr_ref[...], (((1,), (1,)), ((), ())), preferred_element_type=jnp.float32)
    dx_ref[...] = dx.astype(LOW)
    x_t = x.T
    xt_ref[...] = x_t
    dfft_ref[...] = dff.T
    gr_ref[...] += jnp.dot(x_t, dlogits, preferred_element_type=jnp.float32)

def expert_rows(x, g, mine, wr, wi, wo, experts, low, high, tile=256, chunk=1024):
    n, width = x.shape
    inner = wi.shape[1]
    sources, room = g.shape[0], high - low
    tile = min(tile, n)
    group = tile // room
    gspec = pl.BlockSpec((group, room, width), lambda i: (i, low // room, 0))
    once = lambda s: pl.BlockSpec(s, lambda i: (0,) * len(s), pipeline_mode=pl.Buffered(1))
    rowspec = lambda w: pl.BlockSpec((tile, w), lambda i: (i, 0))
    anywhere = pl.BlockSpec(memory_space=pl.ANY)
    return pl.pallas_call(
        functools.partial(expert_kernel, experts, chunk),
        grid=(n // tile,),
        in_specs=[rowspec(width), gspec, once(mine.shape), once(wr.shape), anywhere, anywhere],
        out_specs=[rowspec(width), rowspec(width), rowspec(inner), rowspec(inner),
                   pl.BlockSpec((width, tile), lambda i: (0, i)), pl.BlockSpec((width, tile), lambda i: (0, i)),
                   pl.BlockSpec((width, wr.shape[1]), lambda i: (0, 0))],
        out_shape=[jax.ShapeDtypeStruct((n, width), LOW)] * 2 + [jax.ShapeDtypeStruct((n, inner), LOW)] * 2
            + [jax.ShapeDtypeStruct((width, n), LOW)] * 2 + [jax.ShapeDtypeStruct((width, wr.shape[1]), jnp.float32)],
        scratch_shapes=[pltpu.VMEM(wi.shape, LOW), pltpu.VMEM(wo.shape, LOW), pltpu.SemaphoreType.DMA((2, inner // chunk))],
        compiler_params=params(60),
        cost_estimate=cost(flops=8 * n * width * inner, bytes_accessed=4 * n * inner + 8 * width * inner, transcendentals=n * inner),
        name="expert_rows",
    )(x, g, mine, wr, wi, wo)

def expert_weights_kernel(parts, *refs):
    ins, (gi_ref, go_ref) = refs[:4 * parts], refs[4 * parts:]
    gi = None
    go = None
    for c in range(parts):
        xt, dfft, hid, da = ins[4 * c:4 * c + 4]
        gi_c = jnp.dot(xt[...], da[...], preferred_element_type=jnp.float32)
        go_c = jnp.dot(dfft[...], hid[...], preferred_element_type=jnp.float32)
        gi = gi_c if gi is None else gi + gi_c
        go = go_c if go is None else go + go_c
    gi_ref[0] = gi
    go_ref[0] = go.T

def expert_weights(parts, tile=512):
    inner = parts[0][2].shape[1]
    width = parts[0][0].shape[0]
    specs, args, rows = [], [], 0
    for xt, dfft, hid, da in parts:
        n = hid.shape[0]
        rows += n
        specs += [pl.BlockSpec((width, n), lambda f: (0, 0), pipeline_mode=pl.Buffered(1))] * 2
        specs += [pl.BlockSpec((n, tile), lambda f: (0, f))] * 2
        args += [xt, dfft, hid, da]
    return pl.pallas_call(
        functools.partial(expert_weights_kernel, len(parts)),
        grid=(inner // tile,),
        in_specs=specs,
        out_specs=[pl.BlockSpec((1, width, tile), lambda f: (0, 0, f)), pl.BlockSpec((1, tile, width), lambda f: (0, f, 0))],
        out_shape=[jax.ShapeDtypeStruct((1, width, inner), jnp.float32), jax.ShapeDtypeStruct((1, inner, width), jnp.float32)],
        compiler_params=params(60),
        cost_estimate=cost(flops=4 * rows * width * inner, bytes_accessed=4 * rows * inner + 8 * width * inner, transcendentals=0),
        name="expert_weights",
    )(*args)


def sum_parts(bits, units):
    upper = list(range(1, bits))
    turns = min(6, units, 2 * max(1, min(3, len(upper))))
    sizes = [(units + t) // turns for t in range(turns)]
    orders = [[0] + upper[t % 3 :] + upper[: t % 3] for t in range(turns)]
    return sizes, orders


def sum_kernel(cores, bits, sizes, orders, x_ref, out_ref, work_ref, got_ref, send, recv):
    n = 1 << bits
    me = lax.axis_index("grp") * cores + lax.axis_index("exp")
    barrier = pltpu.get_barrier_semaphore()
    def place(d):
        return dict(device_id=(d // cores, d % cores), device_id_type=pl.DeviceIdType.MESH)
    def other(b):
        bit = (me // (1 << b)) % 2
        return bit, me + (1 - 2 * bit) * (1 << b)
    for b in range(bits):
        pl.semaphore_signal(barrier, inc=1, **place(other(b)[1]))
    pl.semaphore_wait(barrier, bits)
    parts = len(sizes)
    starts = [sum(sizes[:p]) * 16 * n for p in range(parts)]
    base = list(starts)
    got_at = list(starts)
    def rows(start, length):
        return pl.ds(pl.multiple_of(start, 16), length)
    def halving(p, s):
        length = sizes[p] * 16 * (n >> (s + 1))
        bit, partner = other(orders[p][s])
        source = x_ref if s == 0 else work_ref
        return pltpu.make_async_remote_copy(
            src_ref=source.at[rows(base[p] + (1 - bit) * length, length)],
            dst_ref=got_ref.at[rows(got_at[p], length)],
            send_sem=send.at[p, s], recv_sem=recv.at[p, s], **place(partner))
    pending = {}
    for p in range(parts):
        pending[p] = halving(p, 0); pending[p].start()
    sends = []
    for s in range(bits):
        for p in range(parts):
            length = sizes[p] * 16 * (n >> (s + 1))
            bit, partner = other(orders[p][s])
            keep = base[p] + bit * length
            pending[p].wait_recv()
            sends.append(pending[p])
            step = sizes[p] * 16
            source = x_ref if s == 0 else work_ref
            target = work_ref if s + 1 < bits else out_ref
            def add(i, _, keep=keep, source=source, target=target, at=got_at[p], step=step):
                here = rows(keep + i * step, step)
                arrived = got_ref[rows(at + i * step, step), :].astype(jnp.float32)
                target[here, :] = (source[here, :].astype(jnp.float32) + arrived).astype(LOW)
                return 0
            lax.fori_loop(0, length // step, add, 0)
            base[p] = keep
            got_at[p] += length
            if s + 1 < bits:
                pending[p] = halving(p, s + 1); pending[p].start()
    for c in sends:
        c.wait_send()
    back = {}
    def doubling(p, s):
        length = sizes[p] * 16 * (n >> (s + 1))
        bit, partner = other(orders[p][s])
        return pltpu.make_async_remote_copy(
            src_ref=out_ref.at[rows(base[p], length)], dst_ref=out_ref.at[rows(base[p], length)],
            send_sem=send.at[p, bits + s], recv_sem=recv.at[p, bits + s], **place(partner))
    for p in range(parts):
        back[p] = doubling(p, bits - 1); back[p].start()
    sends = []
    for s in reversed(range(bits)):
        for p in range(parts):
            length = sizes[p] * 16 * (n >> (s + 1))
            bit, partner = other(orders[p][s])
            back[p].wait_recv()
            sends.append(back[p])
            base[p] = base[p] - bit * length
            if s > 0:
                back[p] = doubling(p, s - 1); back[p].start()
    for c in sends:
        c.wait_send()

def all_sum(x, cid=1):
    cores = lax.axis_size("exp")
    n = lax.axis_size(AXES)
    bits = n.bit_length() - 1
    units = x.shape[0] // (16 * n)
    sizes, orders = sum_parts(bits, units)
    parts = len(sizes)
    return pl.pallas_call(
        functools.partial(sum_kernel, cores, bits, sizes, orders),
        out_shape=jax.ShapeDtypeStruct(x.shape, x.dtype),
        in_specs=[pl.BlockSpec(memory_space=pltpu.VMEM)],
        out_specs=pl.BlockSpec(memory_space=pltpu.VMEM),
        scratch_shapes=[pltpu.VMEM(x.shape, x.dtype), pltpu.VMEM(x.shape, x.dtype), pltpu.SemaphoreType.DMA((parts, 2 * bits)), pltpu.SemaphoreType.DMA((parts, 2 * bits))],
        compiler_params=params(40, collective_id=cid, has_side_effects=True),
        name="all_sum",
    )(x)


def local(
    tokens, lengths, expert_ids, slots, w_query, w_key, w_value, w_output,
    gain_attn, gain_ffn, bias_table, w_router, w_in, w_out, cotangent,
):
    rows, seq, width = tokens.shape
    count = rows * seq
    buckets, heads = bias_table.shape
    head = width // heads
    experts = w_router.shape[1]
    devices = lax.axis_size(AXES)
    room = max(4, 2 * count // experts)
    me = lax.axis_index(AXES)
    x = tokens.reshape(count, width)
    g = cotangent.reshape(count, width)
    gain_one = gain_attn.reshape(1, width)
    gain_two = gain_ffn.reshape(1, width)
    wide = max(128, experts)
    mine = (jnp.arange(wide, dtype=jnp.int32) == me).astype(jnp.float32).reshape(1, wide)

    code_c, code_r, rank_c, rank_r, tags, g_out = route(expert_ids, slots, g, experts, room)
    g_in = exchange(g_out, devices)
    code_r, x, w_query, w_key, w_value, w_output, bias_table, w_router = lax.optimization_barrier(
        (code_r, x, w_query, w_key, w_value, w_output, bias_table, w_router)
    )
    router_w = jnp.pad(w_router, ((0, 0), (0, wide - experts)))

    normed, projected = project(x, gain_one, w_query, w_key, w_value)
    near, far = bias_tiles(bias_table)
    joined, weights = attention_forward(lengths, projected, near, far, rows, seq, heads, head)
    y, *h_out = after_attention(joined, x, w_output, gain_two, code_r, rank_r, experts, room)
    h_out, g_in = lax.optimization_barrier((h_out, g_in))

    g_in = g_in.reshape(devices, room, width)
    segments, _ = plan(room)
    h_in, dx_back, ffs, parts, grad_router = [], [], [], [], 0.0
    for h in h_out:
        if h_in:
            h, h_in[-1] = lax.optimization_barrier((h, h_in[-1]))
        h_in.append(exchange(h, devices))
    for n, (low, high) in enumerate(segments):
        ff, dx, hid, da, x_t, dff_t, routed = expert_rows(
            h_in[n], g_in, mine, router_w, w_in[0], w_out[0], experts, low, high
        )
        if n + 1 < len(segments):
            dx, h_in[n + 1] = lax.optimization_barrier((dx, h_in[n + 1]))
        if n:
            dx, dx_back[-1] = lax.optimization_barrier((dx, dx_back[-1]))
        dx_back.append(exchange(dx, devices))
        ffs.append(ff.reshape(devices, high - low, width))
        parts.append((x_t, dff_t, hid, da))
        grad_router = grad_router + routed
    grad_in, grad_out = expert_weights(parts)
    ff = jnp.concatenate(ffs, axis=1).reshape(devices * room, width) if len(ffs) > 1 else ffs[0].reshape(-1, width)
    dx_back, grad_in, grad_out, ff = lax.optimization_barrier((dx_back, grad_in, grad_out, ff))
    ff_back = exchange(ff, devices)
    grad_router = grad_router[:, :experts].reshape(width * experts // TILE, TILE)

    dy, do, grad_output, grad_gain_two = before_attention(
        dx_back, code_c, rank_c, y, g, gain_two, w_output, joined, room
    )
    dq, dk, dv, table = attention_backward(
        projected, do, joined, weights, rows, seq, heads, head
    )
    small = grad_router.shape[0] + -(-2 * width // TILE // 16) * 16 + -(-heads // 16) * 16
    block = width * width // TILE
    rows_packed = -(-(4 * block + small) // (16 * devices)) * 16 * devices
    grad_tokens, packed = finish(
        dq, dk, dv, w_query, w_key, w_value, normed, x, dy, gain_one, grad_output, grad_router, grad_gain_two, table, buckets, rows_packed
    )
    summed = all_sum(packed)
    summed, ff_back = lax.optimization_barrier((summed, ff_back))
    mixed = mix([ff_back], code_c, rank_c, expert_ids, y, gain_two, router_w, experts, room)
    grads = unpack(summed, width)
    at = 4 * block
    rest = summed[at : at + small].astype(jnp.float32)
    routed = grad_router.shape[0]
    grad_router = rest[:routed].reshape(width, experts)
    lines = width // TILE
    grad_gain_one = rest[routed : routed + lines].reshape(width)
    grad_gain_two = rest[routed + lines : routed + 2 * lines].reshape(width)
    grad_table = rest[small - -(-heads // 16) * 16 :][:heads, :buckets].T
    return (
        mixed.reshape(rows, seq, width),
        grad_tokens.reshape(rows, seq, width),
        grads[0], grads[1], grads[2], grads[3],
        grad_gain_one, grad_gain_two, grad_table, grad_router,
        grad_in,
        grad_out,
    )


def solution(mesh):
    split = P(AXES)
    in_specs = (split,) * 4 + (P(),) * 8 + (split,) * 3
    out_specs = (split,) * 2 + (P(),) * 8 + (split,) * 2
    return jax.shard_map(local, mesh=mesh, in_specs=in_specs, out_specs=out_specs, check_vma=False)
```

```python
import functools

import jax
import jax.numpy as jnp
from jax import lax
from jax.experimental import pallas as pl
from jax.experimental.pallas import tpu as pltpu
from jax.sharding import PartitionSpec as P

EPSILON = 1e-06
NEGATIVE = -1e30
THRESHOLDS = (12, 16, 23, 32, 46, 64, 91)
LOG2E = 1.4426950408889634
TILE = 128
GELU_A = 0.7978845608028654
GELU_B = GELU_A * 0.044715
AXES = ("grp", "exp")
LOW = jnp.bfloat16


def dot(a, b):
    return jnp.dot(a, b, preferred_element_type=jnp.float32)


def dot_t(a, b):
    return lax.dot_general(a, b, (((1,), (1,)), ((), ())), preferred_element_type=jnp.float32)


def params(mib, **more):
    return pltpu.CompilerParams(vmem_limit_bytes=mib << 20, **more)


def whole(shape):
    return pl.BlockSpec(shape, lambda *_: (0,) * len(shape), pipeline_mode=pl.Buffered(1))


def cost(flops, bytes_accessed, transcendentals=0):
    return pl.CostEstimate(
        flops=flops, bytes_accessed=bytes_accessed, transcendentals=transcendentals
    )


def bucket_of(offset):
    distance = jnp.abs(offset)
    far = jnp.full_like(distance, 8)
    for border in THRESHOLDS:
        far = far + (distance >= border).astype(jnp.int32)
    return jnp.where(distance < 8, distance, far) + jnp.where(offset > 0, 16, 0).astype(jnp.int32)


def plan(room):
    if room % 64:
        return ((0, room),), room, 0
    return ((0, room // 2), (room // 2, room)), 3 * room // 4, room // 4


def segment(code, room, low, high):
    expert = lax.div(code, room)
    place = code - expert * room
    inside = (code >= 0) & (place >= low) & (place < high)
    return jnp.where(inside, expert * (high - low) + place - low, -1)


def spread(dest, values, out):
    rows = out.shape[0]
    step = min(256, rows)
    for start in range(0, rows, step):
        here = lax.broadcasted_iota(jnp.int32, (step, dest.shape[1]), 0) + start
        out[start : start + step] = dot((dest == here).astype(LOW), values).astype(LOW)


def collect(dest, values):
    here = lax.broadcasted_iota(jnp.int32, (dest.shape[0], values.shape[0]), 1)
    return dot((dest == here).astype(LOW), values)


def spread_all(code, room, values, outs):
    for (low, high), out in zip(plan(room)[0], outs):
        spread(segment(code, room, low, high), values, out)


def collect_all(code, room, refs):
    total = None
    for (low, high), ref in zip(plan(room)[0], refs):
        part = collect(segment(code, room, low, high), ref[...])
        total = part if total is None else total + part
    return total


def buffers(experts, room, width):
    return [
        jax.ShapeDtypeStruct((experts * (high - low), width), LOW) for low, high in plan(room)[0]
    ]


def route_kernel(
    experts, room, eid_c, eid_r, slot_c, slot_r, g_ref, code_c, code_r, rank_c, out, more
):
    tokens = g_ref.shape[0]
    wide = max(TILE, experts)
    _, cut, extra = plan(room)
    at = lax.broadcasted_iota(jnp.int32, (tokens, tokens), 0)
    to = lax.broadcasted_iota(jnp.int32, (tokens, tokens), 1)
    before = (to < at).astype(LOW)
    after = (at < to).astype(LOW)

    ids = eid_c[...]
    picked = ids == lax.broadcasted_iota(jnp.int32, (tokens, wide), 1)
    place = jnp.sum(jnp.where(picked, dot(before, picked.astype(LOW)), 0.0), axis=1, keepdims=True)
    place = place.astype(jnp.int32)
    kept = slot_c[...] >= 0
    code_c[...] = jnp.where(kept, ids * room + place, -1)
    over = jnp.broadcast_to(jnp.where(kept & (place >= cut), 1.0, 0.0), (tokens, TILE))
    rank = jnp.where(over > 0, dot(before, over.astype(LOW)).astype(jnp.int32), -1)
    rank_c[...] = rank[:, :1]
    ids = eid_r[...]
    picked = ids == lax.broadcasted_iota(jnp.int32, (wide, tokens), 0)
    place = jnp.sum(jnp.where(picked, dot(picked.astype(LOW), after), 0.0), axis=0, keepdims=True)
    place = place.astype(jnp.int32)
    kept = slot_r[...] >= 0
    code = jnp.where(kept, ids * room + place, -1)
    code_r[...] = code
    over = jnp.broadcast_to(jnp.where(kept & (place >= cut), 1.0, 0.0), (16, tokens))
    rank = jnp.where(over > 0, dot(over.astype(LOW), after).astype(jnp.int32), -1)[:1]
    spread(segment(code, room, 0, cut), g_ref[...], out)
    if not extra:
        more[...] = jnp.zeros(more.shape, LOW)
        return
    spread(rank, g_ref[...], more.at[:extra])
    rank = rank_c[...]
    lane = lax.broadcasted_iota(jnp.int32, (tokens, g_ref.shape[1]), 1)
    marks = jnp.where((rank == lane) & (lane < extra), eid_c[...] + 1, 0)
    marks = marks.astype(jnp.float32)
    marks = jnp.sum(marks, axis=0, keepdims=True)
    left = jnp.max(jnp.where(rank >= extra, 1.0, 0.0), axis=0, keepdims=True)
    marks = jnp.where(lane[:1] == extra, left, marks)
    line = lax.broadcasted_iota(jnp.int32, (more.shape[0] - extra, g_ref.shape[1]), 0)
    more[extra:] = jnp.where(line == 0, marks, 0.0).astype(LOW)


def route(expert_ids, slots, upstream, experts, room):
    tokens, width = upstream.shape
    column = jax.ShapeDtypeStruct((tokens, 1), jnp.int32)
    line = jax.ShapeDtypeStruct((1, tokens), jnp.int32)
    _, cut, extra = plan(room)
    return pl.pallas_call(
        functools.partial(route_kernel, experts, room),
        out_shape=[
            column, line, column,
            jax.ShapeDtypeStruct((experts * cut, width), LOW),
            jax.ShapeDtypeStruct((extra + 16, width), LOW),
        ],
        compiler_params=params(48),
        cost_estimate=cost(2 * experts * room * tokens * width, 8 << 20),
        name="route",
    )(
        expert_ids.reshape(tokens, 1), expert_ids.reshape(1, tokens),
        slots.reshape(tokens, 1), slots.reshape(1, tokens), upstream,
    )


def exchange(buffer, devices):
    shaped = buffer.reshape(devices, buffer.shape[0] // devices, buffer.shape[1])
    moved = lax.all_to_all(shaped, AXES, split_axis=0, concat_axis=0, tiled=True)
    return moved.reshape(buffer.shape)


def project_kernel(x_ref, gain_ref, wq_ref, wk_ref, wv_ref, normed_ref, out_ref):
    x = x_ref[...].astype(jnp.float32)
    rms = lax.rsqrt(jnp.mean(x * x, axis=-1, keepdims=True) + EPSILON)
    normed = (x * rms * gain_ref[...]).astype(LOW)
    normed_ref[...] = normed.T
    width = x.shape[1]
    for n, w_ref in enumerate((wq_ref, wk_ref, wv_ref)):
        out_ref[:, n * width : (n + 1) * width] = dot(normed, w_ref[...]).astype(LOW)


def project(x, gain, w_query, w_key, w_value):
    tokens, width = x.shape
    out = 3 * width
    step = 256
    rows = lambda w: pl.BlockSpec((step, w), lambda i: (i, 0))
    return pl.pallas_call(
        project_kernel,
        grid=(tokens // step,),
        in_specs=[rows(width), whole((1, width)), *[whole((width, width))] * 3],
        out_specs=[pl.BlockSpec((width, step), lambda i: (0, i)), rows(out)],
        out_shape=[
            jax.ShapeDtypeStruct((width, tokens), LOW),
            jax.ShapeDtypeStruct((tokens, out), LOW),
        ],
        compiler_params=params(60),
        cost_estimate=cost(2 * tokens * width * out, 12 << 20),
        name="project",
    )(x, gain, w_query, w_key, w_value)


def after_attention_kernel(
    experts, room, o_ref, x_ref, w_ref, gain_ref, eid_ref, wr_ref, code_ref, y_ref, gate_ref, *rest
):
    outs, held = rest[:-1], rest[-1]
    step = o_ref.shape[0]
    i = pl.program_id(0)
    y = x_ref[...].astype(jnp.float32) + dot(o_ref[...], w_ref[...])
    y_ref[...] = y
    rms = lax.rsqrt(jnp.mean(y * y, axis=-1, keepdims=True) + EPSILON)
    normed = (y * rms * gain_ref[...]).astype(LOW)
    held[pl.ds(pl.multiple_of(i * step, step), step), :] = normed
    router = route_softmax(dot(normed, wr_ref[...]), experts)
    lane = lax.broadcasted_iota(jnp.int32, router.shape, 1)
    gate_ref[...] = jnp.sum(jnp.where(lane == eid_ref[...], router, 0.0), axis=-1, keepdims=True)

    @pl.when(i == pl.num_programs(0) - 1)
    def _():
        spread_all(code_ref[...], room, held[...], outs)


def after_attention(joined, x, w_output, gain, expert_ids, w_router, code, experts, room):
    tokens, width = x.shape
    step = 256
    rows = pl.BlockSpec((step, width), lambda i: (i, 0))
    single = pl.BlockSpec((step, 1), lambda i: (i, 0))
    outs = buffers(experts, room, width)
    return pl.pallas_call(
        functools.partial(after_attention_kernel, experts, room),
        grid=(tokens // step,),
        in_specs=[
            rows, rows, whole((width, width)), whole((1, width)), single, whole(w_router.shape),
            whole((1, tokens)),
        ],
        out_specs=[rows, single] + [pl.BlockSpec(o.shape, lambda i: (0, 0)) for o in outs],
        out_shape=[
            jax.ShapeDtypeStruct((tokens, width), jnp.float32),
            jax.ShapeDtypeStruct((tokens, 1), jnp.float32),
        ]
        + outs,
        scratch_shapes=[pltpu.VMEM((tokens, width), LOW)],
        compiler_params=params(60),
        cost_estimate=cost(2 * tokens * width * (width + experts * room), 12 << 20),
        name="after_attention",
    )(joined, x, w_output, gain, expert_ids, w_router, code)


def route_softmax(logits, experts):
    lane = lax.broadcasted_iota(jnp.int32, logits.shape, 1)
    logits = jnp.where(lane < experts, logits, NEGATIVE)
    e = jnp.exp(logits - jnp.max(logits, axis=-1, keepdims=True))
    return e / jnp.sum(e, axis=-1, keepdims=True)


def pack(values, first, height, out, at):
    for c in range(values.shape[1] // TILE):
        out[at + c * height : at + (c + 1) * height] = values[
            first : first + height, c * TILE : (c + 1) * TILE
        ].astype(LOW)


def before_attention_kernel(
    room, n_backs, code_ref, y_ref, g_ref, gain_ref, w_ref, o_ref, *rest
):
    backs = rest[:n_backs]
    dy_ref, do_ref, pack_ref, gg_ref, gw_ref = rest[n_backs:]
    i = pl.program_id(0)

    @pl.when(i == 0)
    def _():
        gw_ref[...] = jnp.zeros_like(gw_ref)
        gg_ref[...] = jnp.zeros_like(gg_ref)

    dh = collect_all(code_ref[...], room, backs)
    y = y_ref[...]
    rms = lax.rsqrt(jnp.mean(y * y, axis=-1, keepdims=True) + EPSILON)
    gg_ref[...] += jnp.sum(dh * y * rms, axis=0, keepdims=True)
    u = dh * gain_ref[...]
    dy = (
        g_ref[...].astype(jnp.float32)
        + rms * u
        - y * (rms * rms * rms) * jnp.mean(u * y, axis=-1, keepdims=True)
    )
    dy_ref[...] = dy
    low = dy.astype(LOW)
    do_ref[...] = dot_t(low, w_ref[...]).astype(LOW)
    gw_ref[...] += dot(o_ref[...].T, low)

    @pl.when(i == pl.num_programs(0) - 1)
    def _():
        pack(gw_ref, 0, gw_ref.shape[0], pack_ref, 0)


def before_attention(backs, code, y, g, gain, w_output, joined, room):
    tokens, width = y.shape
    step = 256
    rows = lambda w: pl.BlockSpec((step, w), lambda i: (i, 0))
    return pl.pallas_call(
        functools.partial(before_attention_kernel, room, len(backs)),
        grid=(tokens // step,),
        in_specs=[
            rows(1), rows(width), rows(width), whole((1, width)),
            whole((width, width)), rows(width), *[whole(b.shape) for b in backs],
        ],
        out_specs=[
            rows(width), rows(width),
            pl.BlockSpec((width * width // TILE, TILE), lambda i: (0, 0)),
            pl.BlockSpec((1, width), lambda i: (0, 0)),
        ],
        out_shape=[
            jax.ShapeDtypeStruct((tokens, width), jnp.float32),
            jax.ShapeDtypeStruct((tokens, width), LOW),
            jax.ShapeDtypeStruct((width * width // TILE, TILE), LOW),
            jax.ShapeDtypeStruct((1, width), jnp.float32),
        ],
        scratch_shapes=[pltpu.VMEM((width, width), jnp.float32)],
        compiler_params=params(60),
        cost_estimate=cost(6 * tokens * width * width, 16 << 20),
        name="before_attention",
    )(code, y, g, gain, w_output, joined, *backs)


def unpack_kernel(
    experts, heads, buckets, q_ref, k_ref, v_ref, o_ref, small_ref, part_ref, gate_ref, rank_ref, *refs
):
    more, (gq, gk, gv, go, router, gains, table, mixed) = refs[:-8], refs[-8:]
    for packed_ref, out_ref in ((q_ref, gq), (k_ref, gk), (v_ref, gv), (o_ref, go)):
        out_ref[...] = packed_ref[...].astype(jnp.float32)
    part = part_ref[...]
    if more:
        extra_ref, late_ref = more
        ff = collect(rank_ref[...], extra_ref[...]) + late_ref[...].astype(jnp.float32)
        part = part + gate_ref[...] * ff
    mixed[...] = part.astype(LOW)

    @pl.when(pl.program_id(0) == 0)
    def _():
        lines = router.shape[1] // TILE
        small = small_ref[...].astype(jnp.float32)
        for c in range(lines):
            lanes = slice(c * TILE, (c + 1) * TILE)
            router[:, lanes] = small[c * experts : (c + 1) * experts]
            for n in range(2):
                at = lines * experts + n * lines + c
                gains[n : n + 1, lanes] = small[at : at + 1]
        at = lines * experts + -(-2 * lines // 16) * 16
        table[...] = small[at : at + heads, :buckets]


def unpack(packed, part, gate, rank, more, width, experts, heads, buckets, small_rows):
    blocks = width // TILE
    tokens = part.shape[0]
    source = lambda m: pl.BlockSpec((width, TILE), lambda i: (m * blocks + i, 0))
    column = lambda rows: pl.BlockSpec((rows, TILE), lambda i: (0, i))
    kept = lambda shape: pl.BlockSpec(shape, lambda i: (0, 0))
    return pl.pallas_call(
        functools.partial(unpack_kernel, experts, heads, buckets),
        grid=(blocks,),
        in_specs=[source(m) for m in range(4)]
        + [pl.BlockSpec((small_rows, TILE), lambda i: (4 * blocks * width // small_rows, 0))]
        + [column(tokens), whole((tokens, 1)), whole((tokens, 1))]
        + [column(m.shape[0]) for m in more],
        out_specs=[column(width)] * 4
        + [kept((experts, width)), kept((2, width)), kept((heads, buckets)), column(tokens)],
        out_shape=[jax.ShapeDtypeStruct((width, width), jnp.float32)] * 4
        + [
            jax.ShapeDtypeStruct((experts, width), jnp.float32),
            jax.ShapeDtypeStruct((2, width), jnp.float32),
            jax.ShapeDtypeStruct((heads, buckets), jnp.float32),
            jax.ShapeDtypeStruct((tokens, width), LOW),
        ],
        compiler_params=params(60),
        name="unpack",
    )(*[packed] * 5, part, gate, rank, *more)


def attention_forward_kernel(len_ref, q_ref, k_ref, v_ref, near_ref, far_ref, o_ref, p_ref, s_ref):
    seq = q_ref.shape[0]
    tiles = seq // TILE
    half = q_ref.shape[1] // 2
    row = pl.program_id(0)
    pair = pl.program_id(1)
    live = len_ref[row]
    lane = lax.broadcasted_iota(jnp.int32, (seq, 2 * half), 1)
    dead = lax.broadcasted_iota(jnp.int32, (seq, 2 * half), 0) >= live
    q = q_ref[...]
    k = k_ref[...]
    v_t = v_ref[...].T
    outs = []
    for h in range(2):
        mine = (lane >= h * half) & (lane < (h + 1) * half)
        flag = lane == (1 - h) * half
        k_h = jnp.where(mine, k, jnp.where(flag & dead, -1e30, 0.0).astype(k.dtype))
        q_h = jnp.where(flag, jnp.ones_like(q), q)
        after = far_ref[2 * pair + h, 0]
        before = far_ref[2 * pair + h, 1]
        tops = []
        for i in range(tiles):
            q_i = q_h[i * TILE:(i + 1) * TILE]
            raw = lax.dot_general(k_h, q_i, (((1,), (1,)), ((), ())), preferred_element_type=jnp.float32)
            top = None
            for j in range(tiles):
                x = raw[j * TILE:(j + 1) * TILE] * (0.125 * LOG2E)
                d = j - i
                if -1 <= d <= 1:
                    x = x + near_ref[h, d + 1]
                else:
                    x = x + (after if d > 0 else before)
                s_ref[j * TILE:(j + 1) * TILE, i * TILE:(i + 1) * TILE] = x
                m = jnp.max(x, axis=0, keepdims=True)
                top = m if top is None else jnp.maximum(top, m)
            tops.append(top)
        for i in range(tiles):
            e = jnp.exp2(s_ref[:, i * TILE:(i + 1) * TILE] - tops[i])
            total = jnp.sum(e, axis=0, keepdims=True)
            p_ref[0, h, :, i * TILE:(i + 1) * TILE] = (e * (1.0 / total)).astype(LOW)
        outs.append(lax.dot_general(v_t[h * half:(h + 1) * half], p_ref[0, h], (((1,), (0,)), ((), ())), preferred_element_type=jnp.float32))
    o_ref[...] = jnp.concatenate(outs, axis=0).T.astype(o_ref.dtype)

def attention_forward(lengths, projected, near, far, rows, seq, heads, head):
    width = heads * head
    pairs = heads // 2
    spec = lambda off: pl.BlockSpec((seq, 2 * head), lambda b, p: (b, off + p))
    return pl.pallas_call(
        attention_forward_kernel,
        grid=(rows, pairs),
        in_specs=[
            pl.BlockSpec(memory_space=pltpu.SMEM),
            spec(0), spec(pairs), spec(2 * pairs),
            pl.BlockSpec((2, 3, TILE, TILE), lambda b, p: (p, 0, 0, 0)),
            pl.BlockSpec(memory_space=pltpu.SMEM),
        ],
        out_specs=[
            pl.BlockSpec((seq, 2 * head), lambda b, p: (b, p)),
            pl.BlockSpec((1, 2, seq, seq), lambda b, p: (b, p, 0, 0)),
        ],
        out_shape=[
            jax.ShapeDtypeStruct((rows * seq, width), LOW),
            jax.ShapeDtypeStruct((rows, heads, seq, seq), LOW),
        ],
        scratch_shapes=[pltpu.VMEM((seq, seq), jnp.float32)],
        compiler_params=params(40),
        cost_estimate=cost(flops=4 * rows * heads * seq * seq * head * 4, bytes_accessed=rows * heads * seq * seq * 2, transcendentals=rows * heads * seq * seq),
        name="attention_forward",
    )(lengths, projected, projected, projected, near, far)

def attention_backward_kernel(
    q_ref, k_ref, v_ref, do_ref, o_ref, p_ref, nt_ref, wq_ref, wk_ref, wv_ref, x_ref, dy_ref, gain_ref,
    gr_ref, gg2_ref, out_ref, pack_ref, small_ref,
    near_ref, far_ref, d_ref, lines_ref, acc_ref, dh_ref, gg_ref,
):
    seq = q_ref.shape[0]
    tiles = seq // TILE
    half = q_ref.shape[1] // 2
    width = x_ref.shape[1]
    pair = pl.program_id(0)
    row = pl.program_id(1)
    last_pair = pair == pl.num_programs(0) - 1
    last_row = row == pl.num_programs(1) - 1
    lane = lax.broadcasted_iota(jnp.int32, (seq, 2 * half), 1)
    q = q_ref[...]
    k = k_ref[...]
    k_t = k.T
    v = v_ref[...]
    do = do_ref[...]
    weighed = (do.astype(jnp.float32) * o_ref[...].astype(jnp.float32)).T
    dq_parts = []
    dk_all = None
    dv_all = None

    @pl.when(row == 0)
    def _():
        near_ref[...] = jnp.zeros_like(near_ref)
        far_ref[...] = jnp.zeros_like(far_ref)
        acc_ref[...] = jnp.zeros_like(acc_ref)

    for h in range(2):
        mine = (lane >= h * half) & (lane < (h + 1) * half)
        v_h = jnp.where(mine, v, jnp.zeros_like(v))
        delta = jnp.sum(weighed[h * half : (h + 1) * half], axis=0, keepdims=True)
        far_sum = [jnp.zeros((8, TILE), jnp.float32), jnp.zeros((8, TILE), jnp.float32)]
        for i in range(tiles):
            cols = slice(i * TILE, (i + 1) * TILE)
            dp = dot_t(v_h, do[cols])
            for j in range(tiles):
                rws = slice(j * TILE, (j + 1) * TILE)
                ds = p_ref[0, h, rws, cols].astype(jnp.float32) * (dp[rws] - delta[:, cols])
                d = j - i
                if -1 <= d <= 1:
                    near_ref[h, d + 1] += ds
                else:
                    which = 0 if d > 0 else 1
                    far_sum[which] = far_sum[which] + jnp.sum(ds.reshape(TILE // 8, 8, TILE), axis=0)
                d_ref[rws, cols] = ds.astype(LOW)
        far_ref[h, 0] += far_sum[0]
        far_ref[h, 1] += far_sum[1]
        ds_all = d_ref[...]
        dq_parts.append(dot(k_t[h * half : (h + 1) * half], ds_all))
        dk_h = dot(ds_all, q)
        dv_h = dot(p_ref[0, h], do)
        dk_all = dk_h if h == 0 else jnp.where(mine, dk_h, dk_all)
        dv_all = dv_h if h == 0 else jnp.where(mine, dv_h, dv_all)

    dq = (jnp.concatenate(dq_parts, axis=0).T * 0.125).astype(LOW)
    grads = jnp.concatenate([dq, (dk_all * 0.125).astype(LOW), dv_all.astype(LOW)], axis=1)
    acc_ref[...] += dot(nt_ref[...], grads)
    weights = jnp.concatenate([wq_ref[...], wk_ref[...], wv_ref[...]], axis=1)
    dh = dot_t(grads, weights)
    here = pl.ds(pl.multiple_of(row * seq, seq), seq)

    @pl.when(pair == 0)
    def _():
        dh_ref[here, :] = dh

    @pl.when(pair > 0)
    def _():
        dh_ref[here, :] += dh

    @pl.when(last_row)
    def _():
        bucket_sums(near_ref, far_ref, lines_ref, 2 * pair)
        for n in range(3):
            pack_ref[n, 0] = acc_ref[:, n * TILE : (n + 1) * TILE].astype(LOW)

    @pl.when(last_pair & (row == 0))
    def _():
        gg_ref[...] = jnp.zeros_like(gg_ref)

    @pl.when(last_pair)
    def _():
        total = dh_ref[here, :]
        x = x_ref[...].astype(jnp.float32)
        rms = lax.rsqrt(jnp.mean(x * x, axis=-1, keepdims=True) + EPSILON)
        gg_ref[...] += jnp.sum(total * x * rms, axis=0, keepdims=True)
        u = total * gain_ref[...]
        out_ref[...] = (
            dy_ref[...]
            + rms * u
            - x * (rms * rms * rms) * jnp.mean(u * x, axis=-1, keepdims=True)
        )

    @pl.when(last_pair & last_row)
    def _():
        at = gr_ref.shape[0]
        small_ref[:at] = gr_ref[...].astype(LOW)
        lines = width // TILE
        gains = [gg_ref[:, c * TILE : (c + 1) * TILE] for c in range(lines)]
        gains += [gg2_ref[:, c * TILE : (c + 1) * TILE] for c in range(lines)]
        if 2 * lines % 16:
            gains += [jnp.zeros((16 - 2 * lines % 16, TILE), jnp.float32)]
        gains = jnp.concatenate(gains, axis=0)
        small_ref[at : at + gains.shape[0]] = gains.astype(LOW)
        at = at + gains.shape[0]
        table = bucket_table(lines_ref)
        if table.shape[0] % 16:
            table = jnp.concatenate([table, jnp.zeros((16 - table.shape[0] % 16, TILE), jnp.float32)], axis=0)
        small_ref[at : at + table.shape[0]] = table.astype(LOW)
        at = at + table.shape[0]
        small_ref[at:] = jnp.zeros((small_ref.shape[0] - at, TILE), LOW)


def bucket_sums(near_ref, far_ref, lines_ref, first):
    empty = jnp.zeros((8, TILE), jnp.float32)
    sub = lax.broadcasted_iota(jnp.int32, (8, 2 * TILE), 0)
    for h in range(2):
        lines = []
        for d in range(3):
            turned = None
            for a in range(0, TILE, 8):
                part = jnp.concatenate([near_ref[h, d, a : a + 8], empty], axis=1)
                part = pltpu.roll(part, (2 * TILE - a) % (2 * TILE), 1) if a else part
                turned = part if turned is None else turned + part
            for b in (1, 2, 4):
                turned = jnp.where((sub & b) > 0, pltpu.roll(turned, 2 * TILE - b, 1), turned)
            lines.append(jnp.sum(turned, axis=0, keepdims=True))
        for side in range(2):
            total = jnp.sum(far_ref[h, side], axis=0, keepdims=True)
            lines.append(jnp.concatenate([total, jnp.zeros((1, TILE), jnp.float32)], axis=1))
        lines.append(jnp.zeros((3, 2 * TILE), jnp.float32))
        lines_ref[first + h] = jnp.concatenate(lines, axis=0)


def bucket_table(lines_ref):
    heads = lines_ref.shape[0]
    buckets = 4 * 8
    lane = lax.broadcasted_iota(jnp.int32, (2 * TILE, TILE), 0)
    bucket = lax.broadcasted_iota(jnp.int32, (2 * TILE, TILE), 1)
    turn = jnp.where(lane >= TILE, lane - 2 * TILE, lane)
    total = None
    for r in range(5):
        if r < 3:
            hit = bucket_of((r - 1) * TILE - turn) == bucket
        else:
            hit = bucket == (buckets - 1 if r == 3 else buckets // 2 - 1)
        hit = hit.astype(LOW)
        line = jnp.concatenate([lines_ref[h, r : r + 1, :] for h in range(heads)], axis=0)
        high = line.astype(LOW)
        part = dot(high, hit) + dot((line - high.astype(jnp.float32)).astype(LOW), hit)
        total = part if total is None else total + part
    return total


def attention_backward(
    projected, do, joined, weights, normed_t, w_query, w_key, w_value, x, dy, gain, gr, gg2,
    rows, seq, heads, head, small_rows,
):
    width = heads * head
    pairs = heads // 2
    spec = lambda off: pl.BlockSpec((seq, 2 * head), lambda p, b: (b, off + p))
    column = pl.BlockSpec((width, 2 * head), lambda p, b: (0, p))
    at_end = pl.BlockSpec((seq, width), lambda p, b: (b * (p // (pairs - 1)), 0))
    return pl.pallas_call(
        attention_backward_kernel,
        grid=(pairs, rows),
        in_specs=[
            spec(0), spec(pairs), spec(2 * pairs), spec(0), spec(0),
            pl.BlockSpec((1, 2, seq, seq), lambda p, b: (b, p, 0, 0)),
            pl.BlockSpec((width, seq), lambda p, b: (0, b)),
            column, column, column, at_end, at_end,
            whole((1, width)), whole(gr.shape), whole(gg2.shape),
        ],
        out_specs=[
            at_end,
            pl.BlockSpec((3, 1, width, TILE), lambda p, b: (0, p, 0, 0)),
            pl.BlockSpec((small_rows, TILE), lambda p, b: (0, 0)),
        ],
        out_shape=[
            jax.ShapeDtypeStruct((rows * seq, width), jnp.float32),
            jax.ShapeDtypeStruct((3, pairs, width, TILE), LOW),
            jax.ShapeDtypeStruct((small_rows, TILE), LOW),
        ],
        scratch_shapes=[
            pltpu.VMEM((2, 3, TILE, TILE), jnp.float32),
            pltpu.VMEM((2, 2, 8, TILE), jnp.float32),
            pltpu.VMEM((seq, seq), LOW),
            pltpu.VMEM((heads, 8, 2 * TILE), jnp.float32),
            pltpu.VMEM((width, 3 * TILE), jnp.float32),
            pltpu.VMEM((rows * seq, width), jnp.float32),
            pltpu.VMEM((1, width), jnp.float32),
        ],
        compiler_params=params(60),
        cost_estimate=cost(8 * rows * heads * seq * seq * head * 4, rows * heads * seq * seq * 2),
        name="attention_backward",
    )(
        projected, projected, projected, do, joined, weights, normed_t, w_query, w_key, w_value,
        x, dy, gain, gr, gg2,
    )


def bias_tiles(table):
    j = lax.broadcasted_iota(jnp.int32, (3, TILE, TILE), 1)
    i = lax.broadcasted_iota(jnp.int32, (3, TILE, TILE), 2)
    d = lax.broadcasted_iota(jnp.int32, (3, TILE, TILE), 0) - 1
    b = bucket_of(d * TILE + j - i)
    scaled = table.T * LOG2E
    hot = (b.reshape(1, -1) == jnp.arange(table.shape[0], dtype=jnp.int32)[:, None]).astype(jnp.float32)
    near = jnp.dot(scaled, hot, precision=lax.Precision.HIGHEST).reshape(-1, 3, TILE, TILE)
    far = jnp.stack([scaled[:, -1], scaled[:, table.shape[0] // 2 - 1]], axis=1)
    return near, far


def expert_kernel(experts, chunk, x_ref, g_ref, mine_ref, wr_ref, wi_any, wo_any,
                  ff_ref, dx_ref, hid_ref, da_ref, xt_ref, dfft_ref, gr_ref, wi_ref, wo_ref, sem):
    inner = wi_ref.shape[1]
    first_step = pl.program_id(0) == 0

    def loads(f):
        cols = pl.ds(f, chunk)
        return (pltpu.make_async_copy(wi_any.at[:, cols], wi_ref.at[:, cols], sem.at[0, f // chunk]),
                pltpu.make_async_copy(wo_any.at[cols, :], wo_ref.at[cols, :], sem.at[1, f // chunk]))

    @pl.when(first_step)
    def _():
        for f in range(0, inner, chunk):
            for c in loads(f):
                c.start()
        gr_ref[...] = jnp.zeros_like(gr_ref)

    x = x_ref[...]
    g = g_ref[...].reshape(x.shape).astype(jnp.float32)
    mine = mine_ref[...]
    lane = lax.broadcasted_iota(jnp.int32, (1, wr_ref.shape[1]), 1)
    logits = jnp.dot(x, wr_ref[...], preferred_element_type=jnp.float32)
    logits = jnp.where(lane < experts, logits, -1e30)
    e = jnp.exp(logits - jnp.max(logits, axis=-1, keepdims=True))
    router = e / jnp.sum(e, axis=-1, keepdims=True)
    gate = jnp.sum(router * mine, axis=-1, keepdims=True)
    dff = (g * gate).astype(LOW)
    ff = None
    dx = None
    def first(f):
        @pl.when(first_step)
        def _():
            for c in loads(f):
                c.wait()
        cols = slice(f, f + chunk)
        return (jnp.dot(x, wi_ref[:, cols], preferred_element_type=jnp.float32),
                lax.dot_general(dff, wo_ref[cols, :], (((1,), (1,)), ((), ())), preferred_element_type=jnp.float32))
    for f in range(0, inner, chunk):
        cols = slice(f, f + chunk)
        a, dhid = first(f)
        u = a * a
        t = jnp.tanh(a * (GELU_A + GELU_B * u))
        h = 0.5 + 0.5 * t
        hid = a * h
        slope = h + hid * ((1.0 - t) * (GELU_A + (3.0 * GELU_B) * u))
        da = (dhid * slope).astype(LOW)
        hid = hid.astype(LOW)
        hid_ref[:, cols] = hid
        da_ref[:, cols] = da
        ff_part = jnp.dot(hid, wo_ref[cols, :], preferred_element_type=jnp.float32)
        dx_part = lax.dot_general(da, wi_ref[:, cols], (((1,), (1,)), ((), ())), preferred_element_type=jnp.float32)
        ff = ff_part if ff is None else ff + ff_part
        dx = dx_part if dx is None else dx + dx_part
    ff = ff.astype(LOW)
    ff_ref[...] = ff
    dgate = jnp.sum(g * ff.astype(jnp.float32), axis=-1, keepdims=True)
    dlogits = ((gate * dgate) * (mine - router)).astype(LOW)
    dx = dx + lax.dot_general(dlogits, wr_ref[...], (((1,), (1,)), ((), ())), preferred_element_type=jnp.float32)
    dx_ref[...] = dx.astype(LOW)
    x_t = x.T
    xt_ref[...] = x_t
    dfft_ref[...] = dff.T
    gr_ref[...] += dot(dlogits.T, x)

def expert_rows(x, g, mine, wr, wi, wo, experts, low, high, tile=256, chunk=768):
    n, width = x.shape
    inner = wi.shape[1]
    sources, room = g.shape[0], high - low
    group = max(1, min(sources, tile // room))
    while sources % group or (group * room) % TILE:
        group += 1
    tile = group * room
    gspec = pl.BlockSpec((group, room, width), lambda i: (i, low // room, 0))
    once = lambda s: pl.BlockSpec(s, lambda i: (0,) * len(s), pipeline_mode=pl.Buffered(1))
    rowspec = lambda w: pl.BlockSpec((tile, w), lambda i: (i, 0))
    anywhere = pl.BlockSpec(memory_space=pl.ANY)
    return pl.pallas_call(
        functools.partial(expert_kernel, experts, chunk),
        grid=(n // tile,),
        in_specs=[rowspec(width), gspec, once(mine.shape), once(wr.shape), anywhere, anywhere],
        out_specs=[rowspec(width), rowspec(width), rowspec(inner), rowspec(inner),
                   pl.BlockSpec((width, tile), lambda i: (0, i)), pl.BlockSpec((width, tile), lambda i: (0, i)),
                   pl.BlockSpec((wr.shape[1], width), lambda i: (0, 0))],
        out_shape=[jax.ShapeDtypeStruct((n, width), LOW)] * 2 + [jax.ShapeDtypeStruct((n, inner), LOW)] * 2
            + [jax.ShapeDtypeStruct((width, n), LOW)] * 2 + [jax.ShapeDtypeStruct((wr.shape[1], width), jnp.float32)],
        scratch_shapes=[pltpu.VMEM(wi.shape, LOW), pltpu.VMEM(wo.shape, LOW), pltpu.SemaphoreType.DMA((2, inner // chunk))],
        compiler_params=params(60),
        cost_estimate=cost(flops=8 * n * width * inner, bytes_accessed=4 * n * inner + 8 * width * inner, transcendentals=n * inner),
        name="expert_rows",
    )(x, g, mine, wr, wi, wo)

def expert_weights_kernel(parts, *refs):
    ins, (gi_ref, go_ref) = refs[: 4 * parts], refs[4 * parts :]
    gi = None
    go = None
    for c in range(parts):
        xt, dfft, hid, da = ins[4 * c : 4 * c + 4]
        gi_c = dot(xt[...], da[...])
        go_c = dot(dfft[...], hid[...])
        gi = gi_c if gi is None else gi + gi_c
        go = go_c if go is None else go + go_c
    gi_ref[0] = gi
    go_ref[0] = go.T


def expert_weights(parts, tile=512):
    inner = parts[0][2].shape[1]
    width = parts[0][0].shape[0]
    specs, args, rows = [], [], 0
    for xt, dfft, hid, da in parts:
        n = hid.shape[0]
        rows += n
        specs += [pl.BlockSpec((width, n), lambda f: (0, 0), pipeline_mode=pl.Buffered(1))] * 2
        specs += [pl.BlockSpec((n, tile), lambda f: (0, f))] * 2
        args += [xt, dfft, hid, da]
    return pl.pallas_call(
        functools.partial(expert_weights_kernel, len(parts)),
        grid=(inner // tile,),
        in_specs=specs,
        out_specs=[
            pl.BlockSpec((1, width, tile), lambda f: (0, 0, f)),
            pl.BlockSpec((1, tile, width), lambda f: (0, f, 0)),
        ],
        out_shape=[
            jax.ShapeDtypeStruct((1, width, inner), jnp.float32),
            jax.ShapeDtypeStruct((1, inner, width), jnp.float32),
        ],
        compiler_params=params(60),
        cost_estimate=cost(4 * rows * width * inner, 4 * rows * inner + 8 * width * inner),
        name="expert_weights",
    )(*args)


def device_place(cores, d):
    return dict(device_id=(lax.div(d, cores), lax.rem(d, cores)), device_id_type=pl.DeviceIdType.MESH)


def partner_of(me, b):
    bit = lax.rem(lax.div(me, 1 << b), 2)
    return bit, me + (1 - 2 * bit) * (1 << b)


def greet(cores, bits, me):
    barrier = pltpu.get_barrier_semaphore()
    for b in range(bits):
        pl.semaphore_signal(barrier, inc=1, **device_place(cores, partner_of(me, b)[1]))
    pl.semaphore_wait(barrier, bits)


def rows_at(start, length):
    return pl.ds(pl.multiple_of(start, 16), length)


def sum_parts(n, heights):
    bits = n.bit_length() - 1
    upper = list(range(1, bits))
    parts, first = [], 0
    for ref, rows in enumerate(heights):
        units = rows // (16 * n)
        pieces = max(1, min(units, round(6 * rows / sum(heights))))
        at = 0
        for c in range(pieces):
            size = (units + c) // pieces
            t = len(parts) % 3
            parts.append((ref, at * 16 * n, first, size * 16, [0] + upper[t:] + upper[:t]))
            at += size
            first += size * 16 * n
    return bits, parts


def sum_kernel(
    cores, n, room, heights, code_ref, gate_ref, ff_any, y_any, *refs
):
    xs = refs[: len(heights)]
    mixed_ref, out_ref, *rest = refs[len(heights) :]
    work_ref, got_ref, ff_ref, y_ref, send, recv, local = rest
    bits, parts = sum_parts(n, heights)
    me = lax.axis_index("grp") * cores + lax.axis_index("exp")
    loads = [
        pltpu.make_async_copy(ff_any, ff_ref, local.at[0]),
        pltpu.make_async_copy(y_any, y_ref, local.at[1]),
    ]
    for copy in loads:
        copy.start()
    greet(cores, bits, me)
    base = [first for _, _, first, _, _ in parts]
    got_at = list(base)

    def halving(p, s):
        ref, at, first, step, order = parts[p]
        length = step * (n >> (s + 1))
        bit, partner = partner_of(me, order[s])
        start = base[p] + (1 - bit) * length
        source = xs[ref].at[rows_at(start - first + at, length)] if s == 0 else work_ref.at[rows_at(start, length)]
        return pltpu.make_async_remote_copy(
            src_ref=source, dst_ref=got_ref.at[rows_at(got_at[p], length)],
            send_sem=send.at[p, s], recv_sem=recv.at[p, s], **device_place(cores, partner),
        )

    def doubling(p, s):
        _, _, _, step, order = parts[p]
        here = rows_at(base[p], step * (n >> (s + 1)))
        return pltpu.make_async_remote_copy(
            src_ref=out_ref.at[here], dst_ref=out_ref.at[here],
            send_sem=send.at[p, bits + s], recv_sem=recv.at[p, bits + s],
            **device_place(cores, partner_of(me, order[s])[1]),
        )

    tokens = mixed_ref.shape[0]
    tile = tokens // 4

    def mix_tile(i):
        if i >= 4:
            return
        if i == 0:
            for copy in loads:
                copy.wait()
        here = slice(i * tile, (i + 1) * tile)
        ff = collect(segment(code_ref[here, :], room, 0, plan(room)[1]), ff_ref[...])
        mixed_ref[here, :] = y_ref[here, :] + gate_ref[here, :] * ff

    moving = [halving(p, 0) for p in range(len(parts))]
    for copy in moving:
        copy.start()
    sent = []
    for s in range(bits):
        mix_tile(s - 1 if s else 9)
        for p, (ref, at, first, step, order) in enumerate(parts):
            length = step * (n >> (s + 1))
            moving[p].wait_recv()
            sent.append(moving[p])
            base[p] = base[p] + partner_of(me, order[s])[0] * length
            source, shift = (xs[ref], at - first) if s == 0 else (work_ref, 0)
            target = work_ref if s + 1 < bits else out_ref

            def add(i, _, start=base[p], source=source, shift=shift, target=target, arrived=got_at[p], step=step):
                got = got_ref[rows_at(arrived + i * step, step), :].astype(jnp.float32)
                mine = source[rows_at(start + shift + i * step, step), :].astype(jnp.float32)
                target[rows_at(start + i * step, step), :] = (mine + got).astype(LOW)
                return 0

            lax.fori_loop(0, length // step, add, 0)
            got_at[p] += length
            if s + 1 < bits:
                moving[p] = halving(p, s + 1)
            else:
                moving[p] = doubling(p, s)
            moving[p].start()
    for copy in sent:
        copy.wait_send()
    sent = []
    for s in reversed(range(bits)):
        if s == bits - 1:
            for i in range(bits - 1, 4):
                mix_tile(i)
        for p, (ref, at, first, step, order) in enumerate(parts):
            length = step * (n >> (s + 1))
            moving[p].wait_recv()
            sent.append(moving[p])
            base[p] = base[p] - partner_of(me, order[s])[0] * length
            if s > 0:
                moving[p] = doubling(p, s - 1)
                moving[p].start()
    for copy in sent:
        copy.wait_send()


def all_sum(xs, code, gate, ff, y, room):
    cores = lax.axis_size("exp")
    n = lax.axis_size(AXES)
    heights = [a.shape[0] for a in xs]
    if any(h % (16 * n) for h in heights):
        xs = [jnp.concatenate(xs[:-1], axis=0), xs[-1]]
        heights = [a.shape[0] for a in xs]
    total = sum(heights)
    bits, parts = sum_parts(n, heights)
    tokens, width = y.shape
    buffer = pltpu.VMEM((total, TILE), LOW)
    vmem = pl.BlockSpec(memory_space=pltpu.VMEM)
    anywhere = pl.BlockSpec(memory_space=pl.ANY)
    return pl.pallas_call(
        functools.partial(sum_kernel, cores, n, room, heights),
        out_shape=[
            jax.ShapeDtypeStruct((tokens, width), jnp.float32),
            jax.ShapeDtypeStruct((total, TILE), LOW),
        ],
        in_specs=[vmem, vmem, anywhere, anywhere] + [vmem] * len(xs),
        out_specs=[vmem] * 2,
        scratch_shapes=[
            buffer, buffer, pltpu.VMEM(ff.shape, LOW), pltpu.VMEM(y.shape, jnp.float32),
            pltpu.SemaphoreType.DMA((len(parts), 2 * bits)),
            pltpu.SemaphoreType.DMA((len(parts), 2 * bits)),
            pltpu.SemaphoreType.DMA((2,)),
        ],
        compiler_params=params(60, collective_id=1, has_side_effects=True),
        name="all_sum",
    )(code, gate, ff, y, *xs)


def local(
    tokens, lengths, expert_ids, slots, w_query, w_key, w_value, w_output,
    gain_attn, gain_ffn, bias_table, w_router, w_in, w_out, cotangent,
):
    rows, seq, width = tokens.shape
    count = rows * seq
    buckets, heads = bias_table.shape
    head = width // heads
    experts = w_router.shape[1]
    devices = lax.axis_size(AXES)
    room = max(4, 2 * count // experts)
    me = lax.axis_index(AXES)
    x = tokens.reshape(count, width)
    g = cotangent.reshape(count, width)
    gain_one = gain_attn.reshape(1, width)
    gain_two = gain_ffn.reshape(1, width)
    wide = max(128, experts)
    mine = (jnp.arange(wide, dtype=jnp.int32) == me).astype(jnp.float32).reshape(1, wide)

    segments, cut, extra = plan(room)
    code_c, code_r, rank_c, g_out, g_more = route(expert_ids, slots, g, experts, room)
    if extra:
        g_more = lax.all_gather(g_more, AXES, axis=0, tiled=False)
    g_in = exchange(g_out, devices)
    code_r, x, w_query, w_key, w_value, w_output, bias_table, w_router = lax.optimization_barrier(
        (code_r, x, w_query, w_key, w_value, w_output, bias_table, w_router)
    )
    router_w = jnp.pad(w_router, ((0, 0), (0, wide - experts)))

    normed_t, projected = project(x, gain_one, w_query, w_key, w_value)
    near, far = bias_tiles(bias_table)
    joined, weights = attention_forward(lengths, projected, near, far, rows, seq, heads, head)
    y, gate, *h_out = after_attention(
        joined, x, w_output, gain_two, expert_ids.reshape(count, 1), router_w, code_r, experts, room
    )
    h_out, g_in = lax.optimization_barrier((h_out, g_in))
    g_in = g_in.reshape(devices, cut, width)
    h_in = [exchange(h_out[0], devices)]
    g_parts = [(g_in, low, high) for low, high in segments]
    late = None
    if extra:
        spare = room - cut
        h_in[0], g_more = lax.optimization_barrier((h_in[0], g_more))
        marks = g_more[:, extra, : extra + 1].astype(jnp.float32)
        late = jnp.any(marks[:, extra] > 0)
        mine_marks = marks[:, :extra] == (me + 1).astype(jnp.float32)
        order = jnp.cumsum(mine_marks.astype(jnp.int32), axis=1) - 1
        chosen = (
            mine_marks[:, None, :]
            & (order[:, None, :] == jnp.arange(spare, dtype=jnp.int32)[None, :, None])
        ).astype(LOW)
        flat_code, flat_rank = code_c.reshape(-1), rank_c.reshape(-1)
        flat_expert = flat_code // room
        rest = jnp.where(
            flat_rank >= extra,
            flat_expert * spare + flat_code - flat_expert * room - cut,
            experts * spare,
        )

        def send_rest(rest):
            empty = jnp.zeros((experts * spare, width), LOW)
            return exchange(empty.at[rest].set(g, mode="drop"), devices)

        g_rest = lax.cond(
            late, send_rest, lambda rest: jnp.zeros((experts * spare, width), LOW), rest
        )
        h_out[1], g_rest = lax.optimization_barrier((h_out[1], g_rest))
        g_spare = jnp.einsum(
            "sqr,srw->sqw", chosen, g_more[:, :extra], preferred_element_type=jnp.float32
        ).astype(LOW) + g_rest.reshape(devices, spare, width)
        low, high = segments[1]
        g_parts[1] = (jnp.concatenate([g_in[:, low:], g_spare], axis=1), 0, high - low)
    for h in h_out[1:]:
        h, h_in[-1] = lax.optimization_barrier((h, h_in[-1]))
        h_in.append(exchange(h, devices))
    dx_back, ffs, parts, grad_router = [], [], [], 0.0
    for n, (low, high) in enumerate(segments):
        ff, dx, hid, da, x_t, dff_t, routed = expert_rows(
            h_in[n], g_parts[n][0], mine, router_w, w_in[0], w_out[0], experts, *g_parts[n][1:]
        )
        if n + 1 < len(segments):
            dx, h_in[n + 1] = lax.optimization_barrier((dx, h_in[n + 1]))
        if n:
            dx, dx_back[-1] = lax.optimization_barrier((dx, dx_back[-1]))
        dx_back.append(exchange(dx, devices))
        ffs.append(ff.reshape(devices, high - low, width))
        parts.append((x_t, dff_t, hid, da))
        grad_router = grad_router + routed
    grad_in, grad_out = expert_weights(parts)
    ff = jnp.concatenate(ffs, axis=1) if len(ffs) > 1 else ffs[0]
    more = []
    if extra:
        ff_spare = ff[:, cut:]
        ff_more = jnp.einsum(
            "sqr,sqw->srw", chosen, ff_spare, preferred_element_type=jnp.float32
        ).astype(LOW)
        ff_more = lax.psum_scatter(
            ff_more.reshape(devices * extra, width), AXES, scatter_dimension=0, tiled=True
        )
        dx_back, ff_spare = lax.optimization_barrier((dx_back, ff_spare))

        def return_rest(spare_rows, rest):
            back = exchange(spare_rows.reshape(devices * spare, width), devices)
            return jnp.take(back, rest, axis=0, mode="fill", fill_value=0)

        ff_rest = lax.cond(
            late, return_rest, lambda *_: jnp.zeros((count, width), LOW), ff_spare, rest
        )
        dx_back, ff_rest = lax.optimization_barrier((dx_back, ff_rest))
        more = [ff_more, ff_rest]
    ff = ff[:, :cut].reshape(devices * cut, width)
    dx_back, grad_in, grad_out, ff = lax.optimization_barrier((dx_back, grad_in, grad_out, ff))
    ff_back = exchange(ff, devices)
    grad_router = grad_router[:experts].reshape(experts, width // TILE, TILE)
    grad_router = jnp.swapaxes(grad_router, 0, 1).reshape(-1, TILE)

    dy, do, grad_output, grad_gain_two = before_attention(
        dx_back, code_c, y, g, gain_two, w_output, joined, room
    )
    lines = width // TILE
    small_rows = grad_router.shape[0] + -(-2 * lines // 16) * 16 + -(-heads // 16) * 16
    small_rows = -(-small_rows // (16 * devices)) * 16 * devices
    grad_tokens, packed, small = attention_backward(
        projected, do, joined, weights, normed_t, w_query, w_key, w_value, x, dy, gain_one,
        grad_router, grad_gain_two, rows, seq, heads, head, small_rows,
    )
    mixed, summed = all_sum(
        [packed.reshape(-1, TILE), grad_output, small], code_c, gate, ff_back, y, room
    )
    *grads, router_t, gains, table, mixed = unpack(
        summed, mixed, gate, rank_c, more, width, experts, heads, buckets, small_rows
    )
    return (
        mixed.reshape(rows, seq, width),
        grad_tokens.reshape(rows, seq, width),
        *grads,
        gains[0], gains[1], table.T, router_t.T,
        grad_in,
        grad_out,
    )


def solution(mesh):
    split = P(AXES)
    in_specs = (split,) * 4 + (P(),) * 8 + (split,) * 3
    out_specs = (split,) * 2 + (P(),) * 8 + (split,) * 2
    return jax.shard_map(local, mesh=mesh, in_specs=in_specs, out_specs=out_specs, check_vma=False)
```

```python
import functools

import jax
import jax.numpy as jnp
from jax import lax
from jax.experimental import pallas as pl
from jax.experimental.pallas import tpu as pltpu
from jax.sharding import PartitionSpec as P

EPSILON = 1e-06
NEGATIVE = -1e30
THRESHOLDS = (12, 16, 23, 32, 46, 64, 91)
LOG2E = 1.4426950408889634
TILE = 128
GELU_A = 0.7978845608028654
GELU_B = GELU_A * 0.044715
AXES = ("grp", "exp")
LOW = jnp.bfloat16


def dot(a, b):
    return jnp.dot(a, b, preferred_element_type=jnp.float32)


def dot_t(a, b):
    return lax.dot_general(a, b, (((1,), (1,)), ((), ())), preferred_element_type=jnp.float32)


def params(mib, **more):
    return pltpu.CompilerParams(vmem_limit_bytes=mib << 20, **more)


def whole(shape):
    return pl.BlockSpec(shape, lambda *_: (0,) * len(shape), pipeline_mode=pl.Buffered(1))


def cost(flops, bytes_accessed, transcendentals=0):
    return pl.CostEstimate(
        flops=flops, bytes_accessed=bytes_accessed, transcendentals=transcendentals
    )


def bucket_of(offset):
    distance = jnp.abs(offset)
    far = jnp.full_like(distance, 8)
    for border in THRESHOLDS:
        far = far + (distance >= border).astype(jnp.int32)
    return jnp.where(distance < 8, distance, far) + jnp.where(offset > 0, 16, 0).astype(jnp.int32)


def device_place(cores, d):
    return dict(device_id=(lax.div(d, cores), lax.rem(d, cores)), device_id_type=pl.DeviceIdType.MESH)


def partner_of(me, b):
    bit = lax.rem(lax.div(me, 1 << b), 2)
    return bit, me + (1 - 2 * bit) * (1 << b)


def rows_at(start, length):
    return pl.ds(pl.multiple_of(start, 16), length)


def plan(room):
    if room % 64:
        return ((0, room),), room, 0
    return ((0, room // 2), (room // 2, room)), 3 * room // 4, room // 4


def segment(code, room, low, high):
    expert = lax.div(code, room)
    place = code - expert * room
    inside = (code >= 0) & (place >= low) & (place < high)
    return jnp.where(inside, expert * (high - low) + place - low, -1)


def spread(dest, values, out):
    rows = out.shape[0]
    step = min(256, rows)
    for start in range(0, rows, step):
        here = lax.broadcasted_iota(jnp.int32, (step, dest.shape[1]), 0) + start
        out[start : start + step] = dot((dest == here).astype(LOW), values).astype(LOW)


def collect(dest, values):
    here = lax.broadcasted_iota(jnp.int32, (dest.shape[0], values.shape[0]), 1)
    return dot((dest == here).astype(LOW), values)


def spread_all(code, room, values, outs):
    for (low, high), out in zip(plan(room)[0], outs):
        spread(segment(code, room, low, high), values, out)


def collect_all(code, room, refs):
    total = None
    for (low, high), ref in zip(plan(room)[0], refs):
        part = collect(segment(code, room, low, high), ref[...])
        total = part if total is None else total + part
    return total


def buffers(experts, room, width):
    return [
        jax.ShapeDtypeStruct((experts * (high - low), width), LOW) for low, high in plan(room)[0]
    ]


def route_kernel(
    experts, room, eid_c, eid_r, slot_c, slot_r, g_ref, code_c, code_r, rank_c, flag, out
):
    tokens = g_ref.shape[0]
    wide = max(TILE, experts)
    _, cut, extra = plan(room)
    at = lax.broadcasted_iota(jnp.int32, (tokens, tokens), 0)
    to = lax.broadcasted_iota(jnp.int32, (tokens, tokens), 1)

    ids = eid_r[...]
    picked = ids == lax.broadcasted_iota(jnp.int32, (wide, tokens), 0)
    earlier = dot(picked.astype(LOW), (at < to).astype(LOW))
    place = jnp.sum(jnp.where(picked, earlier, 0.0), axis=0, keepdims=True).astype(jnp.int32)
    code = jnp.where(slot_r[...] >= 0, ids * room + place, -1)
    code_r[...] = code
    spread(code, g_ref[...], out)

    ids = eid_c[...]
    picked = ids == lax.broadcasted_iota(jnp.int32, (tokens, wide), 1)
    earlier = dot((to < at).astype(LOW), picked.astype(LOW))
    place = jnp.sum(jnp.where(picked, earlier, 0.0), axis=1, keepdims=True).astype(jnp.int32)
    kept = slot_c[...] >= 0
    code_c[...] = jnp.where(kept, ids * room + place, -1)
    over = kept & (place >= cut)
    rank_c[...] = jnp.where(over, place - cut, -1)
    named = jnp.max(jnp.where(picked & over, 1.0, 0.0), axis=0, keepdims=True)
    named = jnp.sum(named, axis=1, keepdims=True)
    flag[...] = jnp.broadcast_to(jnp.where(named > 1.0, 1.0, 0.0), flag.shape)


def route(expert_ids, slots, upstream, experts, room):
    tokens, width = upstream.shape
    column = jax.ShapeDtypeStruct((tokens, 1), jnp.int32)
    line = jax.ShapeDtypeStruct((1, tokens), jnp.int32)
    return pl.pallas_call(
        functools.partial(route_kernel, experts, room),
        out_shape=[
            column, line, column, jax.ShapeDtypeStruct((16, TILE), jnp.float32),
            jax.ShapeDtypeStruct((experts * room, width), LOW),
        ],
        compiler_params=params(48),
        cost_estimate=cost(2 * experts * room * tokens * width, 8 << 20),
        name="route",
    )(
        expert_ids.reshape(tokens, 1), expert_ids.reshape(1, tokens),
        slots.reshape(tokens, 1), slots.reshape(1, tokens), upstream,
    )


def exchange(buffer, devices):
    shaped = buffer.reshape(devices, buffer.shape[0] // devices, buffer.shape[1])
    moved = lax.all_to_all(shaped, AXES, split_axis=0, concat_axis=0, tiled=True)
    return moved.reshape(buffer.shape)


def project_kernel(x_ref, gain_ref, wq_ref, wk_ref, wv_ref, normed_ref, out_ref):
    x = x_ref[...].astype(jnp.float32)
    rms = lax.rsqrt(jnp.mean(x * x, axis=-1, keepdims=True) + EPSILON)
    normed = (x * rms * gain_ref[...]).astype(LOW)
    normed_ref[...] = normed.T
    width = x.shape[1]
    for n, w_ref in enumerate((wq_ref, wk_ref, wv_ref)):
        out_ref[:, n * width : (n + 1) * width] = dot(normed, w_ref[...]).astype(LOW)


def project(x, gain, w_query, w_key, w_value):
    tokens, width = x.shape
    out = 3 * width
    step = 256
    rows = lambda w: pl.BlockSpec((step, w), lambda i: (i, 0))
    return pl.pallas_call(
        project_kernel,
        grid=(tokens // step,),
        in_specs=[rows(width), whole((1, width)), *[whole((width, width))] * 3],
        out_specs=[pl.BlockSpec((width, step), lambda i: (0, i)), rows(out)],
        out_shape=[
            jax.ShapeDtypeStruct((width, tokens), LOW),
            jax.ShapeDtypeStruct((tokens, out), LOW),
        ],
        compiler_params=params(40),
        cost_estimate=cost(2 * tokens * width * out, 12 << 20),
        name="project",
    )(x, gain, w_query, w_key, w_value)


def after_attention_kernel(
    experts, room, o_ref, x_ref, w_ref, gain_ref, eid_ref, wr_ref, code_ref, y_ref, gate_ref, *rest
):
    outs, held = rest[:-1], rest[-1]
    step = o_ref.shape[0]
    i = pl.program_id(0)
    y = x_ref[...].astype(jnp.float32) + dot(o_ref[...], w_ref[...])
    y_ref[...] = y
    rms = lax.rsqrt(jnp.mean(y * y, axis=-1, keepdims=True) + EPSILON)
    normed = (y * rms * gain_ref[...]).astype(LOW)
    held[pl.ds(pl.multiple_of(i * step, step), step), :] = normed
    router = route_softmax(dot(normed, wr_ref[...]), experts)
    lane = lax.broadcasted_iota(jnp.int32, router.shape, 1)
    gate_ref[...] = jnp.sum(jnp.where(lane == eid_ref[...], router, 0.0), axis=-1, keepdims=True)

    @pl.when(i == pl.num_programs(0) - 1)
    def _():
        spread_all(code_ref[...], room, held[...], outs)


def after_attention(joined, x, w_output, gain, expert_ids, w_router, code, experts, room):
    tokens, width = x.shape
    step = 256
    rows = pl.BlockSpec((step, width), lambda i: (i, 0))
    single = pl.BlockSpec((step, 1), lambda i: (i, 0))
    outs = buffers(experts, room, width)
    return pl.pallas_call(
        functools.partial(after_attention_kernel, experts, room),
        grid=(tokens // step,),
        in_specs=[
            rows, rows, whole((width, width)), whole((1, width)), single, whole(w_router.shape),
            whole((1, tokens)),
        ],
        out_specs=[rows, single] + [pl.BlockSpec(o.shape, lambda i: (0, 0)) for o in outs],
        out_shape=[
            jax.ShapeDtypeStruct((tokens, width), jnp.float32),
            jax.ShapeDtypeStruct((tokens, 1), jnp.float32),
        ]
        + outs,
        scratch_shapes=[pltpu.VMEM((tokens, width), LOW)],
        compiler_params=params(60),
        cost_estimate=cost(2 * tokens * width * (width + experts * room), 12 << 20),
        name="after_attention",
    )(joined, x, w_output, gain, expert_ids, w_router, code)


def route_softmax(logits, experts):
    lane = lax.broadcasted_iota(jnp.int32, logits.shape, 1)
    logits = jnp.where(lane < experts, logits, NEGATIVE)
    e = jnp.exp(logits - jnp.max(logits, axis=-1, keepdims=True))
    return e / jnp.sum(e, axis=-1, keepdims=True)


def pack(values, first, height, out, at):
    for c in range(values.shape[1] // TILE):
        out[at + c * height : at + (c + 1) * height] = values[
            first : first + height, c * TILE : (c + 1) * TILE
        ].astype(LOW)


def before_attention_kernel(
    room, n_backs, code_ref, y_ref, g_ref, gain_ref, w_ref, o_ref, *rest
):
    backs = rest[:n_backs]
    dy_ref, do_ref, pack_ref, gg_ref, gw_ref = rest[n_backs:]
    i = pl.program_id(0)

    @pl.when(i == 0)
    def _():
        gw_ref[...] = jnp.zeros_like(gw_ref)
        gg_ref[...] = jnp.zeros_like(gg_ref)

    dh = collect_all(code_ref[...], room, backs)
    y = y_ref[...]
    rms = lax.rsqrt(jnp.mean(y * y, axis=-1, keepdims=True) + EPSILON)
    gg_ref[...] += jnp.sum(dh * y * rms, axis=0, keepdims=True)
    u = dh * gain_ref[...]
    dy = (
        g_ref[...].astype(jnp.float32)
        + rms * u
        - y * (rms * rms * rms) * jnp.mean(u * y, axis=-1, keepdims=True)
    )
    dy_ref[...] = dy
    low = dy.astype(LOW)
    do_ref[...] = dot_t(low, w_ref[...]).astype(LOW)
    gw_ref[...] += dot(o_ref[...].T, low)

    @pl.when(i == pl.num_programs(0) - 1)
    def _():
        pack(gw_ref, 0, gw_ref.shape[0], pack_ref, 0)


def before_attention(backs, code, y, g, gain, w_output, joined, room):
    tokens, width = y.shape
    step = 256
    rows = lambda w: pl.BlockSpec((step, w), lambda i: (i, 0))
    return pl.pallas_call(
        functools.partial(before_attention_kernel, room, len(backs)),
        grid=(tokens // step,),
        in_specs=[
            rows(1), rows(width), rows(width), whole((1, width)),
            whole((width, width)), rows(width), *[whole(b.shape) for b in backs],
        ],
        out_specs=[
            rows(width), rows(width),
            pl.BlockSpec((width * width // TILE, TILE), lambda i: (0, 0)),
            pl.BlockSpec((1, width), lambda i: (0, 0)),
        ],
        out_shape=[
            jax.ShapeDtypeStruct((tokens, width), jnp.float32),
            jax.ShapeDtypeStruct((tokens, width), LOW),
            jax.ShapeDtypeStruct((width * width // TILE, TILE), LOW),
            jax.ShapeDtypeStruct((1, width), jnp.float32),
        ],
        scratch_shapes=[pltpu.VMEM((width, width), jnp.float32)],
        compiler_params=params(60),
        cost_estimate=cost(6 * tokens * width * width, 16 << 20),
        name="before_attention",
    )(code, y, g, gain, w_output, joined, *backs)


def unpack_kernel(
    experts, heads, buckets, q_ref, k_ref, v_ref, o_ref, small_ref, gq, gk, gv, go, router, gains, table
):
    for packed_ref, out_ref in ((q_ref, gq), (k_ref, gk), (v_ref, gv), (o_ref, go)):
        out_ref[...] = packed_ref[...].astype(jnp.float32)

    @pl.when(pl.program_id(0) == 0)
    def _():
        lines = router.shape[1] // TILE
        small = small_ref[...].astype(jnp.float32)
        for c in range(lines):
            lanes = slice(c * TILE, (c + 1) * TILE)
            router[:, lanes] = small[c * experts : (c + 1) * experts]
            for n in range(2):
                at = lines * experts + 16 + n * lines + c
                gains[n : n + 1, lanes] = small[at : at + 1]
        at = lines * experts + 16 + -(-2 * lines // 16) * 16
        table[...] = small[at : at + heads, :buckets]


def unpack(packed, width, experts, heads, buckets, small_rows):
    blocks = width // TILE
    source = lambda m: pl.BlockSpec((width, TILE), lambda i: (m * blocks + i, 0))
    column = lambda rows: pl.BlockSpec((rows, TILE), lambda i: (0, i))
    kept = lambda shape: pl.BlockSpec(shape, lambda i: (0, 0))
    return pl.pallas_call(
        functools.partial(unpack_kernel, experts, heads, buckets),
        grid=(blocks,),
        in_specs=[source(m) for m in range(4)]
        + [pl.BlockSpec((small_rows, TILE), lambda i: (4 * blocks * width // small_rows, 0))],
        out_specs=[column(width)] * 4
        + [kept((experts, width)), kept((2, width)), kept((heads, buckets))],
        out_shape=[jax.ShapeDtypeStruct((width, width), jnp.float32)] * 4
        + [
            jax.ShapeDtypeStruct((experts, width), jnp.float32),
            jax.ShapeDtypeStruct((2, width), jnp.float32),
            jax.ShapeDtypeStruct((heads, buckets), jnp.float32),
        ],
        compiler_params=params(32),
        name="unpack",
    )(*[packed] * 5)


def attention_forward_kernel(len_ref, q_ref, k_ref, v_ref, near_ref, far_ref, o_ref, p_ref, s_ref):
    seq = q_ref.shape[0]
    tiles = seq // TILE
    half = q_ref.shape[1] // 2
    row = pl.program_id(0)
    pair = pl.program_id(1)
    live = len_ref[row]
    lane = lax.broadcasted_iota(jnp.int32, (seq, 2 * half), 1)
    dead = lax.broadcasted_iota(jnp.int32, (seq, 2 * half), 0) >= live
    q = q_ref[...]
    k = k_ref[...]
    v_t = v_ref[...].T
    outs = []
    for h in range(2):
        mine = (lane >= h * half) & (lane < (h + 1) * half)
        flag = lane == (1 - h) * half
        k_h = jnp.where(mine, k, jnp.where(flag & dead, -1e30, 0.0).astype(k.dtype))
        q_h = jnp.where(flag, jnp.ones_like(q), q)
        after = far_ref[2 * pair + h, 0]
        before = far_ref[2 * pair + h, 1]
        tops = []
        for i in range(0, tiles, 2):
            q_i = q_h[i * TILE : (i + 2) * TILE]
            raw = dot_t(k_h, q_i)
            for c in range(2):
                cols = slice((i + c) * TILE, (i + c + 1) * TILE)
                top = None
                for j in range(tiles):
                    x = raw[j * TILE : (j + 1) * TILE, c * TILE : (c + 1) * TILE] * (0.125 * LOG2E)
                    d = j - i - c
                    if -1 <= d <= 1:
                        x = x + near_ref[h, d + 1]
                    else:
                        x = x + (after if d > 0 else before)
                    s_ref[h, j * TILE : (j + 1) * TILE, cols] = x
                    m = jnp.max(x, axis=0, keepdims=True)
                    top = m if top is None else jnp.maximum(top, m)
                tops.append(top)
        for i in range(tiles):
            e = jnp.exp2(s_ref[h, :, i * TILE : (i + 1) * TILE] - tops[i])
            total = jnp.sum(e, axis=0, keepdims=True)
            p_ref[0, h, :, i * TILE : (i + 1) * TILE] = (e * (1.0 / total)).astype(LOW)
        outs.append(lax.dot_general(v_t[h * half:(h + 1) * half], p_ref[0, h], (((1,), (0,)), ((), ())), preferred_element_type=jnp.float32))
    o_ref[...] = jnp.concatenate(outs, axis=0).T.astype(o_ref.dtype)

def attention_forward(lengths, projected, near, far, rows, seq, heads, head):
    width = heads * head
    pairs = heads // 2
    spec = lambda off: pl.BlockSpec((seq, 2 * head), lambda b, p: (b, off + p))
    return pl.pallas_call(
        attention_forward_kernel,
        grid=(rows, pairs),
        in_specs=[
            pl.BlockSpec(memory_space=pltpu.SMEM),
            spec(0), spec(pairs), spec(2 * pairs),
            pl.BlockSpec((2, 3, TILE, TILE), lambda b, p: (p, 0, 0, 0)),
            pl.BlockSpec(memory_space=pltpu.SMEM),
        ],
        out_specs=[
            pl.BlockSpec((seq, 2 * head), lambda b, p: (b, p)),
            pl.BlockSpec((1, 2, seq, seq), lambda b, p: (b, p, 0, 0)),
        ],
        out_shape=[
            jax.ShapeDtypeStruct((rows * seq, width), LOW),
            jax.ShapeDtypeStruct((rows, heads, seq, seq), LOW),
        ],
        scratch_shapes=[pltpu.VMEM((2, seq, seq), jnp.float32)],
        compiler_params=params(40),
        cost_estimate=cost(flops=4 * rows * heads * seq * seq * head * 4, bytes_accessed=rows * heads * seq * seq * 2, transcendentals=rows * heads * seq * seq),
        name="attention_forward",
    )(lengths, projected, projected, projected, near, far)

def attention_backward_kernel(
    q_ref, k_ref, v_ref, do_ref, o_ref, p_ref, nt_ref, wq_ref, wk_ref, wv_ref, x_ref, dy_ref, gain_ref,
    gr_ref, gg2_ref, out_ref, pack_ref, small_ref,
    near_ref, far_ref, d_ref, lines_ref, acc_ref, dh_ref, gg_ref,
):
    seq = q_ref.shape[0]
    tiles = seq // TILE
    half = q_ref.shape[1] // 2
    width = x_ref.shape[1]
    pair = pl.program_id(0)
    row = pl.program_id(1)
    last_pair = pair == pl.num_programs(0) - 1
    last_row = row == pl.num_programs(1) - 1
    lane = lax.broadcasted_iota(jnp.int32, (seq, 2 * half), 1)
    q = q_ref[...]
    k = k_ref[...]
    k_t = k.T
    v = v_ref[...]
    do = do_ref[...]
    weighed = (do.astype(jnp.float32) * o_ref[...].astype(jnp.float32)).T
    dq_parts = []
    dk_all = None
    dv_all = None

    @pl.when(row == 0)
    def _():
        near_ref[...] = jnp.zeros_like(near_ref)
        far_ref[...] = jnp.zeros_like(far_ref)
        acc_ref[...] = jnp.zeros_like(acc_ref)

    for h in range(2):
        mine = (lane >= h * half) & (lane < (h + 1) * half)
        v_h = jnp.where(mine, v, jnp.zeros_like(v))
        delta = jnp.sum(weighed[h * half : (h + 1) * half], axis=0, keepdims=True)
        far_sum = [jnp.zeros((8, TILE), jnp.float32), jnp.zeros((8, TILE), jnp.float32)]
        for i in range(0, tiles, 2):
            dp = dot_t(v_h, do[i * TILE : (i + 2) * TILE])
            for c in range(2):
                cols = slice((i + c) * TILE, (i + c + 1) * TILE)
                for j in range(tiles):
                    rws = slice(j * TILE, (j + 1) * TILE)
                    part = dp[rws, c * TILE : (c + 1) * TILE] - delta[:, cols]
                    ds = p_ref[0, h, rws, cols].astype(jnp.float32) * part
                    d = j - i - c
                    if -1 <= d <= 1:
                        near_ref[h, d + 1] += ds
                    else:
                        which = 0 if d > 0 else 1
                        far_sum[which] = far_sum[which] + jnp.sum(
                            ds.reshape(TILE // 8, 8, TILE), axis=0
                        )
                    d_ref[h, rws, cols] = ds.astype(LOW)
        far_ref[h, 0] += far_sum[0]
        far_ref[h, 1] += far_sum[1]
    for h in range(2):
        mine = (lane >= h * half) & (lane < (h + 1) * half)
        ds_all = d_ref[h]
        dq_parts.append(dot(k_t[h * half : (h + 1) * half], ds_all))
        dk_h = dot(ds_all, q)
        dv_h = dot(p_ref[0, h], do)
        dk_all = dk_h if h == 0 else jnp.where(mine, dk_h, dk_all)
        dv_all = dv_h if h == 0 else jnp.where(mine, dv_h, dv_all)

    dq = (jnp.concatenate(dq_parts, axis=0).T * 0.125).astype(LOW)
    grads = jnp.concatenate([dq, (dk_all * 0.125).astype(LOW), dv_all.astype(LOW)], axis=1)
    acc_ref[...] += dot(nt_ref[...], grads)
    weights = jnp.concatenate([wq_ref[...], wk_ref[...], wv_ref[...]], axis=1)
    dh = dot_t(grads, weights)
    here = pl.ds(pl.multiple_of(row * seq, seq), seq)

    @pl.when(pair == 0)
    def _():
        dh_ref[here, :] = dh

    @pl.when(pair > 0)
    def _():
        dh_ref[here, :] += dh

    @pl.when(last_row)
    def _():
        bucket_sums(near_ref, far_ref, lines_ref, 2 * pair)
        for n in range(3):
            pack_ref[n, 0] = acc_ref[:, n * TILE : (n + 1) * TILE].astype(LOW)

    @pl.when(last_pair & (row == 0))
    def _():
        gg_ref[...] = jnp.zeros_like(gg_ref)

    @pl.when(last_pair)
    def _():
        total = dh_ref[here, :]
        x = x_ref[...].astype(jnp.float32)
        rms = lax.rsqrt(jnp.mean(x * x, axis=-1, keepdims=True) + EPSILON)
        gg_ref[...] += jnp.sum(total * x * rms, axis=0, keepdims=True)
        u = total * gain_ref[...]
        out_ref[...] = (
            dy_ref[...]
            + rms * u
            - x * (rms * rms * rms) * jnp.mean(u * x, axis=-1, keepdims=True)
        )

    @pl.when(last_pair & last_row)
    def _():
        at = gr_ref.shape[0]
        small_ref[:at] = gr_ref[...].astype(LOW)
        lines = width // TILE
        gains = [gg_ref[:, c * TILE : (c + 1) * TILE] for c in range(lines)]
        gains += [gg2_ref[:, c * TILE : (c + 1) * TILE] for c in range(lines)]
        if 2 * lines % 16:
            gains += [jnp.zeros((16 - 2 * lines % 16, TILE), jnp.float32)]
        gains = jnp.concatenate(gains, axis=0)
        small_ref[at : at + gains.shape[0]] = gains.astype(LOW)
        at = at + gains.shape[0]
        table = bucket_table(lines_ref)
        if table.shape[0] % 16:
            table = jnp.concatenate([table, jnp.zeros((16 - table.shape[0] % 16, TILE), jnp.float32)], axis=0)
        small_ref[at : at + table.shape[0]] = table.astype(LOW)
        at = at + table.shape[0]
        small_ref[at:] = jnp.zeros((small_ref.shape[0] - at, TILE), LOW)


def bucket_sums(near_ref, far_ref, lines_ref, first):
    empty = jnp.zeros((8, TILE), jnp.float32)
    sub = lax.broadcasted_iota(jnp.int32, (8, 2 * TILE), 0)
    for h in range(2):
        lines = []
        for d in range(3):
            turned = None
            for a in range(0, TILE, 8):
                part = jnp.concatenate([near_ref[h, d, a : a + 8], empty], axis=1)
                part = pltpu.roll(part, (2 * TILE - a) % (2 * TILE), 1) if a else part
                turned = part if turned is None else turned + part
            for b in (1, 2, 4):
                turned = jnp.where((sub & b) > 0, pltpu.roll(turned, 2 * TILE - b, 1), turned)
            lines.append(jnp.sum(turned, axis=0, keepdims=True))
        for side in range(2):
            total = jnp.sum(far_ref[h, side], axis=0, keepdims=True)
            lines.append(jnp.concatenate([total, jnp.zeros((1, TILE), jnp.float32)], axis=1))
        lines.append(jnp.zeros((3, 2 * TILE), jnp.float32))
        lines_ref[first + h] = jnp.concatenate(lines, axis=0)


def bucket_table(lines_ref):
    heads = lines_ref.shape[0]
    buckets = 4 * 8
    lane = lax.broadcasted_iota(jnp.int32, (2 * TILE, TILE), 0)
    bucket = lax.broadcasted_iota(jnp.int32, (2 * TILE, TILE), 1)
    turn = jnp.where(lane >= TILE, lane - 2 * TILE, lane)
    total = None
    for r in range(5):
        if r < 3:
            hit = bucket_of((r - 1) * TILE - turn) == bucket
        else:
            hit = bucket == (buckets - 1 if r == 3 else buckets // 2 - 1)
        hit = hit.astype(LOW)
        line = jnp.concatenate([lines_ref[h, r : r + 1, :] for h in range(heads)], axis=0)
        high = line.astype(LOW)
        part = dot(high, hit) + dot((line - high.astype(jnp.float32)).astype(LOW), hit)
        total = part if total is None else total + part
    return total


def attention_backward(
    projected, do, joined, weights, normed_t, w_query, w_key, w_value, x, dy, gain, gr, gg2,
    rows, seq, heads, head, small_rows,
):
    width = heads * head
    pairs = heads // 2
    spec = lambda off: pl.BlockSpec((seq, 2 * head), lambda p, b: (b, off + p))
    column = pl.BlockSpec((width, 2 * head), lambda p, b: (0, p))
    at_end = pl.BlockSpec((seq, width), lambda p, b: (b * (p // (pairs - 1)), 0))
    return pl.pallas_call(
        attention_backward_kernel,
        grid=(pairs, rows),
        in_specs=[
            spec(0), spec(pairs), spec(2 * pairs), spec(0), spec(0),
            pl.BlockSpec((1, 2, seq, seq), lambda p, b: (b, p, 0, 0)),
            pl.BlockSpec((width, seq), lambda p, b: (0, b)),
            column, column, column, at_end, at_end,
            whole((1, width)), whole(gr.shape), whole(gg2.shape),
        ],
        out_specs=[
            at_end,
            pl.BlockSpec((3, 1, width, TILE), lambda p, b: (0, p, 0, 0)),
            pl.BlockSpec((small_rows, TILE), lambda p, b: (0, 0)),
        ],
        out_shape=[
            jax.ShapeDtypeStruct((rows * seq, width), jnp.float32),
            jax.ShapeDtypeStruct((3, pairs, width, TILE), LOW),
            jax.ShapeDtypeStruct((small_rows, TILE), LOW),
        ],
        scratch_shapes=[
            pltpu.VMEM((2, 3, TILE, TILE), jnp.float32),
            pltpu.VMEM((2, 2, 8, TILE), jnp.float32),
            pltpu.VMEM((2, seq, seq), LOW),
            pltpu.VMEM((heads, 8, 2 * TILE), jnp.float32),
            pltpu.VMEM((width, 3 * TILE), jnp.float32),
            pltpu.VMEM((rows * seq, width), jnp.float32),
            pltpu.VMEM((1, width), jnp.float32),
        ],
        compiler_params=params(60),
        cost_estimate=cost(8 * rows * heads * seq * seq * head * 4, rows * heads * seq * seq * 2),
        name="attention_backward",
    )(
        projected, projected, projected, do, joined, weights, normed_t, w_query, w_key, w_value,
        x, dy, gain, gr, gg2,
    )


def bias_tiles(table):
    j = lax.broadcasted_iota(jnp.int32, (3, TILE, TILE), 1)
    i = lax.broadcasted_iota(jnp.int32, (3, TILE, TILE), 2)
    d = lax.broadcasted_iota(jnp.int32, (3, TILE, TILE), 0) - 1
    b = bucket_of(d * TILE + j - i)
    scaled = table.T * LOG2E
    hot = (b.reshape(1, -1) == jnp.arange(table.shape[0], dtype=jnp.int32)[:, None]).astype(jnp.float32)
    near = jnp.dot(scaled, hot, precision=lax.Precision.HIGHEST).reshape(-1, 3, TILE, TILE)
    far = jnp.stack([scaled[:, -1], scaled[:, table.shape[0] // 2 - 1]], axis=1)
    return near, far


def expert_kernel(experts, chunk, x_ref, g_ref, mine_ref, wr_ref, wi_any, wo_any,
                  ff_ref, dx_ref, hid_ref, da_ref, xt_ref, dfft_ref, gr_ref, wi_ref, wo_ref, sem):
    inner = wi_ref.shape[1]
    first_step = pl.program_id(0) == 0

    def loads(f):
        cols = pl.ds(f, chunk)
        return (pltpu.make_async_copy(wi_any.at[:, cols], wi_ref.at[:, cols], sem.at[0, f // chunk]),
                pltpu.make_async_copy(wo_any.at[cols, :], wo_ref.at[cols, :], sem.at[1, f // chunk]))

    @pl.when(first_step)
    def _():
        for f in range(0, inner, chunk):
            for c in loads(f):
                c.start()
        gr_ref[...] = jnp.zeros_like(gr_ref)

    x = x_ref[...]
    g = g_ref[...].reshape(x.shape).astype(jnp.float32)
    mine = mine_ref[...]
    lane = lax.broadcasted_iota(jnp.int32, (1, wr_ref.shape[1]), 1)
    logits = jnp.dot(x, wr_ref[...], preferred_element_type=jnp.float32)
    logits = jnp.where(lane < experts, logits, -1e30)
    e = jnp.exp(logits - jnp.max(logits, axis=-1, keepdims=True))
    router = e / jnp.sum(e, axis=-1, keepdims=True)
    gate = jnp.sum(router * mine, axis=-1, keepdims=True)
    dff = (g * gate).astype(LOW)
    ff = None
    dx = None
    def first(f):
        @pl.when(first_step)
        def _():
            for c in loads(f):
                c.wait()
        cols = slice(f, f + chunk)
        return (jnp.dot(x, wi_ref[:, cols], preferred_element_type=jnp.float32),
                lax.dot_general(dff, wo_ref[cols, :], (((1,), (1,)), ((), ())), preferred_element_type=jnp.float32))
    for f in range(0, inner, chunk):
        cols = slice(f, f + chunk)
        a, dhid = first(f)
        u = a * a
        t = jnp.tanh(a * (GELU_A + GELU_B * u))
        h = 0.5 + 0.5 * t
        hid = a * h
        slope = h + hid * ((1.0 - t) * (GELU_A + (3.0 * GELU_B) * u))
        da = (dhid * slope).astype(LOW)
        hid = hid.astype(LOW)
        hid_ref[:, cols] = hid
        da_ref[:, cols] = da
        ff_part = jnp.dot(hid, wo_ref[cols, :], preferred_element_type=jnp.float32)
        dx_part = lax.dot_general(da, wi_ref[:, cols], (((1,), (1,)), ((), ())), preferred_element_type=jnp.float32)
        ff = ff_part if ff is None else ff + ff_part
        dx = dx_part if dx is None else dx + dx_part
    ff = ff.astype(LOW)
    ff_ref[...] = ff
    dgate = jnp.sum(g * ff.astype(jnp.float32), axis=-1, keepdims=True)
    dlogits = ((gate * dgate) * (mine - router)).astype(LOW)
    dx = dx + lax.dot_general(dlogits, wr_ref[...], (((1,), (1,)), ((), ())), preferred_element_type=jnp.float32)
    dx_ref[...] = dx.astype(LOW)
    x_t = x.T
    xt_ref[...] = x_t
    dfft_ref[...] = dff.T
    gr_ref[...] += dot(dlogits.T, x)

def expert_rows(x, g, mine, wr, wi, wo, experts, low, high, tile=256, chunk=768):
    n, width = x.shape
    inner = wi.shape[1]
    sources, room = g.shape[0], high - low
    group = max(1, min(sources, tile // room))
    while sources % group or (group * room) % TILE:
        group += 1
    tile = group * room
    gspec = pl.BlockSpec((group, room, width), lambda i: (i, low // room, 0))
    once = lambda s: pl.BlockSpec(s, lambda i: (0,) * len(s), pipeline_mode=pl.Buffered(1))
    rowspec = lambda w: pl.BlockSpec((tile, w), lambda i: (i, 0))
    anywhere = pl.BlockSpec(memory_space=pl.ANY)
    return pl.pallas_call(
        functools.partial(expert_kernel, experts, chunk),
        grid=(n // tile,),
        in_specs=[rowspec(width), gspec, once(mine.shape), once(wr.shape), anywhere, anywhere],
        out_specs=[rowspec(width), rowspec(width), rowspec(inner), rowspec(inner),
                   pl.BlockSpec((width, tile), lambda i: (0, i)), pl.BlockSpec((width, tile), lambda i: (0, i)),
                   pl.BlockSpec((wr.shape[1], width), lambda i: (0, 0))],
        out_shape=[jax.ShapeDtypeStruct((n, width), LOW)] * 2 + [jax.ShapeDtypeStruct((n, inner), LOW)] * 2
            + [jax.ShapeDtypeStruct((width, n), LOW)] * 2 + [jax.ShapeDtypeStruct((wr.shape[1], width), jnp.float32)],
        scratch_shapes=[pltpu.VMEM(wi.shape, LOW), pltpu.VMEM(wo.shape, LOW), pltpu.SemaphoreType.DMA((2, inner // chunk))],
        compiler_params=params(60),
        cost_estimate=cost(flops=8 * n * width * inner, bytes_accessed=4 * n * inner + 8 * width * inner, transcendentals=n * inner),
        name="expert_rows",
    )(x, g, mine, wr, wi, wo)

def expert_weights_kernel(parts, *refs):
    ins, (gi_ref, go_ref) = refs[: 4 * parts], refs[4 * parts :]
    gi = None
    go = None
    for c in range(parts):
        xt, dfft, hid, da = ins[4 * c : 4 * c + 4]
        gi_c = dot(xt[...], da[...])
        go_c = dot(dfft[...], hid[...])
        gi = gi_c if gi is None else gi + gi_c
        go = go_c if go is None else go + go_c
    gi_ref[0] = gi
    go_ref[0] = go.T


def expert_weights(parts, tile=512):
    inner = parts[0][2].shape[1]
    width = parts[0][0].shape[0]
    specs, args, rows = [], [], 0
    for xt, dfft, hid, da in parts:
        n = hid.shape[0]
        rows += n
        specs += [pl.BlockSpec((width, n), lambda f: (0, 0), pipeline_mode=pl.Buffered(1))] * 2
        specs += [pl.BlockSpec((n, tile), lambda f: (0, f))] * 2
        args += [xt, dfft, hid, da]
    return pl.pallas_call(
        functools.partial(expert_weights_kernel, len(parts)),
        grid=(inner // tile,),
        in_specs=specs,
        out_specs=[
            pl.BlockSpec((1, width, tile), lambda f: (0, 0, f)),
            pl.BlockSpec((1, tile, width), lambda f: (0, f, 0)),
        ],
        out_shape=[
            jax.ShapeDtypeStruct((1, width, inner), jnp.float32),
            jax.ShapeDtypeStruct((1, inner, width), jnp.float32),
        ],
        compiler_params=params(60),
        cost_estimate=cost(4 * rows * width * inner, 4 * rows * inner + 8 * width * inner),
        name="expert_weights",
    )(*args)


def split_units(units, weights):
    total, sizes, done, so_far = sum(weights), [], 0, 0
    for w in weights:
        so_far += w
        end = (2 * units * so_far + total) // (2 * total)
        sizes.append(end - done)
        done = end
    return sizes


def sum_parts(n, heights):
    bits = n.bit_length() - 1
    upper = list(range(1, bits))
    orders = [[0] + upper[t:] + upper[:t] for t in range(3)]
    parts, first = [], 0
    for ref, rows in enumerate(heights):
        units = rows // (16 * n)
        turns = (0, 1, 2, 0, 1, 2) if units >= 18 else (0, 1, 2) if units >= 6 else (2,)
        at = 0
        for t, size in zip(turns, split_units(units, [(5, 5, 4)[t] for t in turns])):
            parts.append((ref, at * 16 * n, first, size * 16, orders[t]))
            at += size
            first += size * 16 * n
    return bits, parts


def sum_kernel(cores, n, room, heights, extra, code_ref, gate_ref, rank_ref, ff_any, y_any, *refs):
    _, cut, _ = plan(room)
    xs, refs = refs[: len(heights)], refs[len(heights) :]
    mixed_ref, out_ref, work_ref, got_ref, ff_ref, y_ref, *refs = refs
    loads = [(ff_any, ff_ref), (y_any, y_ref)]
    if extra:
        tail_ref, *refs = refs
    send, recv, local = refs
    loads = [pltpu.make_async_copy(a, b, local.at[i]) for i, (a, b) in enumerate(loads)]
    for copy in loads:
        copy.start()
    summed = heights[:-1] if extra else heights
    bits, parts = sum_parts(n, summed)
    full = len(parts)
    if extra:
        parts = parts + [(len(summed), 0, sum(summed), heights[-1] // n, list(range(bits)))]
    me = lax.axis_index("grp") * cores + lax.axis_index("exp")
    barrier = pltpu.get_barrier_semaphore()
    for b in range(bits):
        pl.semaphore_signal(barrier, inc=1, **device_place(cores, partner_of(me, b)[1]))
    pl.semaphore_wait(barrier, bits)
    base = [first for _, _, first, _, _ in parts]
    got_at = list(base)

    def halving(p, s):
        ref, at, first, step, order = parts[p]
        length = step * (n >> (s + 1))
        bit, partner = partner_of(me, order[s])
        start = base[p] + (1 - bit) * length
        if s == 0:
            source = xs[ref].at[rows_at(start - first + at, length)]
        else:
            source = work_ref.at[rows_at(start, length)]
        return pltpu.make_async_remote_copy(
            src_ref=source, dst_ref=got_ref.at[rows_at(got_at[p], length)],
            send_sem=send.at[p, s], recv_sem=recv.at[p, s], **device_place(cores, partner),
        )

    def doubling(p, s):
        _, _, _, step, order = parts[p]
        here = rows_at(base[p], step * (n >> (s + 1)))
        return pltpu.make_async_remote_copy(
            src_ref=out_ref.at[here], dst_ref=out_ref.at[here],
            send_sem=send.at[p, bits + s], recv_sem=recv.at[p, bits + s],
            **device_place(cores, partner_of(me, order[s])[1]),
        )

    tokens, width = mixed_ref.shape
    tile = tokens // 4

    def mix_tile(i):
        here = slice(i * tile, (i + 1) * tile)
        ff = collect(segment(code_ref[here, :], room, 0, cut), ff_ref[...])
        if extra:
            tail = tail_ref[...]
            tail = [tail[c * extra : (c + 1) * extra] for c in range(width // TILE)]
            ff = ff + collect(rank_ref[here, :], jnp.concatenate(tail, axis=1))
        mixed_ref[here, :] = (y_ref[here, :] + gate_ref[here, :] * ff).astype(LOW)

    moving = [halving(p, 0) for p in range(len(parts))]
    for copy in moving:
        copy.start()
    sent = []
    for s in range(bits):
        for p, (ref, at, first, step, order) in enumerate(parts):
            length = step * (n >> (s + 1))
            moving[p].wait_recv()
            sent.append(moving[p])
            base[p] = base[p] + partner_of(me, order[s])[0] * length
            source, shift = (xs[ref], at - first) if s == 0 else (work_ref, 0)
            last = s + 1 == bits
            target = out_ref if last else work_ref
            if p >= full and last:
                target = tail_ref

            def add(
                i, _, start=base[p], source=source, shift=shift, target=target, arrived=got_at[p],
                step=step, to=0 if p >= full and last else base[p],
            ):
                got = got_ref[rows_at(arrived + i * step, step), :].astype(jnp.float32)
                mine = source[rows_at(start + shift + i * step, step), :].astype(jnp.float32)
                target[rows_at(to + i * step, step), :] = (mine + got).astype(LOW)
                return 0

            lax.fori_loop(0, length // step, add, 0)
            got_at[p] += length
            if not last:
                moving[p] = halving(p, s + 1)
                moving[p].start()
            elif p < full:
                moving[p] = doubling(p, s)
                moving[p].start()
    for copy in sent:
        copy.wait_send()
    for copy in loads:
        copy.wait()
    sent = []
    for turn, s in enumerate(reversed(range(bits))):
        for i in ((), (), (0,), (1, 2), (3,))[turn] if bits == 5 else range(4 * turn // bits, 4 * (turn + 1) // bits):
            mix_tile(i)
        for p, (ref, at, first, step, order) in enumerate(parts[:full]):
            length = step * (n >> (s + 1))
            moving[p].wait_recv()
            sent.append(moving[p])
            base[p] = base[p] - partner_of(me, order[s])[0] * length
            if s > 0:
                moving[p] = doubling(p, s - 1)
                moving[p].start()
    for copy in sent:
        copy.wait_send()


def all_sum(xs, code, gate, rank, ff, y, room, ff_more):
    cores = lax.axis_size("exp")
    n = lax.axis_size(AXES)
    extra = plan(room)[2]
    heights = [a.shape[0] for a in xs]
    if any(h % (16 * n) for h in heights):
        xs = [jnp.concatenate(xs[:-1], axis=0), xs[-1]]
        heights = [a.shape[0] for a in xs]
    total = sum(heights)
    bits, parts = sum_parts(n, heights)
    count = len(parts)
    rows = total
    tokens, width = y.shape
    tail = []
    if extra:
        xs = xs + [ff_more]
        heights = heights + [ff_more.shape[0]]
        rows += ff_more.shape[0]
        count += 1
        tail = [pltpu.VMEM((extra * width // TILE, TILE), LOW)]
    buffer = pltpu.VMEM((rows, TILE), LOW)
    vmem = pl.BlockSpec(memory_space=pltpu.VMEM)
    anywhere = pl.BlockSpec(memory_space=pl.ANY)
    return pl.pallas_call(
        functools.partial(sum_kernel, cores, n, room, heights, extra),
        out_shape=[
            jax.ShapeDtypeStruct((tokens, width), LOW),
            jax.ShapeDtypeStruct((total, TILE), LOW),
        ],
        in_specs=[vmem] * 3 + [anywhere] * 2 + [vmem] * len(xs),
        out_specs=[vmem] * 2,
        scratch_shapes=[
            buffer, buffer, pltpu.VMEM(ff.shape, LOW), pltpu.VMEM(y.shape, jnp.float32), *tail,
            pltpu.SemaphoreType.DMA((count, 2 * bits)),
            pltpu.SemaphoreType.DMA((count, 2 * bits)),
            pltpu.SemaphoreType.DMA((2,)),
        ],
        compiler_params=params(60, collective_id=1, has_side_effects=True),
        name="all_sum",
    )(code, gate, rank, ff, y, *xs)


def local(
    tokens, lengths, expert_ids, slots, w_query, w_key, w_value, w_output,
    gain_attn, gain_ffn, bias_table, w_router, w_in, w_out, cotangent,
):
    rows, seq, width = tokens.shape
    count = rows * seq
    buckets, heads = bias_table.shape
    head = width // heads
    experts = w_router.shape[1]
    devices = lax.axis_size(AXES)
    room = max(4, 2 * count // experts)
    me = lax.axis_index(AXES)
    x = tokens.reshape(count, width)
    g = cotangent.reshape(count, width)
    gain_one = gain_attn.reshape(1, width)
    gain_two = gain_ffn.reshape(1, width)
    wide = max(128, experts)
    mine = (jnp.arange(wide, dtype=jnp.int32) == me).astype(jnp.float32).reshape(1, wide)

    segments, cut, extra = plan(room)
    code_c, code_r, rank_c, flag, g_out = route(expert_ids, slots, g, experts, room)
    g_in = exchange(g_out, devices)
    code_r, x, w_query, w_key, w_value, w_output, bias_table, w_router = lax.optimization_barrier(
        (code_r, x, w_query, w_key, w_value, w_output, bias_table, w_router)
    )
    router_w = jnp.pad(w_router, ((0, 0), (0, wide - experts)))

    normed_t, projected = project(x, gain_one, w_query, w_key, w_value)
    near, far = bias_tiles(bias_table)
    joined, weights = attention_forward(lengths, projected, near, far, rows, seq, heads, head)
    y, gate, *h_out = after_attention(
        joined, x, w_output, gain_two, expert_ids.reshape(count, 1), router_w, code_r, experts, room
    )
    h_out, g_in = lax.optimization_barrier((h_out, g_in))
    g_in = g_in.reshape(devices, room, width)
    h_in = [exchange(h_out[0], devices)]
    for h in h_out[1:]:
        h, h_in[-1] = lax.optimization_barrier((h, h_in[-1]))
        h_in.append(exchange(h, devices))
    dx_back, ffs, parts, grad_router = [], [], [], 0.0
    for n, (low, high) in enumerate(segments):
        ff, dx, hid, da, x_t, dff_t, routed = expert_rows(
            h_in[n], g_in, mine, router_w, w_in[0], w_out[0], experts, low, high
        )
        if n + 1 < len(segments):
            dx, h_in[n + 1] = lax.optimization_barrier((dx, h_in[n + 1]))
        if n:
            dx, dx_back[-1] = lax.optimization_barrier((dx, dx_back[-1]))
        dx_back.append(exchange(dx, devices))
        ffs.append(ff.reshape(devices, high - low, width))
        parts.append((x_t, dff_t, hid, da))
        grad_router = grad_router + routed
    grad_in, grad_out = expert_weights(parts)
    grad_router = grad_router[:experts].reshape(experts, width // TILE, TILE)
    grad_router = jnp.swapaxes(grad_router, 0, 1).reshape(-1, TILE)
    small = jnp.concatenate([grad_router, flag], axis=0)
    ff, ff_more = ffs[0], small
    if extra:
        half = segments[0][1]
        ff = jnp.concatenate([ffs[0], ffs[1][:, : cut - half]], axis=1)
        ff_spare = ffs[1][:, cut - half :]
        bits = devices.bit_length() - 1
        ff_more = ff_spare.reshape((2,) * bits + (extra, width // TILE, TILE))
        order = tuple(reversed(range(bits))) + (bits + 1, bits, bits + 2)
        ff_more = jnp.transpose(ff_more, order).reshape(-1, TILE)
    ff = ff.reshape(devices * cut, width)
    dx_back, grad_in, grad_out, ff, ff_more, small = lax.optimization_barrier(
        (dx_back, grad_in, grad_out, ff, ff_more, small)
    )
    ff_back = exchange(ff, devices)

    dy, do, grad_output, grad_gain_two = before_attention(
        dx_back, code_c, y, g, gain_two, w_output, joined, room
    )
    lines = width // TILE
    small_rows = small.shape[0] + -(-2 * lines // 16) * 16 + -(-heads // 16) * 16
    small_rows = -(-small_rows // (16 * devices)) * 16 * devices
    grad_tokens, packed, small = attention_backward(
        projected, do, joined, weights, normed_t, w_query, w_key, w_value, x, dy, gain_one,
        small, grad_gain_two, rows, seq, heads, head, small_rows,
    )
    mixed, summed = all_sum(
        [packed.reshape(-1, TILE), grad_output, small], code_c, gate, rank_c, ff_back, y, room, ff_more
    )
    if extra:
        crowded = summed[4 * width * width // TILE + lines * experts, 0] > 0

        def mix_all(mixed):
            del mixed
            code = code_c.reshape(-1)
            expert = code // room
            place = code - expert * room
            spare = exchange(ff_spare.reshape(-1, width), devices)
            first = jnp.where((code >= 0) & (place < cut), expert * cut + place, devices * cut)
            rest = jnp.where(place >= cut, expert * extra + place - cut, devices * extra)
            take = lambda a, index: jnp.take(a, index, axis=0, mode="fill", fill_value=0)
            ff = take(ff_back, first) + take(spare, rest)
            return (y + gate * ff.astype(jnp.float32)).astype(LOW)

        mixed = lax.cond(crowded, mix_all, lambda mixed: mixed, mixed)
    *grads, router_t, gains, table = unpack(
        summed, width, experts, heads, buckets, small_rows
    )
    return (
        mixed.reshape(rows, seq, width),
        grad_tokens.reshape(rows, seq, width),
        *grads,
        gains[0], gains[1], table.T, router_t.T,
        grad_in,
        grad_out,
    )


def solution(mesh):
    split = P(AXES)
    in_specs = (split,) * 4 + (P(),) * 8 + (split,) * 3
    out_specs = (split,) * 2 + (P(),) * 8 + (split,) * 2
    return jax.shard_map(local, mesh=mesh, in_specs=in_specs, out_specs=out_specs, check_vma=False)
```

```python
import functools

import jax
import jax.numpy as jnp
from jax import lax
from jax.experimental import pallas as pl
from jax.experimental.pallas import tpu as pltpu
from jax.sharding import PartitionSpec as P

EPSILON = 1e-06
NEGATIVE = -1e30
THRESHOLDS = (12, 16, 23, 32, 46, 64, 91)
LOG2E = 1.4426950408889634
TILE = 128
GELU_A = 0.7978845608028654
GELU_B = GELU_A * 0.044715
AXES = ("grp", "exp")
LOW = jnp.bfloat16


def dot(a, b):
    return jnp.dot(a, b, preferred_element_type=jnp.float32)


def dot_t(a, b):
    return lax.dot_general(a, b, (((1,), (1,)), ((), ())), preferred_element_type=jnp.float32)


def params(mib, **more):
    return pltpu.CompilerParams(vmem_limit_bytes=mib << 20, **more)


def whole(shape):
    return pl.BlockSpec(shape, lambda *_: (0,) * len(shape), pipeline_mode=pl.Buffered(1))


def cost(flops, bytes_accessed, transcendentals=0):
    return pl.CostEstimate(
        flops=flops, bytes_accessed=bytes_accessed, transcendentals=transcendentals
    )


def bucket_of(offset):
    distance = jnp.abs(offset)
    far = jnp.full_like(distance, 8)
    for border in THRESHOLDS:
        far = far + (distance >= border).astype(jnp.int32)
    return jnp.where(distance < 8, distance, far) + jnp.where(offset > 0, 16, 0).astype(jnp.int32)


def device_place(cores, d):
    return dict(device_id=(lax.div(d, cores), lax.rem(d, cores)), device_id_type=pl.DeviceIdType.MESH)


def partner_of(me, b):
    bit = lax.rem(lax.div(me, 1 << b), 2)
    return bit, me + (1 - 2 * bit) * (1 << b)


def rows_at(start, length):
    return pl.ds(pl.multiple_of(start, 16), length)


def plan(room):
    if room % 64:
        return ((0, room),), room, 0
    return ((0, room // 2), (room // 2, room)), 3 * room // 4, room // 4


def segment(code, room, low, high):
    expert = lax.div(code, room)
    place = code - expert * room
    inside = (code >= 0) & (place >= low) & (place < high)
    return jnp.where(inside, expert * (high - low) + place - low, -1)


def spread(dest, values, out):
    rows = out.shape[0]
    step = min(256, rows)
    for start in range(0, rows, step):
        here = lax.broadcasted_iota(jnp.int32, (step, dest.shape[1]), 0) + start
        out[start : start + step] = dot((dest == here).astype(LOW), values).astype(LOW)


def collect(dest, values):
    here = lax.broadcasted_iota(jnp.int32, (dest.shape[0], values.shape[0]), 1)
    return dot((dest == here).astype(LOW), values)


def spread_all(code, room, values, outs):
    for (low, high), out in zip(plan(room)[0], outs):
        spread(segment(code, room, low, high), values, out)


def collect_all(code, room, refs):
    total = None
    for (low, high), ref in zip(plan(room)[0], refs):
        part = collect(segment(code, room, low, high), ref[...])
        total = part if total is None else total + part
    return total


def buffers(experts, room, width):
    return [
        jax.ShapeDtypeStruct((experts * (high - low), width), LOW) for low, high in plan(room)[0]
    ]


def route_kernel(
    experts, room, eid_c, eid_r, slot_c, slot_r, g_ref, code_c, code_r, rank_c, flag, out
):
    tokens = g_ref.shape[0]
    wide = max(TILE, experts)
    _, cut, extra = plan(room)
    at = lax.broadcasted_iota(jnp.int32, (tokens, tokens), 0)
    to = lax.broadcasted_iota(jnp.int32, (tokens, tokens), 1)

    ids = eid_r[...]
    picked = ids == lax.broadcasted_iota(jnp.int32, (wide, tokens), 0)
    earlier = dot(picked.astype(LOW), (at < to).astype(LOW))
    place = jnp.sum(jnp.where(picked, earlier, 0.0), axis=0, keepdims=True).astype(jnp.int32)
    code = jnp.where(slot_r[...] >= 0, ids * room + place, -1)
    code_r[...] = code
    spread(code, g_ref[...], out)

    ids = eid_c[...]
    picked = ids == lax.broadcasted_iota(jnp.int32, (tokens, wide), 1)
    earlier = dot((to < at).astype(LOW), picked.astype(LOW))
    place = jnp.sum(jnp.where(picked, earlier, 0.0), axis=1, keepdims=True).astype(jnp.int32)
    kept = slot_c[...] >= 0
    code_c[...] = jnp.where(kept, ids * room + place, -1)
    over = kept & (place >= cut)
    rank_c[...] = jnp.where(over, place - cut, -1)
    named = jnp.max(jnp.where(picked & over, 1.0, 0.0), axis=0, keepdims=True)
    named = jnp.sum(named, axis=1, keepdims=True)
    flag[...] = jnp.broadcast_to(jnp.where(named > 1.0, 1.0, 0.0), flag.shape)


def route(expert_ids, slots, upstream, experts, room):
    tokens, width = upstream.shape
    column = jax.ShapeDtypeStruct((tokens, 1), jnp.int32)
    line = jax.ShapeDtypeStruct((1, tokens), jnp.int32)
    return pl.pallas_call(
        functools.partial(route_kernel, experts, room),
        out_shape=[
            column, line, column, jax.ShapeDtypeStruct((16, TILE), jnp.float32),
            jax.ShapeDtypeStruct((experts * room, width), LOW),
        ],
        compiler_params=params(48),
        cost_estimate=cost(2 * experts * room * tokens * width, 8 << 20),
        name="route",
    )(
        expert_ids.reshape(tokens, 1), expert_ids.reshape(1, tokens),
        slots.reshape(tokens, 1), slots.reshape(1, tokens), upstream,
    )


def exchange(buffer, devices):
    shaped = buffer.reshape(devices, buffer.shape[0] // devices, buffer.shape[1])
    moved = lax.all_to_all(shaped, AXES, split_axis=0, concat_axis=0, tiled=True)
    return moved.reshape(buffer.shape)


def project_kernel(x_ref, gain_ref, wq_ref, wk_ref, wv_ref, normed_ref, out_ref):
    x = x_ref[...].astype(jnp.float32)
    rms = lax.rsqrt(jnp.mean(x * x, axis=-1, keepdims=True) + EPSILON)
    normed = (x * rms * gain_ref[...]).astype(LOW)
    normed_ref[...] = normed.T
    width = x.shape[1]
    for n, w_ref in enumerate((wq_ref, wk_ref, wv_ref)):
        out_ref[:, n * width : (n + 1) * width] = dot(normed, w_ref[...]).astype(LOW)


def project(x, gain, w_query, w_key, w_value):
    tokens, width = x.shape
    out = 3 * width
    step = 256
    rows = lambda w: pl.BlockSpec((step, w), lambda i: (i, 0))
    return pl.pallas_call(
        project_kernel,
        grid=(tokens // step,),
        in_specs=[rows(width), whole((1, width)), *[whole((width, width))] * 3],
        out_specs=[pl.BlockSpec((width, step), lambda i: (0, i)), rows(out)],
        out_shape=[
            jax.ShapeDtypeStruct((width, tokens), LOW),
            jax.ShapeDtypeStruct((tokens, out), LOW),
        ],
        compiler_params=params(40),
        cost_estimate=cost(2 * tokens * width * out, 12 << 20),
        name="project",
    )(x, gain, w_query, w_key, w_value)


def after_attention_kernel(
    experts, room, o_ref, x_ref, w_ref, gain_ref, eid_ref, wr_ref, code_ref, y_ref, gate_ref, *rest
):
    outs, held = rest[:-1], rest[-1]
    step = o_ref.shape[0]
    i = pl.program_id(0)
    y = x_ref[...].astype(jnp.float32) + dot(o_ref[...], w_ref[...])
    y_ref[...] = y
    rms = lax.rsqrt(jnp.mean(y * y, axis=-1, keepdims=True) + EPSILON)
    normed = (y * rms * gain_ref[...]).astype(LOW)
    held[pl.ds(pl.multiple_of(i * step, step), step), :] = normed
    router = route_softmax(dot(normed, wr_ref[...]), experts)
    lane = lax.broadcasted_iota(jnp.int32, router.shape, 1)
    gate_ref[...] = jnp.sum(jnp.where(lane == eid_ref[...], router, 0.0), axis=-1, keepdims=True)

    @pl.when(i == pl.num_programs(0) - 1)
    def _():
        spread_all(code_ref[...], room, held[...], outs)


def after_attention(joined, x, w_output, gain, expert_ids, w_router, code, experts, room):
    tokens, width = x.shape
    step = 256
    rows = pl.BlockSpec((step, width), lambda i: (i, 0))
    single = pl.BlockSpec((step, 1), lambda i: (i, 0))
    outs = buffers(experts, room, width)
    return pl.pallas_call(
        functools.partial(after_attention_kernel, experts, room),
        grid=(tokens // step,),
        in_specs=[
            rows, rows, whole((width, width)), whole((1, width)), single, whole(w_router.shape),
            whole((1, tokens)),
        ],
        out_specs=[rows, single] + [pl.BlockSpec(o.shape, lambda i: (0, 0)) for o in outs],
        out_shape=[
            jax.ShapeDtypeStruct((tokens, width), jnp.float32),
            jax.ShapeDtypeStruct((tokens, 1), jnp.float32),
        ]
        + outs,
        scratch_shapes=[pltpu.VMEM((tokens, width), LOW)],
        compiler_params=params(60),
        cost_estimate=cost(2 * tokens * width * (width + experts * room), 12 << 20),
        name="after_attention",
    )(joined, x, w_output, gain, expert_ids, w_router, code)


def route_softmax(logits, experts):
    lane = lax.broadcasted_iota(jnp.int32, logits.shape, 1)
    logits = jnp.where(lane < experts, logits, NEGATIVE)
    e = jnp.exp(logits - jnp.max(logits, axis=-1, keepdims=True))
    return e / jnp.sum(e, axis=-1, keepdims=True)


def pack(values, first, height, out, at):
    for c in range(values.shape[1] // TILE):
        out[at + c * height : at + (c + 1) * height] = values[
            first : first + height, c * TILE : (c + 1) * TILE
        ].astype(LOW)


def before_attention_kernel(
    room, n_backs, code_ref, y_ref, g_ref, gain_ref, w_ref, o_ref, *rest
):
    backs = rest[:n_backs]
    dy_ref, do_ref, pack_ref, gg_ref, gw_ref = rest[n_backs:]
    i = pl.program_id(0)

    @pl.when(i == 0)
    def _():
        gw_ref[...] = jnp.zeros_like(gw_ref)
        gg_ref[...] = jnp.zeros_like(gg_ref)

    step = y_ref.shape[0] // 2
    blocks = [slice(n * step, (n + 1) * step) for n in range(2)]
    dhs = [collect_all(code_ref[here, :], room, backs) for here in blocks]
    lows = []
    for here, dh in zip(blocks, dhs):
        y = y_ref[here, :]
        rms = lax.rsqrt(jnp.mean(y * y, axis=-1, keepdims=True) + EPSILON)
        gg_ref[...] += jnp.sum(dh * y * rms, axis=0, keepdims=True)
        u = dh * gain_ref[...]
        dy = (
            g_ref[here, :].astype(jnp.float32)
            + rms * u
            - y * (rms * rms * rms) * jnp.mean(u * y, axis=-1, keepdims=True)
        )
        dy_ref[here, :] = dy
        lows.append(dy.astype(LOW))
        do_ref[here, :] = dot_t(lows[-1], w_ref[...]).astype(LOW)
    gw_ref[...] += dot(o_ref[...].T, jnp.concatenate(lows, axis=0))

    @pl.when(i == pl.num_programs(0) - 1)
    def _():
        pack(gw_ref, 0, gw_ref.shape[0], pack_ref, 0)


def before_attention(backs, code, y, g, gain, w_output, joined, room):
    tokens, width = y.shape
    step = 512
    rows = lambda w: pl.BlockSpec((step, w), lambda i: (i, 0))
    return pl.pallas_call(
        functools.partial(before_attention_kernel, room, len(backs)),
        grid=(tokens // step,),
        in_specs=[
            rows(1), rows(width), rows(width), whole((1, width)),
            whole((width, width)), rows(width), *[whole(b.shape) for b in backs],
        ],
        out_specs=[
            rows(width), rows(width),
            pl.BlockSpec((width * width // TILE, TILE), lambda i: (0, 0)),
            pl.BlockSpec((1, width), lambda i: (0, 0)),
        ],
        out_shape=[
            jax.ShapeDtypeStruct((tokens, width), jnp.float32),
            jax.ShapeDtypeStruct((tokens, width), LOW),
            jax.ShapeDtypeStruct((width * width // TILE, TILE), LOW),
            jax.ShapeDtypeStruct((1, width), jnp.float32),
        ],
        scratch_shapes=[pltpu.VMEM((width, width), jnp.float32)],
        compiler_params=params(60),
        cost_estimate=cost(6 * tokens * width * width, 16 << 20),
        name="before_attention",
    )(code, y, g, gain, w_output, joined, *backs)


def unpack_kernel(
    experts, heads, buckets, q_ref, k_ref, v_ref, o_ref, small_ref, mix_ref,
    gq, gk, gv, go, router, gains, table, mixed,
):
    mixed[...] = mix_ref[...]
    for packed_ref, out_ref in ((q_ref, gq), (k_ref, gk), (v_ref, gv), (o_ref, go)):
        for c in range(packed_ref.shape[0]):
            out_ref[:, c * TILE : (c + 1) * TILE] = packed_ref[c].astype(jnp.float32)

    @pl.when(pl.program_id(0) == 0)
    def _():
        lines = router.shape[1] // TILE
        small = small_ref[...].astype(jnp.float32)
        for c in range(lines):
            lanes = slice(c * TILE, (c + 1) * TILE)
            router[:, lanes] = small[c * experts : (c + 1) * experts]
            for n in range(2):
                at = lines * experts + 16 + n * lines + c
                gains[n : n + 1, lanes] = small[at : at + 1]
        at = lines * experts + 16 + -(-2 * lines // 16) * 16
        table[...] = small[at : at + heads, :buckets]


def unpack(packed, small, mixed, experts, heads, buckets):
    tokens, width = mixed.shape
    blocks = width // TILE
    steps = 4
    source = lambda m: pl.BlockSpec((blocks, width // steps, TILE), lambda i: (m, i, 0))
    rows = lambda count: pl.BlockSpec((count // steps, width), lambda i: (i, 0))
    kept = lambda shape: pl.BlockSpec(shape, lambda i: (0, 0))
    return pl.pallas_call(
        functools.partial(unpack_kernel, experts, heads, buckets),
        grid=(steps,),
        in_specs=[source(m) for m in range(4)] + [whole(small.shape), rows(tokens)],
        out_specs=[rows(width)] * 4
        + [kept((experts, width)), kept((2, width)), kept((heads, buckets)), rows(tokens)],
        out_shape=[jax.ShapeDtypeStruct((width, width), jnp.float32)] * 4
        + [
            jax.ShapeDtypeStruct((experts, width), jnp.float32),
            jax.ShapeDtypeStruct((2, width), jnp.float32),
            jax.ShapeDtypeStruct((heads, buckets), jnp.float32),
            jax.ShapeDtypeStruct((tokens, width), LOW),
        ],
        compiler_params=params(60),
        name="unpack",
    )(*[packed.reshape(4 * blocks, width, TILE)] * 4, small, mixed)


def attention_forward_kernel(len_ref, q_ref, k_ref, v_ref, near_ref, far_ref, o_ref, p_ref, s_ref):
    seq = q_ref.shape[0]
    tiles = seq // TILE
    half = q_ref.shape[1] // 2
    row = pl.program_id(0)
    pair = pl.program_id(1)
    live = len_ref[row]
    lane = lax.broadcasted_iota(jnp.int32, (seq, 2 * half), 1)
    dead = lax.broadcasted_iota(jnp.int32, (seq, 2 * half), 0) >= live
    q = q_ref[...]
    k = k_ref[...]
    v_t = v_ref[...].T
    outs = []
    for h in range(2):
        mine = (lane >= h * half) & (lane < (h + 1) * half)
        flag = lane == (1 - h) * half
        k_h = jnp.where(mine, k, jnp.where(flag & dead, -1e30, 0.0).astype(k.dtype))
        q_h = jnp.where(flag, jnp.ones_like(q), q)
        after = far_ref[2 * pair + h, 0]
        before = far_ref[2 * pair + h, 1]
        tops = []
        for i in range(0, tiles, 2):
            q_i = q_h[i * TILE : (i + 2) * TILE]
            raw = dot_t(k_h, q_i)
            for c in range(2):
                cols = slice((i + c) * TILE, (i + c + 1) * TILE)
                top = None
                for j in range(tiles):
                    x = raw[j * TILE : (j + 1) * TILE, c * TILE : (c + 1) * TILE] * (0.125 * LOG2E)
                    d = j - i - c
                    if -1 <= d <= 1:
                        x = x + near_ref[h, d + 1]
                    else:
                        x = x + (after if d > 0 else before)
                    s_ref[h, j * TILE : (j + 1) * TILE, cols] = x
                    m = jnp.max(x, axis=0, keepdims=True)
                    top = m if top is None else jnp.maximum(top, m)
                tops.append(top)
        for i in range(tiles):
            e = jnp.exp2(s_ref[h, :, i * TILE : (i + 1) * TILE] - tops[i])
            total = jnp.sum(e, axis=0, keepdims=True)
            p_ref[0, h, :, i * TILE : (i + 1) * TILE] = (e * (1.0 / total)).astype(LOW)
        outs.append(lax.dot_general(v_t[h * half:(h + 1) * half], p_ref[0, h], (((1,), (0,)), ((), ())), preferred_element_type=jnp.float32))
    o_ref[...] = jnp.concatenate(outs, axis=0).T.astype(o_ref.dtype)

def attention_forward(lengths, projected, near, far, rows, seq, heads, head):
    width = heads * head
    pairs = heads // 2
    spec = lambda off: pl.BlockSpec((seq, 2 * head), lambda b, p: (b, off + p))
    return pl.pallas_call(
        attention_forward_kernel,
        grid=(rows, pairs),
        in_specs=[
            pl.BlockSpec(memory_space=pltpu.SMEM),
            spec(0), spec(pairs), spec(2 * pairs),
            pl.BlockSpec((2, 3, TILE, TILE), lambda b, p: (p, 0, 0, 0)),
            pl.BlockSpec(memory_space=pltpu.SMEM),
        ],
        out_specs=[
            pl.BlockSpec((seq, 2 * head), lambda b, p: (b, p)),
            pl.BlockSpec((1, 2, seq, seq), lambda b, p: (b, p, 0, 0)),
        ],
        out_shape=[
            jax.ShapeDtypeStruct((rows * seq, width), LOW),
            jax.ShapeDtypeStruct((rows, heads, seq, seq), LOW),
        ],
        scratch_shapes=[pltpu.VMEM((2, seq, seq), jnp.float32)],
        compiler_params=params(40),
        cost_estimate=cost(flops=4 * rows * heads * seq * seq * head * 4, bytes_accessed=rows * heads * seq * seq * 2, transcendentals=rows * heads * seq * seq),
        name="attention_forward",
    )(lengths, projected, projected, projected, near, far)

def attention_backward_kernel(
    rows, q_ref, k_ref, v_ref, do_ref, o_ref, p_ref, nt_ref, wq_ref, wk_ref, wv_ref, x_ref, dy_ref, gain_ref,
    gr_ref, gg2_ref, out_ref, pack_ref, small_ref,
    near_ref, far_ref, d_ref, lines_ref, dh_ref,
):
    seq = q_ref.shape[0] // rows
    tiles = seq // TILE
    half = q_ref.shape[1] // 2
    width = x_ref.shape[1]
    pair = pl.program_id(0)
    last_pair = pair == pl.num_programs(0) - 1
    lane = lax.broadcasted_iota(jnp.int32, (seq, 2 * half), 1)
    weights = jnp.concatenate([wq_ref[...], wk_ref[...], wv_ref[...]], axis=1)
    near_ref[...] = jnp.zeros_like(near_ref)
    for row in range(rows):
        here = slice(row * seq, (row + 1) * seq)
        v = v_ref[here, :]
        do = do_ref[here, :]
        weighed = (do.astype(jnp.float32) * o_ref[here, :].astype(jnp.float32)).T
        for h in range(2):
            mine = (lane >= h * half) & (lane < (h + 1) * half)
            v_h = jnp.where(mine, v, jnp.zeros_like(v))
            delta = jnp.sum(weighed[h * half : (h + 1) * half], axis=0, keepdims=True)
            far_sum = [jnp.zeros((8, TILE), jnp.float32), jnp.zeros((8, TILE), jnp.float32)]
            for i in range(0, tiles, 2):
                dp = dot_t(v_h, do[i * TILE : (i + 2) * TILE])
                for c in range(2):
                    cols = slice((i + c) * TILE, (i + c + 1) * TILE)
                    for j in range(tiles):
                        rws = slice(j * TILE, (j + 1) * TILE)
                        part = dp[rws, c * TILE : (c + 1) * TILE] - delta[:, cols]
                        ds = p_ref[row, h, rws, cols].astype(jnp.float32) * part
                        d = j - i - c
                        if -1 <= d <= 1:
                            near_ref[row, h, d + 1] += ds
                        else:
                            which = 0 if d > 0 else 1
                            far_sum[which] = far_sum[which] + jnp.sum(
                                ds.reshape(TILE // 8, 8, TILE), axis=0
                            )
                        d_ref[row, h, rws, cols] = ds.astype(LOW)
            for which in range(2):
                far_ref[row, h, which] = far_sum[which]
    grads_all = []
    for row in range(rows):
        here = slice(row * seq, (row + 1) * seq)
        q = q_ref[here, :]
        do = do_ref[here, :]
        k_t = k_ref[here, :].T
        dq_parts = []
        dk_all = None
        dv_all = None
        for h in range(2):
            mine = (lane >= h * half) & (lane < (h + 1) * half)
            ds_all = d_ref[row, h]
            dq_parts.append(dot(k_t[h * half : (h + 1) * half], ds_all))
            dk_h = dot(ds_all, q)
            dv_h = dot(p_ref[row, h], do)
            dk_all = dk_h if h == 0 else jnp.where(mine, dk_h, dk_all)
            dv_all = dv_h if h == 0 else jnp.where(mine, dv_h, dv_all)
        dq = (jnp.concatenate(dq_parts, axis=0).T * 0.125).astype(LOW)
        grads_all.append(
            jnp.concatenate([dq, (dk_all * 0.125).astype(LOW), dv_all.astype(LOW)], axis=1)
        )
    grads = jnp.concatenate(grads_all, axis=0)
    acc = dot(nt_ref[...], grads)
    for n in range(3):
        pack_ref[n, 0] = acc[:, n * TILE : (n + 1) * TILE].astype(LOW)
    dh = dot_t(grads, weights)

    @pl.when(pair == 0)
    def _():
        dh_ref[...] = dh

    @pl.when(pair > 0)
    def _():
        dh_ref[...] += dh

    near_ref[0] = sum(near_ref[row] for row in range(rows))
    far_ref[0] = sum(far_ref[row] for row in range(rows))
    bucket_sums(near_ref.at[0], far_ref.at[0], lines_ref, 2 * pair)

    @pl.when(last_pair)
    def _():
        total = dh_ref[...]
        x = x_ref[...].astype(jnp.float32)
        rms = lax.rsqrt(jnp.mean(x * x, axis=-1, keepdims=True) + EPSILON)
        gg = jnp.sum(total * x * rms, axis=0, keepdims=True)
        u = total * gain_ref[...]
        out_ref[...] = (
            dy_ref[...]
            + rms * u
            - x * (rms * rms * rms) * jnp.mean(u * x, axis=-1, keepdims=True)
        )
        at = gr_ref.shape[0]
        small_ref[:at] = gr_ref[...].astype(LOW)
        lines = width // TILE
        gains = [gg[:, c * TILE : (c + 1) * TILE] for c in range(lines)]
        gains += [gg2_ref[:, c * TILE : (c + 1) * TILE] for c in range(lines)]
        if 2 * lines % 16:
            gains += [jnp.zeros((16 - 2 * lines % 16, TILE), jnp.float32)]
        gains = jnp.concatenate(gains, axis=0)
        small_ref[at : at + gains.shape[0]] = gains.astype(LOW)
        at = at + gains.shape[0]
        table = bucket_table(lines_ref)
        if table.shape[0] % 16:
            table = jnp.concatenate([table, jnp.zeros((16 - table.shape[0] % 16, TILE), jnp.float32)], axis=0)
        small_ref[at : at + table.shape[0]] = table.astype(LOW)
        at = at + table.shape[0]
        small_ref[at:] = jnp.zeros((small_ref.shape[0] - at, TILE), LOW)


def bucket_sums(near_ref, far_ref, lines_ref, first):
    empty = jnp.zeros((8, TILE), jnp.float32)
    sub = lax.broadcasted_iota(jnp.int32, (8, 2 * TILE), 0)
    for h in range(2):
        lines = []
        for d in range(3):
            turned = None
            for a in range(0, TILE, 8):
                part = jnp.concatenate([near_ref[h, d, a : a + 8], empty], axis=1)
                part = pltpu.roll(part, (2 * TILE - a) % (2 * TILE), 1) if a else part
                turned = part if turned is None else turned + part
            for b in (1, 2, 4):
                turned = jnp.where((sub & b) > 0, pltpu.roll(turned, 2 * TILE - b, 1), turned)
            lines.append(jnp.sum(turned, axis=0, keepdims=True))
        for side in range(2):
            total = jnp.sum(far_ref[h, side], axis=0, keepdims=True)
            lines.append(jnp.concatenate([total, jnp.zeros((1, TILE), jnp.float32)], axis=1))
        lines.append(jnp.zeros((3, 2 * TILE), jnp.float32))
        lines_ref[first + h] = jnp.concatenate(lines, axis=0)


def bucket_table(lines_ref):
    heads = lines_ref.shape[0]
    buckets = 4 * 8
    lane = lax.broadcasted_iota(jnp.int32, (2 * TILE, TILE), 0)
    bucket = lax.broadcasted_iota(jnp.int32, (2 * TILE, TILE), 1)
    turn = jnp.where(lane >= TILE, lane - 2 * TILE, lane)
    total = None
    for r in range(5):
        if r < 3:
            hit = bucket_of((r - 1) * TILE - turn) == bucket
        else:
            hit = bucket == (buckets - 1 if r == 3 else buckets // 2 - 1)
        hit = hit.astype(LOW)
        line = jnp.concatenate([lines_ref[h, r : r + 1, :] for h in range(heads)], axis=0)
        high = line.astype(LOW)
        part = dot(high, hit) + dot((line - high.astype(jnp.float32)).astype(LOW), hit)
        total = part if total is None else total + part
    return total


def attention_backward(
    projected, do, joined, weights, normed_t, w_query, w_key, w_value, x, dy, gain, gr, gg2,
    rows, seq, heads, head, small_rows,
):
    width = heads * head
    pairs = heads // 2
    tokens = rows * seq
    spec = lambda off: pl.BlockSpec((tokens, 2 * head), lambda p: (0, off + p))
    column = pl.BlockSpec((width, 2 * head), lambda p: (0, p))
    return pl.pallas_call(
        functools.partial(attention_backward_kernel, rows),
        grid=(pairs,),
        in_specs=[
            spec(0), spec(pairs), spec(2 * pairs), spec(0), spec(0),
            pl.BlockSpec((rows, 2, seq, seq), lambda p: (0, p, 0, 0)),
            whole((width, tokens)),
            column, column, column, whole((tokens, width)), whole((tokens, width)),
            whole((1, width)), whole(gr.shape), whole(gg2.shape),
        ],
        out_specs=[
            pl.BlockSpec((tokens, width), lambda p: (0, 0)),
            pl.BlockSpec((3, 1, width, TILE), lambda p: (0, p, 0, 0)),
            pl.BlockSpec((small_rows, TILE), lambda p: (0, 0)),
        ],
        out_shape=[
            jax.ShapeDtypeStruct((tokens, width), jnp.float32),
            jax.ShapeDtypeStruct((3, pairs, width, TILE), LOW),
            jax.ShapeDtypeStruct((small_rows, TILE), LOW),
        ],
        scratch_shapes=[
            pltpu.VMEM((rows, 2, 3, TILE, TILE), jnp.float32),
            pltpu.VMEM((rows, 2, 2, 8, TILE), jnp.float32),
            pltpu.VMEM((rows, 2, seq, seq), LOW),
            pltpu.VMEM((heads, 8, 2 * TILE), jnp.float32),
            pltpu.VMEM((tokens, width), jnp.float32),
        ],
        compiler_params=params(60),
        cost_estimate=cost(8 * rows * heads * seq * seq * head * 4, rows * heads * seq * seq * 2),
        name="attention_backward",
    )(
        projected, projected, projected, do, joined, weights, normed_t, w_query, w_key, w_value,
        x, dy, gain, gr, gg2,
    )


def bias_tiles(table):
    j = lax.broadcasted_iota(jnp.int32, (3, TILE, TILE), 1)
    i = lax.broadcasted_iota(jnp.int32, (3, TILE, TILE), 2)
    d = lax.broadcasted_iota(jnp.int32, (3, TILE, TILE), 0) - 1
    b = bucket_of(d * TILE + j - i)
    scaled = table.T * LOG2E
    hot = (b.reshape(1, -1) == jnp.arange(table.shape[0], dtype=jnp.int32)[:, None]).astype(jnp.float32)
    near = jnp.dot(scaled, hot, precision=lax.Precision.HIGHEST).reshape(-1, 3, TILE, TILE)
    far = jnp.stack([scaled[:, -1], scaled[:, table.shape[0] // 2 - 1]], axis=1)
    return near, far


def expert_kernel(experts, chunk, x_ref, g_ref, mine_ref, wr_ref, wi_any, wo_any,
                  ff_ref, dx_ref, hid_ref, da_ref, xt_ref, dfft_ref, gr_ref, wi_ref, wo_ref, sem):
    inner = wi_ref.shape[1]
    first_step = pl.program_id(0) == 0

    def loads(f):
        cols = pl.ds(f, chunk)
        return (pltpu.make_async_copy(wi_any.at[:, cols], wi_ref.at[:, cols], sem.at[0, f // chunk]),
                pltpu.make_async_copy(wo_any.at[cols, :], wo_ref.at[cols, :], sem.at[1, f // chunk]))

    @pl.when(first_step)
    def _():
        for f in range(0, inner, chunk):
            for c in loads(f):
                c.start()
        gr_ref[...] = jnp.zeros_like(gr_ref)

    x = x_ref[...]
    g = g_ref[...].reshape(x.shape).astype(jnp.float32)
    mine = mine_ref[...]
    lane = lax.broadcasted_iota(jnp.int32, (1, wr_ref.shape[1]), 1)
    logits = jnp.dot(x, wr_ref[...], preferred_element_type=jnp.float32)
    logits = jnp.where(lane < experts, logits, -1e30)
    e = jnp.exp(logits - jnp.max(logits, axis=-1, keepdims=True))
    router = e / jnp.sum(e, axis=-1, keepdims=True)
    gate = jnp.sum(router * mine, axis=-1, keepdims=True)
    dff = (g * gate).astype(LOW)
    ff = None
    dx = None
    def first(f):
        @pl.when(first_step)
        def _():
            for c in loads(f):
                c.wait()
        cols = slice(f, f + chunk)
        return (jnp.dot(x, wi_ref[:, cols], preferred_element_type=jnp.float32),
                lax.dot_general(dff, wo_ref[cols, :], (((1,), (1,)), ((), ())), preferred_element_type=jnp.float32))
    for f in range(0, inner, chunk):
        cols = slice(f, f + chunk)
        a, dhid = first(f)
        u = a * a
        t = jnp.tanh(a * (GELU_A + GELU_B * u))
        h = 0.5 + 0.5 * t
        hid = a * h
        slope = h + hid * ((1.0 - t) * (GELU_A + (3.0 * GELU_B) * u))
        da = (dhid * slope).astype(LOW)
        hid = hid.astype(LOW)
        hid_ref[:, cols] = hid
        da_ref[:, cols] = da
        ff_part = jnp.dot(hid, wo_ref[cols, :], preferred_element_type=jnp.float32)
        dx_part = lax.dot_general(da, wi_ref[:, cols], (((1,), (1,)), ((), ())), preferred_element_type=jnp.float32)
        ff = ff_part if ff is None else ff + ff_part
        dx = dx_part if dx is None else dx + dx_part
    ff = ff.astype(LOW)
    ff_ref[...] = ff
    dgate = jnp.sum(g * ff.astype(jnp.float32), axis=-1, keepdims=True)
    dlogits = ((gate * dgate) * (mine - router)).astype(LOW)
    dx = dx + lax.dot_general(dlogits, wr_ref[...], (((1,), (1,)), ((), ())), preferred_element_type=jnp.float32)
    dx_ref[...] = dx.astype(LOW)
    x_t = x.T
    xt_ref[...] = x_t
    dfft_ref[...] = dff.T
    gr_ref[...] += dot(dlogits.T, x)

def expert_rows(x, g, mine, wr, wi, wo, experts, low, high, tile=256, chunk=768):
    n, width = x.shape
    inner = wi.shape[1]
    sources, room = g.shape[0], high - low
    group = max(1, min(sources, tile // room))
    while sources % group or (group * room) % TILE:
        group += 1
    tile = group * room
    gspec = pl.BlockSpec((group, room, width), lambda i: (i, low // room, 0))
    once = lambda s: pl.BlockSpec(s, lambda i: (0,) * len(s), pipeline_mode=pl.Buffered(1))
    rowspec = lambda w: pl.BlockSpec((tile, w), lambda i: (i, 0))
    anywhere = pl.BlockSpec(memory_space=pl.ANY)
    return pl.pallas_call(
        functools.partial(expert_kernel, experts, chunk),
        grid=(n // tile,),
        in_specs=[rowspec(width), gspec, once(mine.shape), once(wr.shape), anywhere, anywhere],
        out_specs=[rowspec(width), rowspec(width), rowspec(inner), rowspec(inner),
                   pl.BlockSpec((width, tile), lambda i: (0, i)), pl.BlockSpec((width, tile), lambda i: (0, i)),
                   pl.BlockSpec((wr.shape[1], width), lambda i: (0, 0))],
        out_shape=[jax.ShapeDtypeStruct((n, width), LOW)] * 2 + [jax.ShapeDtypeStruct((n, inner), LOW)] * 2
            + [jax.ShapeDtypeStruct((width, n), LOW)] * 2 + [jax.ShapeDtypeStruct((wr.shape[1], width), jnp.float32)],
        scratch_shapes=[pltpu.VMEM(wi.shape, LOW), pltpu.VMEM(wo.shape, LOW), pltpu.SemaphoreType.DMA((2, inner // chunk))],
        compiler_params=params(60),
        cost_estimate=cost(flops=8 * n * width * inner, bytes_accessed=4 * n * inner + 8 * width * inner, transcendentals=n * inner),
        name="expert_rows",
    )(x, g, mine, wr, wi, wo)

def expert_weights_kernel(parts, *refs):
    ins, (gi_ref, go_ref) = refs[: 4 * parts], refs[4 * parts :]
    gi = None
    go = None
    for c in range(parts):
        xt, dfft, hid, da = ins[4 * c : 4 * c + 4]
        gi_c = dot(xt[...], da[...])
        go_c = dot(dfft[...], hid[...])
        gi = gi_c if gi is None else gi + gi_c
        go = go_c if go is None else go + go_c
    gi_ref[0] = gi
    go_ref[0] = go.T


def expert_weights(parts, tile=512):
    inner = parts[0][2].shape[1]
    width = parts[0][0].shape[0]
    specs, args, rows = [], [], 0
    for xt, dfft, hid, da in parts:
        n = hid.shape[0]
        rows += n
        specs += [pl.BlockSpec((width, n), lambda f: (0, 0), pipeline_mode=pl.Buffered(1))] * 2
        specs += [pl.BlockSpec((n, tile), lambda f: (0, f))] * 2
        args += [xt, dfft, hid, da]
    return pl.pallas_call(
        functools.partial(expert_weights_kernel, len(parts)),
        grid=(inner // tile,),
        in_specs=specs,
        out_specs=[
            pl.BlockSpec((1, width, tile), lambda f: (0, 0, f)),
            pl.BlockSpec((1, tile, width), lambda f: (0, f, 0)),
        ],
        out_shape=[
            jax.ShapeDtypeStruct((1, width, inner), jnp.float32),
            jax.ShapeDtypeStruct((1, inner, width), jnp.float32),
        ],
        compiler_params=params(60),
        cost_estimate=cost(4 * rows * width * inner, 4 * rows * inner + 8 * width * inner),
        name="expert_weights",
    )(*args)


def split_units(units, weights):
    total, sizes, done, so_far = sum(weights), [], 0, 0
    for w in weights:
        so_far += w
        end = (2 * units * so_far + total) // (2 * total)
        sizes.append(end - done)
        done = end
    return sizes


def sum_parts(n, heights):
    bits = n.bit_length() - 1
    upper = list(range(1, bits))
    orders = [[0] + upper[t:] + upper[:t] for t in range(3)]
    parts, first = [], 0
    for ref, rows in enumerate(heights):
        units = rows // (16 * n)
        turns = (0, 1, 2, 0, 1, 2) if units >= 18 else (0, 1, 2) if units >= 6 else (2,)
        at = 0
        for t, size in zip(turns, split_units(units, [(5, 5, 4)[t] for t in turns])):
            parts.append((ref, at * 16 * n, first, size * 16, orders[t]))
            at += size
            first += size * 16 * n
    return bits, parts


def sum_kernel(cores, n, room, heights, extra, code_ref, gate_ref, rank_ref, ff_any, y_any, *refs):
    _, cut, _ = plan(room)
    xs, refs = refs[: len(heights)], refs[len(heights) :]
    mixed_any, sum_any, small_any, out_ref, work_ref, got_ref, ff_ref, y_ref, mixed_ref, *refs = refs
    if extra:
        tail_ref, *refs = refs
    send, recv, local, load, store = refs
    loads = [
        pltpu.make_async_copy(ff_any, ff_ref, local.at[0]),
        pltpu.make_async_copy(y_any, y_ref, local.at[1]),
    ]
    summed = heights[:-1] if extra else heights
    bits, parts = sum_parts(n, summed)
    full = len(parts)
    if extra:
        parts = parts + [(len(summed), 0, sum(summed), heights[-1] // n, list(range(bits)))]
    me = lax.axis_index("grp") * cores + lax.axis_index("exp")
    base = [first for _, _, first, _, _ in parts]
    got_at = list(base)
    kept = []
    for p, (ref, at, first, step, order) in enumerate(parts):
        length = step * (n >> 1)
        start = base[p] + partner_of(me, order[0])[0] * length
        kept.append(
            pltpu.make_async_copy(
                xs[ref].at[rows_at(start - first + at, length)],
                work_ref.at[rows_at(start, length)],
                load.at[p],
            )
        )
        kept[p].start()
    for copy in loads:
        copy.start()
    barrier = pltpu.get_barrier_semaphore()
    for b in range(bits):
        pl.semaphore_signal(barrier, inc=1, **device_place(cores, partner_of(me, b)[1]))
    pl.semaphore_wait(barrier, bits)

    def halving(p, s):
        ref, at, first, step, order = parts[p]
        length = step * (n >> (s + 1))
        bit, partner = partner_of(me, order[s])
        start = base[p] + (1 - bit) * length
        if s == 0:
            source = xs[ref].at[rows_at(start - first + at, length)]
        else:
            source = work_ref.at[rows_at(start, length)]
        return pltpu.make_async_remote_copy(
            src_ref=source, dst_ref=got_ref.at[rows_at(got_at[p], length)],
            send_sem=send.at[p, s], recv_sem=recv.at[p, s], **device_place(cores, partner),
        )

    def doubling(p, s):
        _, _, _, step, order = parts[p]
        here = rows_at(base[p], step * (n >> (s + 1)))
        return pltpu.make_async_remote_copy(
            src_ref=out_ref.at[here], dst_ref=out_ref.at[here],
            send_sem=send.at[p, bits + s], recv_sem=recv.at[p, bits + s],
            **device_place(cores, partner_of(me, order[s])[1]),
        )

    main = sum(summed[:-1])

    def keep_out(p, s, start, length):
        here = rows_at(start, length)
        target = sum_any.at[here]
        if parts[p][0] == len(summed) - 1:
            target = small_any.at[rows_at(start - main, length)]
        copy = pltpu.make_async_copy(out_ref.at[here], target, store.at[p, s])
        copy.start()
        return copy

    tokens, width = mixed_ref.shape
    tile = tokens // 4
    tiles = [slice(i * tile, (i + 1) * tile) for i in range(4)]

    def mix_most():
        for copy in loads:
            copy.wait()
        for here in tiles:
            ff = collect(segment(code_ref[here, :], room, 0, cut), ff_ref[...])
            y_ref[here, :] += gate_ref[here, :] * ff

    def mix_rest():
        stores = []
        for i, here in enumerate(tiles):
            total = y_ref[here, :]
            if extra:
                tail = tail_ref[...]
                tail = [tail[c * extra : (c + 1) * extra] for c in range(width // TILE)]
                more = collect(rank_ref[here, :], jnp.concatenate(tail, axis=1))
                total = total + gate_ref[here, :] * more
            mixed_ref[here, :] = total.astype(LOW)
            stores.append(
                pltpu.make_async_copy(mixed_ref.at[here], mixed_any.at[here], local.at[2 + i])
            )
            stores[i].start()
        return stores

    moving = [halving(p, 0) for p in range(len(parts))]
    for copy in moving:
        copy.start()
    sent, stores = [], []
    for s in range(bits):
        if s == 1:
            mix_most()
        for p, (ref, at, first, step, order) in enumerate(parts):
            length = step * (n >> (s + 1))
            if s == 0:
                kept[p].wait()
            moving[p].wait_recv()
            sent.append(moving[p])
            base[p] = base[p] + partner_of(me, order[s])[0] * length
            last = s + 1 == bits
            target = out_ref if last else work_ref
            if p >= full and last:
                target = tail_ref

            def add(
                i, _, start=base[p], target=target, arrived=got_at[p], step=step,
                to=0 if p >= full and last else base[p],
            ):
                got = got_ref[rows_at(arrived + i * step, step), :].astype(jnp.float32)
                mine = work_ref[rows_at(start + i * step, step), :].astype(jnp.float32)
                target[rows_at(to + i * step, step), :] = (mine + got).astype(LOW)
                return 0

            lax.fori_loop(0, length // step, add, 0)
            got_at[p] += length
            if not last:
                moving[p] = halving(p, s + 1)
                moving[p].start()
            elif p < full:
                moving[p] = doubling(p, s)
                moving[p].start()
                stores.append(keep_out(p, bits, base[p], step))
    for copy in sent:
        copy.wait_send()
    sent = []
    for s in reversed(range(bits)):
        if s == min(1, bits - 1):
            stores += mix_rest()
        for p, (ref, at, first, step, order) in enumerate(parts[:full]):
            length = step * (n >> (s + 1))
            moving[p].wait_recv()
            sent.append(moving[p])
            bit = partner_of(me, order[s])[0]
            arrived = base[p] + (1 - 2 * bit) * length
            base[p] = base[p] - bit * length
            if s > 0:
                moving[p] = doubling(p, s - 1)
                moving[p].start()
            stores.append(keep_out(p, s, arrived, length))
    for copy in sent:
        copy.wait_send()
    for copy in stores:
        copy.wait()


def all_sum(xs, code, gate, rank, ff, y, room, ff_more):
    cores = lax.axis_size("exp")
    n = lax.axis_size(AXES)
    extra = plan(room)[2]
    heights = [a.shape[0] for a in xs]
    if any(h % (16 * n) for h in heights):
        xs = [jnp.concatenate(xs[:-1], axis=0), xs[-1]]
        heights = [a.shape[0] for a in xs]
    total, small = sum(heights), heights[-1]
    bits, parts = sum_parts(n, heights)
    count = len(parts)
    rows = total
    tokens, width = y.shape
    tail = []
    if extra:
        xs = xs + [ff_more]
        heights = heights + [ff_more.shape[0]]
        rows += ff_more.shape[0]
        count += 1
        tail = [pltpu.VMEM((extra * width // TILE, TILE), LOW)]
    buffer = pltpu.VMEM((rows, TILE), LOW)
    vmem = pl.BlockSpec(memory_space=pltpu.VMEM)
    anywhere = pl.BlockSpec(memory_space=pl.ANY)
    return pl.pallas_call(
        functools.partial(sum_kernel, cores, n, room, heights, extra),
        out_shape=[
            jax.ShapeDtypeStruct((tokens, width), LOW),
            jax.ShapeDtypeStruct((total - small, TILE), LOW),
            jax.ShapeDtypeStruct((small, TILE), LOW),
        ],
        in_specs=[vmem] * 3 + [anywhere] * (2 + len(xs)),
        out_specs=[anywhere] * 3,
        scratch_shapes=[
            pltpu.VMEM((total, TILE), LOW), buffer, buffer, pltpu.VMEM(ff.shape, LOW),
            pltpu.VMEM(y.shape, jnp.float32), pltpu.VMEM(y.shape, LOW), *tail,
            pltpu.SemaphoreType.DMA((count, 2 * bits)),
            pltpu.SemaphoreType.DMA((count, 2 * bits)),
            pltpu.SemaphoreType.DMA((6,)),
            pltpu.SemaphoreType.DMA((count,)),
            pltpu.SemaphoreType.DMA((count, bits + 1)),
        ],
        compiler_params=params(60, collective_id=1, has_side_effects=True),
        name="all_sum",
    )(code, gate, rank, ff, y, *xs)


def local(
    tokens, lengths, expert_ids, slots, w_query, w_key, w_value, w_output,
    gain_attn, gain_ffn, bias_table, w_router, w_in, w_out, cotangent,
):
    rows, seq, width = tokens.shape
    count = rows * seq
    buckets, heads = bias_table.shape
    head = width // heads
    experts = w_router.shape[1]
    devices = lax.axis_size(AXES)
    room = max(4, 2 * count // experts)
    me = lax.axis_index(AXES)
    x = tokens.reshape(count, width)
    g = cotangent.reshape(count, width)
    gain_one = gain_attn.reshape(1, width)
    gain_two = gain_ffn.reshape(1, width)
    wide = max(128, experts)
    mine = (jnp.arange(wide, dtype=jnp.int32) == me).astype(jnp.float32).reshape(1, wide)

    segments, cut, extra = plan(room)
    code_c, code_r, rank_c, flag, g_out = route(expert_ids, slots, g, experts, room)
    g_in = exchange(g_out, devices)
    code_r, x, w_query, w_key, w_value, w_output, bias_table, w_router = lax.optimization_barrier(
        (code_r, x, w_query, w_key, w_value, w_output, bias_table, w_router)
    )
    router_w = jnp.pad(w_router, ((0, 0), (0, wide - experts)))

    normed_t, projected = project(x, gain_one, w_query, w_key, w_value)
    near, far = bias_tiles(bias_table)
    joined, weights = attention_forward(lengths, projected, near, far, rows, seq, heads, head)
    y, gate, *h_out = after_attention(
        joined, x, w_output, gain_two, expert_ids.reshape(count, 1), router_w, code_r, experts, room
    )
    h_out, g_in = lax.optimization_barrier((h_out, g_in))
    g_in = g_in.reshape(devices, room, width)
    h_in = [exchange(h_out[0], devices)]
    for h in h_out[1:]:
        h, h_in[-1] = lax.optimization_barrier((h, h_in[-1]))
        h_in.append(exchange(h, devices))
    dx_back, ffs, parts, grad_router = [], [], [], 0.0
    for n, (low, high) in enumerate(segments):
        ff, dx, hid, da, x_t, dff_t, routed = expert_rows(
            h_in[n], g_in, mine, router_w, w_in[0], w_out[0], experts, low, high
        )
        if n + 1 < len(segments):
            dx, h_in[n + 1] = lax.optimization_barrier((dx, h_in[n + 1]))
        if n:
            dx, dx_back[-1] = lax.optimization_barrier((dx, dx_back[-1]))
        dx_back.append(exchange(dx, devices))
        ffs.append(ff.reshape(devices, high - low, width))
        parts.append((x_t, dff_t, hid, da))
        grad_router = grad_router + routed
    grad_in, grad_out = expert_weights(parts)
    grad_router = grad_router[:experts].reshape(experts, width // TILE, TILE)
    grad_router = jnp.swapaxes(grad_router, 0, 1).reshape(-1, TILE)
    small = jnp.concatenate([grad_router, flag], axis=0)
    ff, ff_more = ffs[0], small
    if extra:
        half = segments[0][1]
        ff = jnp.concatenate([ffs[0], ffs[1][:, : cut - half]], axis=1)
        ff_spare = ffs[1][:, cut - half :]
        bits = devices.bit_length() - 1
        ff_more = ff_spare.reshape((2,) * bits + (extra, width // TILE, TILE))
        order = tuple(reversed(range(bits))) + (bits + 1, bits, bits + 2)
        ff_more = jnp.transpose(ff_more, order).reshape(-1, TILE)
    ff = ff.reshape(devices * cut, width)
    dx_back, grad_in, grad_out, ff, ff_more, small = lax.optimization_barrier(
        (dx_back, grad_in, grad_out, ff, ff_more, small)
    )
    ff_back = exchange(ff, devices)

    dy, do, grad_output, grad_gain_two = before_attention(
        dx_back, code_c, y, g, gain_two, w_output, joined, room
    )
    lines = width // TILE
    small_rows = small.shape[0] + -(-2 * lines // 16) * 16 + -(-heads // 16) * 16
    small_rows = -(-small_rows // (16 * devices)) * 16 * devices
    grad_tokens, packed, small = attention_backward(
        projected, do, joined, weights, normed_t, w_query, w_key, w_value, x, dy, gain_one,
        small, grad_gain_two, rows, seq, heads, head, small_rows,
    )
    mixed, summed, small = all_sum(
        [packed.reshape(-1, TILE), grad_output, small], code_c, gate, rank_c, ff_back, y, room, ff_more
    )
    if extra:
        crowded = small[lines * experts, 0] > 0

        def mix_all(_):
            code = code_c.reshape(-1)
            expert = code // room
            place = code - expert * room
            spare = exchange(ff_spare.reshape(-1, width), devices)
            first = jnp.where((code >= 0) & (place < cut), expert * cut + place, devices * cut)
            rest = jnp.where(place >= cut, expert * extra + place - cut, devices * extra)
            take = lambda a, index: jnp.take(a, index, axis=0, mode="fill", fill_value=0)
            ff = take(ff_back, first) + take(spare, rest)
            return False, (y + gate * ff.astype(jnp.float32)).astype(LOW)

        _, mixed = lax.while_loop(lambda held: held[0], mix_all, (crowded, mixed))
    *grads, router_t, gains, table, mixed = unpack(summed, small, mixed, experts, heads, buckets)
    return (
        mixed.reshape(rows, seq, width),
        grad_tokens.reshape(rows, seq, width),
        *grads,
        gains[0], gains[1], table.T, router_t.T,
        grad_in,
        grad_out,
    )


def solution(mesh):
    split = P(AXES)
    in_specs = (split,) * 4 + (P(),) * 8 + (split,) * 3
    out_specs = (split,) * 2 + (P(),) * 8 + (split,) * 2
    return jax.shard_map(local, mesh=mesh, in_specs=in_specs, out_specs=out_specs, check_vma=False)
```

```python
import functools

import jax
import jax.numpy as jnp
from jax import lax
from jax.experimental import pallas as pl
from jax.experimental.pallas import tpu as pltpu
from jax.sharding import PartitionSpec as P

EPSILON = 1e-06
NEGATIVE = -1e30
THRESHOLDS = (12, 16, 23, 32, 46, 64, 91)
LOG2E = 1.4426950408889634
TILE = 128
GELU_A = 0.7978845608028654
GELU_B = GELU_A * 0.044715
AXES = ("grp", "exp")
LOW = jnp.bfloat16


def dot(a, b):
    return jnp.dot(a, b, preferred_element_type=jnp.float32)


def dot_t(a, b):
    return lax.dot_general(a, b, (((1,), (1,)), ((), ())), preferred_element_type=jnp.float32)


def params(mib, **more):
    return pltpu.CompilerParams(vmem_limit_bytes=mib << 20, **more)


def whole(shape):
    return pl.BlockSpec(shape, lambda *_: (0,) * len(shape), pipeline_mode=pl.Buffered(1))


def cost(flops, bytes_accessed, transcendentals=0):
    return pl.CostEstimate(
        flops=flops, bytes_accessed=bytes_accessed, transcendentals=transcendentals
    )


def bucket_of(offset):
    distance = jnp.abs(offset)
    far = jnp.full_like(distance, 8)
    for border in THRESHOLDS:
        far = far + (distance >= border).astype(jnp.int32)
    return jnp.where(distance < 8, distance, far) + jnp.where(offset > 0, 16, 0).astype(jnp.int32)


def device_place(cores, d):
    return dict(device_id=(lax.div(d, cores), lax.rem(d, cores)), device_id_type=pl.DeviceIdType.MESH)


def partner_of(me, b):
    bit = lax.rem(lax.div(me, 1 << b), 2)
    return bit, me + (1 - 2 * bit) * (1 << b)


def rows_at(start, length):
    return pl.ds(pl.multiple_of(start, 16), length)


def plan(room):
    if room % 64:
        return ((0, room),), room, 0
    half = room // 2
    return ((half, half + room // 4), (0, half)), 3 * room // 4, room // 4


def back_plan(room):
    if room % 64:
        return ((0, room),)
    return ((room // 2, room), (0, room // 2))


def segment(code, room, low, high):
    expert = lax.div(code, room)
    place = code - expert * room
    inside = (code >= 0) & (place >= low) & (place < high)
    return jnp.where(inside, expert * (high - low) + place - low, -1)


def spread(dest, values, out):
    rows = out.shape[0]
    step = min(256, rows)
    for start in range(0, rows, step):
        here = lax.broadcasted_iota(jnp.int32, (step, dest.shape[1]), 0) + start
        out[start : start + step] = dot((dest == here).astype(LOW), values).astype(LOW)


def collect(dest, values):
    here = lax.broadcasted_iota(jnp.int32, (dest.shape[0], values.shape[0]), 1)
    return dot((dest == here).astype(LOW), values)


def spread_all(code, room, values, outs):
    for (low, high), out in zip(plan(room)[0], outs):
        spread(segment(code, room, low, high), values, out)


def collect_all(code, room, refs):
    total = None
    for (low, high), ref in zip(back_plan(room), refs):
        part = collect(segment(code, room, low, high), ref[...])
        total = part if total is None else total + part
    return total


def buffers(experts, room, width):
    return [
        jax.ShapeDtypeStruct((experts * (high - low), width), LOW) for low, high in plan(room)[0]
    ]


def route_kernel(
    experts, room, eid_ref, slot_ref, g_ref, code_c, code_r, rank_c, rank_r, marks, out, more
):
    tokens = g_ref.shape[0]
    wide = max(TILE, experts)
    _, cut, extra = plan(room)
    at = lax.broadcasted_iota(jnp.int32, (tokens, tokens), 0)
    to = lax.broadcasted_iota(jnp.int32, (tokens, tokens), 1)

    line = lambda ref: jnp.concatenate([ref[i : i + 1] for i in range(ref.shape[0])], axis=1)
    ids = line(eid_ref)
    slots = line(slot_ref)
    both = jnp.concatenate([ids, slots] + [jnp.zeros((6, tokens), jnp.int32)], axis=0)
    columns = both.astype(jnp.float32).T.astype(jnp.int32)
    picked = ids == lax.broadcasted_iota(jnp.int32, (wide, tokens), 0)
    earlier = dot(picked.astype(LOW), (at < to).astype(LOW))
    place = jnp.sum(jnp.where(picked, earlier, 0.0), axis=0, keepdims=True).astype(jnp.int32)
    kept = slots >= 0
    code = jnp.where(kept, ids * room + place, -1)
    code_r[...] = code
    rank = jnp.where(kept & (place >= cut), place - cut, -1)
    rank_r[...] = rank
    spread(segment(code, room, 0, cut), g_ref[...], out)
    spread(rank, g_ref[...], more)

    ids = columns[:, :1]
    picked = ids == lax.broadcasted_iota(jnp.int32, (tokens, wide), 1)
    earlier = dot((to < at).astype(LOW), picked.astype(LOW))
    place = jnp.sum(jnp.where(picked, earlier, 0.0), axis=1, keepdims=True).astype(jnp.int32)
    kept = columns[:, 1:2] >= 0
    code_c[...] = jnp.where(kept, ids * room + place, -1)
    over = kept & (place >= cut)
    rank_c[...] = jnp.where(over, place - cut, -1)
    named = jnp.max(jnp.where(picked & over, 1.0, 0.0), axis=0, keepdims=True)
    named = jnp.sum(named, axis=1, keepdims=True)
    owner = jnp.max(jnp.where(over, ids + 1, 0).astype(jnp.float32), axis=0, keepdims=True)
    lane = lax.broadcasted_iota(jnp.int32, marks.shape, 1)
    crowded = jnp.where(named > 1.0, 1.0, 0.0)
    marks[...] = jnp.where(lane == 0, owner, jnp.where(lane == 1, crowded, 0.0))


def route(expert_ids, slots, upstream, experts, room):
    tokens, width = upstream.shape
    column = jax.ShapeDtypeStruct((tokens, 1), jnp.int32)
    line = jax.ShapeDtypeStruct((1, tokens), jnp.int32)
    _, cut, extra = plan(room)
    return pl.pallas_call(
        functools.partial(route_kernel, experts, room),
        out_shape=[
            column, line, column, line, jax.ShapeDtypeStruct((8, TILE), jnp.float32),
            jax.ShapeDtypeStruct((experts * cut, width), LOW),
            jax.ShapeDtypeStruct((max(extra, 16), width), LOW),
        ],
        compiler_params=params(60),
        cost_estimate=cost(2 * experts * room * tokens * width, 8 << 20),
        name="route",
    )(expert_ids, slots, upstream)


def exchange(buffer, devices):
    shaped = buffer.reshape(devices, buffer.shape[0] // devices, buffer.shape[1])
    moved = lax.all_to_all(shaped, AXES, split_axis=0, concat_axis=0, tiled=True)
    return moved.reshape(buffer.shape)


def project_kernel(x_ref, gain_ref, wq_ref, wk_ref, wv_ref, normed_ref, out_ref):
    x = x_ref[...].astype(jnp.float32)
    rms = lax.rsqrt(jnp.mean(x * x, axis=-1, keepdims=True) + EPSILON)
    normed = (x * rms * gain_ref[...]).astype(LOW)
    normed_ref[...] = normed.T
    width = x.shape[1]
    for n, w_ref in enumerate((wq_ref, wk_ref, wv_ref)):
        out_ref[:, n * width : (n + 1) * width] = dot(normed, w_ref[...]).astype(LOW)


def project(x, gain, w_query, w_key, w_value):
    tokens, width = x.shape
    out = 3 * width
    step = 256
    rows = lambda w: pl.BlockSpec((step, w), lambda i: (i, 0))
    return pl.pallas_call(
        project_kernel,
        grid=(tokens // step,),
        in_specs=[rows(width), whole((1, width)), *[whole((width, width))] * 3],
        out_specs=[pl.BlockSpec((width, step), lambda i: (0, i)), rows(out)],
        out_shape=[
            jax.ShapeDtypeStruct((width, tokens), LOW),
            jax.ShapeDtypeStruct((tokens, out), LOW),
        ],
        compiler_params=params(40),
        cost_estimate=cost(2 * tokens * width * out, 12 << 20),
        name="project",
    )(x, gain, w_query, w_key, w_value)


def gather_orders(bits):
    far = tuple(range(3, bits))
    return [[(0,), (1,), (2,), far], [(0,), (2,), (1,), far], [(0,), (1,), (2,), far]]


def span(order, s, n):
    for group in order[: s + 1]:
        n >>= len(group)
    return n


def digit_of(d, group):
    if isinstance(d, int):
        return sum(((d >> b) & 1) << i for i, b in enumerate(group))
    return sum(lax.rem(lax.div(d, 1 << b), 2) * (1 << i) for i, b in enumerate(group))


def peer_of(me, group, r):
    for i, b in enumerate(group):
        if (r >> i) & 1:
            me = partner_of(me, b)[1]
    return me


def rank_in(order, d):
    n = 1 << sum(len(group) for group in order)
    return sum(digit_of(d, group) * span(order, s, n) for s, group in enumerate(order))


def after_attention_kernel(
    experts, room, cores, n, o_ref, x_ref, w_ref, gain_ref, eid_ref, wr_ref, code_ref, *rest
):
    segments, _, extra = plan(room)
    if extra:
        rank_ref, g_ref, mark_ref, *rest = rest
    y_ref, gate_ref, *rest = rest
    outs, rest = rest[: len(segments)], rest[len(segments) :]
    if extra:
        h_more, g_more, flag_ref, *rest = rest
        own, moved, marks, send, recv, *rest = rest
    (held,) = rest
    step = o_ref.shape[0]
    i = pl.program_id(0)
    bits = n.bit_length() - 1
    if extra:
        me = lax.axis_index("grp") * cores + lax.axis_index("exp")
        barrier = pltpu.get_barrier_semaphore()
        greeted = [(g, r) for g in gather_orders(bits)[0] for r in range(1, 1 << len(g))]

        @pl.when(i == 0)
        def _():
            for group, r in greeted:
                pl.semaphore_signal(barrier, inc=1, **device_place(cores, peer_of(me, group, r)))

    y = x_ref[...].astype(jnp.float32) + dot(o_ref[...], w_ref[...])
    y_ref[...] = y
    rms = lax.rsqrt(jnp.mean(y * y, axis=-1, keepdims=True) + EPSILON)
    normed = (y * rms * gain_ref[...]).astype(LOW)
    held[pl.ds(pl.multiple_of(i * step, step), step), :] = normed
    router = route_softmax(dot(normed, wr_ref[...]), experts)
    lane = lax.broadcasted_iota(jnp.int32, router.shape, 1)
    expert = lax.div(jnp.maximum(eid_ref[...], 0), room)
    gate_ref[...] = jnp.sum(jnp.where(lane == expert, router, 0.0), axis=-1, keepdims=True)

    @pl.when(i == pl.num_programs(0) - 1)
    def _():
        chunks = []
        for (low, high), out in zip(segments, outs):
            dest = segment(code_ref[...], room, low, high)
            size = min(256, out.shape[0])
            chunks += [(dest, out, start, size) for start in range(0, out.shape[0], size)]

        def spread_some(count):
            for dest, out, start, size in chunks[:count]:
                spread(dest - start, held[...], out.at[start : start + size])
            del chunks[:count]

        if not extra:
            spread_some(len(chunks))
            return
        single, width = g_ref.shape
        block = 2 * single
        orders = gather_orders(bits)
        phases = len(orders[0])
        third = width // 3
        spread(rank_ref[...], held[...], own)
        base = []
        for p, order in enumerate(orders):
            lanes = slice(p * third, (p + 1) * third)
            base.append(rank_in(order, me) * block)
            moved[p, rows_at(base[p], single), :] = own[:, lanes]
            moved[p, rows_at(base[p] + single, single), :] = g_ref[:, lanes]
        tall = mark_ref.shape[0]
        marks[pl.ds(pl.multiple_of(rank_in(orders[0], me) * tall, 8), tall), :] = mark_ref[...]
        pl.semaphore_wait(barrier, len(greeted))

        def doubling(s):
            copies = []
            for p, order in enumerate(orders):
                size = span(order, s, n)
                for r in range(1, 1 << len(order[s])):
                    place = device_place(cores, peer_of(me, order[s], r))
                    here = rows_at(base[p], block * size)
                    copies.append(
                        pltpu.make_async_remote_copy(
                            src_ref=moved.at[p, here], dst_ref=moved.at[p, here],
                            send_sem=send.at[p, s, r - 1], recv_sem=recv.at[p, s, r - 1], **place,
                        )
                    )
                    if p == 0:
                        start = lax.div(base[0], block) * tall
                        here = pl.ds(pl.multiple_of(start, 8), tall * size)
                        copies.append(
                            pltpu.make_async_remote_copy(
                                src_ref=marks.at[here], dst_ref=marks.at[here],
                                send_sem=send.at[3, s, r - 1], recv_sem=recv.at[3, s, r - 1], **place,
                            )
                        )
            for copy in copies:
                copy.start()
            return copies

        sent = []
        for s in reversed(range(phases)):
            copies = doubling(s)
            spread_some(2)
            for copy in copies:
                copy.wait_recv()
            sent += copies
            for p, order in enumerate(orders):
                base[p] = base[p] - digit_of(me, order[s]) * block * span(order, s, n)
        spread_some(len(chunks))
        for copy in sent:
            copy.wait_send()
        for d in range(n):
            here = slice(d * single, (d + 1) * single)
            first = rank_in(orders[0], d) * tall
            keep = marks[first : first + 1, :1] == (me + 1).astype(jnp.float32)
            for p, order in enumerate(orders):
                lanes = slice(p * third, (p + 1) * third)
                at = rank_in(order, d) * block
                for out, start in ((h_more, at), (g_more, at + single)):
                    got = moved[p, start : start + single, :].astype(jnp.float32)
                    out[here, lanes] = jnp.where(keep, got, 0.0).astype(LOW)
        flag_ref[...] = jnp.broadcast_to(
            jnp.max(marks[:, 1:2], axis=0, keepdims=True), flag_ref.shape
        )


def after_attention(
    joined, x, w_output, gain, expert_ids, w_router, code, rank, g_extra, marks, experts, room
):
    tokens, width = x.shape
    step = 256
    cores = lax.axis_size("exp")
    n = lax.axis_size(AXES)
    bits = n.bit_length() - 1
    segments, _, extra = plan(room)
    rows = pl.BlockSpec((step, width), lambda i: (i, 0))
    single = pl.BlockSpec((step, 1), lambda i: (i, 0))
    outs = buffers(experts, room, width)
    more, scratch, options = [], [], {}
    if extra:
        more = [rank, g_extra, marks]
        outs = outs + [jax.ShapeDtypeStruct((n * extra, width), LOW)] * 2
        outs = outs + [jax.ShapeDtypeStruct((8, TILE), jnp.float32)]
        scratch = [
            pltpu.VMEM((extra, width), LOW), pltpu.VMEM((3, 2 * n * extra, width // 3), LOW),
            pltpu.VMEM((8 * n, TILE), jnp.float32),
            pltpu.SemaphoreType.DMA((4, 4, (n >> 3) - 1)), pltpu.SemaphoreType.DMA((4, 4, (n >> 3) - 1)),
        ]
        options = dict(collective_id=2, has_side_effects=True)
    return pl.pallas_call(
        functools.partial(after_attention_kernel, experts, room, cores, n),
        grid=(tokens // step,),
        in_specs=[
            rows, rows, whole((width, width)), whole((1, width)), single, whole(w_router.shape),
            whole((1, tokens)), *[whole(m.shape) for m in more],
        ],
        out_specs=[rows, single] + [pl.BlockSpec(o.shape, lambda i: (0, 0)) for o in outs],
        out_shape=[
            jax.ShapeDtypeStruct((tokens, width), jnp.float32),
            jax.ShapeDtypeStruct((tokens, 1), jnp.float32),
        ]
        + outs,
        scratch_shapes=scratch + [pltpu.VMEM((tokens, width), LOW)],
        compiler_params=params(60, **options),
        cost_estimate=cost(2 * tokens * width * (width + experts * room), 12 << 20),
        name="after_attention",
    )(joined, x, w_output, gain, expert_ids, w_router, code, *more)


def route_softmax(logits, experts):
    lane = lax.broadcasted_iota(jnp.int32, logits.shape, 1)
    logits = jnp.where(lane < experts, logits, NEGATIVE)
    e = jnp.exp(logits - jnp.max(logits, axis=-1, keepdims=True))
    return e / jnp.sum(e, axis=-1, keepdims=True)


def pack(values, first, height, out, at):
    for c in range(values.shape[1] // TILE):
        out[at + c * height : at + (c + 1) * height] = values[
            first : first + height, c * TILE : (c + 1) * TILE
        ].astype(LOW)


def before_attention_kernel(
    room, n_backs, code_ref, y_ref, g_ref, gain_ref, w_ref, o_ref, *rest
):
    backs = rest[:n_backs]
    dy_ref, do_ref, pack_ref, gg_ref, gw_ref = rest[n_backs:]
    i = pl.program_id(0)

    @pl.when(i == 0)
    def _():
        gw_ref[...] = jnp.zeros_like(gw_ref)
        gg_ref[...] = jnp.zeros_like(gg_ref)

    step = y_ref.shape[0] // 2
    blocks = [slice(n * step, (n + 1) * step) for n in range(2)]
    dhs = [collect_all(code_ref[here, :], room, backs) for here in blocks]
    lows = []
    for here, dh in zip(blocks, dhs):
        y = y_ref[here, :]
        rms = lax.rsqrt(jnp.mean(y * y, axis=-1, keepdims=True) + EPSILON)
        gg_ref[...] += jnp.sum(dh * y * rms, axis=0, keepdims=True)
        u = dh * gain_ref[...]
        dy = (
            g_ref[here, :].astype(jnp.float32)
            + rms * u
            - y * (rms * rms * rms) * jnp.mean(u * y, axis=-1, keepdims=True)
        )
        dy_ref[here, :] = dy
        lows.append(dy.astype(LOW))
        do_ref[here, :] = dot_t(lows[-1], w_ref[...]).astype(LOW)
    gw_ref[...] += dot(o_ref[...].T, jnp.concatenate(lows, axis=0))

    @pl.when(i == pl.num_programs(0) - 1)
    def _():
        pack(gw_ref, 0, gw_ref.shape[0], pack_ref, 0)


def before_attention(backs, code, y, g, gain, w_output, joined, room):
    tokens, width = y.shape
    step = 512
    rows = lambda w: pl.BlockSpec((step, w), lambda i: (i, 0))
    return pl.pallas_call(
        functools.partial(before_attention_kernel, room, len(backs)),
        grid=(tokens // step,),
        in_specs=[
            rows(1), rows(width), rows(width), whole((1, width)),
            whole((width, width)), rows(width), *[whole(b.shape) for b in backs],
        ],
        out_specs=[
            rows(width), rows(width),
            pl.BlockSpec((width * width // TILE, TILE), lambda i: (0, 0)),
            pl.BlockSpec((1, width), lambda i: (0, 0)),
        ],
        out_shape=[
            jax.ShapeDtypeStruct((tokens, width), jnp.float32),
            jax.ShapeDtypeStruct((tokens, width), LOW),
            jax.ShapeDtypeStruct((width * width // TILE, TILE), LOW),
            jax.ShapeDtypeStruct((1, width), jnp.float32),
        ],
        scratch_shapes=[pltpu.VMEM((width, width), jnp.float32)],
        compiler_params=params(60),
        cost_estimate=cost(6 * tokens * width * width, 16 << 20),
        name="before_attention",
    )(code, y, g, gain, w_output, joined, *backs)


def unpack_kernel(
    experts, heads, buckets, q_ref, k_ref, v_ref, o_ref, small_ref, mix_ref,
    gq, gk, gv, go, router, gains, table, mixed,
):
    mixed[...] = mix_ref[...]
    for packed_ref, out_ref in ((q_ref, gq), (k_ref, gk), (v_ref, gv), (o_ref, go)):
        for c in range(packed_ref.shape[0]):
            out_ref[:, c * TILE : (c + 1) * TILE] = packed_ref[c].astype(jnp.float32)

    @pl.when(pl.program_id(0) == 0)
    def _():
        lines = router.shape[1] // TILE
        small = small_ref[...].astype(jnp.float32)
        for c in range(lines):
            lanes = slice(c * TILE, (c + 1) * TILE)
            router[:, lanes] = small[c * experts : (c + 1) * experts]
            for n in range(2):
                at = lines * experts + n * lines + c
                gains[n : n + 1, lanes] = small[at : at + 1]
        at = lines * experts + -(-2 * lines // 16) * 16
        table[...] = small[at : at + heads, :buckets]


def unpack(packed, small, mixed, experts, heads, buckets):
    tokens, width = mixed.shape
    blocks = width // TILE
    steps = 4
    source = lambda m: pl.BlockSpec((blocks, width // steps, TILE), lambda i: (m, i, 0))
    rows = lambda count: pl.BlockSpec((count // steps, width), lambda i: (i, 0))
    kept = lambda shape: pl.BlockSpec(shape, lambda i: (0, 0))
    return pl.pallas_call(
        functools.partial(unpack_kernel, experts, heads, buckets),
        grid=(steps,),
        in_specs=[source(m) for m in range(4)] + [whole(small.shape), rows(tokens)],
        out_specs=[rows(width)] * 4
        + [kept((experts, width)), kept((2, width)), kept((heads, buckets)), rows(tokens)],
        out_shape=[jax.ShapeDtypeStruct((width, width), jnp.float32)] * 4
        + [
            jax.ShapeDtypeStruct((experts, width), jnp.float32),
            jax.ShapeDtypeStruct((2, width), jnp.float32),
            jax.ShapeDtypeStruct((heads, buckets), jnp.float32),
            jax.ShapeDtypeStruct((tokens, width), LOW),
        ],
        compiler_params=params(60),
        name="unpack",
    )(*[packed.reshape(4 * blocks, width, TILE)] * 4, small, mixed)


def attention_forward_kernel(len_ref, q_ref, k_ref, v_ref, near_ref, far_ref, o_ref, p_ref, s_ref):
    seq = q_ref.shape[0]
    tiles = seq // TILE
    half = q_ref.shape[1] // 2
    row = pl.program_id(0)
    pair = pl.program_id(1)
    live = len_ref[row]
    lane = lax.broadcasted_iota(jnp.int32, (seq, 2 * half), 1)
    dead = lax.broadcasted_iota(jnp.int32, (seq, 2 * half), 0) >= live
    q = q_ref[...]
    k = k_ref[...]
    v_t = v_ref[...].T
    outs = []
    for h in range(2):
        mine = (lane >= h * half) & (lane < (h + 1) * half)
        flag = lane == (1 - h) * half
        k_h = jnp.where(mine, k, jnp.where(flag & dead, -1e30, 0.0).astype(k.dtype))
        q_h = jnp.where(flag, jnp.ones_like(q), q)
        after = far_ref[2 * pair + h, 0]
        before = far_ref[2 * pair + h, 1]
        tops = []
        for i in range(0, tiles, 2):
            q_i = q_h[i * TILE : (i + 2) * TILE]
            raw = dot_t(k_h, q_i)
            for c in range(2):
                cols = slice((i + c) * TILE, (i + c + 1) * TILE)
                top = None
                for j in range(tiles):
                    x = raw[j * TILE : (j + 1) * TILE, c * TILE : (c + 1) * TILE] * (0.125 * LOG2E)
                    d = j - i - c
                    if -1 <= d <= 1:
                        x = x + near_ref[h, d + 1]
                    else:
                        x = x + (after if d > 0 else before)
                    s_ref[h, j * TILE : (j + 1) * TILE, cols] = x
                    m = jnp.max(x, axis=0, keepdims=True)
                    top = m if top is None else jnp.maximum(top, m)
                tops.append(top)
        for i in range(tiles):
            e = jnp.exp2(s_ref[h, :, i * TILE : (i + 1) * TILE] - tops[i])
            total = jnp.sum(e, axis=0, keepdims=True)
            p_ref[0, h, :, i * TILE : (i + 1) * TILE] = (e * (1.0 / total)).astype(LOW)
        outs.append(lax.dot_general(v_t[h * half:(h + 1) * half], p_ref[0, h], (((1,), (0,)), ((), ())), preferred_element_type=jnp.float32))
    o_ref[...] = jnp.concatenate(outs, axis=0).T.astype(o_ref.dtype)

def attention_forward(lengths, projected, near, far, rows, seq, heads, head):
    width = heads * head
    pairs = heads // 2
    spec = lambda off: pl.BlockSpec((seq, 2 * head), lambda b, p: (b, off + p))
    return pl.pallas_call(
        attention_forward_kernel,
        grid=(rows, pairs),
        in_specs=[
            pl.BlockSpec(memory_space=pltpu.SMEM),
            spec(0), spec(pairs), spec(2 * pairs),
            pl.BlockSpec((2, 3, TILE, TILE), lambda b, p: (p, 0, 0, 0)),
            pl.BlockSpec(memory_space=pltpu.SMEM),
        ],
        out_specs=[
            pl.BlockSpec((seq, 2 * head), lambda b, p: (b, p)),
            pl.BlockSpec((1, 2, seq, seq), lambda b, p: (b, p, 0, 0)),
        ],
        out_shape=[
            jax.ShapeDtypeStruct((rows * seq, width), LOW),
            jax.ShapeDtypeStruct((rows, heads, seq, seq), LOW),
        ],
        scratch_shapes=[pltpu.VMEM((2, seq, seq), jnp.float32)],
        compiler_params=params(40),
        cost_estimate=cost(flops=4 * rows * heads * seq * seq * head * 4, bytes_accessed=rows * heads * seq * seq * 2, transcendentals=rows * heads * seq * seq),
        name="attention_forward",
    )(lengths, projected, projected, projected, near, far)

def attention_backward_kernel(
    rows, q_ref, k_ref, v_ref, do_ref, o_ref, p_ref, nt_ref, wq_ref, wk_ref, wv_ref, x_ref, dy_ref, gain_ref,
    gr_ref, gg2_ref, out_ref, pack_ref, small_ref,
    near_ref, far_ref, d_ref, lines_ref, dh_ref,
):
    seq = q_ref.shape[0] // rows
    tiles = seq // TILE
    half = q_ref.shape[1] // 2
    width = x_ref.shape[1]
    pair = pl.program_id(0)
    last_pair = pair == pl.num_programs(0) - 1
    lane = lax.broadcasted_iota(jnp.int32, (seq, 2 * half), 1)
    weights = jnp.concatenate([wq_ref[...], wk_ref[...], wv_ref[...]], axis=1)
    near_ref[...] = jnp.zeros_like(near_ref)
    for row in range(rows):
        here = slice(row * seq, (row + 1) * seq)
        v = v_ref[here, :]
        do = do_ref[here, :]
        weighed = (do.astype(jnp.float32) * o_ref[here, :].astype(jnp.float32)).T
        for h in range(2):
            mine = (lane >= h * half) & (lane < (h + 1) * half)
            v_h = jnp.where(mine, v, jnp.zeros_like(v))
            delta = jnp.sum(weighed[h * half : (h + 1) * half], axis=0, keepdims=True)
            far_sum = [jnp.zeros((8, TILE), jnp.float32), jnp.zeros((8, TILE), jnp.float32)]
            for i in range(0, tiles, 2):
                dp = dot_t(v_h, do[i * TILE : (i + 2) * TILE])
                for c in range(2):
                    cols = slice((i + c) * TILE, (i + c + 1) * TILE)
                    for j in range(tiles):
                        rws = slice(j * TILE, (j + 1) * TILE)
                        part = dp[rws, c * TILE : (c + 1) * TILE] - delta[:, cols]
                        ds = p_ref[row, h, rws, cols].astype(jnp.float32) * part
                        d = j - i - c
                        if -1 <= d <= 1:
                            near_ref[row, h, d + 1] += ds
                        else:
                            which = 0 if d > 0 else 1
                            far_sum[which] = far_sum[which] + jnp.sum(
                                ds.reshape(TILE // 8, 8, TILE), axis=0
                            )
                        d_ref[row, h, rws, cols] = ds.astype(LOW)
            for which in range(2):
                far_ref[row, h, which] = far_sum[which]
    grads_all = []
    for row in range(rows):
        here = slice(row * seq, (row + 1) * seq)
        q = q_ref[here, :]
        do = do_ref[here, :]
        k_t = k_ref[here, :].T
        dq_parts = []
        dk_all = None
        dv_all = None
        for h in range(2):
            mine = (lane >= h * half) & (lane < (h + 1) * half)
            ds_all = d_ref[row, h]
            dq_parts.append(dot(k_t[h * half : (h + 1) * half], ds_all))
            dk_h = dot(ds_all, q)
            dv_h = dot(p_ref[row, h], do)
            dk_all = dk_h if h == 0 else jnp.where(mine, dk_h, dk_all)
            dv_all = dv_h if h == 0 else jnp.where(mine, dv_h, dv_all)
        dq = (jnp.concatenate(dq_parts, axis=0).T * 0.125).astype(LOW)
        grads_all.append(
            jnp.concatenate([dq, (dk_all * 0.125).astype(LOW), dv_all.astype(LOW)], axis=1)
        )
    grads = jnp.concatenate(grads_all, axis=0)
    acc = dot(nt_ref[...], grads)
    for n in range(3):
        pack_ref[n, 0] = acc[:, n * TILE : (n + 1) * TILE].astype(LOW)
    dh = dot_t(grads, weights)

    @pl.when(pair == 0)
    def _():
        dh_ref[...] = dh

    @pl.when(pair > 0)
    def _():
        dh_ref[...] += dh

    near_ref[0] = sum(near_ref[row] for row in range(rows))
    far_ref[0] = sum(far_ref[row] for row in range(rows))
    bucket_sums(near_ref.at[0], far_ref.at[0], lines_ref, 2 * pair)

    @pl.when(last_pair)
    def _():
        total = dh_ref[...]
        x = x_ref[...].astype(jnp.float32)
        rms = lax.rsqrt(jnp.mean(x * x, axis=-1, keepdims=True) + EPSILON)
        gg = jnp.sum(total * x * rms, axis=0, keepdims=True)
        u = total * gain_ref[...]
        out_ref[...] = (
            dy_ref[...]
            + rms * u
            - x * (rms * rms * rms) * jnp.mean(u * x, axis=-1, keepdims=True)
        )
        at = gr_ref.shape[0]
        small_ref[:at] = gr_ref[...].astype(LOW)
        lines = width // TILE
        gains = [gg[:, c * TILE : (c + 1) * TILE] for c in range(lines)]
        gains += [gg2_ref[:, c * TILE : (c + 1) * TILE] for c in range(lines)]
        if 2 * lines % 16:
            gains += [jnp.zeros((16 - 2 * lines % 16, TILE), jnp.float32)]
        gains = jnp.concatenate(gains, axis=0)
        small_ref[at : at + gains.shape[0]] = gains.astype(LOW)
        at = at + gains.shape[0]
        table = bucket_table(lines_ref)
        if table.shape[0] % 16:
            table = jnp.concatenate([table, jnp.zeros((16 - table.shape[0] % 16, TILE), jnp.float32)], axis=0)
        small_ref[at : at + table.shape[0]] = table.astype(LOW)
        at = at + table.shape[0]
        small_ref[at:] = jnp.zeros((small_ref.shape[0] - at, TILE), LOW)


def bucket_sums(near_ref, far_ref, lines_ref, first):
    empty = jnp.zeros((8, TILE), jnp.float32)
    sub = lax.broadcasted_iota(jnp.int32, (8, 2 * TILE), 0)
    for h in range(2):
        lines = []
        for d in range(3):
            turned = None
            for a in range(0, TILE, 8):
                part = jnp.concatenate([near_ref[h, d, a : a + 8], empty], axis=1)
                part = pltpu.roll(part, (2 * TILE - a) % (2 * TILE), 1) if a else part
                turned = part if turned is None else turned + part
            for b in (1, 2, 4):
                turned = jnp.where((sub & b) > 0, pltpu.roll(turned, 2 * TILE - b, 1), turned)
            lines.append(jnp.sum(turned, axis=0, keepdims=True))
        for side in range(2):
            total = jnp.sum(far_ref[h, side], axis=0, keepdims=True)
            lines.append(jnp.concatenate([total, jnp.zeros((1, TILE), jnp.float32)], axis=1))
        lines.append(jnp.zeros((3, 2 * TILE), jnp.float32))
        lines_ref[first + h] = jnp.concatenate(lines, axis=0)


def bucket_table(lines_ref):
    heads = lines_ref.shape[0]
    buckets = 4 * 8
    lane = lax.broadcasted_iota(jnp.int32, (2 * TILE, TILE), 0)
    bucket = lax.broadcasted_iota(jnp.int32, (2 * TILE, TILE), 1)
    turn = jnp.where(lane >= TILE, lane - 2 * TILE, lane)
    total = None
    for r in range(5):
        if r < 3:
            hit = bucket_of((r - 1) * TILE - turn) == bucket
        else:
            hit = bucket == (buckets - 1 if r == 3 else buckets // 2 - 1)
        hit = hit.astype(LOW)
        line = jnp.concatenate([lines_ref[h, r : r + 1, :] for h in range(heads)], axis=0)
        high = line.astype(LOW)
        part = dot(high, hit) + dot((line - high.astype(jnp.float32)).astype(LOW), hit)
        total = part if total is None else total + part
    return total


def attention_backward(
    projected, do, joined, weights, normed_t, w_query, w_key, w_value, x, dy, gain, gr, gg2,
    rows, seq, heads, head, small_rows,
):
    width = heads * head
    pairs = heads // 2
    tokens = rows * seq
    spec = lambda off: pl.BlockSpec((tokens, 2 * head), lambda p: (0, off + p))
    column = pl.BlockSpec((width, 2 * head), lambda p: (0, p))
    return pl.pallas_call(
        functools.partial(attention_backward_kernel, rows),
        grid=(pairs,),
        in_specs=[
            spec(0), spec(pairs), spec(2 * pairs), spec(0), spec(0),
            pl.BlockSpec((rows, 2, seq, seq), lambda p: (0, p, 0, 0)),
            whole((width, tokens)),
            column, column, column, whole((tokens, width)), whole((tokens, width)),
            whole((1, width)), whole(gr.shape), whole(gg2.shape),
        ],
        out_specs=[
            pl.BlockSpec((tokens, width), lambda p: (0, 0)),
            pl.BlockSpec((3, 1, width, TILE), lambda p: (0, p, 0, 0)),
            pl.BlockSpec((small_rows, TILE), lambda p: (0, 0)),
        ],
        out_shape=[
            jax.ShapeDtypeStruct((tokens, width), jnp.float32),
            jax.ShapeDtypeStruct((3, pairs, width, TILE), LOW),
            jax.ShapeDtypeStruct((small_rows, TILE), LOW),
        ],
        scratch_shapes=[
            pltpu.VMEM((rows, 2, 3, TILE, TILE), jnp.float32),
            pltpu.VMEM((rows, 2, 2, 8, TILE), jnp.float32),
            pltpu.VMEM((rows, 2, seq, seq), LOW),
            pltpu.VMEM((heads, 8, 2 * TILE), jnp.float32),
            pltpu.VMEM((tokens, width), jnp.float32),
        ],
        compiler_params=params(60),
        cost_estimate=cost(8 * rows * heads * seq * seq * head * 4, rows * heads * seq * seq * 2),
        name="attention_backward",
    )(
        projected, projected, projected, do, joined, weights, normed_t, w_query, w_key, w_value,
        x, dy, gain, gr, gg2,
    )


def bias_tiles(table):
    j = lax.broadcasted_iota(jnp.int32, (3, TILE, TILE), 1)
    i = lax.broadcasted_iota(jnp.int32, (3, TILE, TILE), 2)
    d = lax.broadcasted_iota(jnp.int32, (3, TILE, TILE), 0) - 1
    b = bucket_of(d * TILE + j - i)
    scaled = table.T * LOG2E
    hot = (b.reshape(1, -1) == jnp.arange(table.shape[0], dtype=jnp.int32)[:, None]).astype(jnp.float32)
    near = jnp.dot(scaled, hot, precision=lax.Precision.HIGHEST).reshape(-1, 3, TILE, TILE)
    far = jnp.stack([scaled[:, -1], scaled[:, table.shape[0] // 2 - 1]], axis=1)
    return near, far


def expert_kernel(experts, chunk, held, x_ref, g_ref, mine_ref, wr_ref, wi_any, wo_any, *refs):
    ff_ref, dx_ref, hid_ref, da_ref, xt_ref, dfft_ref, gr_ref, wi_ref, wo_ref, sem = refs[held:]
    inner = wi_ref.shape[1]
    first_step = pl.program_id(0) == 0

    def loads(f):
        cols = pl.ds(f, chunk)
        return (pltpu.make_async_copy(wi_any.at[:, cols], wi_ref.at[:, cols], sem.at[0, f // chunk]),
                pltpu.make_async_copy(wo_any.at[cols, :], wo_ref.at[cols, :], sem.at[1, f // chunk]))

    @pl.when(first_step)
    def _():
        for f in range(0, inner, chunk):
            for c in loads(f):
                c.start()
        gr_ref[...] = jnp.zeros_like(gr_ref)

    x = x_ref[...]
    g = g_ref[...].reshape(x.shape).astype(jnp.float32)
    mine = mine_ref[...]
    lane = lax.broadcasted_iota(jnp.int32, (1, wr_ref.shape[1]), 1)
    logits = jnp.dot(x, wr_ref[...], preferred_element_type=jnp.float32)
    logits = jnp.where(lane < experts, logits, -1e30)
    e = jnp.exp(logits - jnp.max(logits, axis=-1, keepdims=True))
    router = e / jnp.sum(e, axis=-1, keepdims=True)
    gate = jnp.sum(router * mine, axis=-1, keepdims=True)
    dff = (g * gate).astype(LOW)
    ff = None
    dx = None
    def first(f):
        @pl.when(first_step)
        def _():
            for c in loads(f):
                c.wait()
        cols = slice(f, f + chunk)
        return (jnp.dot(x, wi_ref[:, cols], preferred_element_type=jnp.float32),
                lax.dot_general(dff, wo_ref[cols, :], (((1,), (1,)), ((), ())), preferred_element_type=jnp.float32))
    for f in range(0, inner, chunk):
        cols = slice(f, f + chunk)
        a, dhid = first(f)
        u = a * a
        t = jnp.tanh(a * (GELU_A + GELU_B * u))
        h = 0.5 + 0.5 * t
        hid = a * h
        slope = h + hid * ((1.0 - t) * (GELU_A + (3.0 * GELU_B) * u))
        da = (dhid * slope).astype(LOW)
        hid = hid.astype(LOW)
        hid_ref[:, cols] = hid
        da_ref[:, cols] = da
        ff_part = jnp.dot(hid, wo_ref[cols, :], preferred_element_type=jnp.float32)
        dx_part = lax.dot_general(da, wi_ref[:, cols], (((1,), (1,)), ((), ())), preferred_element_type=jnp.float32)
        ff = ff_part if ff is None else ff + ff_part
        dx = dx_part if dx is None else dx + dx_part
    ff = ff.astype(LOW)
    ff_ref[...] = ff
    dgate = jnp.sum(g * ff.astype(jnp.float32), axis=-1, keepdims=True)
    dlogits = ((gate * dgate) * (mine - router)).astype(LOW)
    dx = dx + lax.dot_general(dlogits, wr_ref[...], (((1,), (1,)), ((), ())), preferred_element_type=jnp.float32)
    dx_ref[...] = dx.astype(LOW).reshape(dx_ref.shape)
    x_t = x.T
    xt_ref[...] = x_t
    dfft_ref[...] = dff.T
    gr_ref[...] += dot(dlogits.T, x)

def expert_rows(x, g, mine, wr, wi, wo, experts, low, high, at=0, total=0, dx=None, tile=256, chunk=768):
    n, width = x.shape
    inner = wi.shape[1]
    sources, room = g.shape[0], high - low
    total = total or room
    group = max(1, min(sources, tile // room))
    while sources % group or (group * room) % TILE:
        group += 1
    tile = group * room
    once = lambda s: pl.BlockSpec(s, lambda i: (0,) * len(s), pipeline_mode=pl.Buffered(1))
    rowspec = lambda w: pl.BlockSpec((tile, w), lambda i: (i, 0))
    column = pl.BlockSpec((width, tile), lambda i: (0, i))
    anywhere = pl.BlockSpec(memory_space=pl.ANY)
    held = [] if dx is None else [dx]
    return pl.pallas_call(
        functools.partial(expert_kernel, experts, chunk, len(held)),
        grid=(n // tile,),
        in_specs=[
            rowspec(width), pl.BlockSpec((group, room, width), lambda i: (i, low // room, 0)),
            once(mine.shape), once(wr.shape), anywhere, anywhere, *[anywhere] * len(held),
        ],
        out_specs=[
            rowspec(width), pl.BlockSpec((group, room, width), lambda i: (i, at // room, 0)),
            rowspec(inner), rowspec(inner), column, column,
            pl.BlockSpec((wr.shape[1], width), lambda i: (0, 0)),
        ],
        out_shape=[
            jax.ShapeDtypeStruct((n, width), LOW),
            jax.ShapeDtypeStruct((sources, total, width), LOW),
            *[jax.ShapeDtypeStruct((n, inner), LOW)] * 2,
            *[jax.ShapeDtypeStruct((width, n), LOW)] * 2,
            jax.ShapeDtypeStruct((wr.shape[1], width), jnp.float32),
        ],
        scratch_shapes=[
            pltpu.VMEM(wi.shape, LOW), pltpu.VMEM(wo.shape, LOW),
            pltpu.SemaphoreType.DMA((2, inner // chunk)),
        ],
        input_output_aliases={6: 1} if held else {},
        compiler_params=params(60),
        cost_estimate=cost(8 * n * width * inner, 4 * n * inner + 8 * width * inner, n * inner),
        name="expert_rows",
    )(x, g, mine, wr, wi, wo, *held)


def expert_weights_kernel(parts, *refs):
    ins, (gi_ref, go_ref) = refs[: 4 * parts], refs[4 * parts :]
    gi = None
    go = None
    for c in range(parts):
        xt, dfft, hid, da = ins[4 * c : 4 * c + 4]
        gi_c = dot(xt[...], da[...])
        go_c = dot(dfft[...], hid[...])
        gi = gi_c if gi is None else gi + gi_c
        go = go_c if go is None else go + go_c
    gi_ref[0] = gi
    go_ref[0] = go.T


def expert_weights(parts, tile=512):
    inner = parts[0][2].shape[1]
    width = parts[0][0].shape[0]
    specs, args, rows = [], [], 0
    for xt, dfft, hid, da in parts:
        n = hid.shape[0]
        rows += n
        specs += [pl.BlockSpec((width, n), lambda f: (0, 0), pipeline_mode=pl.Buffered(1))] * 2
        specs += [pl.BlockSpec((n, tile), lambda f: (0, f))] * 2
        args += [xt, dfft, hid, da]
    return pl.pallas_call(
        functools.partial(expert_weights_kernel, len(parts)),
        grid=(inner // tile,),
        in_specs=specs,
        out_specs=[
            pl.BlockSpec((1, width, tile), lambda f: (0, 0, f)),
            pl.BlockSpec((1, tile, width), lambda f: (0, f, 0)),
        ],
        out_shape=[
            jax.ShapeDtypeStruct((1, width, inner), jnp.float32),
            jax.ShapeDtypeStruct((1, inner, width), jnp.float32),
        ],
        compiler_params=params(60),
        cost_estimate=cost(4 * rows * width * inner, 4 * rows * inner + 8 * width * inner),
        name="expert_weights",
    )(*args)


def split_units(units, weights):
    total, sizes, done, so_far = sum(weights), [], 0, 0
    for w in weights:
        so_far += w
        end = (2 * units * so_far + total) // (2 * total)
        sizes.append(end - done)
        done = end
    return sizes


def sum_parts(n, heights):
    bits = n.bit_length() - 1
    upper = list(range(1, bits))
    orders = [[0] + upper[t:] + upper[:t] for t in range(3)]
    parts, first = [], 0
    for ref, rows in enumerate(heights):
        units = rows // (16 * n)
        turns = (0, 1, 2, 0, 1, 2) if units >= 18 else (0, 1, 2) if units >= 6 else (2,)
        at = 0
        for t, size in zip(turns, split_units(units, [(5, 5, 4)[t] for t in turns])):
            parts.append((ref, at * 16 * n, first, size * 16, orders[t]))
            at += size
            first += size * 16 * n
    return bits, parts


def sum_kernel(cores, n, room, heights, extra, code_ref, gate_ref, rank_ref, ff_any, y_any, *refs):
    _, cut, _ = plan(room)
    xs, refs = refs[: len(heights)], refs[len(heights) :]
    mixed_any, sum_any, small_any, out_ref, work_ref, got_ref, ff_ref, y_ref, mixed_ref, *refs = refs
    if extra:
        tail_ref, *refs = refs
    send, recv, local, load, store = refs
    loads = [
        pltpu.make_async_copy(ff_any, ff_ref, local.at[0]),
        pltpu.make_async_copy(y_any, y_ref, local.at[1]),
    ]
    summed = heights[:-1] if extra else heights
    bits, parts = sum_parts(n, summed)
    full = len(parts)
    if extra:
        parts = parts + [(len(summed), 0, sum(summed), heights[-1] // n, list(range(bits)))]
    me = lax.axis_index("grp") * cores + lax.axis_index("exp")
    base = [first for _, _, first, _, _ in parts]
    got_at = list(base)
    kept = []
    for p, (ref, at, first, step, order) in enumerate(parts):
        length = step * (n >> 1)
        start = base[p] + partner_of(me, order[0])[0] * length
        kept.append(
            pltpu.make_async_copy(
                xs[ref].at[rows_at(start - first + at, length)],
                work_ref.at[rows_at(start, length)],
                load.at[p],
            )
        )
        kept[p].start()
    for copy in loads:
        copy.start()
    barrier = pltpu.get_barrier_semaphore()
    for b in range(bits):
        pl.semaphore_signal(barrier, inc=1, **device_place(cores, partner_of(me, b)[1]))
    pl.semaphore_wait(barrier, bits)

    def halving(p, s):
        ref, at, first, step, order = parts[p]
        length = step * (n >> (s + 1))
        bit, partner = partner_of(me, order[s])
        start = base[p] + (1 - bit) * length
        if s == 0:
            source = xs[ref].at[rows_at(start - first + at, length)]
        else:
            source = work_ref.at[rows_at(start, length)]
        return pltpu.make_async_remote_copy(
            src_ref=source, dst_ref=got_ref.at[rows_at(got_at[p], length)],
            send_sem=send.at[p, s], recv_sem=recv.at[p, s], **device_place(cores, partner),
        )

    def doubling(p, s):
        _, _, _, step, order = parts[p]
        here = rows_at(base[p], step * (n >> (s + 1)))
        return pltpu.make_async_remote_copy(
            src_ref=out_ref.at[here], dst_ref=out_ref.at[here],
            send_sem=send.at[p, bits + s], recv_sem=recv.at[p, bits + s],
            **device_place(cores, partner_of(me, order[s])[1]),
        )

    main = sum(summed[:-1])

    def keep_out(p, s, start, length):
        here = rows_at(start, length)
        target = sum_any.at[here]
        if parts[p][0] == len(summed) - 1:
            target = small_any.at[rows_at(start - main, length)]
        copy = pltpu.make_async_copy(out_ref.at[here], target, store.at[p, s])
        copy.start()
        return copy

    tokens, width = mixed_ref.shape
    tile = tokens // 4
    tiles = [slice(i * tile, (i + 1) * tile) for i in range(4)]

    def mix_most():
        for copy in loads:
            copy.wait()
        for here in tiles:
            ff = collect(segment(code_ref[here, :], room, 0, cut), ff_ref[...])
            y_ref[here, :] += gate_ref[here, :] * ff

    def mix_rest():
        stores = []
        for i, here in enumerate(tiles):
            total = y_ref[here, :]
            if extra:
                tail = tail_ref[...]
                tail = [tail[c * extra : (c + 1) * extra] for c in range(width // TILE)]
                more = collect(rank_ref[here, :], jnp.concatenate(tail, axis=1))
                total = total + gate_ref[here, :] * more
            mixed_ref[here, :] = total.astype(LOW)
            stores.append(
                pltpu.make_async_copy(mixed_ref.at[here], mixed_any.at[here], local.at[2 + i])
            )
            stores[i].start()
        return stores

    moving = [halving(p, 0) for p in range(len(parts))]
    for copy in moving:
        copy.start()
    sent, stores = [], []
    for s in range(bits):
        if s == 1:
            mix_most()
        for p, (ref, at, first, step, order) in enumerate(parts):
            length = step * (n >> (s + 1))
            if s == 0:
                kept[p].wait()
            moving[p].wait_recv()
            sent.append(moving[p])
            base[p] = base[p] + partner_of(me, order[s])[0] * length
            last = s + 1 == bits
            target = out_ref if last else work_ref
            if p >= full and last:
                target = tail_ref

            def add(
                i, _, start=base[p], target=target, arrived=got_at[p], step=step,
                to=0 if p >= full and last else base[p],
            ):
                got = got_ref[rows_at(arrived + i * step, step), :].astype(jnp.float32)
                mine = work_ref[rows_at(start + i * step, step), :].astype(jnp.float32)
                target[rows_at(to + i * step, step), :] = (mine + got).astype(LOW)
                return 0

            lax.fori_loop(0, length // step, add, 0)
            got_at[p] += length
            if not last:
                moving[p] = halving(p, s + 1)
                moving[p].start()
            elif p < full:
                moving[p] = doubling(p, s)
                moving[p].start()
                stores.append(keep_out(p, bits, base[p], step))
    for copy in sent:
        copy.wait_send()
    sent = []
    for s in reversed(range(bits)):
        if s == min(1, bits - 1):
            stores += mix_rest()
        for p, (ref, at, first, step, order) in enumerate(parts[:full]):
            length = step * (n >> (s + 1))
            moving[p].wait_recv()
            sent.append(moving[p])
            bit = partner_of(me, order[s])[0]
            arrived = base[p] + (1 - 2 * bit) * length
            base[p] = base[p] - bit * length
            if s > 0:
                moving[p] = doubling(p, s - 1)
                moving[p].start()
            stores.append(keep_out(p, s, arrived, length))
    for copy in sent:
        copy.wait_send()
    for copy in stores:
        copy.wait()


def all_sum(xs, code, gate, rank, ff, y, room, ff_more):
    cores = lax.axis_size("exp")
    n = lax.axis_size(AXES)
    extra = plan(room)[2]
    heights = [a.shape[0] for a in xs]
    if any(h % (16 * n) for h in heights):
        xs = [jnp.concatenate(xs[:-1], axis=0), xs[-1]]
        heights = [a.shape[0] for a in xs]
    total, small = sum(heights), heights[-1]
    bits, parts = sum_parts(n, heights)
    count = len(parts)
    rows = total
    tokens, width = y.shape
    tail = []
    if extra:
        xs = xs + [ff_more]
        heights = heights + [ff_more.shape[0]]
        rows += ff_more.shape[0]
        count += 1
        tail = [pltpu.VMEM((extra * width // TILE, TILE), LOW)]
    buffer = pltpu.VMEM((rows, TILE), LOW)
    vmem = pl.BlockSpec(memory_space=pltpu.VMEM)
    anywhere = pl.BlockSpec(memory_space=pl.ANY)
    return pl.pallas_call(
        functools.partial(sum_kernel, cores, n, room, heights, extra),
        out_shape=[
            jax.ShapeDtypeStruct((tokens, width), LOW),
            jax.ShapeDtypeStruct((total - small, TILE), LOW),
            jax.ShapeDtypeStruct((small, TILE), LOW),
        ],
        in_specs=[vmem] * 3 + [anywhere] * (2 + len(xs)),
        out_specs=[anywhere] * 3,
        scratch_shapes=[
            pltpu.VMEM((total, TILE), LOW), buffer, buffer, pltpu.VMEM(ff.shape, LOW),
            pltpu.VMEM(y.shape, jnp.float32), pltpu.VMEM(y.shape, LOW), *tail,
            pltpu.SemaphoreType.DMA((count, 2 * bits)),
            pltpu.SemaphoreType.DMA((count, 2 * bits)),
            pltpu.SemaphoreType.DMA((6,)),
            pltpu.SemaphoreType.DMA((count,)),
            pltpu.SemaphoreType.DMA((count, bits + 1)),
        ],
        compiler_params=params(60, collective_id=1, has_side_effects=True),
        name="all_sum",
    )(code, gate, rank, ff, y, *xs)


def local(
    tokens, lengths, expert_ids, slots, w_query, w_key, w_value, w_output,
    gain_attn, gain_ffn, bias_table, w_router, w_in, w_out, cotangent,
):
    rows, seq, width = tokens.shape
    count = rows * seq
    buckets, heads = bias_table.shape
    head = width // heads
    experts = w_router.shape[1]
    devices = lax.axis_size(AXES)
    room = max(4, 2 * count // experts)
    me = lax.axis_index(AXES)
    x = tokens.reshape(count, width)
    g = cotangent.reshape(count, width)
    gain_one = gain_attn.reshape(1, width)
    gain_two = gain_ffn.reshape(1, width)
    mine = (jnp.arange(experts, dtype=jnp.int32) == me).astype(jnp.float32).reshape(1, experts)

    segments, cut, extra = plan(room)
    code_c, code_r, rank_c, rank_r, marks, g_out, g_extra = route(expert_ids, slots, g, experts, room)
    g_in = exchange(g_out, devices)
    code_r, gain_one, bias_table = lax.optimization_barrier((code_r, gain_one, bias_table))

    normed_t, projected = project(x, gain_one, w_query, w_key, w_value)
    near, far = bias_tiles(bias_table)
    joined, weights = attention_forward(lengths, projected, near, far, rows, seq, heads, head)
    y, gate, *h_out = after_attention(
        joined, x, w_output, gain_two, code_c, w_router, code_r, rank_r,
        g_extra, marks, experts, room,
    )
    code = code_c.reshape(-1)
    expert = code // room
    place = code - expert * room
    rest = jnp.where((code >= 0) & (place >= cut), expert * extra + place - cut, experts * extra)

    def experts_on(h, g_rows, low, high, *more):
        return expert_rows(h, g_rows, mine, w_router, w_in[0], w_out[0], experts, low, high, *more)

    parts, grad_router, ff_more, crowded = [], 0.0, None, None
    if extra:
        h_more, g_more, flag = h_out[-3:]
        h_out = h_out[:-3]
        crowded = flag[0, 0] > 0
    h_out, g_in = lax.optimization_barrier((h_out, g_in))
    g_in = g_in.reshape(devices, cut, width)
    h_in = [exchange(h_out[0], devices)]
    if extra:

        def exchange_rest(_):
            rms = lax.rsqrt(jnp.mean(y * y, axis=-1, keepdims=True) + EPSILON)
            h = (y * rms * gain_two).astype(LOW)
            empty = jnp.zeros((experts * extra, width), LOW)
            send = lambda a: exchange(empty.at[rest].set(a, mode="drop"), devices)
            return False, send(h), send(g)

        h_in[0], h_more, g_more = lax.optimization_barrier((h_in[0], h_more, g_more))
        _, h_more, g_more = lax.while_loop(
            lambda held: held[0], exchange_rest, (crowded, h_more, g_more)
        )
        h_out[1], h_more, g_more = lax.optimization_barrier((h_out[1], h_more, g_more))
    for h in h_out[1:]:
        h, h_in[-1] = lax.optimization_barrier((h, h_in[-1]))
        h_in.append(exchange(h, devices))
    ffs, dx_back, dx = [], [], None
    if extra:
        ff_more, dx, hid, da, x_t, dff_t, routed = experts_on(
            h_more, g_more.reshape(devices, extra, width), 0, extra, room - cut, 2 * extra
        )
        ff_more = ff_more.reshape(devices, extra, width)
        parts.append((x_t, dff_t, hid, da))
        grad_router = grad_router + routed
    for m, (low, high) in enumerate(segments):
        held = (0, 2 * extra, dx) if extra and not m else ()
        ff, dx, hid, da, x_t, dff_t, routed = experts_on(h_in[m], g_in, low, high, *held)
        if m + 1 < len(segments):
            dx, h_in[m + 1] = lax.optimization_barrier((dx, h_in[m + 1]))
        if m:
            dx, dx_back[-1] = lax.optimization_barrier((dx, dx_back[-1]))
        dx_back.append(exchange(dx.reshape(-1, width), devices))
        ffs.append(ff.reshape(devices, high - low, width))
        parts.append((x_t, dff_t, hid, da))
        grad_router = grad_router + routed
    grad_in, grad_out = expert_weights(parts)
    grad_router = grad_router.reshape(experts, width // TILE, TILE)
    small = jnp.swapaxes(grad_router, 0, 1).reshape(-1, TILE)
    ff, ff_packed = ffs[0], small
    if extra:
        ff = jnp.concatenate([ffs[1], ffs[0]], axis=1)
        bits = devices.bit_length() - 1
        ff_packed = ff_more.reshape((2,) * bits + (extra, width // TILE, TILE))
        order = tuple(reversed(range(bits))) + (bits + 1, bits, bits + 2)
        ff_packed = jnp.transpose(ff_packed, order).reshape(-1, TILE)
    ff = ff.reshape(devices * cut, width)
    dx_back, grad_in, grad_out, ff, ff_packed, small = lax.optimization_barrier(
        (dx_back, grad_in, grad_out, ff, ff_packed, small)
    )
    ff_back = exchange(ff, devices)

    dy, do, grad_output, grad_gain_two = before_attention(
        dx_back, code_c, y, g, gain_two, w_output, joined, room
    )
    lines = width // TILE
    small_rows = small.shape[0] + -(-2 * lines // 16) * 16 + -(-heads // 16) * 16
    small_rows = -(-small_rows // (16 * devices)) * 16 * devices
    grad_tokens, packed, small = attention_backward(
        projected, do, joined, weights, normed_t, w_query, w_key, w_value, x, dy, gain_one,
        small, grad_gain_two, rows, seq, heads, head, small_rows,
    )
    mixed, summed, small = all_sum(
        [packed.reshape(-1, TILE), grad_output, small], code_c, gate, rank_c, ff_back, y, room, ff_packed
    )
    if extra:

        def mix_all(_):
            spare = exchange(ff_more.reshape(-1, width), devices)
            first = jnp.where((code >= 0) & (place < cut), expert * cut + place, devices * cut)
            take = lambda a, index: jnp.take(a, index, axis=0, mode="fill", fill_value=0)
            ff = take(ff_back, first) + take(spare, rest)
            return False, (y + gate * ff.astype(jnp.float32)).astype(LOW)

        _, mixed = lax.while_loop(lambda held: held[0], mix_all, (crowded, mixed))
    *grads, router_t, gains, table, mixed = unpack(summed, small, mixed, experts, heads, buckets)
    return (
        mixed.reshape(rows, seq, width),
        grad_tokens.reshape(rows, seq, width),
        *grads,
        gains[0], gains[1], table.T, router_t.T,
        grad_in,
        grad_out,
    )


def solution(mesh):
    split = P(AXES)
    in_specs = (split,) * 4 + (P(),) * 8 + (split,) * 3
    out_specs = (split,) * 2 + (P(),) * 8 + (split,) * 2
    return jax.shard_map(local, mesh=mesh, in_specs=in_specs, out_specs=out_specs, check_vma=False)
```

```python
import functools

import jax
import jax.numpy as jnp
from jax import lax
from jax.experimental import pallas as pl
from jax.experimental.pallas import tpu as pltpu
from jax.sharding import PartitionSpec as P

EPSILON = 1e-06
NEGATIVE = -1e30
THRESHOLDS = (12, 16, 23, 32, 46, 64, 91)
LOG2E = 1.4426950408889634
TILE = 128
GELU_A = 0.7978845608028654
GELU_B = GELU_A * 0.044715
AXES = ("grp", "exp")
LOW = jnp.bfloat16


def dot(a, b):
    return jnp.dot(a, b, preferred_element_type=jnp.float32)


def dot_t(a, b):
    return lax.dot_general(a, b, (((1,), (1,)), ((), ())), preferred_element_type=jnp.float32)


def params(mib, **more):
    return pltpu.CompilerParams(vmem_limit_bytes=mib << 20, **more)


def whole(shape):
    return pl.BlockSpec(shape, lambda *_: (0,) * len(shape), pipeline_mode=pl.Buffered(1))


def cost(flops, bytes_accessed, transcendentals=0):
    return pl.CostEstimate(
        flops=flops, bytes_accessed=bytes_accessed, transcendentals=transcendentals
    )


def bucket_of(offset):
    distance = jnp.abs(offset)
    far = jnp.full_like(distance, 8)
    for border in THRESHOLDS:
        far = far + (distance >= border).astype(jnp.int32)
    return jnp.where(distance < 8, distance, far) + jnp.where(offset > 0, 16, 0).astype(jnp.int32)


def device_place(cores, d):
    return dict(device_id=(lax.div(d, cores), lax.rem(d, cores)), device_id_type=pl.DeviceIdType.MESH)


def partner_of(me, b):
    bit = lax.rem(lax.div(me, 1 << b), 2)
    return bit, me + (1 - 2 * bit) * (1 << b)


def rows_at(start, length):
    return pl.ds(pl.multiple_of(start, 16), length)


def plan(room):
    if room % 64:
        return ((0, room),), room, 0
    half = room // 2
    return ((half, half + room // 4), (0, half)), 3 * room // 4, room // 4


def back_plan(room):
    if room % 64:
        return ((0, room),)
    return ((room // 2, room), (0, room // 2))


def segment(code, room, low, high):
    expert = lax.div(code, room)
    place = code - expert * room
    inside = (code >= 0) & (place >= low) & (place < high)
    return jnp.where(inside, expert * (high - low) + place - low, -1)


def spread(dest, values, out):
    rows = out.shape[0]
    step = min(256, rows)
    for start in range(0, rows, step):
        here = lax.broadcasted_iota(jnp.int32, (step, dest.shape[1]), 0) + start
        out[start : start + step] = dot((dest == here).astype(LOW), values).astype(LOW)


def collect(dest, values):
    here = lax.broadcasted_iota(jnp.int32, (dest.shape[0], values.shape[0]), 1)
    return dot((dest == here).astype(LOW), values)


def spread_all(code, room, values, outs):
    for (low, high), out in zip(plan(room)[0], outs):
        spread(segment(code, room, low, high), values, out)


def collect_all(code, room, refs):
    total = None
    for (low, high), ref in zip(back_plan(room), refs):
        part = collect(segment(code, room, low, high), ref[...])
        total = part if total is None else total + part
    return total


def buffers(experts, room, width):
    return [
        jax.ShapeDtypeStruct((experts * (high - low), width), LOW) for low, high in plan(room)[0]
    ]


def route_kernel(
    experts, room, eid_ref, slot_ref, g_ref, code_r, rank_r, out, more
):
    tokens = g_ref.shape[0]
    wide = max(TILE, experts)
    _, cut, extra = plan(room)
    at = lax.broadcasted_iota(jnp.int32, (tokens, tokens), 0)
    to = lax.broadcasted_iota(jnp.int32, (tokens, tokens), 1)

    line = lambda ref: jnp.concatenate([ref[i : i + 1] for i in range(ref.shape[0])], axis=1)
    ids = line(eid_ref)
    slots = line(slot_ref)
    picked = ids == lax.broadcasted_iota(jnp.int32, (wide, tokens), 0)
    earlier = dot(picked.astype(LOW), (at < to).astype(LOW))
    place = jnp.sum(jnp.where(picked, earlier, 0.0), axis=0, keepdims=True).astype(jnp.int32)
    kept = slots >= 0
    code = jnp.where(kept, ids * room + place, -1)
    code_r[...] = code
    rank = jnp.where(kept & (place >= cut), place - cut, -1)
    rank_r[...] = rank
    spread(segment(code, room, 0, cut), g_ref[...], out)
    spread(rank, g_ref[...], more)


def columns_kernel(experts, room, code_ref, code_c, rank_c, marks):
    tokens = code_ref.shape[1]
    wide = max(TILE, experts)
    _, cut, _ = plan(room)
    rows = jnp.concatenate([code_ref[...], jnp.zeros((7, tokens), jnp.int32)], axis=0)
    code = rows.astype(jnp.float32).T.astype(jnp.int32)[:, :1]
    code_c[...] = code
    ids = lax.div(code, room)
    place = code - ids * room
    over = (code >= 0) & (place >= cut)
    rank_c[...] = jnp.where(over, place - cut, -1)
    picked = ids == lax.broadcasted_iota(jnp.int32, (tokens, wide), 1)
    named = jnp.max(jnp.where(picked & over, 1.0, 0.0), axis=0, keepdims=True)
    named = jnp.sum(named, axis=1, keepdims=True)
    owner = jnp.max(jnp.where(over, ids + 1, 0).astype(jnp.float32), axis=0, keepdims=True)
    lane = lax.broadcasted_iota(jnp.int32, marks.shape, 1)
    crowded = jnp.where(named > 1.0, 1.0, 0.0)
    marks[...] = jnp.where(lane == 0, owner, jnp.where(lane == 1, crowded, 0.0))


def columns(code, experts, room):
    tokens = code.shape[1]
    column = jax.ShapeDtypeStruct((tokens, 1), jnp.int32)
    return pl.pallas_call(
        functools.partial(columns_kernel, experts, room),
        out_shape=[column, column, jax.ShapeDtypeStruct((8, TILE), jnp.float32)],
        compiler_params=params(32),
        name="columns",
    )(code)


def route(expert_ids, slots, upstream, experts, room):
    tokens, width = upstream.shape
    line = jax.ShapeDtypeStruct((1, tokens), jnp.int32)
    _, cut, extra = plan(room)
    return pl.pallas_call(
        functools.partial(route_kernel, experts, room),
        out_shape=[
            line, line,
            jax.ShapeDtypeStruct((experts * cut, width), LOW),
            jax.ShapeDtypeStruct((max(extra, 16), width), LOW),
        ],
        compiler_params=params(60),
        cost_estimate=cost(2 * experts * room * tokens * width, 8 << 20),
        name="route",
    )(expert_ids, slots, upstream)


def exchange(buffer, devices):
    shaped = buffer.reshape(devices, buffer.shape[0] // devices, buffer.shape[1])
    moved = lax.all_to_all(shaped, AXES, split_axis=0, concat_axis=0, tiled=True)
    return moved.reshape(buffer.shape)


def project_kernel(x_ref, gain_ref, wq_ref, wk_ref, wv_ref, normed_ref, out_ref):
    x = x_ref[...].astype(jnp.float32)
    rms = lax.rsqrt(jnp.mean(x * x, axis=-1, keepdims=True) + EPSILON)
    normed = (x * rms * gain_ref[...]).astype(LOW)
    normed_ref[...] = normed.T
    width = x.shape[1]
    for n, w_ref in enumerate((wq_ref, wk_ref, wv_ref)):
        out_ref[:, n * width : (n + 1) * width] = dot(normed, w_ref[...]).astype(LOW)


def project(x, gain, w_query, w_key, w_value):
    tokens, width = x.shape
    out = 3 * width
    step = 256
    rows = lambda w: pl.BlockSpec((step, w), lambda i: (i, 0))
    return pl.pallas_call(
        project_kernel,
        grid=(tokens // step,),
        in_specs=[rows(width), whole((1, width)), *[whole((width, width))] * 3],
        out_specs=[pl.BlockSpec((width, step), lambda i: (0, i)), rows(out)],
        out_shape=[
            jax.ShapeDtypeStruct((width, tokens), LOW),
            jax.ShapeDtypeStruct((tokens, out), LOW),
        ],
        compiler_params=params(40),
        cost_estimate=cost(2 * tokens * width * out, 12 << 20),
        name="project",
    )(x, gain, w_query, w_key, w_value)


def gather_orders(bits):
    far = tuple(range(3, bits))
    return [[(0,), (1,), (2,), far], [(0,), (2,), far, (1,)], [(0,), far, (1,), (2,)]]


def span(order, s, n):
    for group in order[: s + 1]:
        n >>= len(group)
    return n


def digit_of(d, group):
    if isinstance(d, int):
        return sum(((d >> b) & 1) << i for i, b in enumerate(group))
    return sum(lax.rem(lax.div(d, 1 << b), 2) * (1 << i) for i, b in enumerate(group))


def peer_of(me, group, r):
    for i, b in enumerate(group):
        if (r >> i) & 1:
            me = partner_of(me, b)[1]
    return me


def rank_in(order, d):
    n = 1 << sum(len(group) for group in order)
    return sum(digit_of(d, group) * span(order, s, n) for s, group in enumerate(order))


def after_attention_kernel(
    experts, room, cores, n, o_ref, x_ref, w_ref, gain_ref, eid_ref, wr_ref, code_ref, *rest
):
    segments, _, extra = plan(room)
    if extra:
        rank_ref, g_ref, mark_ref, *rest = rest
    y_ref, gate_ref, *rest = rest
    outs, rest = rest[: len(segments)], rest[len(segments) :]
    if extra:
        h_more, g_more, flag_ref, *rest = rest
        own, moved, marks, send, recv, *rest = rest
    (held,) = rest
    step = o_ref.shape[0]
    i = pl.program_id(0)
    bits = n.bit_length() - 1
    if extra:
        me = lax.axis_index("grp") * cores + lax.axis_index("exp")
        barrier = pltpu.get_barrier_semaphore()
        greeted = [(g, r) for g in gather_orders(bits)[0] for r in range(1, 1 << len(g))]

        @pl.when(i == 0)
        def _():
            for group, r in greeted:
                pl.semaphore_signal(barrier, inc=1, **device_place(cores, peer_of(me, group, r)))

    y = x_ref[...].astype(jnp.float32) + dot(o_ref[...], w_ref[...])
    y_ref[...] = y
    rms = lax.rsqrt(jnp.mean(y * y, axis=-1, keepdims=True) + EPSILON)
    normed = (y * rms * gain_ref[...]).astype(LOW)
    held[pl.ds(pl.multiple_of(i * step, step), step), :] = normed
    router = route_softmax(dot(normed, wr_ref[...]), experts)
    lane = lax.broadcasted_iota(jnp.int32, router.shape, 1)
    expert = lax.div(jnp.maximum(eid_ref[...], 0), room)
    gate_ref[...] = jnp.sum(jnp.where(lane == expert, router, 0.0), axis=-1, keepdims=True)

    @pl.when(i == pl.num_programs(0) - 1)
    def _():
        chunks = []
        for (low, high), out in zip(segments, outs):
            dest = segment(code_ref[...], room, low, high)
            size = min(256, out.shape[0])
            chunks += [(dest, out, start, size) for start in range(0, out.shape[0], size)]

        def spread_some(count):
            for dest, out, start, size in chunks[:count]:
                spread(dest - start, held[...], out.at[start : start + size])
            del chunks[:count]

        if not extra:
            spread_some(len(chunks))
            return
        single, width = g_ref.shape
        block = 2 * single
        orders = gather_orders(bits)
        phases = len(orders[0])
        third = width // 3
        spread(rank_ref[...], held[...], own)
        base = []
        for p, order in enumerate(orders):
            lanes = slice(p * third, (p + 1) * third)
            base.append(rank_in(order, me) * block)
            moved[p, rows_at(base[p], single), :] = own[:, lanes]
            moved[p, rows_at(base[p] + single, single), :] = g_ref[:, lanes]
        tall = mark_ref.shape[0]
        marks[pl.ds(pl.multiple_of(rank_in(orders[0], me) * tall, 8), tall), :] = mark_ref[...]
        pl.semaphore_wait(barrier, len(greeted))

        def doubling(s):
            copies = []
            for p, order in enumerate(orders):
                size = span(order, s, n)
                for r in range(1, 1 << len(order[s])):
                    place = device_place(cores, peer_of(me, order[s], r))
                    here = rows_at(base[p], block * size)
                    copies.append(
                        pltpu.make_async_remote_copy(
                            src_ref=moved.at[p, here], dst_ref=moved.at[p, here],
                            send_sem=send.at[p, s, r - 1], recv_sem=recv.at[p, s, r - 1], **place,
                        )
                    )
                    if p == 0:
                        start = lax.div(base[0], block) * tall
                        here = pl.ds(pl.multiple_of(start, 8), tall * size)
                        copies.append(
                            pltpu.make_async_remote_copy(
                                src_ref=marks.at[here], dst_ref=marks.at[here],
                                send_sem=send.at[3, s, r - 1], recv_sem=recv.at[3, s, r - 1], **place,
                            )
                        )
            for copy in copies:
                copy.start()
            return copies

        sent = []
        for s in reversed(range(phases)):
            copies = doubling(s)
            spread_some(2)
            for copy in copies:
                copy.wait_recv()
            sent += copies
            for p, order in enumerate(orders):
                base[p] = base[p] - digit_of(me, order[s]) * block * span(order, s, n)
        spread_some(len(chunks))
        for copy in sent:
            copy.wait_send()
        for d in range(n):
            here = slice(d * single, (d + 1) * single)
            first = rank_in(orders[0], d) * tall
            keep = marks[first : first + 1, :1] == (me + 1).astype(jnp.float32)
            for p, order in enumerate(orders):
                lanes = slice(p * third, (p + 1) * third)
                at = rank_in(order, d) * block
                for out, start in ((h_more, at), (g_more, at + single)):
                    got = moved[p, start : start + single, :].astype(jnp.float32)
                    out[here, lanes] = jnp.where(keep, got, 0.0).astype(LOW)
        flag_ref[...] = jnp.broadcast_to(
            jnp.max(marks[:, 1:2], axis=0, keepdims=True), flag_ref.shape
        )


def after_attention(
    joined, x, w_output, gain, expert_ids, w_router, code, rank, g_extra, marks, experts, room
):
    tokens, width = x.shape
    step = 256
    cores = lax.axis_size("exp")
    n = lax.axis_size(AXES)
    bits = n.bit_length() - 1
    segments, _, extra = plan(room)
    rows = pl.BlockSpec((step, width), lambda i: (i, 0))
    single = pl.BlockSpec((step, 1), lambda i: (i, 0))
    outs = buffers(experts, room, width)
    more, scratch, options = [], [], {}
    if extra:
        more = [rank, g_extra, marks]
        outs = outs + [jax.ShapeDtypeStruct((n * extra, width), LOW)] * 2
        outs = outs + [jax.ShapeDtypeStruct((8, TILE), jnp.float32)]
        scratch = [
            pltpu.VMEM((extra, width), LOW), pltpu.VMEM((3, 2 * n * extra, width // 3), LOW),
            pltpu.VMEM((8 * n, TILE), jnp.float32),
            pltpu.SemaphoreType.DMA((4, 4, (n >> 3) - 1)), pltpu.SemaphoreType.DMA((4, 4, (n >> 3) - 1)),
        ]
        options = dict(collective_id=2, has_side_effects=True)
    return pl.pallas_call(
        functools.partial(after_attention_kernel, experts, room, cores, n),
        grid=(tokens // step,),
        in_specs=[
            rows, rows, whole((width, width)), whole((1, width)), single, whole(w_router.shape),
            whole((1, tokens)), *[whole(m.shape) for m in more],
        ],
        out_specs=[rows, single] + [pl.BlockSpec(o.shape, lambda i: (0, 0)) for o in outs],
        out_shape=[
            jax.ShapeDtypeStruct((tokens, width), jnp.float32),
            jax.ShapeDtypeStruct((tokens, 1), jnp.float32),
        ]
        + outs,
        scratch_shapes=scratch + [pltpu.VMEM((tokens, width), LOW)],
        compiler_params=params(60, **options),
        cost_estimate=cost(2 * tokens * width * (width + experts * room), 12 << 20),
        name="after_attention",
    )(joined, x, w_output, gain, expert_ids, w_router, code, *more)


def route_softmax(logits, experts):
    lane = lax.broadcasted_iota(jnp.int32, logits.shape, 1)
    logits = jnp.where(lane < experts, logits, NEGATIVE)
    e = jnp.exp(logits - jnp.max(logits, axis=-1, keepdims=True))
    return e / jnp.sum(e, axis=-1, keepdims=True)


def pack(values, first, height, out, at):
    for c in range(values.shape[1] // TILE):
        out[at + c * height : at + (c + 1) * height] = values[
            first : first + height, c * TILE : (c + 1) * TILE
        ].astype(LOW)


def before_attention_kernel(
    room, n_backs, code_ref, y_ref, g_ref, gain_ref, w_ref, o_ref, *rest
):
    backs = rest[:n_backs]
    dy_ref, do_ref, pack_ref, gg_ref, gw_ref = rest[n_backs:]
    i = pl.program_id(0)

    @pl.when(i == 0)
    def _():
        gw_ref[...] = jnp.zeros_like(gw_ref)
        gg_ref[...] = jnp.zeros_like(gg_ref)

    step = y_ref.shape[0] // 2
    blocks = [slice(n * step, (n + 1) * step) for n in range(2)]
    dhs = [collect_all(code_ref[here, :], room, backs) for here in blocks]
    lows = []
    for here, dh in zip(blocks, dhs):
        y = y_ref[here, :]
        rms = lax.rsqrt(jnp.mean(y * y, axis=-1, keepdims=True) + EPSILON)
        gg_ref[...] += jnp.sum(dh * y * rms, axis=0, keepdims=True)
        u = dh * gain_ref[...]
        dy = (
            g_ref[here, :].astype(jnp.float32)
            + rms * u
            - y * (rms * rms * rms) * jnp.mean(u * y, axis=-1, keepdims=True)
        )
        dy_ref[here, :] = dy
        lows.append(dy.astype(LOW))
        do_ref[here, :] = dot_t(lows[-1], w_ref[...]).astype(LOW)
    gw_ref[...] += dot(o_ref[...].T, jnp.concatenate(lows, axis=0))

    @pl.when(i == pl.num_programs(0) - 1)
    def _():
        pack(gw_ref, 0, gw_ref.shape[0], pack_ref, 0)


def before_attention(backs, code, y, g, gain, w_output, joined, room):
    tokens, width = y.shape
    step = 512
    rows = lambda w: pl.BlockSpec((step, w), lambda i: (i, 0))
    return pl.pallas_call(
        functools.partial(before_attention_kernel, room, len(backs)),
        grid=(tokens // step,),
        in_specs=[
            rows(1), rows(width), rows(width), whole((1, width)),
            whole((width, width)), rows(width), *[whole(b.shape) for b in backs],
        ],
        out_specs=[
            rows(width), rows(width),
            pl.BlockSpec((width * width // TILE, TILE), lambda i: (0, 0)),
            pl.BlockSpec((1, width), lambda i: (0, 0)),
        ],
        out_shape=[
            jax.ShapeDtypeStruct((tokens, width), jnp.float32),
            jax.ShapeDtypeStruct((tokens, width), LOW),
            jax.ShapeDtypeStruct((width * width // TILE, TILE), LOW),
            jax.ShapeDtypeStruct((1, width), jnp.float32),
        ],
        scratch_shapes=[pltpu.VMEM((width, width), jnp.float32)],
        compiler_params=params(60),
        cost_estimate=cost(6 * tokens * width * width, 16 << 20),
        name="before_attention",
    )(code, y, g, gain, w_output, joined, *backs)


def unpack_kernel(
    experts, heads, buckets, q_ref, k_ref, v_ref, o_ref, small_ref, mix_ref,
    gq, gk, gv, go, router, gain_one, gain_two, table, mixed,
):
    mixed[...] = mix_ref[...]
    for packed_ref, out_ref in ((q_ref, gq), (k_ref, gk), (v_ref, gv), (o_ref, go)):
        for c in range(packed_ref.shape[0]):
            out_ref[:, c * TILE : (c + 1) * TILE] = packed_ref[c].astype(jnp.float32)

    @pl.when(pl.program_id(0) == 0)
    def _():
        lines = router.shape[1] // TILE
        small = small_ref[...].astype(jnp.float32)
        for c in range(lines):
            lanes = slice(c * TILE, (c + 1) * TILE)
            router[:, lanes] = small[c * experts : (c + 1) * experts]
            for n, gain in enumerate((gain_one, gain_two)):
                gain[lanes] = small[lines * experts + n * lines + c]
        at = lines * experts + -(-2 * lines // 16) * 16
        table[...] = small[at : at + heads, :buckets]


def unpack(packed, small, mixed, experts, heads, buckets):
    tokens, width = mixed.shape
    blocks = width // TILE
    steps = 4
    source = lambda m: pl.BlockSpec((blocks, width // steps, TILE), lambda i: (m, i, 0))
    rows = lambda count: pl.BlockSpec((count // steps, width), lambda i: (i, 0))
    kept = lambda shape: pl.BlockSpec(shape, lambda i: (0, 0))
    flat = pl.BlockSpec((width,), lambda i: (0,))
    return pl.pallas_call(
        functools.partial(unpack_kernel, experts, heads, buckets),
        grid=(steps,),
        in_specs=[source(m) for m in range(4)] + [whole(small.shape), rows(tokens)],
        out_specs=[rows(width)] * 4
        + [kept((experts, width)), flat, flat, kept((heads, buckets)), rows(tokens)],
        out_shape=[jax.ShapeDtypeStruct((width, width), jnp.float32)] * 4
        + [
            jax.ShapeDtypeStruct((experts, width), jnp.float32),
            jax.ShapeDtypeStruct((width,), jnp.float32),
            jax.ShapeDtypeStruct((width,), jnp.float32),
            jax.ShapeDtypeStruct((heads, buckets), jnp.float32),
            jax.ShapeDtypeStruct((tokens, width), LOW),
        ],
        compiler_params=params(60),
        name="unpack",
    )(*[packed.reshape(4 * blocks, width, TILE)] * 4, small, mixed)


def attention_forward_kernel(len_ref, q_ref, k_ref, v_ref, near_ref, far_ref, o_ref, p_ref, s_ref):
    seq = q_ref.shape[0]
    tiles = seq // TILE
    half = q_ref.shape[1] // 2
    row = pl.program_id(0)
    pair = pl.program_id(1)
    live = len_ref[row]
    lane = lax.broadcasted_iota(jnp.int32, (seq, 2 * half), 1)
    dead = lax.broadcasted_iota(jnp.int32, (seq, 2 * half), 0) >= live
    q = q_ref[...]
    k = k_ref[...]
    v_t = v_ref[...].T
    outs = []
    for h in range(2):
        mine = (lane >= h * half) & (lane < (h + 1) * half)
        flag = lane == (1 - h) * half
        k_h = jnp.where(mine, k, jnp.where(flag & dead, -1e30, 0.0).astype(k.dtype))
        q_h = jnp.where(flag, jnp.ones_like(q), q)
        after = far_ref[2 * pair + h, 0]
        before = far_ref[2 * pair + h, 1]
        tops = []
        for i in range(0, tiles, 2):
            q_i = q_h[i * TILE : (i + 2) * TILE]
            raw = dot_t(k_h, q_i)
            for c in range(2):
                cols = slice((i + c) * TILE, (i + c + 1) * TILE)
                top = None
                for j in range(tiles):
                    x = raw[j * TILE : (j + 1) * TILE, c * TILE : (c + 1) * TILE] * (0.125 * LOG2E)
                    d = j - i - c
                    if -1 <= d <= 1:
                        x = x + near_ref[h, d + 1]
                    else:
                        x = x + (after if d > 0 else before)
                    s_ref[h, j * TILE : (j + 1) * TILE, cols] = x
                    m = jnp.max(x, axis=0, keepdims=True)
                    top = m if top is None else jnp.maximum(top, m)
                tops.append(top)
        for i in range(tiles):
            e = jnp.exp2(s_ref[h, :, i * TILE : (i + 1) * TILE] - tops[i])
            total = jnp.sum(e, axis=0, keepdims=True)
            p_ref[0, h, :, i * TILE : (i + 1) * TILE] = (e * (1.0 / total)).astype(LOW)
        outs.append(lax.dot_general(v_t[h * half:(h + 1) * half], p_ref[0, h], (((1,), (0,)), ((), ())), preferred_element_type=jnp.float32))
    o_ref[...] = jnp.concatenate(outs, axis=0).T.astype(o_ref.dtype)

def attention_forward(lengths, projected, near, far, rows, seq, heads, head):
    width = heads * head
    pairs = heads // 2
    spec = lambda off: pl.BlockSpec((seq, 2 * head), lambda b, p: (b, off + p))
    return pl.pallas_call(
        attention_forward_kernel,
        grid=(rows, pairs),
        in_specs=[
            pl.BlockSpec(memory_space=pltpu.SMEM),
            spec(0), spec(pairs), spec(2 * pairs),
            pl.BlockSpec((2, 3, TILE, TILE), lambda b, p: (p, 0, 0, 0)),
            pl.BlockSpec(memory_space=pltpu.SMEM),
        ],
        out_specs=[
            pl.BlockSpec((seq, 2 * head), lambda b, p: (b, p)),
            pl.BlockSpec((1, 2, seq, seq), lambda b, p: (b, p, 0, 0)),
        ],
        out_shape=[
            jax.ShapeDtypeStruct((rows * seq, width), LOW),
            jax.ShapeDtypeStruct((rows, heads, seq, seq), LOW),
        ],
        scratch_shapes=[pltpu.VMEM((2, seq, seq), jnp.float32)],
        compiler_params=params(40),
        cost_estimate=cost(flops=4 * rows * heads * seq * seq * head * 4, bytes_accessed=rows * heads * seq * seq * 2, transcendentals=rows * heads * seq * seq),
        name="attention_forward",
    )(lengths, projected, projected, projected, near, far)

def attention_backward_kernel(
    rows, q_ref, k_ref, v_ref, do_ref, o_ref, p_ref, nt_ref, wq_ref, wk_ref, wv_ref, x_ref, dy_ref, gain_ref,
    gr_ref, gg2_ref, out_ref, pack_ref, small_ref,
    near_ref, far_ref, d_ref, lines_ref, dh_ref,
):
    seq = q_ref.shape[0] // rows
    tiles = seq // TILE
    half = q_ref.shape[1] // 2
    width = x_ref.shape[1]
    pair = pl.program_id(0)
    last_pair = pair == pl.num_programs(0) - 1
    lane = lax.broadcasted_iota(jnp.int32, (seq, 2 * half), 1)
    weights = jnp.concatenate([wq_ref[...], wk_ref[...], wv_ref[...]], axis=1)
    near_ref[...] = jnp.zeros_like(near_ref)
    for row in range(rows):
        here = slice(row * seq, (row + 1) * seq)
        v = v_ref[here, :]
        do = do_ref[here, :]
        weighed = (do.astype(jnp.float32) * o_ref[here, :].astype(jnp.float32)).T
        for h in range(2):
            mine = (lane >= h * half) & (lane < (h + 1) * half)
            v_h = jnp.where(mine, v, jnp.zeros_like(v))
            delta = jnp.sum(weighed[h * half : (h + 1) * half], axis=0, keepdims=True)
            far_sum = [jnp.zeros((8, TILE), jnp.float32), jnp.zeros((8, TILE), jnp.float32)]
            for i in range(0, tiles, 2):
                dp = dot_t(v_h, do[i * TILE : (i + 2) * TILE])
                for c in range(2):
                    cols = slice((i + c) * TILE, (i + c + 1) * TILE)
                    for j in range(tiles):
                        rws = slice(j * TILE, (j + 1) * TILE)
                        part = dp[rws, c * TILE : (c + 1) * TILE] - delta[:, cols]
                        ds = p_ref[row, h, rws, cols].astype(jnp.float32) * part
                        d = j - i - c
                        if -1 <= d <= 1:
                            near_ref[row, h, d + 1] += ds
                        else:
                            which = 0 if d > 0 else 1
                            far_sum[which] = far_sum[which] + jnp.sum(
                                ds.reshape(TILE // 8, 8, TILE), axis=0
                            )
                        d_ref[row, h, rws, cols] = ds.astype(LOW)
            for which in range(2):
                far_ref[row, h, which] = far_sum[which]
    grads_all = []
    for row in range(rows):
        here = slice(row * seq, (row + 1) * seq)
        q = q_ref[here, :]
        do = do_ref[here, :]
        k_t = k_ref[here, :].T
        dq_parts = []
        dk_all = None
        dv_all = None
        for h in range(2):
            mine = (lane >= h * half) & (lane < (h + 1) * half)
            ds_all = d_ref[row, h]
            dq_parts.append(dot(k_t[h * half : (h + 1) * half], ds_all))
            dk_h = dot(ds_all, q)
            dv_h = dot(p_ref[row, h], do)
            dk_all = dk_h if h == 0 else jnp.where(mine, dk_h, dk_all)
            dv_all = dv_h if h == 0 else jnp.where(mine, dv_h, dv_all)
        dq = (jnp.concatenate(dq_parts, axis=0).T * 0.125).astype(LOW)
        grads_all.append(
            jnp.concatenate([dq, (dk_all * 0.125).astype(LOW), dv_all.astype(LOW)], axis=1)
        )
    grads = jnp.concatenate(grads_all, axis=0)
    acc = dot(nt_ref[...], grads)
    for n in range(3):
        pack_ref[n, 0] = acc[:, n * TILE : (n + 1) * TILE].astype(LOW)
    dh = dot_t(grads, weights)

    @pl.when(pair == 0)
    def _():
        dh_ref[...] = dh

    @pl.when(pair > 0)
    def _():
        dh_ref[...] += dh

    near_ref[0] = sum(near_ref[row] for row in range(rows))
    far_ref[0] = sum(far_ref[row] for row in range(rows))
    bucket_sums(near_ref.at[0], far_ref.at[0], lines_ref, 2 * pair)

    @pl.when(last_pair)
    def _():
        total = dh_ref[...]
        x = x_ref[...].astype(jnp.float32)
        rms = lax.rsqrt(jnp.mean(x * x, axis=-1, keepdims=True) + EPSILON)
        gg = jnp.sum(total * x * rms, axis=0, keepdims=True)
        u = total * gain_ref[...]
        out_ref[...] = (
            dy_ref[...]
            + rms * u
            - x * (rms * rms * rms) * jnp.mean(u * x, axis=-1, keepdims=True)
        )
        at = gr_ref.shape[0]
        small_ref[:at] = gr_ref[...].astype(LOW)
        lines = width // TILE
        gains = [gg[:, c * TILE : (c + 1) * TILE] for c in range(lines)]
        gains += [gg2_ref[:, c * TILE : (c + 1) * TILE] for c in range(lines)]
        if 2 * lines % 16:
            gains += [jnp.zeros((16 - 2 * lines % 16, TILE), jnp.float32)]
        gains = jnp.concatenate(gains, axis=0)
        small_ref[at : at + gains.shape[0]] = gains.astype(LOW)
        at = at + gains.shape[0]
        table = bucket_table(lines_ref)
        if table.shape[0] % 16:
            table = jnp.concatenate([table, jnp.zeros((16 - table.shape[0] % 16, TILE), jnp.float32)], axis=0)
        small_ref[at : at + table.shape[0]] = table.astype(LOW)
        at = at + table.shape[0]
        small_ref[at:] = jnp.zeros((small_ref.shape[0] - at, TILE), LOW)


def bucket_sums(near_ref, far_ref, lines_ref, first):
    empty = jnp.zeros((8, TILE), jnp.float32)
    sub = lax.broadcasted_iota(jnp.int32, (8, 2 * TILE), 0)
    for h in range(2):
        lines = []
        for d in range(3):
            turned = None
            for a in range(0, TILE, 8):
                part = jnp.concatenate([near_ref[h, d, a : a + 8], empty], axis=1)
                part = pltpu.roll(part, (2 * TILE - a) % (2 * TILE), 1) if a else part
                turned = part if turned is None else turned + part
            for b in (1, 2, 4):
                turned = jnp.where((sub & b) > 0, pltpu.roll(turned, 2 * TILE - b, 1), turned)
            lines.append(jnp.sum(turned, axis=0, keepdims=True))
        for side in range(2):
            total = jnp.sum(far_ref[h, side], axis=0, keepdims=True)
            lines.append(jnp.concatenate([total, jnp.zeros((1, TILE), jnp.float32)], axis=1))
        lines.append(jnp.zeros((3, 2 * TILE), jnp.float32))
        lines_ref[first + h] = jnp.concatenate(lines, axis=0)


def bucket_table(lines_ref):
    heads = lines_ref.shape[0]
    buckets = 4 * 8
    lane = lax.broadcasted_iota(jnp.int32, (2 * TILE, TILE), 0)
    bucket = lax.broadcasted_iota(jnp.int32, (2 * TILE, TILE), 1)
    turn = jnp.where(lane >= TILE, lane - 2 * TILE, lane)
    total = None
    for r in range(5):
        if r < 3:
            hit = bucket_of((r - 1) * TILE - turn) == bucket
        else:
            hit = bucket == (buckets - 1 if r == 3 else buckets // 2 - 1)
        hit = hit.astype(LOW)
        line = jnp.concatenate([lines_ref[h, r : r + 1, :] for h in range(heads)], axis=0)
        high = line.astype(LOW)
        part = dot(high, hit) + dot((line - high.astype(jnp.float32)).astype(LOW), hit)
        total = part if total is None else total + part
    return total


def attention_backward(
    projected, do, joined, weights, normed_t, w_query, w_key, w_value, x, dy, gain, gr, gg2,
    rows, seq, heads, head, small_rows,
):
    width = heads * head
    pairs = heads // 2
    tokens = rows * seq
    spec = lambda off: pl.BlockSpec((tokens, 2 * head), lambda p: (0, off + p))
    column = pl.BlockSpec((width, 2 * head), lambda p: (0, p))
    return pl.pallas_call(
        functools.partial(attention_backward_kernel, rows),
        grid=(pairs,),
        in_specs=[
            spec(0), spec(pairs), spec(2 * pairs), spec(0), spec(0),
            pl.BlockSpec((rows, 2, seq, seq), lambda p: (0, p, 0, 0)),
            whole((width, tokens)),
            column, column, column, whole((tokens, width)), whole((tokens, width)),
            whole((1, width)), whole(gr.shape), whole(gg2.shape),
        ],
        out_specs=[
            pl.BlockSpec((tokens, width), lambda p: (0, 0)),
            pl.BlockSpec((3, 1, width, TILE), lambda p: (0, p, 0, 0)),
            pl.BlockSpec((small_rows, TILE), lambda p: (0, 0)),
        ],
        out_shape=[
            jax.ShapeDtypeStruct((tokens, width), jnp.float32),
            jax.ShapeDtypeStruct((3, pairs, width, TILE), LOW),
            jax.ShapeDtypeStruct((small_rows, TILE), LOW),
        ],
        scratch_shapes=[
            pltpu.VMEM((rows, 2, 3, TILE, TILE), jnp.float32),
            pltpu.VMEM((rows, 2, 2, 8, TILE), jnp.float32),
            pltpu.VMEM((rows, 2, seq, seq), LOW),
            pltpu.VMEM((heads, 8, 2 * TILE), jnp.float32),
            pltpu.VMEM((tokens, width), jnp.float32),
        ],
        compiler_params=params(60),
        cost_estimate=cost(8 * rows * heads * seq * seq * head * 4, rows * heads * seq * seq * 2),
        name="attention_backward",
    )(
        projected, projected, projected, do, joined, weights, normed_t, w_query, w_key, w_value,
        x, dy, gain, gr, gg2,
    )


def bias_tiles(table):
    j = lax.broadcasted_iota(jnp.int32, (3, TILE, TILE), 1)
    i = lax.broadcasted_iota(jnp.int32, (3, TILE, TILE), 2)
    d = lax.broadcasted_iota(jnp.int32, (3, TILE, TILE), 0) - 1
    b = bucket_of(d * TILE + j - i)
    scaled = table.T * LOG2E
    hot = (b.reshape(1, -1) == jnp.arange(table.shape[0], dtype=jnp.int32)[:, None]).astype(jnp.float32)
    near = jnp.dot(scaled, hot, precision=lax.Precision.HIGHEST).reshape(-1, 3, TILE, TILE)
    far = jnp.stack([scaled[:, -1], scaled[:, table.shape[0] // 2 - 1]], axis=1)
    return near, far


def expert_kernel(experts, chunk, held, x_ref, g_ref, mine_ref, wr_ref, wi_any, wo_any, *refs):
    ff_ref, dx_ref, hid_ref, da_ref, xt_ref, dfft_ref, gr_ref, wi_ref, wo_ref, sem = refs[held:]
    inner = wi_ref.shape[1]
    first_step = pl.program_id(0) == 0

    def loads(f):
        cols = pl.ds(f, chunk)
        return (pltpu.make_async_copy(wi_any.at[:, cols], wi_ref.at[:, cols], sem.at[0, f // chunk]),
                pltpu.make_async_copy(wo_any.at[cols, :], wo_ref.at[cols, :], sem.at[1, f // chunk]))

    @pl.when(first_step)
    def _():
        for f in range(0, inner, chunk):
            for c in loads(f):
                c.start()
        gr_ref[...] = jnp.zeros_like(gr_ref)

    x = x_ref[...]
    g = g_ref[...].reshape(x.shape).astype(jnp.float32)
    mine = mine_ref[...]
    lane = lax.broadcasted_iota(jnp.int32, (1, wr_ref.shape[1]), 1)
    logits = jnp.dot(x, wr_ref[...], preferred_element_type=jnp.float32)
    logits = jnp.where(lane < experts, logits, -1e30)
    e = jnp.exp(logits - jnp.max(logits, axis=-1, keepdims=True))
    router = e / jnp.sum(e, axis=-1, keepdims=True)
    gate = jnp.sum(router * mine, axis=-1, keepdims=True)
    dff = (g * gate).astype(LOW)
    ff = None
    dx = None
    def first(f):
        @pl.when(first_step)
        def _():
            for c in loads(f):
                c.wait()
        cols = slice(f, f + chunk)
        return (jnp.dot(x, wi_ref[:, cols], preferred_element_type=jnp.float32),
                lax.dot_general(dff, wo_ref[cols, :], (((1,), (1,)), ((), ())), preferred_element_type=jnp.float32))
    for f in range(0, inner, chunk):
        cols = slice(f, f + chunk)
        a, dhid = first(f)
        u = a * a
        t = jnp.tanh(a * (GELU_A + GELU_B * u))
        h = 0.5 + 0.5 * t
        hid = a * h
        slope = h + hid * ((1.0 - t) * (GELU_A + (3.0 * GELU_B) * u))
        da = (dhid * slope).astype(LOW)
        hid = hid.astype(LOW)
        hid_ref[:, cols] = hid
        da_ref[:, cols] = da
        ff_part = jnp.dot(hid, wo_ref[cols, :], preferred_element_type=jnp.float32)
        dx_part = lax.dot_general(da, wi_ref[:, cols], (((1,), (1,)), ((), ())), preferred_element_type=jnp.float32)
        ff = ff_part if ff is None else ff + ff_part
        dx = dx_part if dx is None else dx + dx_part
    ff = ff.astype(LOW)
    ff_ref[...] = ff
    dgate = jnp.sum(g * ff.astype(jnp.float32), axis=-1, keepdims=True)
    dlogits = ((gate * dgate) * (mine - router)).astype(LOW)
    dx = dx + lax.dot_general(dlogits, wr_ref[...], (((1,), (1,)), ((), ())), preferred_element_type=jnp.float32)
    dx_ref[...] = dx.astype(LOW).reshape(dx_ref.shape)
    x_t = x.T
    xt_ref[...] = x_t
    dfft_ref[...] = dff.T
    gr_ref[...] += dot(dlogits.T, x)

def expert_rows(x, g, mine, wr, wi, wo, experts, low, high, at=0, total=0, dx=None, tile=256, chunk=768):
    n, width = x.shape
    inner = wi.shape[1]
    sources, room = g.shape[0], high - low
    total = total or room
    group = max(1, min(sources, tile // room))
    while sources % group or (group * room) % TILE:
        group += 1
    tile = group * room
    once = lambda s: pl.BlockSpec(s, lambda i: (0,) * len(s), pipeline_mode=pl.Buffered(1))
    rowspec = lambda w: pl.BlockSpec((tile, w), lambda i: (i, 0))
    column = pl.BlockSpec((width, tile), lambda i: (0, i))
    anywhere = pl.BlockSpec(memory_space=pl.ANY)
    held = [] if dx is None else [dx]
    return pl.pallas_call(
        functools.partial(expert_kernel, experts, chunk, len(held)),
        grid=(n // tile,),
        in_specs=[
            rowspec(width), pl.BlockSpec((group, room, width), lambda i: (i, low // room, 0)),
            once(mine.shape), once(wr.shape), anywhere, anywhere, *[anywhere] * len(held),
        ],
        out_specs=[
            rowspec(width), pl.BlockSpec((group, room, width), lambda i: (i, at // room, 0)),
            rowspec(inner), rowspec(inner), column, column,
            pl.BlockSpec((wr.shape[1], width), lambda i: (0, 0)),
        ],
        out_shape=[
            jax.ShapeDtypeStruct((n, width), LOW),
            jax.ShapeDtypeStruct((sources, total, width), LOW),
            *[jax.ShapeDtypeStruct((n, inner), LOW)] * 2,
            *[jax.ShapeDtypeStruct((width, n), LOW)] * 2,
            jax.ShapeDtypeStruct((wr.shape[1], width), jnp.float32),
        ],
        scratch_shapes=[
            pltpu.VMEM(wi.shape, LOW), pltpu.VMEM(wo.shape, LOW),
            pltpu.SemaphoreType.DMA((2, inner // chunk)),
        ],
        input_output_aliases={6: 1} if held else {},
        compiler_params=params(60),
        cost_estimate=cost(8 * n * width * inner, 4 * n * inner + 8 * width * inner, n * inner),
        name="expert_rows",
    )(x, g, mine, wr, wi, wo, *held)


def expert_weights_kernel(parts, *refs):
    ins, (gi_ref, go_ref) = refs[: 4 * parts], refs[4 * parts :]
    gi = None
    go = None
    for c in range(parts):
        xt, dfft, hid, da = ins[4 * c : 4 * c + 4]
        gi_c = dot(xt[...], da[...])
        go_c = dot(dfft[...], hid[...])
        gi = gi_c if gi is None else gi + gi_c
        go = go_c if go is None else go + go_c
    gi_ref[0] = gi
    go_ref[0] = go.T


def expert_weights(parts, tile=512):
    inner = parts[0][2].shape[1]
    width = parts[0][0].shape[0]
    specs, args, rows = [], [], 0
    for xt, dfft, hid, da in parts:
        n = hid.shape[0]
        rows += n
        specs += [pl.BlockSpec((width, n), lambda f: (0, 0), pipeline_mode=pl.Buffered(1))] * 2
        specs += [pl.BlockSpec((n, tile), lambda f: (0, f))] * 2
        args += [xt, dfft, hid, da]
    return pl.pallas_call(
        functools.partial(expert_weights_kernel, len(parts)),
        grid=(inner // tile,),
        in_specs=specs,
        out_specs=[
            pl.BlockSpec((1, width, tile), lambda f: (0, 0, f)),
            pl.BlockSpec((1, tile, width), lambda f: (0, f, 0)),
        ],
        out_shape=[
            jax.ShapeDtypeStruct((1, width, inner), jnp.float32),
            jax.ShapeDtypeStruct((1, inner, width), jnp.float32),
        ],
        compiler_params=params(60),
        cost_estimate=cost(4 * rows * width * inner, 4 * rows * inner + 8 * width * inner),
        name="expert_weights",
    )(*args)


def split_units(units, weights):
    total, sizes, done, so_far = sum(weights), [], 0, 0
    for w in weights:
        so_far += w
        end = (2 * units * so_far + total) // (2 * total)
        sizes.append(end - done)
        done = end
    return sizes


def sum_parts(n, heights):
    bits = n.bit_length() - 1
    upper = list(range(1, bits))
    orders = [[0] + upper[t:] + upper[:t] for t in range(3)]
    parts, first = [], 0
    for ref, rows in enumerate(heights):
        units = rows // (16 * n)
        turns = (0, 1, 2, 0, 1, 2) if units >= 18 else (0, 1, 2) if units >= 6 else (2,)
        at = 0
        for t, size in zip(turns, split_units(units, [(5, 5, 3)[t] for t in turns])):
            parts.append((ref, at * 16 * n, first, size * 16, orders[t]))
            at += size
            first += size * 16 * n
    return bits, parts


def sum_kernel(cores, n, room, heights, extra, code_ref, gate_ref, rank_ref, ff_any, y_any, *refs):
    _, cut, _ = plan(room)
    xs, refs = refs[: len(heights)], refs[len(heights) :]
    mixed_any, sum_any, small_any, out_ref, work_ref, got_ref, ff_ref, y_ref, mixed_ref, *refs = refs
    if extra:
        tail_ref, *refs = refs
    send, recv, local, load, store = refs
    loads = [
        pltpu.make_async_copy(ff_any, ff_ref, local.at[0]),
        pltpu.make_async_copy(y_any, y_ref, local.at[1]),
    ]
    summed = heights[:-1] if extra else heights
    bits, parts = sum_parts(n, summed)
    full = len(parts)
    if extra:
        parts = parts + [(len(summed), 0, sum(summed), heights[-1] // n, list(range(bits)))]
    me = lax.axis_index("grp") * cores + lax.axis_index("exp")
    base = [first for _, _, first, _, _ in parts]
    got_at = list(base)
    kept = []
    for p, (ref, at, first, step, order) in enumerate(parts):
        length = step * (n >> 1)
        start = base[p] + partner_of(me, order[0])[0] * length
        kept.append(
            pltpu.make_async_copy(
                xs[ref].at[rows_at(start - first + at, length)],
                work_ref.at[rows_at(start, length)],
                load.at[p],
            )
        )
        kept[p].start()
    for copy in loads:
        copy.start()
    barrier = pltpu.get_barrier_semaphore()
    for b in range(bits):
        pl.semaphore_signal(barrier, inc=1, **device_place(cores, partner_of(me, b)[1]))
    pl.semaphore_wait(barrier, bits)

    def halving(p, s):
        ref, at, first, step, order = parts[p]
        length = step * (n >> (s + 1))
        bit, partner = partner_of(me, order[s])
        start = base[p] + (1 - bit) * length
        if s == 0:
            source = xs[ref].at[rows_at(start - first + at, length)]
        else:
            source = work_ref.at[rows_at(start, length)]
        return pltpu.make_async_remote_copy(
            src_ref=source, dst_ref=got_ref.at[rows_at(got_at[p], length)],
            send_sem=send.at[p, s], recv_sem=recv.at[p, s], **device_place(cores, partner),
        )

    def doubling(p, s):
        _, _, _, step, order = parts[p]
        here = rows_at(base[p], step * (n >> (s + 1)))
        return pltpu.make_async_remote_copy(
            src_ref=out_ref.at[here], dst_ref=out_ref.at[here],
            send_sem=send.at[p, bits + s], recv_sem=recv.at[p, bits + s],
            **device_place(cores, partner_of(me, order[s])[1]),
        )

    main = sum(summed[:-1])

    def keep_out(p, s, start, length):
        here = rows_at(start, length)
        target = sum_any.at[here]
        if parts[p][0] == len(summed) - 1:
            target = small_any.at[rows_at(start - main, length)]
        copy = pltpu.make_async_copy(out_ref.at[here], target, store.at[p, s])
        copy.start()
        return copy

    tokens, width = mixed_ref.shape
    tile = tokens // 4
    tiles = [slice(i * tile, (i + 1) * tile) for i in range(4)]

    def mix_most():
        for copy in loads:
            copy.wait()
        for here in tiles:
            ff = collect(segment(code_ref[here, :], room, 0, cut), ff_ref[...])
            y_ref[here, :] += gate_ref[here, :] * ff

    def mix_rest():
        stores = []
        for i, here in enumerate(tiles):
            total = y_ref[here, :]
            if extra:
                tail = tail_ref[...]
                tail = [tail[c * extra : (c + 1) * extra] for c in range(width // TILE)]
                more = collect(rank_ref[here, :], jnp.concatenate(tail, axis=1))
                total = total + gate_ref[here, :] * more
            mixed_ref[here, :] = total.astype(LOW)
            stores.append(
                pltpu.make_async_copy(mixed_ref.at[here], mixed_any.at[here], local.at[2 + i])
            )
            stores[i].start()
        return stores

    moving = [halving(p, 0) for p in range(len(parts))]
    for copy in moving:
        copy.start()
    sent, stores = [], []
    for s in range(bits):
        if s == 1:
            mix_most()
        for p, (ref, at, first, step, order) in enumerate(parts):
            length = step * (n >> (s + 1))
            if s == 0:
                kept[p].wait()
            moving[p].wait_recv()
            sent.append(moving[p])
            base[p] = base[p] + partner_of(me, order[s])[0] * length
            last = s + 1 == bits
            target = out_ref if last else work_ref
            if p >= full and last:
                target = tail_ref

            def add(
                i, _, start=base[p], target=target, arrived=got_at[p], step=step,
                to=0 if p >= full and last else base[p],
            ):
                got = got_ref[rows_at(arrived + i * step, step), :].astype(jnp.float32)
                mine = work_ref[rows_at(start + i * step, step), :].astype(jnp.float32)
                target[rows_at(to + i * step, step), :] = (mine + got).astype(LOW)
                return 0

            lax.fori_loop(0, length // step, add, 0)
            got_at[p] += length
            if not last:
                moving[p] = halving(p, s + 1)
                moving[p].start()
            elif p < full:
                moving[p] = doubling(p, s)
                moving[p].start()
                stores.append(keep_out(p, bits, base[p], step))
    for copy in sent:
        copy.wait_send()
    sent = []
    for s in reversed(range(bits)):
        if s == min(1, bits - 1):
            stores += mix_rest()
        for p, (ref, at, first, step, order) in enumerate(parts[:full]):
            length = step * (n >> (s + 1))
            moving[p].wait_recv()
            sent.append(moving[p])
            bit = partner_of(me, order[s])[0]
            arrived = base[p] + (1 - 2 * bit) * length
            base[p] = base[p] - bit * length
            if s > 0:
                moving[p] = doubling(p, s - 1)
                moving[p].start()
            stores.append(keep_out(p, s, arrived, length))
    for copy in sent:
        copy.wait_send()
    for copy in stores:
        copy.wait()


def all_sum(xs, code, gate, rank, ff, y, room, ff_more):
    cores = lax.axis_size("exp")
    n = lax.axis_size(AXES)
    extra = plan(room)[2]
    heights = [a.shape[0] for a in xs]
    if any(h % (16 * n) for h in heights):
        xs = [jnp.concatenate(xs[:-1], axis=0), xs[-1]]
        heights = [a.shape[0] for a in xs]
    total, small = sum(heights), heights[-1]
    bits, parts = sum_parts(n, heights)
    count = len(parts)
    rows = total
    tokens, width = y.shape
    tail = []
    if extra:
        xs = xs + [ff_more]
        heights = heights + [ff_more.shape[0]]
        rows += ff_more.shape[0]
        count += 1
        tail = [pltpu.VMEM((extra * width // TILE, TILE), LOW)]
    buffer = pltpu.VMEM((rows, TILE), LOW)
    vmem = pl.BlockSpec(memory_space=pltpu.VMEM)
    anywhere = pl.BlockSpec(memory_space=pl.ANY)
    return pl.pallas_call(
        functools.partial(sum_kernel, cores, n, room, heights, extra),
        out_shape=[
            jax.ShapeDtypeStruct((tokens, width), LOW),
            jax.ShapeDtypeStruct((total - small, TILE), LOW),
            jax.ShapeDtypeStruct((small, TILE), LOW),
        ],
        in_specs=[vmem] * 3 + [anywhere] * (2 + len(xs)),
        out_specs=[anywhere] * 3,
        scratch_shapes=[
            pltpu.VMEM((total, TILE), LOW), buffer, buffer, pltpu.VMEM(ff.shape, LOW),
            pltpu.VMEM(y.shape, jnp.float32), pltpu.VMEM(y.shape, LOW), *tail,
            pltpu.SemaphoreType.DMA((count, 2 * bits)),
            pltpu.SemaphoreType.DMA((count, 2 * bits)),
            pltpu.SemaphoreType.DMA((6,)),
            pltpu.SemaphoreType.DMA((count,)),
            pltpu.SemaphoreType.DMA((count, bits + 1)),
        ],
        compiler_params=params(60, collective_id=1, has_side_effects=True),
        name="all_sum",
    )(code, gate, rank, ff, y, *xs)


def local(
    tokens, lengths, expert_ids, slots, w_query, w_key, w_value, w_output,
    gain_attn, gain_ffn, bias_table, w_router, w_in, w_out, cotangent,
):
    rows, seq, width = tokens.shape
    count = rows * seq
    buckets, heads = bias_table.shape
    head = width // heads
    experts = w_router.shape[1]
    devices = lax.axis_size(AXES)
    room = max(4, 2 * count // experts)
    me = lax.axis_index(AXES)
    x = tokens.reshape(count, width)
    g = cotangent.reshape(count, width)
    gain_one = gain_attn.reshape(1, width)
    gain_two = gain_ffn.reshape(1, width)
    mine = (jnp.arange(experts, dtype=jnp.int32) == me).astype(jnp.float32).reshape(1, experts)

    segments, cut, extra = plan(room)
    code_r, rank_r, g_out, g_extra = route(expert_ids, slots, g, experts, room)
    g_in = exchange(g_out, devices)
    code_r, gain_one, bias_table = lax.optimization_barrier((code_r, gain_one, bias_table))

    code_c, rank_c, marks = columns(code_r, experts, room)
    normed_t, projected = project(x, gain_one, w_query, w_key, w_value)
    near, far = bias_tiles(bias_table)
    joined, weights = attention_forward(lengths, projected, near, far, rows, seq, heads, head)
    y, gate, *h_out = after_attention(
        joined, x, w_output, gain_two, code_c, w_router, code_r, rank_r,
        g_extra, marks, experts, room,
    )
    code = code_c.reshape(-1)
    expert = code // room
    place = code - expert * room
    rest = jnp.where((code >= 0) & (place >= cut), expert * extra + place - cut, experts * extra)

    def experts_on(h, g_rows, low, high, *more):
        return expert_rows(h, g_rows, mine, w_router, w_in[0], w_out[0], experts, low, high, *more)

    parts, grad_router, ff_more, crowded = [], 0.0, None, None
    if extra:
        h_more, g_more, flag = h_out[-3:]
        h_out = h_out[:-3]
        crowded = flag[0, 0] > 0
        h_more, g_more, g_in = lax.optimization_barrier((h_more, g_more, g_in))

        def exchange_rest(_):
            rms = lax.rsqrt(jnp.mean(y * y, axis=-1, keepdims=True) + EPSILON)
            h = (y * rms * gain_two).astype(LOW)
            empty = jnp.zeros((experts * extra, width), LOW)
            send = lambda a: exchange(empty.at[rest].set(a, mode="drop"), devices)
            return False, send(h), send(g)

        _, h_more, g_more = lax.while_loop(
            lambda held: held[0], exchange_rest, (crowded, h_more, g_more)
        )
        h_out[0], h_more, g_more = lax.optimization_barrier((h_out[0], h_more, g_more))
    h_out, g_in = lax.optimization_barrier((h_out, g_in))
    g_in = g_in.reshape(devices, cut, width)
    h_in = [exchange(h_out[0], devices)]
    for h in h_out[1:]:
        h, h_in[-1] = lax.optimization_barrier((h, h_in[-1]))
        h_in.append(exchange(h, devices))
    ffs, dx_back, dx = [], [], None
    if extra:
        ff_more, dx, hid, da, x_t, dff_t, routed = experts_on(
            h_more, g_more.reshape(devices, extra, width), 0, extra, room - cut, 2 * extra
        )
        ff_more = ff_more.reshape(devices, extra, width)
        parts.append((x_t, dff_t, hid, da))
        grad_router = grad_router + routed
    for m, (low, high) in enumerate(segments):
        held = (0, 2 * extra, dx) if extra and not m else ()
        ff, dx, hid, da, x_t, dff_t, routed = experts_on(h_in[m], g_in, low, high, *held)
        if m + 1 < len(segments):
            dx, h_in[m + 1] = lax.optimization_barrier((dx, h_in[m + 1]))
        if m:
            dx, dx_back[-1] = lax.optimization_barrier((dx, dx_back[-1]))
        dx_back.append(exchange(dx.reshape(-1, width), devices))
        ffs.append(ff.reshape(devices, high - low, width))
        parts.append((x_t, dff_t, hid, da))
        grad_router = grad_router + routed
    grad_in, grad_out = expert_weights(parts)
    grad_router = grad_router.reshape(experts, width // TILE, TILE)
    small = jnp.swapaxes(grad_router, 0, 1).reshape(-1, TILE)
    ff, ff_packed = ffs[0], small
    if extra:
        ff = jnp.concatenate([ffs[1], ffs[0]], axis=1)
        bits = devices.bit_length() - 1
        ff_packed = ff_more.reshape((2,) * bits + (extra, width // TILE, TILE))
        order = tuple(reversed(range(bits))) + (bits + 1, bits, bits + 2)
        ff_packed = jnp.transpose(ff_packed, order).reshape(-1, TILE)
    ff = ff.reshape(devices * cut, width)
    dx_back, grad_in, grad_out, ff, ff_packed, small = lax.optimization_barrier(
        (dx_back, grad_in, grad_out, ff, ff_packed, small)
    )
    ff_back = exchange(ff, devices)

    dy, do, grad_output, grad_gain_two = before_attention(
        dx_back, code_c, y, g, gain_two, w_output, joined, room
    )
    lines = width // TILE
    small_rows = small.shape[0] + -(-2 * lines // 16) * 16 + -(-heads // 16) * 16
    small_rows = -(-small_rows // (16 * devices)) * 16 * devices
    grad_tokens, packed, small = attention_backward(
        projected, do, joined, weights, normed_t, w_query, w_key, w_value, x, dy, gain_one,
        small, grad_gain_two, rows, seq, heads, head, small_rows,
    )
    mixed, summed, small = all_sum(
        [packed.reshape(-1, TILE), grad_output, small], code_c, gate, rank_c, ff_back, y, room, ff_packed
    )
    if extra:

        def mix_all(_):
            spare = exchange(ff_more.reshape(-1, width), devices)
            first = jnp.where((code >= 0) & (place < cut), expert * cut + place, devices * cut)
            take = lambda a, index: jnp.take(a, index, axis=0, mode="fill", fill_value=0)
            ff = take(ff_back, first) + take(spare, rest)
            return False, (y + gate * ff.astype(jnp.float32)).astype(LOW)

        _, mixed = lax.while_loop(lambda held: held[0], mix_all, (crowded, mixed))
    *grads, router_t, gain_grad_one, gain_grad_two, table, mixed = unpack(summed, small, mixed, experts, heads, buckets)
    return (
        mixed.reshape(rows, seq, width),
        grad_tokens.reshape(rows, seq, width),
        *grads,
        gain_grad_one, gain_grad_two, table.T, router_t.T,
        grad_in,
        grad_out,
    )


def solution(mesh):
    split = P(AXES)
    in_specs = (split,) * 4 + (P(),) * 8 + (split,) * 3
    out_specs = (split,) * 2 + (P(),) * 8 + (split,) * 2
    return jax.shard_map(local, mesh=mesh, in_specs=in_specs, out_specs=out_specs, check_vma=False)
```

```python
import functools

import jax
import jax.numpy as jnp
from jax import lax
from jax.experimental import pallas as pl
from jax.experimental.pallas import tpu as pltpu
from jax.sharding import PartitionSpec as P

EPSILON = 1e-06
NEGATIVE = -1e30
THRESHOLDS = (12, 16, 23, 32, 46, 64, 91)
LOG2E = 1.4426950408889634
TILE = 128
GELU_A = 0.7978845608028654
GELU_B = GELU_A * 0.044715
AXES = ("grp", "exp")
LOW = jnp.bfloat16


def dot(a, b):
    return jnp.dot(a, b, preferred_element_type=jnp.float32)


def dot_t(a, b):
    return lax.dot_general(a, b, (((1,), (1,)), ((), ())), preferred_element_type=jnp.float32)


def params(mib, **more):
    return pltpu.CompilerParams(vmem_limit_bytes=mib << 20, **more)


def whole(shape):
    return pl.BlockSpec(shape, lambda *_: (0,) * len(shape), pipeline_mode=pl.Buffered(1))


def cost(flops, bytes_accessed, transcendentals=0):
    return pl.CostEstimate(
        flops=flops, bytes_accessed=bytes_accessed, transcendentals=transcendentals
    )


def bucket_of(offset):
    distance = jnp.abs(offset)
    far = jnp.full_like(distance, 8)
    for border in THRESHOLDS:
        far = far + (distance >= border).astype(jnp.int32)
    return jnp.where(distance < 8, distance, far) + jnp.where(offset > 0, 16, 0).astype(jnp.int32)


def device_place(cores, d):
    return dict(device_id=(lax.div(d, cores), lax.rem(d, cores)), device_id_type=pl.DeviceIdType.MESH)


def partner_of(me, b):
    bit = lax.rem(lax.div(me, 1 << b), 2)
    return bit, me + (1 - 2 * bit) * (1 << b)


def rows_at(start, length):
    return pl.ds(pl.multiple_of(start, 16), length)


def plan(room):
    if room % 64:
        return ((0, room),), room, 0
    half = room // 2
    return ((half, half + room // 4), (0, half)), 3 * room // 4, room // 4


def back_plan(room):
    if room % 64:
        return ((0, room),)
    return ((room // 2, room), (0, room // 2))


def segment(code, room, low, high):
    expert = lax.div(code, room)
    place = code - expert * room
    inside = (code >= 0) & (place >= low) & (place < high)
    return jnp.where(inside, expert * (high - low) + place - low, -1)


def spread(dest, values, out):
    rows = out.shape[0]
    step = min(256, rows)
    for start in range(0, rows, step):
        here = lax.broadcasted_iota(jnp.int32, (step, dest.shape[1]), 0) + start
        out[start : start + step] = dot((dest == here).astype(LOW), values).astype(LOW)


def collect(dest, values):
    here = lax.broadcasted_iota(jnp.int32, (dest.shape[0], values.shape[0]), 1)
    return dot((dest == here).astype(LOW), values)


def spread_all(code, room, values, outs):
    for (low, high), out in zip(plan(room)[0], outs):
        spread(segment(code, room, low, high), values, out)


def collect_all(code, room, refs):
    total = None
    for (low, high), ref in zip(back_plan(room), refs):
        part = collect(segment(code, room, low, high), ref[...])
        total = part if total is None else total + part
    return total


def buffers(experts, room, width):
    return [
        jax.ShapeDtypeStruct((experts * (high - low), width), LOW) for low, high in plan(room)[0]
    ]


def route_kernel(
    experts, room, eid_ref, slot_ref, g_ref, code_r, rank_r, out, more
):
    tokens = g_ref.shape[0]
    wide = max(TILE, experts)
    _, cut, extra = plan(room)
    at = lax.broadcasted_iota(jnp.int32, (tokens, tokens), 0)
    to = lax.broadcasted_iota(jnp.int32, (tokens, tokens), 1)

    line = lambda ref: jnp.concatenate([ref[i : i + 1] for i in range(ref.shape[0])], axis=1)
    ids = line(eid_ref)
    slots = line(slot_ref)
    picked = ids == lax.broadcasted_iota(jnp.int32, (wide, tokens), 0)
    earlier = dot(picked.astype(LOW), (at < to).astype(LOW))
    place = jnp.sum(jnp.where(picked, earlier, 0.0), axis=0, keepdims=True).astype(jnp.int32)
    kept = slots >= 0
    code = jnp.where(kept, ids * room + place, -1)
    code_r[...] = code
    rank = jnp.where(kept & (place >= cut), place - cut, -1)
    rank_r[...] = rank
    spread(segment(code, room, 0, cut), g_ref[...], out)
    spread(rank, g_ref[...], more)


def columns_kernel(experts, room, code_ref, code_c, rank_c, marks):
    tokens = code_ref.shape[1]
    wide = max(TILE, experts)
    _, cut, _ = plan(room)
    rows = jnp.concatenate([code_ref[...], jnp.zeros((7, tokens), jnp.int32)], axis=0)
    code = rows.astype(jnp.float32).T.astype(jnp.int32)[:, :1]
    code_c[...] = code
    ids = lax.div(code, room)
    place = code - ids * room
    over = (code >= 0) & (place >= cut)
    rank_c[...] = jnp.where(over, place - cut, -1)
    picked = ids == lax.broadcasted_iota(jnp.int32, (tokens, wide), 1)
    named = jnp.max(jnp.where(picked & over, 1.0, 0.0), axis=0, keepdims=True)
    named = jnp.sum(named, axis=1, keepdims=True)
    owner = jnp.max(jnp.where(over, ids + 1, 0).astype(jnp.float32), axis=0, keepdims=True)
    lane = lax.broadcasted_iota(jnp.int32, marks.shape, 1)
    crowded = jnp.where(named > 1.0, 1.0, 0.0)
    marks[...] = jnp.where(lane == 0, owner, jnp.where(lane == 1, crowded, 0.0))


def columns(code, experts, room):
    tokens = code.shape[1]
    column = jax.ShapeDtypeStruct((tokens, 1), jnp.int32)
    return pl.pallas_call(
        functools.partial(columns_kernel, experts, room),
        out_shape=[column, column, jax.ShapeDtypeStruct((8, TILE), jnp.float32)],
        compiler_params=params(32),
        name="columns",
    )(code)


def route(expert_ids, slots, upstream, experts, room):
    tokens, width = upstream.shape
    line = jax.ShapeDtypeStruct((1, tokens), jnp.int32)
    _, cut, extra = plan(room)
    return pl.pallas_call(
        functools.partial(route_kernel, experts, room),
        out_shape=[
            line, line,
            jax.ShapeDtypeStruct((experts * cut, width), LOW),
            jax.ShapeDtypeStruct((max(extra, 16), width), LOW),
        ],
        compiler_params=params(60),
        cost_estimate=cost(2 * experts * room * tokens * width, 8 << 20),
        name="route",
    )(expert_ids, slots, upstream)


def exchange(buffer, devices):
    shaped = buffer.reshape(devices, buffer.shape[0] // devices, buffer.shape[1])
    moved = lax.all_to_all(shaped, AXES, split_axis=0, concat_axis=0, tiled=True)
    return moved.reshape(buffer.shape)


def project_kernel(x_ref, gain_ref, wq_ref, wk_ref, wv_ref, normed_ref, out_ref):
    x = x_ref[...].astype(jnp.float32)
    rms = lax.rsqrt(jnp.mean(x * x, axis=-1, keepdims=True) + EPSILON)
    normed = (x * rms * gain_ref[...]).astype(LOW)
    normed_ref[...] = normed.T
    width = x.shape[1]
    for n, w_ref in enumerate((wq_ref, wk_ref, wv_ref)):
        out_ref[:, n * width : (n + 1) * width] = dot(normed, w_ref[...]).astype(LOW)


def project(x, gain, w_query, w_key, w_value):
    tokens, width = x.shape
    out = 3 * width
    step = 256
    rows = lambda w: pl.BlockSpec((step, w), lambda i: (i, 0))
    return pl.pallas_call(
        project_kernel,
        grid=(tokens // step,),
        in_specs=[rows(width), whole((1, width)), *[whole((width, width))] * 3],
        out_specs=[pl.BlockSpec((width, step), lambda i: (0, i)), rows(out)],
        out_shape=[
            jax.ShapeDtypeStruct((width, tokens), LOW),
            jax.ShapeDtypeStruct((tokens, out), LOW),
        ],
        compiler_params=params(40),
        cost_estimate=cost(2 * tokens * width * out, 12 << 20),
        name="project",
    )(x, gain, w_query, w_key, w_value)


def gather_orders(bits):
    far = tuple(range(3, bits))
    return [[(0,), (1,), (2,), far], [(0,), (2,), far, (1,)], [(0,), far, (1,), (2,)]]


def span(order, s, n):
    for group in order[: s + 1]:
        n >>= len(group)
    return n


def digit_of(d, group):
    if isinstance(d, int):
        return sum(((d >> b) & 1) << i for i, b in enumerate(group))
    return sum(lax.rem(lax.div(d, 1 << b), 2) * (1 << i) for i, b in enumerate(group))


def peer_of(me, group, r):
    for i, b in enumerate(group):
        if (r >> i) & 1:
            me = partner_of(me, b)[1]
    return me


def rank_in(order, d):
    n = 1 << sum(len(group) for group in order)
    return sum(digit_of(d, group) * span(order, s, n) for s, group in enumerate(order))


def after_attention_kernel(
    experts, room, cores, n, o_ref, x_ref, w_ref, gain_ref, eid_ref, wr_ref, code_ref, *rest
):
    segments, _, extra = plan(room)
    if extra:
        rank_ref, g_ref, mark_ref, *rest = rest
    y_ref, gate_ref, *rest = rest
    outs, rest = rest[: len(segments)], rest[len(segments) :]
    if extra:
        h_more, g_more, flag_ref, *rest = rest
        own, moved, marks, send, recv, *rest = rest
    (held,) = rest
    step = o_ref.shape[0]
    i = pl.program_id(0)
    bits = n.bit_length() - 1
    if extra:
        me = lax.axis_index("grp") * cores + lax.axis_index("exp")
        barrier = pltpu.get_barrier_semaphore()
        greeted = [(g, r) for g in gather_orders(bits)[0] for r in range(1, 1 << len(g))]

        @pl.when(i == 0)
        def _():
            for group, r in greeted:
                pl.semaphore_signal(barrier, inc=1, **device_place(cores, peer_of(me, group, r)))

    y = x_ref[...].astype(jnp.float32) + dot(o_ref[...], w_ref[...])
    y_ref[...] = y
    rms = lax.rsqrt(jnp.mean(y * y, axis=-1, keepdims=True) + EPSILON)
    normed = (y * rms * gain_ref[...]).astype(LOW)
    held[pl.ds(pl.multiple_of(i * step, step), step), :] = normed
    router = route_softmax(dot(normed, wr_ref[...]), experts)
    lane = lax.broadcasted_iota(jnp.int32, router.shape, 1)
    expert = lax.div(jnp.maximum(eid_ref[...], 0), room)
    gate_ref[...] = jnp.sum(jnp.where(lane == expert, router, 0.0), axis=-1, keepdims=True)

    @pl.when(i == pl.num_programs(0) - 1)
    def _():
        chunks = []
        for (low, high), out in zip(segments, outs):
            dest = segment(code_ref[...], room, low, high)
            size = min(256, out.shape[0])
            chunks += [(dest, out, start, size) for start in range(0, out.shape[0], size)]

        def spread_some(count):
            for dest, out, start, size in chunks[:count]:
                spread(dest - start, held[...], out.at[start : start + size])
            del chunks[:count]

        if not extra:
            spread_some(len(chunks))
            return
        single, width = g_ref.shape
        block = 2 * single
        orders = gather_orders(bits)
        phases = len(orders[0])
        third = width // 3
        spread(rank_ref[...], held[...], own)
        base = []
        for p, order in enumerate(orders):
            lanes = slice(p * third, (p + 1) * third)
            base.append(rank_in(order, me) * block)
            moved[p, rows_at(base[p], single), :] = own[:, lanes]
            moved[p, rows_at(base[p] + single, single), :] = g_ref[:, lanes]
        tall = mark_ref.shape[0]
        marks[pl.ds(pl.multiple_of(rank_in(orders[0], me) * tall, 8), tall), :] = mark_ref[...]
        pl.semaphore_wait(barrier, len(greeted))

        def doubling(s):
            copies = []
            for p, order in enumerate(orders):
                size = span(order, s, n)
                for r in range(1, 1 << len(order[s])):
                    place = device_place(cores, peer_of(me, order[s], r))
                    here = rows_at(base[p], block * size)
                    copies.append(
                        pltpu.make_async_remote_copy(
                            src_ref=moved.at[p, here], dst_ref=moved.at[p, here],
                            send_sem=send.at[p, s, r - 1], recv_sem=recv.at[p, s, r - 1], **place,
                        )
                    )
                    if p == 0:
                        start = lax.div(base[0], block) * tall
                        here = pl.ds(pl.multiple_of(start, 8), tall * size)
                        copies.append(
                            pltpu.make_async_remote_copy(
                                src_ref=marks.at[here], dst_ref=marks.at[here],
                                send_sem=send.at[3, s, r - 1], recv_sem=recv.at[3, s, r - 1], **place,
                            )
                        )
            for copy in copies:
                copy.start()
            return copies

        sent = []
        for s in reversed(range(phases)):
            copies = doubling(s)
            spread_some(2)
            for copy in copies:
                copy.wait_recv()
            sent += copies
            for p, order in enumerate(orders):
                base[p] = base[p] - digit_of(me, order[s]) * block * span(order, s, n)
        spread_some(len(chunks))
        for copy in sent:
            copy.wait_send()
        for d in range(n):
            here = slice(d * single, (d + 1) * single)
            first = rank_in(orders[0], d) * tall
            keep = marks[first : first + 1, :1] == (me + 1).astype(jnp.float32)
            for p, order in enumerate(orders):
                lanes = slice(p * third, (p + 1) * third)
                at = rank_in(order, d) * block
                for out, start in ((h_more, at), (g_more, at + single)):
                    got = moved[p, start : start + single, :].astype(jnp.float32)
                    out[here, lanes] = jnp.where(keep, got, 0.0).astype(LOW)
        flag_ref[0, 0] = jnp.max(marks[:, 1:2]).astype(jnp.int32)


def after_attention(
    joined, x, w_output, gain, expert_ids, w_router, code, rank, g_extra, marks, experts, room
):
    tokens, width = x.shape
    step = 256
    cores = lax.axis_size("exp")
    n = lax.axis_size(AXES)
    bits = n.bit_length() - 1
    segments, _, extra = plan(room)
    rows = pl.BlockSpec((step, width), lambda i: (i, 0))
    single = pl.BlockSpec((step, 1), lambda i: (i, 0))
    outs = buffers(experts, room, width)
    more, scratch, options, flag = [], [], {}, []
    if extra:
        more = [rank, g_extra, marks]
        outs = outs + [jax.ShapeDtypeStruct((n * extra, width), LOW)] * 2
        flag = [jax.ShapeDtypeStruct((1, 1), jnp.int32)]
        scratch = [
            pltpu.VMEM((extra, width), LOW), pltpu.VMEM((3, 2 * n * extra, width // 3), LOW),
            pltpu.VMEM((8 * n, TILE), jnp.float32),
            pltpu.SemaphoreType.DMA((4, 4, (n >> 3) - 1)), pltpu.SemaphoreType.DMA((4, 4, (n >> 3) - 1)),
        ]
        options = dict(collective_id=2, has_side_effects=True)
    return pl.pallas_call(
        functools.partial(after_attention_kernel, experts, room, cores, n),
        grid=(tokens // step,),
        in_specs=[
            rows, rows, whole((width, width)), whole((1, width)), single, whole(w_router.shape),
            whole((1, tokens)), *[whole(m.shape) for m in more],
        ],
        out_specs=[rows, single]
        + [pl.BlockSpec(o.shape, lambda i: (0, 0)) for o in outs]
        + [pl.BlockSpec(memory_space=pltpu.SMEM)] * len(flag),
        out_shape=[
            jax.ShapeDtypeStruct((tokens, width), jnp.float32),
            jax.ShapeDtypeStruct((tokens, 1), jnp.float32),
        ]
        + outs
        + flag,
        scratch_shapes=scratch + [pltpu.VMEM((tokens, width), LOW)],
        compiler_params=params(60, **options),
        cost_estimate=cost(2 * tokens * width * (width + experts * room), 12 << 20),
        name="after_attention",
    )(joined, x, w_output, gain, expert_ids, w_router, code, *more)


def route_softmax(logits, experts):
    lane = lax.broadcasted_iota(jnp.int32, logits.shape, 1)
    logits = jnp.where(lane < experts, logits, NEGATIVE)
    e = jnp.exp(logits - jnp.max(logits, axis=-1, keepdims=True))
    return e / jnp.sum(e, axis=-1, keepdims=True)


def pack(values, first, height, out, at):
    for c in range(values.shape[1] // TILE):
        out[at + c * height : at + (c + 1) * height] = values[
            first : first + height, c * TILE : (c + 1) * TILE
        ].astype(LOW)


def before_attention_kernel(
    room, n_backs, code_ref, y_ref, g_ref, gain_ref, w_ref, o_ref, *rest
):
    backs = rest[:n_backs]
    dy_ref, do_ref, pack_ref, gg_ref, gw_ref = rest[n_backs:]
    i = pl.program_id(0)

    @pl.when(i == 0)
    def _():
        gw_ref[...] = jnp.zeros_like(gw_ref)
        gg_ref[...] = jnp.zeros_like(gg_ref)

    step = y_ref.shape[0] // 2
    blocks = [slice(n * step, (n + 1) * step) for n in range(2)]
    dhs = [collect_all(code_ref[here, :], room, backs) for here in blocks]
    lows = []
    for here, dh in zip(blocks, dhs):
        y = y_ref[here, :]
        rms = lax.rsqrt(jnp.mean(y * y, axis=-1, keepdims=True) + EPSILON)
        gg_ref[...] += jnp.sum(dh * y * rms, axis=0, keepdims=True)
        u = dh * gain_ref[...]
        dy = (
            g_ref[here, :].astype(jnp.float32)
            + rms * u
            - y * (rms * rms * rms) * jnp.mean(u * y, axis=-1, keepdims=True)
        )
        dy_ref[here, :] = dy
        lows.append(dy.astype(LOW))
        do_ref[here, :] = dot_t(lows[-1], w_ref[...]).astype(LOW)
    gw_ref[...] += dot(o_ref[...].T, jnp.concatenate(lows, axis=0))

    @pl.when(i == pl.num_programs(0) - 1)
    def _():
        pack(gw_ref, 0, gw_ref.shape[0], pack_ref, 0)


def before_attention(backs, code, y, g, gain, w_output, joined, room):
    tokens, width = y.shape
    step = 512
    rows = lambda w: pl.BlockSpec((step, w), lambda i: (i, 0))
    return pl.pallas_call(
        functools.partial(before_attention_kernel, room, len(backs)),
        grid=(tokens // step,),
        in_specs=[
            rows(1), rows(width), rows(width), whole((1, width)),
            whole((width, width)), rows(width), *[whole(b.shape) for b in backs],
        ],
        out_specs=[
            rows(width), rows(width),
            pl.BlockSpec((width * width // TILE, TILE), lambda i: (0, 0)),
            pl.BlockSpec((1, width), lambda i: (0, 0)),
        ],
        out_shape=[
            jax.ShapeDtypeStruct((tokens, width), jnp.float32),
            jax.ShapeDtypeStruct((tokens, width), LOW),
            jax.ShapeDtypeStruct((width * width // TILE, TILE), LOW),
            jax.ShapeDtypeStruct((1, width), jnp.float32),
        ],
        scratch_shapes=[pltpu.VMEM((width, width), jnp.float32)],
        compiler_params=params(60),
        cost_estimate=cost(6 * tokens * width * width, 16 << 20),
        name="before_attention",
    )(code, y, g, gain, w_output, joined, *backs)


def unpack_kernel(
    experts, heads, buckets, q_ref, k_ref, v_ref, o_ref, small_ref, mix_ref,
    gq, gk, gv, go, router, gain_one, gain_two, table, mixed,
):
    mixed[...] = mix_ref[...]
    for packed_ref, out_ref in ((q_ref, gq), (k_ref, gk), (v_ref, gv), (o_ref, go)):
        for c in range(packed_ref.shape[0]):
            out_ref[:, c * TILE : (c + 1) * TILE] = packed_ref[c].astype(jnp.float32)

    @pl.when(pl.program_id(0) == 0)
    def _():
        lines = router.shape[1] // TILE
        small = small_ref[...].astype(jnp.float32)
        for c in range(lines):
            lanes = slice(c * TILE, (c + 1) * TILE)
            router[:, lanes] = small[c * experts : (c + 1) * experts]
            for n, gain in enumerate((gain_one, gain_two)):
                gain[lanes] = small[lines * experts + n * lines + c]
        at = lines * experts + -(-2 * lines // 16) * 16
        table[...] = small[at : at + heads, :buckets]


def unpack(packed, small, mixed, experts, heads, buckets):
    tokens, width = mixed.shape
    blocks = width // TILE
    steps = 4
    source = lambda m: pl.BlockSpec((blocks, width // steps, TILE), lambda i: (m, i, 0))
    rows = lambda count: pl.BlockSpec((count // steps, width), lambda i: (i, 0))
    kept = lambda shape: pl.BlockSpec(shape, lambda i: (0, 0))
    flat = pl.BlockSpec((width,), lambda i: (0,))
    return pl.pallas_call(
        functools.partial(unpack_kernel, experts, heads, buckets),
        grid=(steps,),
        in_specs=[source(m) for m in range(4)] + [whole(small.shape), rows(tokens)],
        out_specs=[rows(width)] * 4
        + [kept((experts, width)), flat, flat, kept((heads, buckets)), rows(tokens)],
        out_shape=[jax.ShapeDtypeStruct((width, width), jnp.float32)] * 4
        + [
            jax.ShapeDtypeStruct((experts, width), jnp.float32),
            jax.ShapeDtypeStruct((width,), jnp.float32),
            jax.ShapeDtypeStruct((width,), jnp.float32),
            jax.ShapeDtypeStruct((heads, buckets), jnp.float32),
            jax.ShapeDtypeStruct((tokens, width), LOW),
        ],
        compiler_params=params(60),
        name="unpack",
    )(*[packed.reshape(4 * blocks, width, TILE)] * 4, small, mixed)


def attention_forward_kernel(len_ref, q_ref, k_ref, v_ref, near_ref, far_ref, o_ref, p_ref, s_ref):
    seq = q_ref.shape[0]
    tiles = seq // TILE
    half = q_ref.shape[1] // 2
    row = pl.program_id(0)
    pair = pl.program_id(1)
    live = len_ref[row]
    lane = lax.broadcasted_iota(jnp.int32, (seq, 2 * half), 1)
    dead = lax.broadcasted_iota(jnp.int32, (seq, 2 * half), 0) >= live
    q = q_ref[...]
    k = k_ref[...]
    v_t = v_ref[...].T
    outs = []
    for h in range(2):
        mine = (lane >= h * half) & (lane < (h + 1) * half)
        flag = lane == (1 - h) * half
        k_h = jnp.where(mine, k, jnp.where(flag & dead, -1e30, 0.0).astype(k.dtype))
        q_h = jnp.where(flag, jnp.ones_like(q), q)
        after = far_ref[2 * pair + h, 0]
        before = far_ref[2 * pair + h, 1]
        tops = []
        for i in range(0, tiles, 2):
            q_i = q_h[i * TILE : (i + 2) * TILE]
            raw = dot_t(k_h, q_i)
            for c in range(2):
                cols = slice((i + c) * TILE, (i + c + 1) * TILE)
                top = None
                for j in range(tiles):
                    x = raw[j * TILE : (j + 1) * TILE, c * TILE : (c + 1) * TILE] * (0.125 * LOG2E)
                    d = j - i - c
                    if -1 <= d <= 1:
                        x = x + near_ref[h, d + 1]
                    else:
                        x = x + (after if d > 0 else before)
                    s_ref[h, j * TILE : (j + 1) * TILE, cols] = x
                    m = jnp.max(x, axis=0, keepdims=True)
                    top = m if top is None else jnp.maximum(top, m)
                tops.append(top)
        for i in range(tiles):
            e = jnp.exp2(s_ref[h, :, i * TILE : (i + 1) * TILE] - tops[i])
            total = jnp.sum(e, axis=0, keepdims=True)
            p_ref[0, h, :, i * TILE : (i + 1) * TILE] = (e * (1.0 / total)).astype(LOW)
        outs.append(lax.dot_general(v_t[h * half:(h + 1) * half], p_ref[0, h], (((1,), (0,)), ((), ())), preferred_element_type=jnp.float32))
    o_ref[...] = jnp.concatenate(outs, axis=0).T.astype(o_ref.dtype)

def attention_forward(lengths, projected, near, far, rows, seq, heads, head):
    width = heads * head
    pairs = heads // 2
    spec = lambda off: pl.BlockSpec((seq, 2 * head), lambda b, p: (b, off + p))
    return pl.pallas_call(
        attention_forward_kernel,
        grid=(rows, pairs),
        in_specs=[
            pl.BlockSpec(memory_space=pltpu.SMEM),
            spec(0), spec(pairs), spec(2 * pairs),
            pl.BlockSpec((2, 3, TILE, TILE), lambda b, p: (p, 0, 0, 0)),
            pl.BlockSpec(memory_space=pltpu.SMEM),
        ],
        out_specs=[
            pl.BlockSpec((seq, 2 * head), lambda b, p: (b, p)),
            pl.BlockSpec((1, 2, seq, seq), lambda b, p: (b, p, 0, 0)),
        ],
        out_shape=[
            jax.ShapeDtypeStruct((rows * seq, width), LOW),
            jax.ShapeDtypeStruct((rows, heads, seq, seq), LOW),
        ],
        scratch_shapes=[pltpu.VMEM((2, seq, seq), jnp.float32)],
        compiler_params=params(40),
        cost_estimate=cost(flops=4 * rows * heads * seq * seq * head * 4, bytes_accessed=rows * heads * seq * seq * 2, transcendentals=rows * heads * seq * seq),
        name="attention_forward",
    )(lengths, projected, projected, projected, near, far)

def attention_backward_kernel(
    rows, q_ref, k_ref, v_ref, do_ref, o_ref, p_ref, nt_ref, wq_ref, wk_ref, wv_ref, x_ref, dy_ref, gain_ref,
    gr_ref, gg2_ref, out_ref, pack_ref, small_ref,
    near_ref, far_ref, d_ref, lines_ref, dh_ref,
):
    seq = q_ref.shape[0] // rows
    tiles = seq // TILE
    half = q_ref.shape[1] // 2
    width = x_ref.shape[1]
    pair = pl.program_id(0)
    last_pair = pair == pl.num_programs(0) - 1
    lane = lax.broadcasted_iota(jnp.int32, (seq, 2 * half), 1)
    weights = jnp.concatenate([wq_ref[...], wk_ref[...], wv_ref[...]], axis=1)
    near_ref[...] = jnp.zeros_like(near_ref)
    for row in range(rows):
        here = slice(row * seq, (row + 1) * seq)
        v = v_ref[here, :]
        do = do_ref[here, :]
        weighed = (do.astype(jnp.float32) * o_ref[here, :].astype(jnp.float32)).T
        for h in range(2):
            mine = (lane >= h * half) & (lane < (h + 1) * half)
            v_h = jnp.where(mine, v, jnp.zeros_like(v))
            delta = jnp.sum(weighed[h * half : (h + 1) * half], axis=0, keepdims=True)
            far_sum = [jnp.zeros((8, TILE), jnp.float32), jnp.zeros((8, TILE), jnp.float32)]
            for i in range(0, tiles, 2):
                dp = dot_t(v_h, do[i * TILE : (i + 2) * TILE])
                for c in range(2):
                    cols = slice((i + c) * TILE, (i + c + 1) * TILE)
                    for j in range(tiles):
                        rws = slice(j * TILE, (j + 1) * TILE)
                        part = dp[rws, c * TILE : (c + 1) * TILE] - delta[:, cols]
                        ds = p_ref[row, h, rws, cols].astype(jnp.float32) * part
                        d = j - i - c
                        if -1 <= d <= 1:
                            near_ref[row, h, d + 1] += ds
                        else:
                            which = 0 if d > 0 else 1
                            far_sum[which] = far_sum[which] + jnp.sum(
                                ds.reshape(TILE // 8, 8, TILE), axis=0
                            )
                        d_ref[row, h, rws, cols] = ds.astype(LOW)
            for which in range(2):
                far_ref[row, h, which] = far_sum[which]
    grads_all = []
    for row in range(rows):
        here = slice(row * seq, (row + 1) * seq)
        q = q_ref[here, :]
        do = do_ref[here, :]
        k_t = k_ref[here, :].T
        dq_parts = []
        dk_all = None
        dv_all = None
        for h in range(2):
            mine = (lane >= h * half) & (lane < (h + 1) * half)
            ds_all = d_ref[row, h]
            dq_parts.append(dot(k_t[h * half : (h + 1) * half], ds_all))
            dk_h = dot(ds_all, q)
            dv_h = dot(p_ref[row, h], do)
            dk_all = dk_h if h == 0 else jnp.where(mine, dk_h, dk_all)
            dv_all = dv_h if h == 0 else jnp.where(mine, dv_h, dv_all)
        dq = (jnp.concatenate(dq_parts, axis=0).T * 0.125).astype(LOW)
        grads_all.append(
            jnp.concatenate([dq, (dk_all * 0.125).astype(LOW), dv_all.astype(LOW)], axis=1)
        )
    grads = jnp.concatenate(grads_all, axis=0)
    acc = dot(nt_ref[...], grads)
    for n in range(3):
        pack_ref[n, 0] = acc[:, n * TILE : (n + 1) * TILE].astype(LOW)
    dh = dot_t(grads, weights)

    @pl.when(pair == 0)
    def _():
        dh_ref[...] = dh

    @pl.when(pair > 0)
    def _():
        dh_ref[...] += dh

    near_ref[0] = sum(near_ref[row] for row in range(rows))
    far_ref[0] = sum(far_ref[row] for row in range(rows))
    bucket_sums(near_ref.at[0], far_ref.at[0], lines_ref, 2 * pair)

    @pl.when(last_pair)
    def _():
        total = dh_ref[...]
        x = x_ref[...].astype(jnp.float32)
        rms = lax.rsqrt(jnp.mean(x * x, axis=-1, keepdims=True) + EPSILON)
        gg = jnp.sum(total * x * rms, axis=0, keepdims=True)
        u = total * gain_ref[...]
        out_ref[...] = (
            dy_ref[...]
            + rms * u
            - x * (rms * rms * rms) * jnp.mean(u * x, axis=-1, keepdims=True)
        )
        at = gr_ref.shape[0]
        small_ref[:at] = gr_ref[...].astype(LOW)
        lines = width // TILE
        gains = [gg[:, c * TILE : (c + 1) * TILE] for c in range(lines)]
        gains += [gg2_ref[:, c * TILE : (c + 1) * TILE] for c in range(lines)]
        if 2 * lines % 16:
            gains += [jnp.zeros((16 - 2 * lines % 16, TILE), jnp.float32)]
        gains = jnp.concatenate(gains, axis=0)
        small_ref[at : at + gains.shape[0]] = gains.astype(LOW)
        at = at + gains.shape[0]
        table = bucket_table(lines_ref)
        if table.shape[0] % 16:
            table = jnp.concatenate([table, jnp.zeros((16 - table.shape[0] % 16, TILE), jnp.float32)], axis=0)
        small_ref[at : at + table.shape[0]] = table.astype(LOW)
        at = at + table.shape[0]
        small_ref[at:] = jnp.zeros((small_ref.shape[0] - at, TILE), LOW)


def bucket_sums(near_ref, far_ref, lines_ref, first):
    empty = jnp.zeros((8, TILE), jnp.float32)
    sub = lax.broadcasted_iota(jnp.int32, (8, 2 * TILE), 0)
    for h in range(2):
        lines = []
        for d in range(3):
            turned = None
            for a in range(0, TILE, 8):
                part = jnp.concatenate([near_ref[h, d, a : a + 8], empty], axis=1)
                part = pltpu.roll(part, (2 * TILE - a) % (2 * TILE), 1) if a else part
                turned = part if turned is None else turned + part
            for b in (1, 2, 4):
                turned = jnp.where((sub & b) > 0, pltpu.roll(turned, 2 * TILE - b, 1), turned)
            lines.append(jnp.sum(turned, axis=0, keepdims=True))
        for side in range(2):
            total = jnp.sum(far_ref[h, side], axis=0, keepdims=True)
            lines.append(jnp.concatenate([total, jnp.zeros((1, TILE), jnp.float32)], axis=1))
        lines.append(jnp.zeros((3, 2 * TILE), jnp.float32))
        lines_ref[first + h] = jnp.concatenate(lines, axis=0)


def bucket_table(lines_ref):
    heads = lines_ref.shape[0]
    buckets = 4 * 8
    lane = lax.broadcasted_iota(jnp.int32, (2 * TILE, TILE), 0)
    bucket = lax.broadcasted_iota(jnp.int32, (2 * TILE, TILE), 1)
    turn = jnp.where(lane >= TILE, lane - 2 * TILE, lane)
    total = None
    for r in range(5):
        if r < 3:
            hit = bucket_of((r - 1) * TILE - turn) == bucket
        else:
            hit = bucket == (buckets - 1 if r == 3 else buckets // 2 - 1)
        hit = hit.astype(LOW)
        line = jnp.concatenate([lines_ref[h, r : r + 1, :] for h in range(heads)], axis=0)
        high = line.astype(LOW)
        part = dot(high, hit) + dot((line - high.astype(jnp.float32)).astype(LOW), hit)
        total = part if total is None else total + part
    return total


def attention_backward(
    projected, do, joined, weights, normed_t, w_query, w_key, w_value, x, dy, gain, gr, gg2,
    rows, seq, heads, head, small_rows,
):
    width = heads * head
    pairs = heads // 2
    tokens = rows * seq
    spec = lambda off: pl.BlockSpec((tokens, 2 * head), lambda p: (0, off + p))
    column = pl.BlockSpec((width, 2 * head), lambda p: (0, p))
    return pl.pallas_call(
        functools.partial(attention_backward_kernel, rows),
        grid=(pairs,),
        in_specs=[
            spec(0), spec(pairs), spec(2 * pairs), spec(0), spec(0),
            pl.BlockSpec((rows, 2, seq, seq), lambda p: (0, p, 0, 0)),
            whole((width, tokens)),
            column, column, column, whole((tokens, width)), whole((tokens, width)),
            whole((1, width)), whole(gr.shape), whole(gg2.shape),
        ],
        out_specs=[
            pl.BlockSpec((tokens, width), lambda p: (0, 0)),
            pl.BlockSpec((3, 1, width, TILE), lambda p: (0, p, 0, 0)),
            pl.BlockSpec((small_rows, TILE), lambda p: (0, 0)),
        ],
        out_shape=[
            jax.ShapeDtypeStruct((tokens, width), jnp.float32),
            jax.ShapeDtypeStruct((3, pairs, width, TILE), LOW),
            jax.ShapeDtypeStruct((small_rows, TILE), LOW),
        ],
        scratch_shapes=[
            pltpu.VMEM((rows, 2, 3, TILE, TILE), jnp.float32),
            pltpu.VMEM((rows, 2, 2, 8, TILE), jnp.float32),
            pltpu.VMEM((rows, 2, seq, seq), LOW),
            pltpu.VMEM((heads, 8, 2 * TILE), jnp.float32),
            pltpu.VMEM((tokens, width), jnp.float32),
        ],
        compiler_params=params(60),
        cost_estimate=cost(8 * rows * heads * seq * seq * head * 4, rows * heads * seq * seq * 2),
        name="attention_backward",
    )(
        projected, projected, projected, do, joined, weights, normed_t, w_query, w_key, w_value,
        x, dy, gain, gr, gg2,
    )


def bias_tiles(table):
    j = lax.broadcasted_iota(jnp.int32, (3, TILE, TILE), 1)
    i = lax.broadcasted_iota(jnp.int32, (3, TILE, TILE), 2)
    d = lax.broadcasted_iota(jnp.int32, (3, TILE, TILE), 0) - 1
    b = bucket_of(d * TILE + j - i)
    scaled = table.T * LOG2E
    hot = (b.reshape(1, -1) == jnp.arange(table.shape[0], dtype=jnp.int32)[:, None]).astype(jnp.float32)
    near = jnp.dot(scaled, hot, precision=lax.Precision.HIGHEST).reshape(-1, 3, TILE, TILE)
    far = jnp.stack([scaled[:, -1], scaled[:, table.shape[0] // 2 - 1]], axis=1)
    return near, far


def expert_kernel(experts, chunk, held, x_ref, g_ref, mine_ref, wr_ref, wi_any, wo_any, *refs):
    ff_ref, dx_ref, hid_ref, da_ref, xt_ref, dfft_ref, gr_ref, wi_ref, wo_ref, sem = refs[held:]
    inner = wi_ref.shape[1]
    first_step = pl.program_id(0) == 0

    def loads(f):
        cols = pl.ds(f, chunk)
        return (pltpu.make_async_copy(wi_any.at[:, cols], wi_ref.at[:, cols], sem.at[0, f // chunk]),
                pltpu.make_async_copy(wo_any.at[cols, :], wo_ref.at[cols, :], sem.at[1, f // chunk]))

    @pl.when(first_step)
    def _():
        for f in range(0, inner, chunk):
            for c in loads(f):
                c.start()
        gr_ref[...] = jnp.zeros_like(gr_ref)

    x = x_ref[...]
    g = g_ref[...].reshape(x.shape).astype(jnp.float32)
    mine = mine_ref[...]
    lane = lax.broadcasted_iota(jnp.int32, (1, wr_ref.shape[1]), 1)
    logits = jnp.dot(x, wr_ref[...], preferred_element_type=jnp.float32)
    logits = jnp.where(lane < experts, logits, -1e30)
    e = jnp.exp(logits - jnp.max(logits, axis=-1, keepdims=True))
    router = e / jnp.sum(e, axis=-1, keepdims=True)
    gate = jnp.sum(router * mine, axis=-1, keepdims=True)
    dff = (g * gate).astype(LOW)
    ff = None
    dx = None
    def first(f):
        @pl.when(first_step)
        def _():
            for c in loads(f):
                c.wait()
        cols = slice(f, f + chunk)
        return (jnp.dot(x, wi_ref[:, cols], preferred_element_type=jnp.float32),
                lax.dot_general(dff, wo_ref[cols, :], (((1,), (1,)), ((), ())), preferred_element_type=jnp.float32))
    for f in range(0, inner, chunk):
        cols = slice(f, f + chunk)
        a, dhid = first(f)
        u = a * a
        t = jnp.tanh(a * (GELU_A + GELU_B * u))
        h = 0.5 + 0.5 * t
        hid = a * h
        slope = h + hid * ((1.0 - t) * (GELU_A + (3.0 * GELU_B) * u))
        da = (dhid * slope).astype(LOW)
        hid = hid.astype(LOW)
        hid_ref[:, cols] = hid
        da_ref[:, cols] = da
        ff_part = jnp.dot(hid, wo_ref[cols, :], preferred_element_type=jnp.float32)
        dx_part = lax.dot_general(da, wi_ref[:, cols], (((1,), (1,)), ((), ())), preferred_element_type=jnp.float32)
        ff = ff_part if ff is None else ff + ff_part
        dx = dx_part if dx is None else dx + dx_part
    ff = ff.astype(LOW)
    ff_ref[...] = ff
    dgate = jnp.sum(g * ff.astype(jnp.float32), axis=-1, keepdims=True)
    dlogits = ((gate * dgate) * (mine - router)).astype(LOW)
    dx = dx + lax.dot_general(dlogits, wr_ref[...], (((1,), (1,)), ((), ())), preferred_element_type=jnp.float32)
    dx_ref[...] = dx.astype(LOW).reshape(dx_ref.shape)
    x_t = x.T
    xt_ref[...] = x_t
    dfft_ref[...] = dff.T
    gr_ref[...] += dot(dlogits.T, x)

def expert_rows(x, g, mine, wr, wi, wo, experts, low, high, at=0, total=0, dx=None, tile=256, chunk=768):
    n, width = x.shape
    inner = wi.shape[1]
    sources, room = g.shape[0], high - low
    total = total or room
    group = max(1, min(sources, tile // room))
    while sources % group or (group * room) % TILE:
        group += 1
    tile = group * room
    once = lambda s: pl.BlockSpec(s, lambda i: (0,) * len(s), pipeline_mode=pl.Buffered(1))
    rowspec = lambda w: pl.BlockSpec((tile, w), lambda i: (i, 0))
    column = pl.BlockSpec((width, tile), lambda i: (0, i))
    anywhere = pl.BlockSpec(memory_space=pl.ANY)
    held = [] if dx is None else [dx]
    return pl.pallas_call(
        functools.partial(expert_kernel, experts, chunk, len(held)),
        grid=(n // tile,),
        in_specs=[
            rowspec(width), pl.BlockSpec((group, room, width), lambda i: (i, low // room, 0)),
            once(mine.shape), once(wr.shape), anywhere, anywhere, *[anywhere] * len(held),
        ],
        out_specs=[
            rowspec(width), pl.BlockSpec((group, room, width), lambda i: (i, at // room, 0)),
            rowspec(inner), rowspec(inner), column, column,
            pl.BlockSpec((wr.shape[1], width), lambda i: (0, 0)),
        ],
        out_shape=[
            jax.ShapeDtypeStruct((n, width), LOW),
            jax.ShapeDtypeStruct((sources, total, width), LOW),
            *[jax.ShapeDtypeStruct((n, inner), LOW)] * 2,
            *[jax.ShapeDtypeStruct((width, n), LOW)] * 2,
            jax.ShapeDtypeStruct((wr.shape[1], width), jnp.float32),
        ],
        scratch_shapes=[
            pltpu.VMEM(wi.shape, LOW), pltpu.VMEM(wo.shape, LOW),
            pltpu.SemaphoreType.DMA((2, inner // chunk)),
        ],
        input_output_aliases={6: 1} if held else {},
        compiler_params=params(60),
        cost_estimate=cost(8 * n * width * inner, 4 * n * inner + 8 * width * inner, n * inner),
        name="expert_rows",
    )(x, g, mine, wr, wi, wo, *held)


def expert_weights_kernel(parts, *refs):
    ins, (gi_ref, go_ref) = refs[: 4 * parts], refs[4 * parts :]
    gi = None
    go = None
    for c in range(parts):
        xt, dfft, hid, da = ins[4 * c : 4 * c + 4]
        gi_c = dot(xt[...], da[...])
        go_c = dot(dfft[...], hid[...])
        gi = gi_c if gi is None else gi + gi_c
        go = go_c if go is None else go + go_c
    gi_ref[0] = gi
    go_ref[0] = go.T


def expert_weights(parts, tile=512):
    inner = parts[0][2].shape[1]
    width = parts[0][0].shape[0]
    specs, args, rows = [], [], 0
    for xt, dfft, hid, da in parts:
        n = hid.shape[0]
        rows += n
        specs += [pl.BlockSpec((width, n), lambda f: (0, 0), pipeline_mode=pl.Buffered(1))] * 2
        specs += [pl.BlockSpec((n, tile), lambda f: (0, f))] * 2
        args += [xt, dfft, hid, da]
    return pl.pallas_call(
        functools.partial(expert_weights_kernel, len(parts)),
        grid=(inner // tile,),
        in_specs=specs,
        out_specs=[
            pl.BlockSpec((1, width, tile), lambda f: (0, 0, f)),
            pl.BlockSpec((1, tile, width), lambda f: (0, f, 0)),
        ],
        out_shape=[
            jax.ShapeDtypeStruct((1, width, inner), jnp.float32),
            jax.ShapeDtypeStruct((1, inner, width), jnp.float32),
        ],
        compiler_params=params(60),
        cost_estimate=cost(4 * rows * width * inner, 4 * rows * inner + 8 * width * inner),
        name="expert_weights",
    )(*args)


def split_units(units, weights):
    total, sizes, done, so_far = sum(weights), [], 0, 0
    for w in weights:
        so_far += w
        end = (2 * units * so_far + total) // (2 * total)
        sizes.append(end - done)
        done = end
    return sizes


def sum_parts(n, heights):
    bits = n.bit_length() - 1
    upper = list(range(1, bits))
    orders = [[0] + upper[t:] + upper[:t] for t in range(3)]
    parts, first = [], 0
    for ref, rows in enumerate(heights):
        units = rows // (16 * n)
        turns = (0, 1, 2, 0, 1, 2) if units >= 18 else (0, 1, 2) if units >= 6 else (2,)
        at = 0
        for t, size in zip(turns, split_units(units, [(5, 5, 3)[t] for t in turns])):
            parts.append((ref, at * 16 * n, first, size * 16, orders[t]))
            at += size
            first += size * 16 * n
    return bits, parts


def sum_kernel(cores, n, room, heights, extra, code_ref, gate_ref, rank_ref, ff_any, y_any, *refs):
    _, cut, _ = plan(room)
    xs, refs = refs[: len(heights)], refs[len(heights) :]
    mixed_any, sum_any, small_any, out_ref, work_ref, got_ref, ff_ref, y_ref, mixed_ref, *refs = refs
    if extra:
        tail_ref, *refs = refs
    send, recv, local, load, store = refs
    loads = [
        pltpu.make_async_copy(ff_any, ff_ref, local.at[0]),
        pltpu.make_async_copy(y_any, y_ref, local.at[1]),
    ]
    summed = heights[:-1] if extra else heights
    bits, parts = sum_parts(n, summed)
    full = len(parts)
    if extra:
        parts = parts + [(len(summed), 0, sum(summed), heights[-1] // n, list(range(bits)))]
    me = lax.axis_index("grp") * cores + lax.axis_index("exp")
    base = [first for _, _, first, _, _ in parts]
    got_at = list(base)
    kept = []
    for p, (ref, at, first, step, order) in enumerate(parts):
        length = step * (n >> 1)
        start = base[p] + partner_of(me, order[0])[0] * length
        kept.append(
            pltpu.make_async_copy(
                xs[ref].at[rows_at(start - first + at, length)],
                work_ref.at[rows_at(start, length)],
                load.at[p],
            )
        )
        kept[p].start()
    for copy in loads:
        copy.start()
    barrier = pltpu.get_barrier_semaphore()
    for b in range(bits):
        pl.semaphore_signal(barrier, inc=1, **device_place(cores, partner_of(me, b)[1]))
    pl.semaphore_wait(barrier, bits)

    def halving(p, s):
        ref, at, first, step, order = parts[p]
        length = step * (n >> (s + 1))
        bit, partner = partner_of(me, order[s])
        start = base[p] + (1 - bit) * length
        if s == 0:
            source = xs[ref].at[rows_at(start - first + at, length)]
        else:
            source = work_ref.at[rows_at(start, length)]
        return pltpu.make_async_remote_copy(
            src_ref=source, dst_ref=got_ref.at[rows_at(got_at[p], length)],
            send_sem=send.at[p, s], recv_sem=recv.at[p, s], **device_place(cores, partner),
        )

    def doubling(p, s):
        _, _, _, step, order = parts[p]
        here = rows_at(base[p], step * (n >> (s + 1)))
        return pltpu.make_async_remote_copy(
            src_ref=out_ref.at[here], dst_ref=out_ref.at[here],
            send_sem=send.at[p, bits + s], recv_sem=recv.at[p, bits + s],
            **device_place(cores, partner_of(me, order[s])[1]),
        )

    main = sum(summed[:-1])

    def keep_out(p, s, start, length):
        here = rows_at(start, length)
        target = sum_any.at[here]
        if parts[p][0] == len(summed) - 1:
            target = small_any.at[rows_at(start - main, length)]
        copy = pltpu.make_async_copy(out_ref.at[here], target, store.at[p, s])
        copy.start()
        return copy

    tokens, width = mixed_ref.shape
    tile = tokens // 4
    tiles = [slice(i * tile, (i + 1) * tile) for i in range(4)]

    def mix_most():
        for copy in loads:
            copy.wait()
        for here in tiles:
            ff = collect(segment(code_ref[here, :], room, 0, cut), ff_ref[...])
            y_ref[here, :] += gate_ref[here, :] * ff

    def mix_rest():
        stores = []
        for i, here in enumerate(tiles):
            total = y_ref[here, :]
            if extra:
                tail = tail_ref[...]
                tail = [tail[c * extra : (c + 1) * extra] for c in range(width // TILE)]
                more = collect(rank_ref[here, :], jnp.concatenate(tail, axis=1))
                total = total + gate_ref[here, :] * more
            mixed_ref[here, :] = total.astype(LOW)
            stores.append(
                pltpu.make_async_copy(mixed_ref.at[here], mixed_any.at[here], local.at[2 + i])
            )
            stores[i].start()
        return stores

    moving = [halving(p, 0) for p in range(len(parts))]
    for copy in moving:
        copy.start()
    sent, stores = [], []
    for s in range(bits):
        if s == 1:
            mix_most()
        for p, (ref, at, first, step, order) in enumerate(parts):
            length = step * (n >> (s + 1))
            if s == 0:
                kept[p].wait()
            moving[p].wait_recv()
            sent.append(moving[p])
            base[p] = base[p] + partner_of(me, order[s])[0] * length
            last = s + 1 == bits
            target = out_ref if last else work_ref
            if p >= full and last:
                target = tail_ref

            def add(
                i, _, start=base[p], target=target, arrived=got_at[p], step=step,
                to=0 if p >= full and last else base[p],
            ):
                got = got_ref[rows_at(arrived + i * step, step), :].astype(jnp.float32)
                mine = work_ref[rows_at(start + i * step, step), :].astype(jnp.float32)
                target[rows_at(to + i * step, step), :] = (mine + got).astype(LOW)
                return 0

            lax.fori_loop(0, length // step, add, 0)
            got_at[p] += length
            if not last:
                moving[p] = halving(p, s + 1)
                moving[p].start()
            elif p < full:
                moving[p] = doubling(p, s)
                moving[p].start()
                stores.append(keep_out(p, bits, base[p], step))
    for copy in sent:
        copy.wait_send()
    sent = []
    for s in reversed(range(bits)):
        if s == min(1, bits - 1):
            stores += mix_rest()
        for p, (ref, at, first, step, order) in enumerate(parts[:full]):
            length = step * (n >> (s + 1))
            moving[p].wait_recv()
            sent.append(moving[p])
            bit = partner_of(me, order[s])[0]
            arrived = base[p] + (1 - 2 * bit) * length
            base[p] = base[p] - bit * length
            if s > 0:
                moving[p] = doubling(p, s - 1)
                moving[p].start()
            stores.append(keep_out(p, s, arrived, length))
    for copy in sent:
        copy.wait_send()
    for copy in stores:
        copy.wait()


def all_sum(xs, code, gate, rank, ff, y, room, ff_more):
    cores = lax.axis_size("exp")
    n = lax.axis_size(AXES)
    extra = plan(room)[2]
    heights = [a.shape[0] for a in xs]
    if any(h % (16 * n) for h in heights):
        xs = [jnp.concatenate(xs[:-1], axis=0), xs[-1]]
        heights = [a.shape[0] for a in xs]
    total, small = sum(heights), heights[-1]
    bits, parts = sum_parts(n, heights)
    count = len(parts)
    rows = total
    tokens, width = y.shape
    tail = []
    if extra:
        xs = xs + [ff_more]
        heights = heights + [ff_more.shape[0]]
        rows += ff_more.shape[0]
        count += 1
        tail = [pltpu.VMEM((extra * width // TILE, TILE), LOW)]
    buffer = pltpu.VMEM((rows, TILE), LOW)
    vmem = pl.BlockSpec(memory_space=pltpu.VMEM)
    anywhere = pl.BlockSpec(memory_space=pl.ANY)
    return pl.pallas_call(
        functools.partial(sum_kernel, cores, n, room, heights, extra),
        out_shape=[
            jax.ShapeDtypeStruct((tokens, width), LOW),
            jax.ShapeDtypeStruct((total - small, TILE), LOW),
            jax.ShapeDtypeStruct((small, TILE), LOW),
        ],
        in_specs=[vmem] * 3 + [anywhere] * (2 + len(xs)),
        out_specs=[anywhere] * 3,
        scratch_shapes=[
            pltpu.VMEM((total, TILE), LOW), buffer, buffer, pltpu.VMEM(ff.shape, LOW),
            pltpu.VMEM(y.shape, jnp.float32), pltpu.VMEM(y.shape, LOW), *tail,
            pltpu.SemaphoreType.DMA((count, 2 * bits)),
            pltpu.SemaphoreType.DMA((count, 2 * bits)),
            pltpu.SemaphoreType.DMA((6,)),
            pltpu.SemaphoreType.DMA((count,)),
            pltpu.SemaphoreType.DMA((count, bits + 1)),
        ],
        compiler_params=params(60, collective_id=1, has_side_effects=True),
        name="all_sum",
    )(code, gate, rank, ff, y, *xs)


def local(
    tokens, lengths, expert_ids, slots, w_query, w_key, w_value, w_output,
    gain_attn, gain_ffn, bias_table, w_router, w_in, w_out, cotangent,
):
    rows, seq, width = tokens.shape
    count = rows * seq
    buckets, heads = bias_table.shape
    head = width // heads
    experts = w_router.shape[1]
    devices = lax.axis_size(AXES)
    room = max(4, 2 * count // experts)
    me = lax.axis_index(AXES)
    x = tokens.reshape(count, width)
    g = cotangent.reshape(count, width)
    gain_one = gain_attn.reshape(1, width)
    gain_two = gain_ffn.reshape(1, width)
    mine = (jnp.arange(experts, dtype=jnp.int32) == me).astype(jnp.float32).reshape(1, experts)

    segments, cut, extra = plan(room)
    code_r, rank_r, g_out, g_extra = route(expert_ids, slots, g, experts, room)
    g_in = exchange(g_out, devices)
    code_r, gain_one, bias_table = lax.optimization_barrier((code_r, gain_one, bias_table))

    code_c, rank_c, marks = columns(code_r, experts, room)
    normed_t, projected = project(x, gain_one, w_query, w_key, w_value)
    near, far = bias_tiles(bias_table)
    joined, weights = attention_forward(lengths, projected, near, far, rows, seq, heads, head)
    y, gate, *h_out = after_attention(
        joined, x, w_output, gain_two, code_c, w_router, code_r, rank_r,
        g_extra, marks, experts, room,
    )
    code = code_c.reshape(-1)
    expert = code // room
    place = code - expert * room
    rest = jnp.where((code >= 0) & (place >= cut), expert * extra + place - cut, experts * extra)

    def experts_on(h, g_rows, low, high, *more):
        return expert_rows(h, g_rows, mine, w_router, w_in[0], w_out[0], experts, low, high, *more)

    parts, grad_router, ff_more, crowded = [], 0.0, None, None
    if extra:
        h_more, g_more, flag = h_out[-3:]
        h_out = h_out[:-3]
        crowded = flag[0, 0] > 0
        h_more, g_more, g_in = lax.optimization_barrier((h_more, g_more, g_in))

        def exchange_rest(_):
            rms = lax.rsqrt(jnp.mean(y * y, axis=-1, keepdims=True) + EPSILON)
            h = (y * rms * gain_two).astype(LOW)
            empty = jnp.zeros((experts * extra, width), LOW)
            send = lambda a: exchange(empty.at[rest].set(a, mode="drop"), devices)
            return False, send(h), send(g)

        _, h_more, g_more = lax.while_loop(
            lambda held: held[0], exchange_rest, (crowded, h_more, g_more)
        )
        h_out[0], h_more, g_more = lax.optimization_barrier((h_out[0], h_more, g_more))
    h_out, g_in = lax.optimization_barrier((h_out, g_in))
    g_in = g_in.reshape(devices, cut, width)
    h_in = [exchange(h_out[0], devices)]
    for h in h_out[1:]:
        h, h_in[-1] = lax.optimization_barrier((h, h_in[-1]))
        h_in.append(exchange(h, devices))
    ffs, dx_back, dx = [], [], None
    if extra:
        ff_more, dx, hid, da, x_t, dff_t, routed = experts_on(
            h_more, g_more.reshape(devices, extra, width), 0, extra, room - cut, 2 * extra
        )
        ff_more = ff_more.reshape(devices, extra, width)
        parts.append((x_t, dff_t, hid, da))
        grad_router = grad_router + routed
    for m, (low, high) in enumerate(segments):
        held = (0, 2 * extra, dx) if extra and not m else ()
        ff, dx, hid, da, x_t, dff_t, routed = experts_on(h_in[m], g_in, low, high, *held)
        if m + 1 < len(segments):
            dx, h_in[m + 1] = lax.optimization_barrier((dx, h_in[m + 1]))
        if m:
            dx, dx_back[-1] = lax.optimization_barrier((dx, dx_back[-1]))
        dx_back.append(exchange(dx.reshape(-1, width), devices))
        ffs.append(ff.reshape(devices, high - low, width))
        parts.append((x_t, dff_t, hid, da))
        grad_router = grad_router + routed
    grad_in, grad_out = expert_weights(parts)
    grad_router = grad_router.reshape(experts, width // TILE, TILE)
    small = jnp.swapaxes(grad_router, 0, 1).reshape(-1, TILE)
    ff, ff_packed = ffs[0], small
    if extra:
        ff = jnp.concatenate([ffs[1], ffs[0]], axis=1)
        bits = devices.bit_length() - 1
        ff_packed = ff_more.reshape((2,) * bits + (extra, width // TILE, TILE))
        order = tuple(reversed(range(bits))) + (bits + 1, bits, bits + 2)
        ff_packed = jnp.transpose(ff_packed, order).reshape(-1, TILE)
    ff = ff.reshape(devices * cut, width)
    dx_back, grad_in, grad_out, ff, ff_packed, small = lax.optimization_barrier(
        (dx_back, grad_in, grad_out, ff, ff_packed, small)
    )
    ff_back = exchange(ff, devices)

    dy, do, grad_output, grad_gain_two = before_attention(
        dx_back, code_c, y, g, gain_two, w_output, joined, room
    )
    lines = width // TILE
    small_rows = small.shape[0] + -(-2 * lines // 16) * 16 + -(-heads // 16) * 16
    small_rows = -(-small_rows // (16 * devices)) * 16 * devices
    grad_tokens, packed, small = attention_backward(
        projected, do, joined, weights, normed_t, w_query, w_key, w_value, x, dy, gain_one,
        small, grad_gain_two, rows, seq, heads, head, small_rows,
    )
    mixed, summed, small = all_sum(
        [packed.reshape(-1, TILE), grad_output, small], code_c, gate, rank_c, ff_back, y, room, ff_packed
    )
    if extra:

        def mix_all(_):
            spare = exchange(ff_more.reshape(-1, width), devices)
            first = jnp.where((code >= 0) & (place < cut), expert * cut + place, devices * cut)
            take = lambda a, index: jnp.take(a, index, axis=0, mode="fill", fill_value=0)
            ff = take(ff_back, first) + take(spare, rest)
            return False, (y + gate * ff.astype(jnp.float32)).astype(LOW)

        _, mixed = lax.while_loop(lambda held: held[0], mix_all, (crowded, mixed))
    *grads, router_t, gain_grad_one, gain_grad_two, table, mixed = unpack(summed, small, mixed, experts, heads, buckets)
    return (
        mixed.reshape(rows, seq, width),
        grad_tokens.reshape(rows, seq, width),
        *grads,
        gain_grad_one, gain_grad_two, table.T, router_t.T,
        grad_in,
        grad_out,
    )


def solution(mesh):
    split = P(AXES)
    in_specs = (split,) * 4 + (P(),) * 8 + (split,) * 3
    out_specs = (split,) * 2 + (P(),) * 8 + (split,) * 2
    return jax.shard_map(local, mesh=mesh, in_specs=in_specs, out_specs=out_specs, check_vma=False)
```

```python
import functools

import jax
import jax.numpy as jnp
from jax import lax
from jax.experimental import pallas as pl
from jax.experimental.pallas import tpu as pltpu
from jax.sharding import PartitionSpec as P

EPSILON = 1e-06
NEGATIVE = -1e30
THRESHOLDS = (12, 16, 23, 32, 46, 64, 91)
LOG2E = 1.4426950408889634
TILE = 128
GELU_A = 0.7978845608028654
GELU_B = GELU_A * 0.044715
AXES = ("grp", "exp")
LOW = jnp.bfloat16


def dot(a, b):
    return jnp.dot(a, b, preferred_element_type=jnp.float32)


def dot_t(a, b):
    return lax.dot_general(a, b, (((1,), (1,)), ((), ())), preferred_element_type=jnp.float32)


def params(mib, **more):
    return pltpu.CompilerParams(vmem_limit_bytes=mib << 20, **more)


def whole(shape):
    return pl.BlockSpec(shape, lambda *_: (0,) * len(shape), pipeline_mode=pl.Buffered(1))


def cost(flops, bytes_accessed, transcendentals=0):
    return pl.CostEstimate(
        flops=flops, bytes_accessed=bytes_accessed, transcendentals=transcendentals
    )


def bucket_of(offset):
    distance = jnp.abs(offset)
    far = jnp.full_like(distance, 8)
    for border in THRESHOLDS:
        far = far + (distance >= border).astype(jnp.int32)
    return jnp.where(distance < 8, distance, far) + jnp.where(offset > 0, 16, 0).astype(jnp.int32)


def device_place(cores, d):
    return dict(device_id=(lax.div(d, cores), lax.rem(d, cores)), device_id_type=pl.DeviceIdType.MESH)


def partner_of(me, b):
    bit = lax.rem(lax.div(me, 1 << b), 2)
    return bit, me + (1 - 2 * bit) * (1 << b)


def rows_at(start, length):
    return pl.ds(pl.multiple_of(start, 16), length)


def plan(room):
    if room % 64:
        return ((0, room),), room, 0
    half = room // 2
    return ((half, half + room // 4), (0, half)), 3 * room // 4, room // 4


def back_plan(room):
    if room % 64:
        return ((0, room),)
    return ((room // 2, room), (0, room // 2))


def segment(code, room, low, high):
    expert = lax.div(code, room)
    place = code - expert * room
    inside = (code >= 0) & (place >= low) & (place < high)
    return jnp.where(inside, expert * (high - low) + place - low, -1)


def spread(dest, values, out):
    rows = out.shape[0]
    step = min(256, rows)
    for start in range(0, rows, step):
        here = lax.broadcasted_iota(jnp.int32, (step, dest.shape[1]), 0) + start
        out[start : start + step] = dot((dest == here).astype(LOW), values).astype(LOW)


def collect(dest, values):
    here = lax.broadcasted_iota(jnp.int32, (dest.shape[0], values.shape[0]), 1)
    return dot((dest == here).astype(LOW), values)


def spread_all(code, room, values, outs):
    for (low, high), out in zip(plan(room)[0], outs):
        spread(segment(code, room, low, high), values, out)


def collect_all(code, room, refs):
    total = None
    for (low, high), ref in zip(back_plan(room), refs):
        part = collect(segment(code, room, low, high), ref[...])
        total = part if total is None else total + part
    return total


def buffers(experts, room, width):
    return [
        jax.ShapeDtypeStruct((experts * (high - low), width), LOW) for low, high in plan(room)[0]
    ]


def route_kernel(
    experts, room, eid_ref, slot_ref, g_ref, code_r, rank_r, out, more
):
    tokens = g_ref.shape[0]
    wide = max(TILE, experts)
    _, cut, extra = plan(room)
    line = lambda ref: jnp.concatenate([ref[i : i + 1] for i in range(ref.shape[0])], axis=1)
    ids = line(eid_ref)
    slots = line(slot_ref)
    picked = ids == lax.broadcasted_iota(jnp.int32, (wide, tokens), 0)
    block = 256
    at = lax.broadcasted_iota(jnp.int32, (block, block), 0)
    to = lax.broadcasted_iota(jnp.int32, (block, block), 1)
    before = (at < to).astype(LOW)
    passed = jnp.zeros((wide, 1), jnp.float32)
    places = []
    for start in range(0, tokens, block):
        here = picked[:, start : start + block]
        ones = jnp.where(here, 1.0, 0.0)
        earlier = dot(ones.astype(LOW), before) + passed
        places.append(jnp.sum(jnp.where(here, earlier, 0.0), axis=0, keepdims=True))
        passed = passed + jnp.sum(ones, axis=1, keepdims=True)
    place = jnp.concatenate(places, axis=1).astype(jnp.int32)
    kept = slots >= 0
    code = jnp.where(kept, ids * room + place, -1)
    code_r[...] = code
    rank = jnp.where(kept & (place >= cut), place - cut, -1)
    rank_r[...] = rank
    spread(segment(code, room, 0, cut), g_ref[...], out)
    spread(rank, g_ref[...], more)


def columns_kernel(experts, room, code_ref, code_c, rank_c, marks):
    tokens = code_ref.shape[1]
    wide = max(TILE, experts)
    _, cut, _ = plan(room)
    rows = jnp.concatenate([code_ref[...], jnp.zeros((7, tokens), jnp.int32)], axis=0)
    code = rows.astype(jnp.float32).T.astype(jnp.int32)[:, :1]
    code_c[...] = code
    ids = lax.div(code, room)
    place = code - ids * room
    over = (code >= 0) & (place >= cut)
    rank_c[...] = jnp.where(over, place - cut, -1)
    picked = ids == lax.broadcasted_iota(jnp.int32, (tokens, wide), 1)
    named = jnp.max(jnp.where(picked & over, 1.0, 0.0), axis=0, keepdims=True)
    named = jnp.sum(named, axis=1, keepdims=True)
    owner = jnp.max(jnp.where(over, ids + 1, 0).astype(jnp.float32), axis=0, keepdims=True)
    lane = lax.broadcasted_iota(jnp.int32, marks.shape, 1)
    crowded = jnp.where(named > 1.0, 1.0, 0.0)
    marks[...] = jnp.where(lane == 0, owner, jnp.where(lane == 1, crowded, 0.0))


def columns(code, experts, room):
    tokens = code.shape[1]
    column = jax.ShapeDtypeStruct((tokens, 1), jnp.int32)
    return pl.pallas_call(
        functools.partial(columns_kernel, experts, room),
        out_shape=[column, column, jax.ShapeDtypeStruct((8, TILE), jnp.float32)],
        compiler_params=params(32),
        name="columns",
    )(code)


def route(expert_ids, slots, upstream, experts, room):
    tokens, width = upstream.shape
    line = jax.ShapeDtypeStruct((1, tokens), jnp.int32)
    _, cut, extra = plan(room)
    return pl.pallas_call(
        functools.partial(route_kernel, experts, room),
        out_shape=[
            line, line,
            jax.ShapeDtypeStruct((experts * cut, width), LOW),
            jax.ShapeDtypeStruct((max(extra, 16), width), LOW),
        ],
        compiler_params=params(60),
        cost_estimate=cost(2 * experts * room * tokens * width, 8 << 20),
        name="route",
    )(expert_ids, slots, upstream)


def exchange(buffer, devices):
    shaped = buffer.reshape(devices, buffer.shape[0] // devices, buffer.shape[1])
    moved = lax.all_to_all(shaped, AXES, split_axis=0, concat_axis=0, tiled=True)
    return moved.reshape(buffer.shape)


def project_kernel(x_ref, gain_ref, wq_ref, wk_ref, wv_ref, normed_ref, out_ref):
    x = x_ref[...].astype(jnp.float32)
    rms = lax.rsqrt(jnp.mean(x * x, axis=-1, keepdims=True) + EPSILON)
    normed = (x * rms * gain_ref[...]).astype(LOW)
    normed_ref[...] = normed.T
    width = x.shape[1]
    for n, w_ref in enumerate((wq_ref, wk_ref, wv_ref)):
        out_ref[:, n * width : (n + 1) * width] = dot(normed, w_ref[...]).astype(LOW)


def project(x, gain, w_query, w_key, w_value):
    tokens, width = x.shape
    out = 3 * width
    step = 256
    rows = lambda w: pl.BlockSpec((step, w), lambda i: (i, 0))
    return pl.pallas_call(
        project_kernel,
        grid=(tokens // step,),
        in_specs=[rows(width), whole((1, width)), *[whole((width, width))] * 3],
        out_specs=[pl.BlockSpec((width, step), lambda i: (0, i)), rows(out)],
        out_shape=[
            jax.ShapeDtypeStruct((width, tokens), LOW),
            jax.ShapeDtypeStruct((tokens, out), LOW),
        ],
        compiler_params=params(40),
        cost_estimate=cost(2 * tokens * width * out, 12 << 20),
        name="project",
    )(x, gain, w_query, w_key, w_value)


def gather_orders(bits):
    far = tuple(range(3, bits))
    return [[(0,), (1,), (2,), far], [(0,), (2,), far, (1,)], [(0,), far, (1,), (2,)]]


def span(order, s, n):
    for group in order[: s + 1]:
        n >>= len(group)
    return n


def digit_of(d, group):
    if isinstance(d, int):
        return sum(((d >> b) & 1) << i for i, b in enumerate(group))
    return sum(lax.rem(lax.div(d, 1 << b), 2) * (1 << i) for i, b in enumerate(group))


def peer_of(me, group, r):
    for i, b in enumerate(group):
        if (r >> i) & 1:
            me = partner_of(me, b)[1]
    return me


def rank_in(order, d):
    n = 1 << sum(len(group) for group in order)
    return sum(digit_of(d, group) * span(order, s, n) for s, group in enumerate(order))


def after_attention_kernel(
    experts, room, cores, n, o_ref, x_ref, w_ref, gain_ref, eid_ref, wr_ref, code_ref, *rest
):
    segments, _, extra = plan(room)
    if extra:
        rank_ref, g_ref, mark_ref, *rest = rest
    y_ref, gate_ref, *rest = rest
    outs, rest = rest[: len(segments)], rest[len(segments) :]
    if extra:
        h_more, g_more, flag_ref, *rest = rest
        own, moved, marks, send, recv, *rest = rest
    (held,) = rest
    step = o_ref.shape[0]
    i = pl.program_id(0)
    bits = n.bit_length() - 1
    if extra:
        me = lax.axis_index("grp") * cores + lax.axis_index("exp")
        barrier = pltpu.get_barrier_semaphore()
        greeted = [(g, r) for g in gather_orders(bits)[0] for r in range(1, 1 << len(g))]

        @pl.when(i == 0)
        def _():
            for group, r in greeted:
                pl.semaphore_signal(barrier, inc=1, **device_place(cores, peer_of(me, group, r)))

    y = x_ref[...].astype(jnp.float32) + dot(o_ref[...], w_ref[...])
    y_ref[...] = y
    rms = lax.rsqrt(jnp.mean(y * y, axis=-1, keepdims=True) + EPSILON)
    normed = (y * rms * gain_ref[...]).astype(LOW)
    held[pl.ds(pl.multiple_of(i * step, step), step), :] = normed
    router = route_softmax(dot(normed, wr_ref[...]), experts)
    lane = lax.broadcasted_iota(jnp.int32, router.shape, 1)
    expert = lax.div(jnp.maximum(eid_ref[...], 0), room)
    gate_ref[...] = jnp.sum(jnp.where(lane == expert, router, 0.0), axis=-1, keepdims=True)

    @pl.when(i == pl.num_programs(0) - 1)
    def _():
        chunks = []
        for (low, high), out in zip(segments, outs):
            dest = segment(code_ref[...], room, low, high)
            size = min(256, out.shape[0])
            chunks += [(dest, out, start, size) for start in range(0, out.shape[0], size)]

        def spread_some(count):
            for dest, out, start, size in chunks[:count]:
                spread(dest - start, held[...], out.at[start : start + size])
            del chunks[:count]

        if not extra:
            spread_some(len(chunks))
            return
        single, width = g_ref.shape
        block = 2 * single
        orders = gather_orders(bits)
        phases = len(orders[0])
        third = width // 3
        spread(rank_ref[...], held[...], own)
        base = []
        for p, order in enumerate(orders):
            lanes = slice(p * third, (p + 1) * third)
            base.append(rank_in(order, me) * block)
            moved[p, rows_at(base[p], single), :] = own[:, lanes]
            moved[p, rows_at(base[p] + single, single), :] = g_ref[:, lanes]
        tall = mark_ref.shape[0]
        marks[pl.ds(pl.multiple_of(rank_in(orders[0], me) * tall, 8), tall), :] = mark_ref[...]
        pl.semaphore_wait(barrier, len(greeted))

        def doubling(s):
            copies = []
            for p, order in enumerate(orders):
                size = span(order, s, n)
                for r in range(1, 1 << len(order[s])):
                    place = device_place(cores, peer_of(me, order[s], r))
                    here = rows_at(base[p], block * size)
                    copies.append(
                        pltpu.make_async_remote_copy(
                            src_ref=moved.at[p, here], dst_ref=moved.at[p, here],
                            send_sem=send.at[p, s, r - 1], recv_sem=recv.at[p, s, r - 1], **place,
                        )
                    )
                    if p == 0:
                        start = lax.div(base[0], block) * tall
                        here = pl.ds(pl.multiple_of(start, 8), tall * size)
                        copies.append(
                            pltpu.make_async_remote_copy(
                                src_ref=marks.at[here], dst_ref=marks.at[here],
                                send_sem=send.at[3, s, r - 1], recv_sem=recv.at[3, s, r - 1], **place,
                            )
                        )
            for copy in copies:
                copy.start()
            return copies

        sent = []
        for s in reversed(range(phases)):
            copies = doubling(s)
            spread_some(2)
            for copy in copies:
                copy.wait_recv()
            sent += copies
            for p, order in enumerate(orders):
                base[p] = base[p] - digit_of(me, order[s]) * block * span(order, s, n)
        spread_some(len(chunks))
        for copy in sent:
            copy.wait_send()
        for d in range(n):
            here = slice(d * single, (d + 1) * single)
            first = rank_in(orders[0], d) * tall
            keep = marks[first : first + 1, :1] == (me + 1).astype(jnp.float32)
            for p, order in enumerate(orders):
                lanes = slice(p * third, (p + 1) * third)
                at = rank_in(order, d) * block
                for out, start in ((h_more, at), (g_more, at + single)):
                    got = moved[p, start : start + single, :].astype(jnp.float32)
                    out[here, lanes] = jnp.where(keep, got, 0.0).astype(LOW)
        flag_ref[0, 0] = jnp.max(marks[:, 1:2]).astype(jnp.int32)


def after_attention(
    joined, x, w_output, gain, expert_ids, w_router, code, rank, g_extra, marks, experts, room
):
    tokens, width = x.shape
    step = 256
    cores = lax.axis_size("exp")
    n = lax.axis_size(AXES)
    bits = n.bit_length() - 1
    segments, _, extra = plan(room)
    rows = pl.BlockSpec((step, width), lambda i: (i, 0))
    single = pl.BlockSpec((step, 1), lambda i: (i, 0))
    outs = buffers(experts, room, width)
    more, scratch, options, flag = [], [], {}, []
    if extra:
        more = [rank, g_extra, marks]
        outs = outs + [jax.ShapeDtypeStruct((n * extra, width), LOW)] * 2
        flag = [jax.ShapeDtypeStruct((1, 1), jnp.int32)]
        scratch = [
            pltpu.VMEM((extra, width), LOW), pltpu.VMEM((3, 2 * n * extra, width // 3), LOW),
            pltpu.VMEM((8 * n, TILE), jnp.float32),
            pltpu.SemaphoreType.DMA((4, 4, (n >> 3) - 1)), pltpu.SemaphoreType.DMA((4, 4, (n >> 3) - 1)),
        ]
        options = dict(collective_id=2, has_side_effects=True)
    return pl.pallas_call(
        functools.partial(after_attention_kernel, experts, room, cores, n),
        grid=(tokens // step,),
        in_specs=[
            rows, rows, whole((width, width)), whole((1, width)), single, whole(w_router.shape),
            whole((1, tokens)), *[whole(m.shape) for m in more],
        ],
        out_specs=[rows, single]
        + [pl.BlockSpec(o.shape, lambda i: (0, 0)) for o in outs]
        + [pl.BlockSpec(memory_space=pltpu.SMEM)] * len(flag),
        out_shape=[
            jax.ShapeDtypeStruct((tokens, width), jnp.float32),
            jax.ShapeDtypeStruct((tokens, 1), jnp.float32),
        ]
        + outs
        + flag,
        scratch_shapes=scratch + [pltpu.VMEM((tokens, width), LOW)],
        compiler_params=params(60, **options),
        cost_estimate=cost(2 * tokens * width * (width + experts * room), 12 << 20),
        name="after_attention",
    )(joined, x, w_output, gain, expert_ids, w_router, code, *more)


def route_softmax(logits, experts):
    lane = lax.broadcasted_iota(jnp.int32, logits.shape, 1)
    logits = jnp.where(lane < experts, logits, NEGATIVE)
    e = jnp.exp(logits - jnp.max(logits, axis=-1, keepdims=True))
    return e / jnp.sum(e, axis=-1, keepdims=True)


def pack(values, first, height, out, at):
    for c in range(values.shape[1] // TILE):
        out[at + c * height : at + (c + 1) * height] = values[
            first : first + height, c * TILE : (c + 1) * TILE
        ].astype(LOW)


def before_attention_kernel(
    room, n_backs, code_ref, y_ref, g_ref, gain_ref, w_ref, o_ref, *rest
):
    backs = rest[:n_backs]
    dy_ref, do_ref, pack_ref, gg_ref, gw_ref = rest[n_backs:]
    i = pl.program_id(0)

    @pl.when(i == 0)
    def _():
        gw_ref[...] = jnp.zeros_like(gw_ref)
        gg_ref[...] = jnp.zeros_like(gg_ref)

    step = y_ref.shape[0] // 2
    blocks = [slice(n * step, (n + 1) * step) for n in range(2)]
    dhs = [collect_all(code_ref[here, :], room, backs) for here in blocks]
    lows = []
    for here, dh in zip(blocks, dhs):
        y = y_ref[here, :]
        rms = lax.rsqrt(jnp.mean(y * y, axis=-1, keepdims=True) + EPSILON)
        gg_ref[...] += jnp.sum(dh * y * rms, axis=0, keepdims=True)
        u = dh * gain_ref[...]
        dy = (
            g_ref[here, :].astype(jnp.float32)
            + rms * u
            - y * (rms * rms * rms) * jnp.mean(u * y, axis=-1, keepdims=True)
        )
        dy_ref[here, :] = dy
        lows.append(dy.astype(LOW))
        do_ref[here, :] = dot_t(lows[-1], w_ref[...]).astype(LOW)
    gw_ref[...] += dot(o_ref[...].T, jnp.concatenate(lows, axis=0))

    @pl.when(i == pl.num_programs(0) - 1)
    def _():
        pack(gw_ref, 0, gw_ref.shape[0], pack_ref, 0)


def before_attention(backs, code, y, g, gain, w_output, joined, room):
    tokens, width = y.shape
    step = 512
    rows = lambda w: pl.BlockSpec((step, w), lambda i: (i, 0))
    return pl.pallas_call(
        functools.partial(before_attention_kernel, room, len(backs)),
        grid=(tokens // step,),
        in_specs=[
            rows(1), rows(width), rows(width), whole((1, width)),
            whole((width, width)), rows(width), *[whole(b.shape) for b in backs],
        ],
        out_specs=[
            rows(width), rows(width),
            pl.BlockSpec((width * width // TILE, TILE), lambda i: (0, 0)),
            pl.BlockSpec((1, width), lambda i: (0, 0)),
        ],
        out_shape=[
            jax.ShapeDtypeStruct((tokens, width), jnp.float32),
            jax.ShapeDtypeStruct((tokens, width), LOW),
            jax.ShapeDtypeStruct((width * width // TILE, TILE), LOW),
            jax.ShapeDtypeStruct((1, width), jnp.float32),
        ],
        scratch_shapes=[pltpu.VMEM((width, width), jnp.float32)],
        compiler_params=params(60),
        cost_estimate=cost(6 * tokens * width * width, 16 << 20),
        name="before_attention",
    )(code, y, g, gain, w_output, joined, *backs)


def unpack_kernel(
    experts, heads, buckets, q_ref, k_ref, v_ref, o_ref, small_ref, mix_ref,
    gq, gk, gv, go, router, gain_one, gain_two, table, mixed,
):
    mixed[...] = mix_ref[...]
    for packed_ref, out_ref in ((q_ref, gq), (k_ref, gk), (v_ref, gv), (o_ref, go)):
        for c in range(packed_ref.shape[0]):
            out_ref[:, c * TILE : (c + 1) * TILE] = packed_ref[c].astype(jnp.float32)

    @pl.when(pl.program_id(0) == 0)
    def _():
        lines = router.shape[1] // TILE
        small = small_ref[...].astype(jnp.float32)
        for c in range(lines):
            lanes = slice(c * TILE, (c + 1) * TILE)
            router[:, lanes] = small[c * experts : (c + 1) * experts]
            for n, gain in enumerate((gain_one, gain_two)):
                gain[lanes] = small[lines * experts + n * lines + c]
        at = lines * experts + -(-2 * lines // 16) * 16
        table[...] = small[at : at + heads, :buckets]


def unpack(packed, small, mixed, experts, heads, buckets):
    tokens, width = mixed.shape
    blocks = width // TILE
    steps = 4
    source = lambda m: pl.BlockSpec((blocks, width // steps, TILE), lambda i: (m, i, 0))
    rows = lambda count: pl.BlockSpec((count // steps, width), lambda i: (i, 0))
    kept = lambda shape: pl.BlockSpec(shape, lambda i: (0, 0))
    flat = pl.BlockSpec((width,), lambda i: (0,))
    return pl.pallas_call(
        functools.partial(unpack_kernel, experts, heads, buckets),
        grid=(steps,),
        in_specs=[source(m) for m in range(4)] + [whole(small.shape), rows(tokens)],
        out_specs=[rows(width)] * 4
        + [kept((experts, width)), flat, flat, kept((heads, buckets)), rows(tokens)],
        out_shape=[jax.ShapeDtypeStruct((width, width), jnp.float32)] * 4
        + [
            jax.ShapeDtypeStruct((experts, width), jnp.float32),
            jax.ShapeDtypeStruct((width,), jnp.float32),
            jax.ShapeDtypeStruct((width,), jnp.float32),
            jax.ShapeDtypeStruct((heads, buckets), jnp.float32),
            jax.ShapeDtypeStruct((tokens, width), LOW),
        ],
        compiler_params=params(60),
        name="unpack",
    )(*[packed.reshape(4 * blocks, width, TILE)] * 4, small, mixed)


def attention_forward_kernel(len_ref, q_ref, k_ref, v_ref, near_ref, far_ref, o_ref, p_ref, s_ref):
    seq = q_ref.shape[0]
    tiles = seq // TILE
    half = q_ref.shape[1] // 2
    row = pl.program_id(0)
    pair = pl.program_id(1)
    live = len_ref[row]
    lane = lax.broadcasted_iota(jnp.int32, (seq, 2 * half), 1)
    dead = lax.broadcasted_iota(jnp.int32, (seq, 2 * half), 0) >= live
    q = q_ref[...]
    k = k_ref[...]
    v_t = v_ref[...].T
    outs = []
    for h in range(2):
        mine = (lane >= h * half) & (lane < (h + 1) * half)
        flag = lane == (1 - h) * half
        k_h = jnp.where(mine, k, jnp.where(flag & dead, -1e30, 0.0).astype(k.dtype))
        q_h = jnp.where(flag, jnp.ones_like(q), q)
        after = far_ref[2 * pair + h, 0]
        before = far_ref[2 * pair + h, 1]
        tops = []
        for i in range(0, tiles, 2):
            q_i = q_h[i * TILE : (i + 2) * TILE]
            raw = dot_t(k_h, q_i)
            for c in range(2):
                cols = slice((i + c) * TILE, (i + c + 1) * TILE)
                top = None
                for j in range(tiles):
                    x = raw[j * TILE : (j + 1) * TILE, c * TILE : (c + 1) * TILE] * (0.125 * LOG2E)
                    d = j - i - c
                    if -1 <= d <= 1:
                        x = x + near_ref[h, d + 1]
                    else:
                        x = x + (after if d > 0 else before)
                    s_ref[h, j * TILE : (j + 1) * TILE, cols] = x
                    m = jnp.max(x, axis=0, keepdims=True)
                    top = m if top is None else jnp.maximum(top, m)
                tops.append(top)
        for i in range(tiles):
            e = jnp.exp2(s_ref[h, :, i * TILE : (i + 1) * TILE] - tops[i])
            total = jnp.sum(e, axis=0, keepdims=True)
            p_ref[0, h, :, i * TILE : (i + 1) * TILE] = (e * (1.0 / total)).astype(LOW)
        outs.append(lax.dot_general(v_t[h * half:(h + 1) * half], p_ref[0, h], (((1,), (0,)), ((), ())), preferred_element_type=jnp.float32))
    o_ref[...] = jnp.concatenate(outs, axis=0).T.astype(o_ref.dtype)

def attention_forward(lengths, projected, near, far, rows, seq, heads, head):
    width = heads * head
    pairs = heads // 2
    spec = lambda off: pl.BlockSpec((seq, 2 * head), lambda b, p: (b, off + p))
    return pl.pallas_call(
        attention_forward_kernel,
        grid=(rows, pairs),
        in_specs=[
            pl.BlockSpec(memory_space=pltpu.SMEM),
            spec(0), spec(pairs), spec(2 * pairs),
            pl.BlockSpec((2, 3, TILE, TILE), lambda b, p: (p, 0, 0, 0)),
            pl.BlockSpec(memory_space=pltpu.SMEM),
        ],
        out_specs=[
            pl.BlockSpec((seq, 2 * head), lambda b, p: (b, p)),
            pl.BlockSpec((1, 2, seq, seq), lambda b, p: (b, p, 0, 0)),
        ],
        out_shape=[
            jax.ShapeDtypeStruct((rows * seq, width), LOW),
            jax.ShapeDtypeStruct((rows, heads, seq, seq), LOW),
        ],
        scratch_shapes=[pltpu.VMEM((2, seq, seq), jnp.float32)],
        compiler_params=params(40),
        cost_estimate=cost(flops=4 * rows * heads * seq * seq * head * 4, bytes_accessed=rows * heads * seq * seq * 2, transcendentals=rows * heads * seq * seq),
        name="attention_forward",
    )(lengths, projected, projected, projected, near, far)

def attention_backward_kernel(
    rows, q_ref, k_ref, v_ref, do_ref, o_ref, p_ref, nt_ref, wq_ref, wk_ref, wv_ref, x_ref, dy_ref, gain_ref,
    gr_ref, gg2_ref, out_ref, pack_ref, small_ref,
    near_ref, far_ref, d_ref, lines_ref, dh_ref,
):
    seq = q_ref.shape[0] // rows
    tiles = seq // TILE
    half = q_ref.shape[1] // 2
    width = x_ref.shape[1]
    pair = pl.program_id(0)
    last_pair = pair == pl.num_programs(0) - 1
    lane = lax.broadcasted_iota(jnp.int32, (seq, 2 * half), 1)
    weights = jnp.concatenate([wq_ref[...], wk_ref[...], wv_ref[...]], axis=1)
    near_ref[...] = jnp.zeros_like(near_ref)
    for row in range(rows):
        here = slice(row * seq, (row + 1) * seq)
        v = v_ref[here, :]
        do = do_ref[here, :]
        weighed = (do.astype(jnp.float32) * o_ref[here, :].astype(jnp.float32)).T
        for h in range(2):
            mine = (lane >= h * half) & (lane < (h + 1) * half)
            v_h = jnp.where(mine, v, jnp.zeros_like(v))
            delta = jnp.sum(weighed[h * half : (h + 1) * half], axis=0, keepdims=True)
            far_sum = [jnp.zeros((8, TILE), jnp.float32), jnp.zeros((8, TILE), jnp.float32)]
            for i in range(0, tiles, 2):
                dp = dot_t(v_h, do[i * TILE : (i + 2) * TILE])
                for c in range(2):
                    cols = slice((i + c) * TILE, (i + c + 1) * TILE)
                    for j in range(tiles):
                        rws = slice(j * TILE, (j + 1) * TILE)
                        part = dp[rws, c * TILE : (c + 1) * TILE] - delta[:, cols]
                        ds = p_ref[row, h, rws, cols].astype(jnp.float32) * part
                        d = j - i - c
                        if -1 <= d <= 1:
                            near_ref[row, h, d + 1] += ds
                        else:
                            which = 0 if d > 0 else 1
                            far_sum[which] = far_sum[which] + jnp.sum(
                                ds.reshape(TILE // 8, 8, TILE), axis=0
                            )
                        d_ref[row, h, rws, cols] = ds.astype(LOW)
            for which in range(2):
                far_ref[row, h, which] = far_sum[which]
    grads_all = []
    for row in range(rows):
        here = slice(row * seq, (row + 1) * seq)
        q = q_ref[here, :]
        do = do_ref[here, :]
        k_t = k_ref[here, :].T
        dq_parts = []
        dk_all = None
        dv_all = None
        for h in range(2):
            mine = (lane >= h * half) & (lane < (h + 1) * half)
            ds_all = d_ref[row, h]
            dq_parts.append(dot(k_t[h * half : (h + 1) * half], ds_all))
            dk_h = dot(ds_all, q)
            dv_h = dot(p_ref[row, h], do)
            dk_all = dk_h if h == 0 else jnp.where(mine, dk_h, dk_all)
            dv_all = dv_h if h == 0 else jnp.where(mine, dv_h, dv_all)
        dq = (jnp.concatenate(dq_parts, axis=0).T * 0.125).astype(LOW)
        grads_all.append(
            jnp.concatenate([dq, (dk_all * 0.125).astype(LOW), dv_all.astype(LOW)], axis=1)
        )
    grads = jnp.concatenate(grads_all, axis=0)
    acc = dot(nt_ref[...], grads)
    for n in range(3):
        pack_ref[n, 0] = acc[:, n * TILE : (n + 1) * TILE].astype(LOW)
    dh = dot_t(grads, weights)

    @pl.when(pair == 0)
    def _():
        dh_ref[...] = dh

    @pl.when(pair > 0)
    def _():
        dh_ref[...] += dh

    near_ref[0] = sum(near_ref[row] for row in range(rows))
    far_ref[0] = sum(far_ref[row] for row in range(rows))
    bucket_sums(near_ref.at[0], far_ref.at[0], lines_ref, 2 * pair)

    @pl.when(last_pair)
    def _():
        total = dh_ref[...]
        x = x_ref[...].astype(jnp.float32)
        rms = lax.rsqrt(jnp.mean(x * x, axis=-1, keepdims=True) + EPSILON)
        gg = jnp.sum(total * x * rms, axis=0, keepdims=True)
        u = total * gain_ref[...]
        out_ref[...] = (
            dy_ref[...]
            + rms * u
            - x * (rms * rms * rms) * jnp.mean(u * x, axis=-1, keepdims=True)
        )
        at = gr_ref.shape[0]
        small_ref[:at] = gr_ref[...].astype(LOW)
        lines = width // TILE
        gains = [gg[:, c * TILE : (c + 1) * TILE] for c in range(lines)]
        gains += [gg2_ref[:, c * TILE : (c + 1) * TILE] for c in range(lines)]
        if 2 * lines % 16:
            gains += [jnp.zeros((16 - 2 * lines % 16, TILE), jnp.float32)]
        gains = jnp.concatenate(gains, axis=0)
        small_ref[at : at + gains.shape[0]] = gains.astype(LOW)
        at = at + gains.shape[0]
        table = bucket_table(lines_ref)
        if table.shape[0] % 16:
            table = jnp.concatenate([table, jnp.zeros((16 - table.shape[0] % 16, TILE), jnp.float32)], axis=0)
        small_ref[at : at + table.shape[0]] = table.astype(LOW)
        at = at + table.shape[0]
        small_ref[at:] = jnp.zeros((small_ref.shape[0] - at, TILE), LOW)


def bucket_sums(near_ref, far_ref, lines_ref, first):
    empty = jnp.zeros((8, TILE), jnp.float32)
    sub = lax.broadcasted_iota(jnp.int32, (8, 2 * TILE), 0)
    for h in range(2):
        lines = []
        for d in range(3):
            turned = None
            for a in range(0, TILE, 8):
                part = jnp.concatenate([near_ref[h, d, a : a + 8], empty], axis=1)
                part = pltpu.roll(part, (2 * TILE - a) % (2 * TILE), 1) if a else part
                turned = part if turned is None else turned + part
            for b in (1, 2, 4):
                turned = jnp.where((sub & b) > 0, pltpu.roll(turned, 2 * TILE - b, 1), turned)
            lines.append(jnp.sum(turned, axis=0, keepdims=True))
        for side in range(2):
            total = jnp.sum(far_ref[h, side], axis=0, keepdims=True)
            lines.append(jnp.concatenate([total, jnp.zeros((1, TILE), jnp.float32)], axis=1))
        lines.append(jnp.zeros((3, 2 * TILE), jnp.float32))
        lines_ref[first + h] = jnp.concatenate(lines, axis=0)


def bucket_table(lines_ref):
    heads = lines_ref.shape[0]
    buckets = 4 * 8
    lane = lax.broadcasted_iota(jnp.int32, (2 * TILE, TILE), 0)
    bucket = lax.broadcasted_iota(jnp.int32, (2 * TILE, TILE), 1)
    turn = jnp.where(lane >= TILE, lane - 2 * TILE, lane)
    total = None
    for r in range(5):
        if r < 3:
            hit = bucket_of((r - 1) * TILE - turn) == bucket
        else:
            hit = bucket == (buckets - 1 if r == 3 else buckets // 2 - 1)
        hit = hit.astype(LOW)
        line = jnp.concatenate([lines_ref[h, r : r + 1, :] for h in range(heads)], axis=0)
        high = line.astype(LOW)
        part = dot(high, hit) + dot((line - high.astype(jnp.float32)).astype(LOW), hit)
        total = part if total is None else total + part
    return total


def attention_backward(
    projected, do, joined, weights, normed_t, w_query, w_key, w_value, x, dy, gain, gr, gg2,
    rows, seq, heads, head, small_rows,
):
    width = heads * head
    pairs = heads // 2
    tokens = rows * seq
    spec = lambda off: pl.BlockSpec((tokens, 2 * head), lambda p: (0, off + p))
    column = pl.BlockSpec((width, 2 * head), lambda p: (0, p))
    return pl.pallas_call(
        functools.partial(attention_backward_kernel, rows),
        grid=(pairs,),
        in_specs=[
            spec(0), spec(pairs), spec(2 * pairs), spec(0), spec(0),
            pl.BlockSpec((rows, 2, seq, seq), lambda p: (0, p, 0, 0)),
            whole((width, tokens)),
            column, column, column, whole((tokens, width)), whole((tokens, width)),
            whole((1, width)), whole(gr.shape), whole(gg2.shape),
        ],
        out_specs=[
            pl.BlockSpec((tokens, width), lambda p: (0, 0)),
            pl.BlockSpec((3, 1, width, TILE), lambda p: (0, p, 0, 0)),
            pl.BlockSpec((small_rows, TILE), lambda p: (0, 0)),
        ],
        out_shape=[
            jax.ShapeDtypeStruct((tokens, width), jnp.float32),
            jax.ShapeDtypeStruct((3, pairs, width, TILE), LOW),
            jax.ShapeDtypeStruct((small_rows, TILE), LOW),
        ],
        scratch_shapes=[
            pltpu.VMEM((rows, 2, 3, TILE, TILE), jnp.float32),
            pltpu.VMEM((rows, 2, 2, 8, TILE), jnp.float32),
            pltpu.VMEM((rows, 2, seq, seq), LOW),
            pltpu.VMEM((heads, 8, 2 * TILE), jnp.float32),
            pltpu.VMEM((tokens, width), jnp.float32),
        ],
        compiler_params=params(60),
        cost_estimate=cost(8 * rows * heads * seq * seq * head * 4, rows * heads * seq * seq * 2),
        name="attention_backward",
    )(
        projected, projected, projected, do, joined, weights, normed_t, w_query, w_key, w_value,
        x, dy, gain, gr, gg2,
    )


def bias_tiles(table):
    j = lax.broadcasted_iota(jnp.int32, (3, TILE, TILE), 1)
    i = lax.broadcasted_iota(jnp.int32, (3, TILE, TILE), 2)
    d = lax.broadcasted_iota(jnp.int32, (3, TILE, TILE), 0) - 1
    b = bucket_of(d * TILE + j - i)
    scaled = table.T * LOG2E
    hot = (b.reshape(1, -1) == jnp.arange(table.shape[0], dtype=jnp.int32)[:, None]).astype(jnp.float32)
    near = jnp.dot(scaled, hot, precision=lax.Precision.HIGHEST).reshape(-1, 3, TILE, TILE)
    far = jnp.stack([scaled[:, -1], scaled[:, table.shape[0] // 2 - 1]], axis=1)
    return near, far


def expert_kernel(experts, chunk, held, x_ref, g_ref, mine_ref, wr_ref, wi_any, wo_any, *refs):
    ff_ref, dx_ref, hid_ref, da_ref, xt_ref, dfft_ref, gr_ref, wi_ref, wo_ref, sem = refs[held:]
    inner = wi_ref.shape[1]
    first_step = pl.program_id(0) == 0

    def loads(f):
        cols = pl.ds(f, chunk)
        return (pltpu.make_async_copy(wi_any.at[:, cols], wi_ref.at[:, cols], sem.at[0, f // chunk]),
                pltpu.make_async_copy(wo_any.at[cols, :], wo_ref.at[cols, :], sem.at[1, f // chunk]))

    @pl.when(first_step)
    def _():
        for f in range(0, inner, chunk):
            for c in loads(f):
                c.start()
        gr_ref[...] = jnp.zeros_like(gr_ref)

    x = x_ref[...]
    g = g_ref[...].reshape(x.shape).astype(jnp.float32)
    mine = mine_ref[...]
    lane = lax.broadcasted_iota(jnp.int32, (1, wr_ref.shape[1]), 1)
    logits = jnp.dot(x, wr_ref[...], preferred_element_type=jnp.float32)
    logits = jnp.where(lane < experts, logits, -1e30)
    e = jnp.exp(logits - jnp.max(logits, axis=-1, keepdims=True))
    router = e / jnp.sum(e, axis=-1, keepdims=True)
    gate = jnp.sum(router * mine, axis=-1, keepdims=True)
    dff = (g * gate).astype(LOW)
    ff = None
    dx = None
    def first(f):
        @pl.when(first_step)
        def _():
            for c in loads(f):
                c.wait()
        cols = slice(f, f + chunk)
        return (jnp.dot(x, wi_ref[:, cols], preferred_element_type=jnp.float32),
                lax.dot_general(dff, wo_ref[cols, :], (((1,), (1,)), ((), ())), preferred_element_type=jnp.float32))
    for f in range(0, inner, chunk):
        cols = slice(f, f + chunk)
        a, dhid = first(f)
        u = a * a
        t = jnp.tanh(a * (GELU_A + GELU_B * u))
        h = 0.5 + 0.5 * t
        hid = a * h
        slope = h + hid * ((1.0 - t) * (GELU_A + (3.0 * GELU_B) * u))
        da = (dhid * slope).astype(LOW)
        hid = hid.astype(LOW)
        hid_ref[:, cols] = hid
        da_ref[:, cols] = da
        ff_part = jnp.dot(hid, wo_ref[cols, :], preferred_element_type=jnp.float32)
        dx_part = lax.dot_general(da, wi_ref[:, cols], (((1,), (1,)), ((), ())), preferred_element_type=jnp.float32)
        ff = ff_part if ff is None else ff + ff_part
        dx = dx_part if dx is None else dx + dx_part
    ff = ff.astype(LOW)
    ff_ref[...] = ff
    dgate = jnp.sum(g * ff.astype(jnp.float32), axis=-1, keepdims=True)
    dlogits = ((gate * dgate) * (mine - router)).astype(LOW)
    dx = dx + lax.dot_general(dlogits, wr_ref[...], (((1,), (1,)), ((), ())), preferred_element_type=jnp.float32)
    dx_ref[...] = dx.astype(LOW).reshape(dx_ref.shape)
    x_t = x.T
    xt_ref[...] = x_t
    dfft_ref[...] = dff.T
    gr_ref[...] += dot(dlogits.T, x)

def expert_rows(x, g, mine, wr, wi, wo, experts, low, high, at=0, total=0, dx=None, tile=256, chunk=768):
    n, width = x.shape
    inner = wi.shape[1]
    sources, room = g.shape[0], high - low
    total = total or room
    group = max(1, min(sources, tile // room))
    while sources % group or (group * room) % TILE:
        group += 1
    tile = group * room
    once = lambda s: pl.BlockSpec(s, lambda i: (0,) * len(s), pipeline_mode=pl.Buffered(1))
    rowspec = lambda w: pl.BlockSpec((tile, w), lambda i: (i, 0))
    column = pl.BlockSpec((width, tile), lambda i: (0, i))
    anywhere = pl.BlockSpec(memory_space=pl.ANY)
    held = [] if dx is None else [dx]
    return pl.pallas_call(
        functools.partial(expert_kernel, experts, chunk, len(held)),
        grid=(n // tile,),
        in_specs=[
            rowspec(width), pl.BlockSpec((group, room, width), lambda i: (i, low // room, 0)),
            once(mine.shape), once(wr.shape), anywhere, anywhere, *[anywhere] * len(held),
        ],
        out_specs=[
            rowspec(width), pl.BlockSpec((group, room, width), lambda i: (i, at // room, 0)),
            rowspec(inner), rowspec(inner), column, column,
            pl.BlockSpec((wr.shape[1], width), lambda i: (0, 0)),
        ],
        out_shape=[
            jax.ShapeDtypeStruct((n, width), LOW),
            jax.ShapeDtypeStruct((sources, total, width), LOW),
            *[jax.ShapeDtypeStruct((n, inner), LOW)] * 2,
            *[jax.ShapeDtypeStruct((width, n), LOW)] * 2,
            jax.ShapeDtypeStruct((wr.shape[1], width), jnp.float32),
        ],
        scratch_shapes=[
            pltpu.VMEM(wi.shape, LOW), pltpu.VMEM(wo.shape, LOW),
            pltpu.SemaphoreType.DMA((2, inner // chunk)),
        ],
        input_output_aliases={6: 1} if held else {},
        compiler_params=params(60),
        cost_estimate=cost(8 * n * width * inner, 4 * n * inner + 8 * width * inner, n * inner),
        name="expert_rows",
    )(x, g, mine, wr, wi, wo, *held)


def expert_weights_kernel(parts, *refs):
    ins, (gi_ref, go_ref) = refs[: 4 * parts], refs[4 * parts :]
    gi = None
    go = None
    for c in range(parts):
        xt, dfft, hid, da = ins[4 * c : 4 * c + 4]
        gi_c = dot(xt[...], da[...])
        go_c = dot(dfft[...], hid[...])
        gi = gi_c if gi is None else gi + gi_c
        go = go_c if go is None else go + go_c
    gi_ref[0] = gi
    go_ref[0] = go.T


def expert_weights(parts, tile=512):
    inner = parts[0][2].shape[1]
    width = parts[0][0].shape[0]
    specs, args, rows = [], [], 0
    for xt, dfft, hid, da in parts:
        n = hid.shape[0]
        rows += n
        specs += [pl.BlockSpec((width, n), lambda f: (0, 0), pipeline_mode=pl.Buffered(1))] * 2
        specs += [pl.BlockSpec((n, tile), lambda f: (0, f))] * 2
        args += [xt, dfft, hid, da]
    return pl.pallas_call(
        functools.partial(expert_weights_kernel, len(parts)),
        grid=(inner // tile,),
        in_specs=specs,
        out_specs=[
            pl.BlockSpec((1, width, tile), lambda f: (0, 0, f)),
            pl.BlockSpec((1, tile, width), lambda f: (0, f, 0)),
        ],
        out_shape=[
            jax.ShapeDtypeStruct((1, width, inner), jnp.float32),
            jax.ShapeDtypeStruct((1, inner, width), jnp.float32),
        ],
        compiler_params=params(60),
        cost_estimate=cost(4 * rows * width * inner, 4 * rows * inner + 8 * width * inner),
        name="expert_weights",
    )(*args)


def split_units(units, weights):
    total, sizes, done, so_far = sum(weights), [], 0, 0
    for w in weights:
        so_far += w
        end = (2 * units * so_far + total) // (2 * total)
        sizes.append(end - done)
        done = end
    return sizes


def sum_parts(n, heights):
    bits = n.bit_length() - 1
    upper = list(range(1, bits))
    orders = [[0] + upper[t:] + upper[:t] for t in range(3)]
    parts, first = [], 0
    for ref, rows in enumerate(heights):
        units = rows // (16 * n)
        turns = (0, 1, 2, 0, 1, 2) if units >= 18 else (0, 1, 2) if units >= 6 else (2,)
        at = 0
        for t, size in zip(turns, split_units(units, [(5, 5, 3)[t] for t in turns])):
            parts.append((ref, at * 16 * n, first, size * 16, orders[t]))
            at += size
            first += size * 16 * n
    return bits, parts


def sum_kernel(cores, n, room, heights, extra, code_ref, gate_ref, rank_ref, ff_any, y_any, *refs):
    _, cut, _ = plan(room)
    xs, refs = refs[: len(heights)], refs[len(heights) :]
    mixed_any, sum_any, small_any, out_ref, work_ref, got_ref, ff_ref, y_ref, mixed_ref, *refs = refs
    if extra:
        tail_ref, *refs = refs
    send, recv, local, load, store = refs
    loads = [
        pltpu.make_async_copy(ff_any, ff_ref, local.at[0]),
        pltpu.make_async_copy(y_any, y_ref, local.at[1]),
    ]
    summed = heights[:-1] if extra else heights
    bits, parts = sum_parts(n, summed)
    full = len(parts)
    if extra:
        parts = parts + [(len(summed), 0, sum(summed), heights[-1] // n, list(range(bits)))]
    me = lax.axis_index("grp") * cores + lax.axis_index("exp")
    barrier = pltpu.get_barrier_semaphore()
    for b in range(bits):
        pl.semaphore_signal(barrier, inc=1, **device_place(cores, partner_of(me, b)[1]))
    base = [first for _, _, first, _, _ in parts]
    got_at = list(base)
    kept = []
    for p, (ref, at, first, step, order) in enumerate(parts):
        length = step * (n >> 1)
        start = base[p] + partner_of(me, order[0])[0] * length
        kept.append(
            pltpu.make_async_copy(
                xs[ref].at[rows_at(start - first + at, length)],
                work_ref.at[rows_at(start, length)],
                load.at[p],
            )
        )
        kept[p].start()
    for copy in loads:
        copy.start()
    pl.semaphore_wait(barrier, bits)

    def halving(p, s):
        ref, at, first, step, order = parts[p]
        length = step * (n >> (s + 1))
        bit, partner = partner_of(me, order[s])
        start = base[p] + (1 - bit) * length
        if s == 0:
            source = xs[ref].at[rows_at(start - first + at, length)]
        else:
            source = work_ref.at[rows_at(start, length)]
        return pltpu.make_async_remote_copy(
            src_ref=source, dst_ref=got_ref.at[rows_at(got_at[p], length)],
            send_sem=send.at[p, s], recv_sem=recv.at[p, s], **device_place(cores, partner),
        )

    def doubling(p, s):
        _, _, _, step, order = parts[p]
        here = rows_at(base[p], step * (n >> (s + 1)))
        return pltpu.make_async_remote_copy(
            src_ref=out_ref.at[here], dst_ref=out_ref.at[here],
            send_sem=send.at[p, bits + s], recv_sem=recv.at[p, bits + s],
            **device_place(cores, partner_of(me, order[s])[1]),
        )

    main = sum(summed[:-1])

    def keep_out(p, s, start, length):
        here = rows_at(start, length)
        target = sum_any.at[here]
        if parts[p][0] == len(summed) - 1:
            target = small_any.at[rows_at(start - main, length)]
        copy = pltpu.make_async_copy(out_ref.at[here], target, store.at[p, s])
        copy.start()
        return copy

    tokens, width = mixed_ref.shape
    tile = tokens // 4
    tiles = [slice(i * tile, (i + 1) * tile) for i in range(4)]

    def mix_most():
        for copy in loads:
            copy.wait()
        for here in tiles:
            ff = collect(segment(code_ref[here, :], room, 0, cut), ff_ref[...])
            y_ref[here, :] += gate_ref[here, :] * ff

    def mix_rest():
        stores = []
        for i, here in enumerate(tiles):
            total = y_ref[here, :]
            if extra:
                tail = tail_ref[...]
                tail = [tail[c * extra : (c + 1) * extra] for c in range(width // TILE)]
                more = collect(rank_ref[here, :], jnp.concatenate(tail, axis=1))
                total = total + gate_ref[here, :] * more
            mixed_ref[here, :] = total.astype(LOW)
            stores.append(
                pltpu.make_async_copy(mixed_ref.at[here], mixed_any.at[here], local.at[2 + i])
            )
            stores[i].start()
        return stores

    moving = [halving(p, 0) for p in range(len(parts))]
    for copy in moving:
        copy.start()
    sent, stores = [], []
    for s in range(bits):
        if s == 1:
            mix_most()
        for p, (ref, at, first, step, order) in enumerate(parts):
            length = step * (n >> (s + 1))
            if s == 0:
                kept[p].wait()
            moving[p].wait_recv()
            sent.append(moving[p])
            base[p] = base[p] + partner_of(me, order[s])[0] * length
            last = s + 1 == bits
            target = out_ref if last else work_ref
            if p >= full and last:
                target = tail_ref

            def add(
                i, _, start=base[p], target=target, arrived=got_at[p], step=step,
                to=0 if p >= full and last else base[p],
            ):
                got = got_ref[rows_at(arrived + i * step, step), :].astype(jnp.float32)
                mine = work_ref[rows_at(start + i * step, step), :].astype(jnp.float32)
                target[rows_at(to + i * step, step), :] = (mine + got).astype(LOW)
                return 0

            lax.fori_loop(0, length // step, add, 0)
            got_at[p] += length
            if not last:
                moving[p] = halving(p, s + 1)
                moving[p].start()
            elif p < full:
                moving[p] = doubling(p, s)
                moving[p].start()
                stores.append(keep_out(p, bits, base[p], step))
    for s in reversed(range(bits)):
        if s == min(1, bits - 1):
            stores += mix_rest()
        for p, (ref, at, first, step, order) in enumerate(parts[:full]):
            length = step * (n >> (s + 1))
            moving[p].wait_recv()
            sent.append(moving[p])
            bit = partner_of(me, order[s])[0]
            arrived = base[p] + (1 - 2 * bit) * length
            base[p] = base[p] - bit * length
            if s > 0:
                moving[p] = doubling(p, s - 1)
                moving[p].start()
            stores.append(keep_out(p, s, arrived, length))
    for copy in sent:
        copy.wait_send()
    for copy in stores:
        copy.wait()


def all_sum(xs, code, gate, rank, ff, y, room, ff_more):
    cores = lax.axis_size("exp")
    n = lax.axis_size(AXES)
    extra = plan(room)[2]
    heights = [a.shape[0] for a in xs]
    if any(h % (16 * n) for h in heights):
        xs = [jnp.concatenate(xs[:-1], axis=0), xs[-1]]
        heights = [a.shape[0] for a in xs]
    total, small = sum(heights), heights[-1]
    bits, parts = sum_parts(n, heights)
    count = len(parts)
    rows = total
    tokens, width = y.shape
    tail = []
    if extra:
        xs = xs + [ff_more]
        heights = heights + [ff_more.shape[0]]
        rows += ff_more.shape[0]
        count += 1
        tail = [pltpu.VMEM((extra * width // TILE, TILE), LOW)]
    buffer = pltpu.VMEM((rows, TILE), LOW)
    vmem = pl.BlockSpec(memory_space=pltpu.VMEM)
    anywhere = pl.BlockSpec(memory_space=pl.ANY)
    return pl.pallas_call(
        functools.partial(sum_kernel, cores, n, room, heights, extra),
        out_shape=[
            jax.ShapeDtypeStruct((tokens, width), LOW),
            jax.ShapeDtypeStruct((total - small, TILE), LOW),
            jax.ShapeDtypeStruct((small, TILE), LOW),
        ],
        in_specs=[vmem] * 3 + [anywhere] * (2 + len(xs)),
        out_specs=[anywhere] * 3,
        scratch_shapes=[
            pltpu.VMEM((total, TILE), LOW), buffer, buffer, pltpu.VMEM(ff.shape, LOW),
            pltpu.VMEM(y.shape, jnp.float32), pltpu.VMEM(y.shape, LOW), *tail,
            pltpu.SemaphoreType.DMA((count, 2 * bits)),
            pltpu.SemaphoreType.DMA((count, 2 * bits)),
            pltpu.SemaphoreType.DMA((6,)),
            pltpu.SemaphoreType.DMA((count,)),
            pltpu.SemaphoreType.DMA((count, bits + 1)),
        ],
        compiler_params=params(60, collective_id=1, has_side_effects=True),
        name="all_sum",
    )(code, gate, rank, ff, y, *xs)


def local(
    tokens, lengths, expert_ids, slots, w_query, w_key, w_value, w_output,
    gain_attn, gain_ffn, bias_table, w_router, w_in, w_out, cotangent,
):
    rows, seq, width = tokens.shape
    count = rows * seq
    buckets, heads = bias_table.shape
    head = width // heads
    experts = w_router.shape[1]
    devices = lax.axis_size(AXES)
    room = max(4, 2 * count // experts)
    me = lax.axis_index(AXES)
    x = tokens.reshape(count, width)
    g = cotangent.reshape(count, width)
    gain_one = gain_attn.reshape(1, width)
    gain_two = gain_ffn.reshape(1, width)
    mine = (jnp.arange(experts, dtype=jnp.int32) == me).astype(jnp.float32).reshape(1, experts)

    segments, cut, extra = plan(room)
    code_r, rank_r, g_out, g_extra = route(expert_ids, slots, g, experts, room)
    g_in = exchange(g_out, devices)
    code_r, gain_one, bias_table = lax.optimization_barrier((code_r, gain_one, bias_table))

    code_c, rank_c, marks = columns(code_r, experts, room)
    normed_t, projected = project(x, gain_one, w_query, w_key, w_value)
    near, far = bias_tiles(bias_table)
    joined, weights = attention_forward(lengths, projected, near, far, rows, seq, heads, head)
    y, gate, *h_out = after_attention(
        joined, x, w_output, gain_two, code_c, w_router, code_r, rank_r,
        g_extra, marks, experts, room,
    )
    code = code_c.reshape(-1)
    expert = code // room
    place = code - expert * room
    rest = jnp.where((code >= 0) & (place >= cut), expert * extra + place - cut, experts * extra)

    def experts_on(h, g_rows, low, high, *more):
        return expert_rows(h, g_rows, mine, w_router, w_in[0], w_out[0], experts, low, high, *more)

    parts, grad_router, ff_more, crowded = [], 0.0, None, None
    if extra:
        h_more, g_more, flag = h_out[-3:]
        h_out = h_out[:-3]
        crowded = flag[0, 0] > 0
        h_more, g_more, g_in = lax.optimization_barrier((h_more, g_more, g_in))

        def exchange_rest(_):
            rms = lax.rsqrt(jnp.mean(y * y, axis=-1, keepdims=True) + EPSILON)
            h = (y * rms * gain_two).astype(LOW)
            empty = jnp.zeros((experts * extra, width), LOW)
            send = lambda a: exchange(empty.at[rest].set(a, mode="drop"), devices)
            return False, send(h), send(g)

        _, h_more, g_more = lax.while_loop(
            lambda held: held[0], exchange_rest, (crowded, h_more, g_more)
        )
        h_out[0], h_more, g_more = lax.optimization_barrier((h_out[0], h_more, g_more))
    h_out, g_in = lax.optimization_barrier((h_out, g_in))
    g_in = g_in.reshape(devices, cut, width)
    h_in = [exchange(h_out[0], devices)]
    for h in h_out[1:]:
        h, h_in[-1] = lax.optimization_barrier((h, h_in[-1]))
        h_in.append(exchange(h, devices))
    ffs, dx_back, dx = [], [], None
    if extra:
        ff_more, dx, hid, da, x_t, dff_t, routed = experts_on(
            h_more, g_more.reshape(devices, extra, width), 0, extra, room - cut, 2 * extra
        )
        ff_more = ff_more.reshape(devices, extra, width)
        parts.append((x_t, dff_t, hid, da))
        grad_router = grad_router + routed
    for m, (low, high) in enumerate(segments):
        held = (0, 2 * extra, dx) if extra and not m else ()
        ff, dx, hid, da, x_t, dff_t, routed = experts_on(h_in[m], g_in, low, high, *held)
        if m + 1 < len(segments):
            dx, h_in[m + 1] = lax.optimization_barrier((dx, h_in[m + 1]))
        if m:
            dx, dx_back[-1] = lax.optimization_barrier((dx, dx_back[-1]))
        dx_back.append(exchange(dx.reshape(-1, width), devices))
        ffs.append(ff.reshape(devices, high - low, width))
        parts.append((x_t, dff_t, hid, da))
        grad_router = grad_router + routed
    grad_in, grad_out = expert_weights(parts)
    grad_router = grad_router.reshape(experts, width // TILE, TILE)
    small = jnp.swapaxes(grad_router, 0, 1).reshape(-1, TILE)
    ff, ff_packed = ffs[0], small
    if extra:
        ff = jnp.concatenate([ffs[1], ffs[0]], axis=1)
        bits = devices.bit_length() - 1
        ff_packed = ff_more.reshape((2,) * bits + (extra, width // TILE, TILE))
        order = tuple(reversed(range(bits))) + (bits + 1, bits, bits + 2)
        ff_packed = jnp.transpose(ff_packed, order).reshape(-1, TILE)
    ff = ff.reshape(devices * cut, width)
    dx_back, grad_in, grad_out, ff, ff_packed, small = lax.optimization_barrier(
        (dx_back, grad_in, grad_out, ff, ff_packed, small)
    )
    ff_back = exchange(ff, devices)

    dy, do, grad_output, grad_gain_two = before_attention(
        dx_back, code_c, y, g, gain_two, w_output, joined, room
    )
    lines = width // TILE
    small_rows = small.shape[0] + -(-2 * lines // 16) * 16 + -(-heads // 16) * 16
    small_rows = -(-small_rows // (16 * devices)) * 16 * devices
    grad_tokens, packed, small = attention_backward(
        projected, do, joined, weights, normed_t, w_query, w_key, w_value, x, dy, gain_one,
        small, grad_gain_two, rows, seq, heads, head, small_rows,
    )
    mixed, summed, small = all_sum(
        [packed.reshape(-1, TILE), grad_output, small], code_c, gate, rank_c, ff_back, y, room, ff_packed
    )
    if extra:

        def mix_all(_):
            spare = exchange(ff_more.reshape(-1, width), devices)
            first = jnp.where((code >= 0) & (place < cut), expert * cut + place, devices * cut)
            take = lambda a, index: jnp.take(a, index, axis=0, mode="fill", fill_value=0)
            ff = take(ff_back, first) + take(spare, rest)
            return False, (y + gate * ff.astype(jnp.float32)).astype(LOW)

        _, mixed = lax.while_loop(lambda held: held[0], mix_all, (crowded, mixed))
    *grads, router_t, gain_grad_one, gain_grad_two, table, mixed = unpack(summed, small, mixed, experts, heads, buckets)
    return (
        mixed.reshape(rows, seq, width),
        grad_tokens.reshape(rows, seq, width),
        *grads,
        gain_grad_one, gain_grad_two, table.T, router_t.T,
        grad_in,
        grad_out,
    )


def solution(mesh):
    split = P(AXES)
    in_specs = (split,) * 4 + (P(),) * 8 + (split,) * 3
    out_specs = (split,) * 2 + (P(),) * 8 + (split,) * 2
    return jax.shard_map(local, mesh=mesh, in_specs=in_specs, out_specs=out_specs, check_vma=False)
```
